32 devices in a mesh: groups: 1, ep: 8 (over z, core), tp: 4 (over y, x).
Axes of the slice: x: 2, y: 2, z: 4, core: 2. Of those that a mesh axis runs over, the one named last changes fastest.
Arguments:
- hidden: bfloat16 [2048, 3584], P(('groups', 'ep')), may hold values from -2.1 to 2.1
- moe_gain: float32 [3584], replicated, may hold values from 0.5 to 1.5
- route_logits: float32 [2048, 8], P(('groups', 'ep')), may hold values from -2 to 2
- routes: int32 [2048, 8], P(('groups', 'ep')), may hold values from 0 to 255, as said below
- gate_weight: bfloat16 [8, 3584, 1024], P('ep', None, 'tp'), may hold values from -0.09375 to 0.09375
- up_weight: bfloat16 [8, 3584, 1024], P('ep', None, 'tp'), may hold values from -0.09375 to 0.09375
- down_weight: bfloat16 [8, 1024, 3584], P('ep', 'tp'), may hold values from -0.5 to 0.5
- attn_gain: float32 [3584], P('tp'), may hold values from 0.5 to 1.5
- latent_weight: bfloat16 [3584, 576], P('tp'), may hold values from -0.09375 to 0.09375
- latent_gain: float32 [512], replicated, may hold values from 0.5 to 1.5
- positions: int32 [2048], P(('groups', 'ep')), may hold values from 0 to 32767
- owners: int32 [2048], P(('groups', 'ep')), may hold values from 0 to 3, as said below
Outputs:
- cache_latent: bfloat16 [2048, 512], P(('groups', 'ep', 'tp'))
- cache_rotary: bfloat16 [2048, 64], P(('groups', 'ep', 'tp'))
The draws below stay inside these ranges and needn't reach their ends.
Inputs may be any that keep to these rules, and one draw needn't show every extreme that they name: `routes`: each row names 8 different experts. Within each ep block of 256 rows every expert below 8 is named by at most 16 rows, and one such expert is named by exactly 16 rows in every block. `owners`: within each aligned block of 64 rows each owner is named by at most 16 rows, and one owner reaches 16 in every block.
All inputs are finite; a program needn't handle non-finite values.
Results may differ from the reference program's by a relative error of at most 0.014.
Values may be sent and summed in bfloat16 or wider, within the bound.
No kernel may reach another device: no remote copies, remote signals or barrier semaphores. Data moves between devices by JAX's collectives and lax.ppermute only.
A program may use at most 64 MiB of HBM per device.

```python
import math
import jax
import jax.numpy as jnp
from jax import lax

D = 3584
MOE_FF = 1024
EXPERTS = 256
TOP = 8
KV_RANK = 512
ROPE_DIM = 64
CAP = 16
TOK_EP = 256
LIVE = 8
TOKENS = 2048
KV_ROWS = 64
KCAP = 16
CACHE_WIDTH = 576
N_EP = 8
N_TP = 4


def draw_hidden(key, part):
    key = jax.random.fold_in(key, 29)
    keys = jax.random.split(key, 3)
    place = jnp.arange(D, dtype=jnp.float32) / D
    row_scale = jnp.exp(jax.random.uniform(keys[0], (TOKENS, 1), minval=0.0, maxval=math.log(10.0)))
    column_scale = 3.0 ** place * jnp.exp(jax.random.uniform(keys[1], (D,), minval=0.0, maxval=math.log(3.4)))
    base = jnp.clip(jax.random.normal(keys[2], (TOKENS, D)), -4.0, 4.0)
    return (0.005 * base * column_scale[None, :] * row_scale).astype(jnp.bfloat16)


def draw_down_weight(key, part):
    key = jax.random.fold_in(key, 31)
    keys = jax.random.split(key, 2)
    place = jnp.arange(D, dtype=jnp.float32) / D
    level = 3.0 ** (2.0 * place - 1.0) * jax.random.uniform(keys[0], (D,), minval=0.7, maxval=1.3)
    base = jnp.clip(jax.random.normal(keys[1], (LIVE, MOE_FF, D)), -4.0, 4.0)
    return (base * level[None, None, :] * MOE_FF ** (-0.5)).astype(jnp.bfloat16)


def draw_routes(key, part):
    key = jax.random.fold_in(key, 17)
    keys = jax.random.split(key, 6)
    blocks = TOKENS // TOK_EP
    live_count = N_EP
    hottest = jax.random.randint(keys[0], (), 0, live_count)
    raw_loads = jax.random.randint(keys[2], (blocks, live_count), 0, 1 << 16)
    loads = CAP // 2 + raw_loads % (CAP - CAP // 2 + 1)
    loads = jnp.where(jnp.arange(live_count, dtype=jnp.int32)[None, :] == hottest, CAP, loads).astype(jnp.int32)
    starts = (jnp.cumsum(loads, axis=1) - loads).astype(jnp.int32)
    seat_rank = jnp.arange(CAP, dtype=jnp.int32)
    seat_index = starts[:, :, None] + seat_rank[None, None, :]
    active = seat_rank[None, None, :] < loads[:, :, None]
    orders = jax.vmap(lambda sub: jax.random.permutation(sub, TOK_EP))(jax.random.split(keys[3], blocks)).astype(jnp.int32)
    token_pick = jnp.take_along_axis(orders, (seat_index % TOK_EP).reshape(blocks, live_count * CAP), axis=1)
    token_pick = jnp.where(active, token_pick.reshape(blocks, live_count, CAP), TOK_EP)
    column = seat_index // TOK_EP
    block_index = jnp.broadcast_to(jnp.arange(blocks, dtype=jnp.int32)[:, None, None], token_pick.shape)
    expert_index = jnp.broadcast_to(jnp.arange(live_count, dtype=jnp.int32)[None, :, None], token_pick.shape)
    table = jnp.full((blocks, TOK_EP, TOP), -1, jnp.int32)
    table = table.at[block_index, token_pick, column].set(expert_index, mode='drop').reshape(TOKENS, TOP)
    spare = EXPERTS - live_count
    scores = jax.random.randint(keys[4], (TOKENS, spare), 0, 1 << 16) * spare + jnp.arange(spare, dtype=jnp.int32)[None, :]
    filler = lax.top_k(scores, TOP)[1].astype(jnp.int32) + live_count
    merged = jnp.where(table >= 0, table, filler)
    shuffle = jax.random.randint(keys[5], (TOKENS, TOP), 0, 1 << 16) * TOP + jnp.arange(TOP, dtype=jnp.int32)[None, :]
    ordering = jnp.argsort(shuffle, axis=1)
    return jnp.take_along_axis(merged, ordering, axis=1).astype(jnp.int32)


def draw_owners(key, part):
    key = jax.random.fold_in(key, 23)
    keys = jax.random.split(key, 3)
    blocks = TOKENS // KV_ROWS
    hottest = jax.random.randint(keys[0], (), 0, N_TP)
    others = jax.vmap(lambda sub: jax.random.permutation(sub, N_TP - 1))(jax.random.split(keys[1], blocks)).astype(jnp.int32)
    others = others + (others >= hottest).astype(jnp.int32)
    place = jnp.arange(KV_ROWS, dtype=jnp.int32)
    cycled = others[:, (place - KCAP) % (N_TP - 1)]
    values = jnp.where(place[None, :] < KCAP, hottest, cycled).astype(jnp.int32)
    orders = jax.vmap(lambda sub: jax.random.permutation(sub, KV_ROWS))(jax.random.split(keys[2], blocks)).astype(jnp.int32)
    return jnp.take_along_axis(values, orders, axis=1).reshape(TOKENS).astype(jnp.int32)


def plant(drawn, stream_key, least, high):
    extent = drawn.shape
    spot = [jax.random.randint(jax.random.fold_in(stream_key, axis), (), 0, extent[axis]) for axis in range(len(extent))]
    drawn = drawn.at[tuple(spot)].set(least)
    longest = extent.index(max(extent))
    spot[longest] = (spot[longest] + 1) % extent[longest]
    return drawn.at[tuple(spot)].set(high)


def steps_of(key, extent, cuts, smallest, top_value):
    factor_of = 1.0
    for dim, blocks in cuts:
        heights = jax.random.uniform(jax.random.fold_in(jax.random.fold_in(key, 6), dim), (blocks,), jnp.float32, smallest / len(cuts), top_value / len(cuts))
        factor_of = factor_of * jnp.repeat(jnp.exp(heights), extent[dim] // blocks).reshape((-1,) + (1,) * (len(extent) - 1 - dim))
    return factor_of


def centred(rng, shape, deviation, bound, shards=(), held_as=jnp.bfloat16):
    entries = jax.random.normal(rng, shape, jnp.float32) * deviation
    if len(shards) > 0:
        entries = steps_of(rng, shape, shards, -0.22, 0.18) * entries
    return jnp.clip(entries, min=-bound, max=bound).astype(held_as)


def setup_inputs(seed: int = 0, part: int = 0) -> dict:
    arg_keys = jax.random.split(jax.random.key(seed), 13)
    part_keys = jax.random.split(jax.random.fold_in(arg_keys[12], part), 13)
    hidden = draw_hidden(jax.random.fold_in(jax.random.fold_in(arg_keys[12], part), 71), part)
    moe_gain = jnp.clip(jax.random.uniform(arg_keys[1], (D,), jnp.float32, 0.5, 1.5), 0.5, 1.5)
    route_logits = centred(part_keys[2], (TOKENS, TOP), 0.5, 2.0, ((0, 8),), jnp.float32)
    routes = draw_routes(jax.random.fold_in(jax.random.fold_in(arg_keys[12], part), 71), part)
    gate_weight = centred(arg_keys[4], (LIVE, D, MOE_FF), D ** -0.5, 0.09375, ((0, 8), (2, 4)))
    up_weight = centred(arg_keys[5], (LIVE, D, MOE_FF), D ** -0.5, 0.09375, ((0, 8), (2, 4)))
    down_weight = draw_down_weight(jax.random.fold_in(arg_keys[12], 71), part)
    attn_gain = jnp.clip(0.5 + 1.0 * jax.random.uniform(arg_keys[7], (D,), jnp.float32) ** steps_of(arg_keys[7], (D,), ((0, 4),), -0.2, 0.2), 0.5, 1.5)
    latent_weight = centred(arg_keys[8], (D, CACHE_WIDTH), D ** -0.5, 0.09375, ((0, 4),))
    latent_gain = jnp.clip(jax.random.uniform(arg_keys[9], (KV_RANK,), jnp.float32, 0.5, 1.5), 0.5, 1.5)
    positions = plant(jax.random.randint(part_keys[10], (TOKENS,), 0, 32768), jax.random.fold_in(part_keys[10], 1), 0, 32767).astype(jnp.int32)
    owners = draw_owners(jax.random.fold_in(jax.random.fold_in(arg_keys[12], part), 71), part)
    return {"hidden": hidden, "moe_gain": moe_gain, "route_logits": route_logits, "routes": routes, "gate_weight": gate_weight, "up_weight": up_weight, "down_weight": down_weight, "attn_gain": attn_gain, "latent_weight": latent_weight, "latent_gain": latent_gain, "positions": positions, "owners": owners}


eps = 1e-06
route_scale = 2.5
rope_base = 10000.0

def rms_scale(values):
    return lax.rsqrt(lax.optimization_barrier(jnp.mean(values * values, axis=-1, keepdims=True)) + eps)

def rotate(keys, token_positions):
    half = keys.shape[-1] // 2
    freqs = rope_base ** (-jnp.arange(half, dtype=jnp.float32) / half)
    angles = token_positions.astype(jnp.float32)[:, None] * freqs[None, :]
    cosine = jnp.cos(angles)
    sine = jnp.sin(angles)
    first = keys[:, :half]
    second = keys[:, half:]
    return jnp.concatenate([first * cosine - second * sine, second * cosine + first * sine], axis=-1)

def route_slots(block_routes, expert_count, capacity):
    row_count, width = block_routes.shape
    flat_ids = block_routes.reshape(row_count * width)
    onehot = (flat_ids[:, None] == jnp.arange(expert_count, dtype=jnp.int32)[None, :]).astype(jnp.int32)
    earlier = (jnp.cumsum(onehot, axis=0) - onehot).astype(jnp.int32)
    ranking = lax.optimization_barrier(jnp.sum(earlier * onehot, axis=1)).astype(jnp.int32)
    slot_of = jnp.where(flat_ids < expert_count, flat_ids * capacity + ranking, -1).astype(jnp.int32)
    return slot_of.reshape(row_count, width)

def reference(hidden, moe_gain, route_logits, routes, gate_weight, up_weight, down_weight, attn_gain, latent_weight, latent_gain, positions, owners):
    live_count = N_EP
    token_total = hidden.shape[0]
    wide = hidden.astype(jnp.float32)
    moe_input = (wide * rms_scale(wide) * moe_gain).astype(jnp.bfloat16)
    affinity = jax.nn.sigmoid(route_logits)
    route_weight = (route_scale * affinity / lax.optimization_barrier(jnp.sum(affinity, axis=1, keepdims=True))).astype(jnp.bfloat16)
    slots = jax.vmap(lambda part_routes: route_slots(part_routes, live_count, CAP))(routes.reshape(N_EP, TOK_EP, TOP))
    slot_ids = jnp.arange(live_count * CAP, dtype=jnp.int32)
    pair_token = jnp.arange(TOK_EP * TOP, dtype=jnp.int32) // TOP

    def slot_tokens(block_slots):
        match = block_slots.reshape(TOK_EP * TOP)[:, None] == slot_ids[None, :]
        filled = jnp.any(match, axis=0)
        token_of = lax.optimization_barrier(jnp.sum(jnp.where(match, pair_token[:, None], 0), axis=0)).astype(jnp.int32)
        return (token_of, filled)
    token_of, filled = jax.vmap(slot_tokens)(slots)
    global_token = (token_of + (jnp.arange(N_EP, dtype=jnp.int32) * TOK_EP)[:, None]).astype(jnp.int32)
    dispatched = jnp.where(filled[:, :, None], moe_input[global_token], jnp.zeros((), jnp.bfloat16))
    per_expert = dispatched.reshape(N_EP, live_count, CAP, D).transpose(1, 0, 2, 3).reshape(live_count, N_EP * CAP, D)
    share = MOE_FF // N_TP

    def expert(operands):
        rows_in, gate_part, up_part, down_part = operands
        gate = jnp.dot(rows_in, gate_part, preferred_element_type=jnp.float32)
        upper = jnp.dot(rows_in, up_part, preferred_element_type=jnp.float32)
        inner = (jax.nn.silu(gate) * upper).astype(jnp.bfloat16)
        total = jnp.zeros((rows_in.shape[0], D), jnp.float32)
        for piece in range(N_TP):
            term = jnp.dot(inner[:, piece * share:(piece + 1) * share], down_part[piece * share:(piece + 1) * share], preferred_element_type=jnp.float32)
            total = total + lax.optimization_barrier(term.astype(jnp.bfloat16)).astype(jnp.float32)
        return total.astype(jnp.bfloat16)
    expert_out = lax.map(expert, (per_expert, gate_weight, up_weight, down_weight))
    out_flat = expert_out.reshape(live_count * N_EP * CAP, D)
    flat_slots = slots.reshape(token_total, TOP)
    block_of = (jnp.arange(token_total, dtype=jnp.int32) // TOK_EP)[:, None]
    row_index = (flat_slots // CAP * N_EP + block_of) * CAP + flat_slots % CAP
    mixed = jnp.zeros((token_total, D), jnp.float32)
    for route in range(TOP):
        active = flat_slots[:, route] >= 0
        picked = out_flat[jnp.where(active, row_index[:, route], 0).astype(jnp.int32)]
        term = route_weight[:, route:route + 1].astype(jnp.float32) * picked.astype(jnp.float32)
        mixed = mixed + jnp.where(active[:, None], term, jnp.zeros((), jnp.float32))
    state = wide + mixed
    normed = (state * rms_scale(state) * attn_gain).astype(jnp.bfloat16)
    width_share = D // N_TP
    cache = jnp.zeros((token_total, KV_RANK + ROPE_DIM), jnp.float32)
    for piece in range(N_TP):
        term = jnp.dot(normed[:, piece * width_share:(piece + 1) * width_share], latent_weight[piece * width_share:(piece + 1) * width_share], preferred_element_type=jnp.float32)
        cache = cache + lax.optimization_barrier(term.astype(jnp.bfloat16)).astype(jnp.float32)
    latent_part = cache[:, :KV_RANK]
    latent = (latent_part * rms_scale(latent_part) * latent_gain).astype(jnp.bfloat16)
    rotary = rotate(cache[:, KV_RANK:], positions).astype(jnp.bfloat16)
    source_rows = TOK_EP // N_TP
    seat_cap = max(2, source_rows // 4)
    owner_grid = owners.reshape(N_EP, N_TP, source_rows)
    owner_hot = (owner_grid[..., None] == jnp.arange(N_TP, dtype=jnp.int32)).astype(jnp.int32)
    before = (jnp.cumsum(owner_hot, axis=2) - owner_hot).astype(jnp.int32)
    seat = (owner_grid * seat_cap + lax.optimization_barrier(jnp.sum(before * owner_hot, axis=3))).astype(jnp.int32)
    seat_match = seat[..., None] == jnp.arange(N_TP * seat_cap, dtype=jnp.int32)
    seat_found = jnp.any(seat_match, axis=2)
    seat_row = lax.optimization_barrier(jnp.sum(jnp.where(seat_match, jnp.arange(source_rows, dtype=jnp.int32)[None, None, :, None], 0), axis=2)).astype(jnp.int32)
    global_row = (seat_row + (jnp.arange(N_EP, dtype=jnp.int32) * TOK_EP)[:, None, None] + (jnp.arange(N_TP, dtype=jnp.int32) * source_rows)[None, :, None]).astype(jnp.int32)

    def place(values):
        width = values.shape[1]
        picked = jnp.where(seat_found[..., None], values[global_row], jnp.zeros((), jnp.bfloat16))
        arranged = picked.reshape(N_EP, N_TP, N_TP, seat_cap, width).transpose(0, 2, 1, 3, 4)
        return arranged.reshape(N_EP * N_TP * N_TP * seat_cap, width)
    return (place(latent), place(rotary))
```

```python
import functools

import jax
import jax.numpy as jnp
from jax import lax
from jax.experimental import pallas as pl
from jax.experimental.pallas import tpu as pltpu
from jax.sharding import PartitionSpec as P

CAP = 16
EPS = 1e-06
ROUTE_SCALE = 2.5
ROPE_BASE = 10000.0
BF16 = jnp.bfloat16
F32 = jnp.float32
VMEM_LIMIT = 40 * 1024 * 1024


def columns_of(ref, index, count, share):
    if share % 128 == 0:
        return ref[:, pl.ds(pl.multiple_of(index * share, 128), share)]
    out = ref[:, 0:share]
    for q in range(1, count):
        out = jnp.where(index == q, ref[:, q * share : (q + 1) * share], out)
    return out


def dispatch_kernel(n_ep, n_tp, routes_ref, logits_ref, hidden_ref, gain_ref, *refs):
    outs, combine_ref, pick_ref, rows_ref = refs[:n_ep], refs[n_ep], refs[n_ep + 1], refs[n_ep + 2]
    me = lax.axis_index("ep")
    part = lax.axis_index("tp")
    tokens, width = hidden_ref.shape
    share = width // n_tp
    routes = routes_ref[...]
    affinity = jax.nn.sigmoid(logits_ref[...])
    weight = ROUTE_SCALE * affinity / jnp.sum(affinity, axis=0, keepdims=True)
    weight = weight.astype(BF16).astype(F32)
    expert = lax.broadcasted_iota(jnp.int32, (n_ep, tokens), 0)
    hit = jnp.zeros((n_ep, tokens), F32)
    gain_of = jnp.zeros((n_ep, tokens), F32)
    for k in range(routes.shape[0]):
        same = routes[k : k + 1, :] == expert
        hit = jnp.where(same, 1.0, hit)
        gain_of = jnp.where(same, weight[k : k + 1, :], gain_of)
    earlier = lax.broadcasted_iota(jnp.int32, (tokens, tokens), 0) < lax.broadcasted_iota(
        jnp.int32, (tokens, tokens), 1
    )
    rank = jnp.dot(hit.astype(BF16), earlier.astype(F32).astype(BF16), preferred_element_type=F32)
    rank = jnp.where(hit > 0, rank, -1.0)
    place = lax.broadcasted_iota(jnp.int32, (CAP, tokens), 0).astype(F32)
    for e in range(n_ep):
        match = rank[e : e + 1, :] == place
        rows = slice(e * CAP, (e + 1) * CAP)
        pick_ref[rows, :] = jnp.where(match, 1.0, 0.0).astype(BF16)
        combine_ref[rows, :] = jnp.where(match, gain_of[e : e + 1, :], 0.0).astype(BF16)
    pick = pick_ref[...]
    square = jnp.zeros((n_ep * CAP, 1), F32)
    step = 512 if width % 512 == 0 else width
    for c in range(0, width, step):
        got = jnp.dot(pick, hidden_ref[:, c : c + step], preferred_element_type=F32)
        square = square + jnp.sum(got * got, axis=1, keepdims=True)
    scale = lax.rsqrt(square / width + EPS)
    got = jnp.dot(pick, columns_of(hidden_ref, part, n_tp, share), preferred_element_type=F32)
    rows_ref[...] = (got * scale * columns_of(gain_ref, part, n_tp, share)).astype(BF16)
    for d in range(n_ep):
        outs[d][...] = rows_ref[pl.ds(pl.multiple_of((me ^ d) * CAP, CAP), CAP), :]


def expert_kernel(n_tp, *refs):
    rows = refs[:n_tp]
    gate_ref, up_ref, down_ref = refs[n_tp : n_tp + 3]
    outs = refs[n_tp + 3 : 2 * n_tp + 3]
    part = lax.axis_index("tp")
    share = rows[0].shape[1]
    gate = upper = None
    for d in range(n_tp):
        value = rows[d][...]
        depth = pl.ds(pl.multiple_of((part ^ d) * share, CAP), share)
        g = jnp.dot(value, gate_ref[depth, :], preferred_element_type=F32)
        u = jnp.dot(value, up_ref[depth, :], preferred_element_type=F32)
        gate = g if gate is None else gate + g
        upper = u if upper is None else upper + u
    inner = (gate / (1.0 + jnp.exp(-gate)) * upper).astype(BF16)
    for d in range(n_tp):
        down = columns_of(down_ref, part ^ d, n_tp, share)
        outs[d][...] = jnp.dot(inner, down, preferred_element_type=F32).astype(BF16)


def sum_kernel(n_tp, n_ep, *refs):
    parts, outs = refs[:n_tp], refs[n_tp:]
    for d in range(n_ep):
        rows = slice(d * CAP, (d + 1) * CAP)
        total = parts[0][rows, :].astype(F32)
        for other in parts[1:]:
            total = total + other[rows, :].astype(F32)
        outs[d][...] = total.astype(BF16)


def seats_kernel(n_tp, seat_cap, owners_ref, positions_ref, code_ref, at_ref):
    part = lax.axis_index("tp")
    tokens = owners_ref.shape[1]
    source_rows = tokens // n_tp
    owners = owners_ref[...]
    owner = lax.broadcasted_iota(jnp.int32, (n_tp, tokens), 0)
    hot = jnp.where(owners == owner, 1.0, 0.0)
    first = lax.broadcasted_iota(jnp.int32, (tokens, tokens), 0)
    second = lax.broadcasted_iota(jnp.int32, (tokens, tokens), 1)
    earlier = jnp.where((first < second) & (first // source_rows == second // source_rows), 1.0, 0.0)
    before = jnp.dot(hot.astype(BF16), earlier.astype(BF16), preferred_element_type=F32)
    seat = jnp.sum(before * hot, axis=0, keepdims=True).astype(jnp.int32)
    source = lax.broadcasted_iota(jnp.int32, (1, tokens), 1) // source_rows
    code = owners * (n_tp * seat_cap) + source * seat_cap + seat
    code_ref[...] = code
    mine = lax.broadcasted_iota(jnp.int32, (n_tp * seat_cap, tokens), 0) + part * (n_tp * seat_cap)
    held = jnp.where(mine == code, positions_ref[...].astype(F32), 0.0)
    at_ref[...] = jnp.sum(held, axis=1, keepdims=True)


def cache_kernel(n_ep, n_tp, cache_width, *refs):
    pieces = refs[:n_ep]
    combine_ref, hidden_ref, gain_ref, weight_ref, code_ref = refs[n_ep : n_ep + 5]
    outs = refs[n_ep + 5 : n_ep + 5 + n_tp]
    back_ref, wide_ref = refs[n_ep + 5 + n_tp :]
    me = lax.axis_index("ep")
    part = lax.axis_index("tp")
    tokens, width = hidden_ref.shape
    share = width // n_tp
    for d in range(n_ep):
        back_ref[pl.ds(pl.multiple_of((me ^ d) * CAP, CAP), CAP), :] = pieces[d][...]
    mixed = lax.dot_general(
        combine_ref[...], back_ref[...], (((0,), (0,)), ((), ())), preferred_element_type=F32
    )
    state = columns_of(hidden_ref, part, n_tp, share).astype(F32) + mixed
    square = jnp.sum(state * state, axis=1, keepdims=True)
    scaled = (state * gain_ref[...]).astype(BF16)
    value = lax.dot_general(
        scaled, weight_ref[...], (((1,), (1,)), ((), ())), preferred_element_type=F32
    )
    high = square.astype(BF16).astype(F32)
    rest = square - high
    middle = rest.astype(BF16).astype(F32)
    low = rest - middle
    spare = wide_ref.shape[1] - cache_width
    lane = lax.broadcasted_iota(jnp.int32, (tokens, spare), 1)
    extra = jnp.where(lane == 0, high, jnp.where(lane == 1, middle, jnp.where(lane == 2, low, 0.0)))
    wide_ref[:, :cache_width] = value.astype(BF16)
    wide_ref[:, cache_width:] = extra.astype(BF16)
    code = code_ref[...]
    seats = outs[0].shape[0]
    row = lax.broadcasted_iota(jnp.int32, (seats, tokens), 0)
    wide = wide_ref[...]
    for d in range(n_tp):
        pick = jnp.where(row + (part ^ d) * seats == code, 1.0, 0.0).astype(BF16)
        outs[d][...] = jnp.dot(pick, wide, preferred_element_type=F32).astype(BF16)


def finish_kernel(n_tp, width, rank_width, *refs):
    parts = refs[:n_tp]
    gain_ref, cos_ref, sin_ref, latent_ref, rotary_ref = refs[n_tp:]
    total = parts[0][...].astype(F32)
    for other in parts[1:]:
        total = total + other[...].astype(F32)
    half = cos_ref.shape[1]
    cache_width = rank_width + 2 * half
    square = jnp.sum(total[:, cache_width : cache_width + 3], axis=1, keepdims=True)
    cache = total[:, :cache_width] * lax.rsqrt(square / width + EPS)
    latent = cache[:, :rank_width]
    scale = lax.rsqrt(jnp.mean(latent * latent, axis=1, keepdims=True) + EPS)
    latent_ref[...] = (latent * scale * gain_ref[...]).astype(BF16)
    first = cache[:, rank_width : rank_width + half]
    second = cache[:, rank_width + half :]
    cosine, sine = cos_ref[...], sin_ref[...]
    rotary_ref[:, :half] = (first * cosine - second * sine).astype(BF16)
    rotary_ref[:, half:] = (second * cosine + first * sine).astype(BF16)


def call(kernel, out_shape, args, scratch=(), flops=0):
    moved = sum(a.size * a.dtype.itemsize for a in args)
    return pl.pallas_call(
        kernel,
        out_shape=out_shape,
        in_specs=[pl.BlockSpec(memory_space=pltpu.VMEM)] * len(args),
        out_specs=jax.tree.map(lambda _: pl.BlockSpec(memory_space=pltpu.VMEM), out_shape),
        scratch_shapes=list(scratch),
        compiler_params=pltpu.CompilerParams(vmem_limit_bytes=VMEM_LIMIT),
        cost_estimate=pl.CostEstimate(flops=flops, bytes_accessed=moved, transcendentals=0),
    )(*args)


def exchange(value, axis, size, d):
    return lax.ppermute(value, axis, [(i, i ^ d) for i in range(size)])


def on_device(
    hidden,
    moe_gain,
    route_logits,
    routes,
    gate_weight,
    up_weight,
    down_weight,
    attn_gain,
    latent_weight,
    latent_gain,
    positions,
    owners,
):
    n_ep = lax.axis_size("ep")
    n_tp = lax.axis_size("tp")
    tokens, width = hidden.shape
    share = width // n_tp
    slots = n_ep * CAP
    seat_cap = max(2, tokens // n_tp // 4)
    seats = n_tp * seat_cap
    rank_width = latent_gain.shape[0]
    cache_width = latent_weight.shape[1]
    half = (cache_width - rank_width) // 2
    wide = (cache_width + 3 + 127) // 128 * 128
    struct = jax.ShapeDtypeStruct

    *outgoing, combine = call(
        functools.partial(dispatch_kernel, n_ep, n_tp),
        [struct((CAP, share), BF16)] * n_ep + [struct((slots, tokens), BF16)],
        (routes.T, route_logits.T, hidden, moe_gain[None, :]),
        [pltpu.VMEM((slots, tokens), BF16), pltpu.VMEM((slots, share), BF16)],
        flops=4 * slots * tokens * width,
    )
    code, at = call(
        functools.partial(seats_kernel, n_tp, seat_cap),
        [struct((1, tokens), jnp.int32), struct((seats, 1), F32)],
        (owners[None, :], positions[None, :]),
    )
    freqs = ROPE_BASE ** (-jnp.arange(half, dtype=F32) / half)
    angles = at * freqs[None, :]
    cosine, sine = jnp.cos(angles), jnp.sin(angles)

    arrived = [outgoing[0]] + [exchange(outgoing[d], "ep", n_ep, d) for d in range(1, n_ep)]
    mine = jnp.concatenate(arrived, axis=0)
    shares = [mine] + [exchange(mine, "tp", n_tp, d) for d in range(1, n_tp)]
    terms = call(
        functools.partial(expert_kernel, n_tp),
        [struct((slots, share), BF16)] * n_tp,
        (*shares, gate_weight[0], up_weight[0], down_weight[0]),
        flops=2 * slots * width * gate_weight.shape[2] * 3,
    )
    terms = [terms[0]] + [exchange(terms[d], "tp", n_tp, d) for d in range(1, n_tp)]
    done = call(
        functools.partial(sum_kernel, n_tp, n_ep),
        [struct((CAP, share), BF16)] * n_ep,
        terms,
    )
    back = [done[0]] + [exchange(done[d], "ep", n_ep, d) for d in range(1, n_ep)]
    partial = call(
        functools.partial(cache_kernel, n_ep, n_tp, cache_width),
        [struct((seats, wide), BF16)] * n_tp,
        (*back, combine, hidden, attn_gain[None, :], latent_weight.T, code),
        [pltpu.VMEM((slots, share), BF16), pltpu.VMEM((tokens, wide), BF16)],
        flops=2 * tokens * share * (slots + cache_width),
    )
    partial = [partial[0]] + [exchange(partial[d], "tp", n_tp, d) for d in range(1, n_tp)]
    return tuple(
        call(
            functools.partial(finish_kernel, n_tp, width, rank_width),
            [struct((seats, rank_width), BF16), struct((seats, 2 * half), BF16)],
            (*partial, latent_gain[None, :], cosine, sine),
        )
    )


def solution(mesh):
    placed = (
        P(("groups", "ep"), None),
        P(),
        P(("groups", "ep"), None),
        P(("groups", "ep"), None),
        P("ep", None, "tp"),
        P("ep", None, "tp"),
        P("ep", "tp", None),
        P("tp"),
        P("tp", None),
        P(),
        P(("groups", "ep")),
        P(("groups", "ep")),
    )
    return jax.shard_map(
        on_device,
        mesh=mesh,
        in_specs=placed,
        out_specs=(P(("groups", "ep", "tp"), None), P(("groups", "ep", "tp"), None)),
        check_vma=False,
    )
```

```python
import functools

import jax
import jax.numpy as jnp
from jax import lax
from jax.experimental import pallas as pl
from jax.experimental.pallas import tpu as pltpu
from jax.sharding import PartitionSpec as P

CAP = 16
EPS = 1e-06
ROUTE_SCALE = 2.5
ROPE_BASE = 10000.0
BF16 = jnp.bfloat16
F32 = jnp.float32
VMEM_LIMIT = 40 * 1024 * 1024


def columns_of(ref, index, count, share):
    if share % 128 == 0:
        return ref[:, pl.ds(pl.multiple_of(index * share, 128), share)]
    out = ref[:, 0:share]
    for q in range(1, count):
        out = jnp.where(index == q, ref[:, q * share : (q + 1) * share], out)
    return out


def dispatch_kernel(
    n_ep,
    n_tp,
    routes_hbm,
    logits_hbm,
    hidden_hbm,
    gain_hbm,
    own_ref,
    core_ref,
    far_ref,
    combine_ref,
    routes_ref,
    logits_ref,
    hidden_ref,
    gain_ref,
    pick_ref,
    head_ref,
    sems,
):
    me = lax.axis_index("ep")
    part = lax.axis_index("tp")
    tokens, width = hidden_ref.shape
    share = width // n_tp
    step = 512 if width % 512 == 0 else width
    starts = range(0, width, step)
    small = [
        pltpu.make_async_copy(routes_hbm, routes_ref, sems.at[0]),
        pltpu.make_async_copy(logits_hbm, logits_ref, sems.at[1]),
        pltpu.make_async_copy(gain_hbm, gain_ref.at[0], sems.at[2]),
    ]
    large = [
        pltpu.make_async_copy(
            hidden_hbm.at[:, c : c + step], hidden_ref.at[:, c : c + step], sems.at[3 + i]
        )
        for i, c in enumerate(starts)
    ]
    for copy in small + large:
        copy.start()
    small[0].wait()
    small[1].wait()
    routes = routes_ref[...]
    affinity = jax.nn.sigmoid(logits_ref[...])
    weight = ROUTE_SCALE * affinity / jnp.sum(affinity, axis=0, keepdims=True)
    weight = weight.astype(BF16).astype(F32)
    expert = lax.broadcasted_iota(jnp.int32, (n_ep, tokens), 0) ^ me
    hit = jnp.zeros((n_ep, tokens), F32)
    gain_of = jnp.zeros((n_ep, tokens), F32)
    for k in range(routes.shape[0]):
        same = routes[k : k + 1, :] == expert
        hit = jnp.where(same, 1.0, hit)
        gain_of = jnp.where(same, weight[k : k + 1, :], gain_of)
    earlier = lax.broadcasted_iota(jnp.int32, (tokens, tokens), 0) < lax.broadcasted_iota(
        jnp.int32, (tokens, tokens), 1
    )
    rank = jnp.dot(hit.astype(BF16), earlier.astype(F32).astype(BF16), preferred_element_type=F32)
    rank = jnp.where(hit > 0, rank, -1.0)
    place = lax.broadcasted_iota(jnp.int32, (CAP, tokens), 0).astype(F32)
    order = [0, 1, *range(2, n_ep, 2), *range(3, n_ep, 2)]
    for i, d in enumerate(order):
        match = rank[d : d + 1, :] == place
        pick_ref[i * CAP : (i + 1) * CAP, :] = jnp.where(match, 1.0, 0.0).astype(BF16)
        combine_ref[d * CAP : (d + 1) * CAP, :] = jnp.where(
            match, gain_of[d : d + 1, :], 0.0
        ).astype(BF16)
    pick = pick_ref[...]
    head = 2 * CAP
    square = jnp.zeros((n_ep * CAP, 1), F32)
    for copy, c in zip(large, starts):
        copy.wait()
        got = jnp.dot(pick, hidden_ref[:, c : c + step], preferred_element_type=F32)
        square = square + jnp.sum(got * got, axis=1, keepdims=True)
        head_ref[:, c : c + step] = got[:head]
    small[2].wait()
    scale = lax.rsqrt(square / width + EPS)
    near = (head_ref[...] * scale[:head] * gain_ref[...]).astype(BF16)
    got = jnp.dot(pick[head:], columns_of(hidden_ref, part, n_tp, share), preferred_element_type=F32)
    far = (got * scale[head:] * columns_of(gain_ref, part, n_tp, share)).astype(BF16)
    count = far_ref.shape[0]
    own_ref[...] = near[:CAP]
    far_ref[...] = far[:count]
    core_ref[:count, :] = far[count:]
    for q in range(n_tp):
        core_ref[count + q * CAP : count + (q + 1) * CAP, :] = near[
            CAP:, q * share : (q + 1) * share
        ]


def first_kernel(
    n_tp,
    own_ref,
    core_ref,
    mine_ref,
    gate_hbm,
    up_hbm,
    down_hbm,
    gate_ref,
    up_ref,
    down_ref,
    gate_sum_ref,
    up_sum_ref,
    head_ref,
    sems,
):
    part = lax.axis_index("tp")
    share = mine_ref.shape[1]
    count = core_ref.shape[0] - n_tp * CAP
    copies = [
        pltpu.make_async_copy(gate_hbm, gate_ref, sems.at[0]),
        pltpu.make_async_copy(up_hbm, up_ref, sems.at[1]),
        pltpu.make_async_copy(down_hbm, down_ref, sems.at[2]),
    ]
    for copy in copies:
        copy.start()
    head_ref[:CAP, :] = own_ref[...]
    for q in range(n_tp):
        head_ref[CAP:, q * share : (q + 1) * share] = core_ref[
            count + q * CAP : count + (q + 1) * CAP, :
        ]
    depth = pl.ds(pl.multiple_of(part * share, CAP), share)
    head = 2 * CAP
    for copy, weight_ref, sum_ref in zip(
        copies, (gate_ref, up_ref), (gate_sum_ref, up_sum_ref)
    ):
        copy.wait()
        sum_ref[:head, :] = jnp.dot(head_ref[...], weight_ref[...], preferred_element_type=F32)
        sum_ref[head:, :] = jnp.dot(
            mine_ref[...], weight_ref[depth, :], preferred_element_type=F32
        )
    copies[2].wait()


def expert_kernel(n_tp, *refs):
    rows = refs[: n_tp - 1]
    gate_ref, up_ref, down_ref, gate_sum_ref, up_sum_ref = refs[n_tp - 1 : n_tp + 4]
    outs = refs[n_tp + 4 : 2 * n_tp + 4]
    part = lax.axis_index("tp")
    count, share = rows[0].shape
    head = gate_sum_ref.shape[0] - count
    gate = gate_sum_ref[head:, :]
    upper = up_sum_ref[head:, :]
    for d in range(1, n_tp):
        value = rows[d - 1][...]
        depth = pl.ds(pl.multiple_of((part ^ d) * share, CAP), share)
        gate = gate + jnp.dot(value, gate_ref[depth, :], preferred_element_type=F32)
        upper = upper + jnp.dot(value, up_ref[depth, :], preferred_element_type=F32)
    gate = jnp.concatenate([gate_sum_ref[:head, :], gate], axis=0)
    upper = jnp.concatenate([up_sum_ref[:head, :], upper], axis=0)
    inner = (gate / (1.0 + jnp.exp(-gate)) * upper).astype(BF16)
    for d in range(n_tp):
        down = columns_of(down_ref, part ^ d, n_tp, share)
        outs[d][...] = jnp.dot(inner, down, preferred_element_type=F32).astype(BF16)


def sum_kernel(n_tp, *refs):
    parts, outs = refs[:n_tp], refs[n_tp:]
    size = outs[0].shape[0]
    for d, out in enumerate(outs):
        rows = slice(d * size, (d + 1) * size)
        total = parts[0][rows, :].astype(F32)
        for other in parts[1:]:
            total = total + other[rows, :].astype(F32)
        out[...] = total.astype(BF16)


def seats_kernel(
    n_tp, seat_cap, owners_ref, positions_ref, combine_ref, hidden_ref, rows_ref, mix_ref, at_ref
):
    part = lax.axis_index("tp")
    tokens = owners_ref.shape[1]
    source_rows = tokens // n_tp
    owners = owners_ref[...] ^ part
    owner = lax.broadcasted_iota(jnp.int32, (n_tp, tokens), 0)
    hot = jnp.where(owners == owner, 1.0, 0.0)
    first = lax.broadcasted_iota(jnp.int32, (tokens, tokens), 0)
    second = lax.broadcasted_iota(jnp.int32, (tokens, tokens), 1)
    earlier = jnp.where((first < second) & (first // source_rows == second // source_rows), 1.0, 0.0)
    before = jnp.dot(hot.astype(BF16), earlier.astype(BF16), preferred_element_type=F32)
    seat = jnp.sum(before * hot, axis=0, keepdims=True).astype(jnp.int32)
    source = lax.broadcasted_iota(jnp.int32, (1, tokens), 1) // source_rows
    code = owners * (n_tp * seat_cap) + source * seat_cap + seat
    seats = n_tp * seat_cap
    held = lax.broadcasted_iota(jnp.int32, (n_tp * seats, tokens), 0) == code
    pick = jnp.where(held, 1.0, 0.0).astype(BF16)
    rows_ref[...] = jnp.dot(pick, hidden_ref[...], preferred_element_type=F32).astype(BF16)
    mix_ref[...] = lax.dot_general(
        pick, combine_ref[...], (((1,), (1,)), ((), ())), preferred_element_type=F32
    ).astype(BF16)
    place = jnp.where(held[:seats], positions_ref[...].astype(F32), 0.0)
    at_ref[...] = jnp.sum(place, axis=1, keepdims=True)


def cache_kernel(n_z, n_tp, cache_width, *refs):
    pieces, core_ref = refs[:n_z], refs[n_z]
    mix_ref, rows_ref, gain_ref, weight_ref = refs[n_z + 1 : n_z + 5]
    outs, back_ref = refs[n_z + 5 : n_z + 5 + n_tp], refs[n_z + 5 + n_tp]
    for d in range(n_z):
        at = 2 * d * CAP
        back_ref[at : at + CAP, :] = pieces[d][:CAP, :]
        back_ref[at + CAP : at + 2 * CAP, :] = core_ref[d * CAP : (d + 1) * CAP, :]
    mixed = jnp.dot(mix_ref[...], back_ref[...], preferred_element_type=F32)
    state = rows_ref[...].astype(F32) + mixed
    square = jnp.sum(state * state, axis=1, keepdims=True)
    scaled = (state * gain_ref[...]).astype(BF16)
    value = lax.dot_general(
        scaled, weight_ref[...], (((1,), (1,)), ((), ())), preferred_element_type=F32
    ).astype(BF16)
    high = square.astype(BF16).astype(F32)
    rest = square - high
    middle = rest.astype(BF16).astype(F32)
    low = rest - middle
    seats, wide = outs[0].shape
    lane = lax.broadcasted_iota(jnp.int32, (square.shape[0], wide - cache_width), 1)
    extra = jnp.where(lane == 0, high, jnp.where(lane == 1, middle, jnp.where(lane == 2, low, 0.0)))
    extra = extra.astype(BF16)
    for d in range(n_tp):
        outs[d][:, :cache_width] = value[d * seats : (d + 1) * seats]
        outs[d][:, cache_width:] = extra[d * seats : (d + 1) * seats]


def finish_kernel(n_tp, width, rank_width, *refs):
    parts = refs[:n_tp]
    gain_ref, cos_ref, sin_ref, latent_ref, rotary_ref = refs[n_tp:]
    total = parts[0][...].astype(F32)
    for other in parts[1:]:
        total = total + other[...].astype(F32)
    half = cos_ref.shape[1]
    cache_width = rank_width + 2 * half
    square = jnp.sum(total[:, cache_width : cache_width + 3], axis=1, keepdims=True)
    cache = total[:, :cache_width] * lax.rsqrt(square / width + EPS)
    latent = cache[:, :rank_width]
    scale = lax.rsqrt(jnp.mean(latent * latent, axis=1, keepdims=True) + EPS)
    latent_ref[...] = (latent * scale * gain_ref[...]).astype(BF16)
    first = cache[:, rank_width : rank_width + half]
    second = cache[:, rank_width + half :]
    cosine, sine = cos_ref[...], sin_ref[...]
    rotary_ref[:, :half] = (first * cosine - second * sine).astype(BF16)
    rotary_ref[:, half:] = (second * cosine + first * sine).astype(BF16)


def call(kernel, out_shape, args, scratch=(), flops=0, hbm=()):
    moved = sum(a.size * a.dtype.itemsize for a in args)
    vmem = pl.BlockSpec(memory_space=pltpu.VMEM)
    args = [
        pltpu.with_memory_space_constraint(a, pltpu.HBM) if i in hbm else a
        for i, a in enumerate(args)
    ]
    return pl.pallas_call(
        kernel,
        out_shape=out_shape,
        in_specs=[
            pl.BlockSpec(memory_space=pltpu.HBM) if i in hbm else vmem for i in range(len(args))
        ],
        out_specs=[vmem] * len(out_shape),
        scratch_shapes=list(scratch),
        compiler_params=pltpu.CompilerParams(vmem_limit_bytes=VMEM_LIMIT),
        cost_estimate=pl.CostEstimate(flops=flops, bytes_accessed=moved, transcendentals=0),
    )(*args)


def swap(value, axis, d):
    return lax.ppermute(value, axis, [(i, i ^ d) for i in range(lax.axis_size(axis))])


def on_device(
    hidden,
    moe_gain,
    route_logits,
    routes,
    gate_weight,
    up_weight,
    down_weight,
    attn_gain,
    latent_weight,
    latent_gain,
    positions,
    owners,
):
    n_ep = lax.axis_size("ep")
    n_tp = lax.axis_size("tp")
    n_z = n_ep // 2
    tokens, width = hidden.shape
    share = width // n_tp
    ff = gate_weight.shape[2]
    slots = n_ep * CAP
    far_rows = (n_z - 1) * CAP
    seat_cap = max(2, tokens // n_tp // 4)
    seats = n_tp * seat_cap
    rank_width = latent_gain.shape[0]
    cache_width = latent_weight.shape[1]
    half = (cache_width - rank_width) // 2
    wide = (cache_width + 3 + 127) // 128 * 128
    struct = jax.ShapeDtypeStruct
    chunks = width // 512 if width % 512 == 0 else 1

    own, to_core, far, combine = call(
        functools.partial(dispatch_kernel, n_ep, n_tp),
        [
            struct((CAP, width), BF16),
            struct((far_rows + n_tp * CAP, share), BF16),
            struct((far_rows, share), BF16),
            struct((slots, tokens), BF16),
        ],
        (routes.T, route_logits.T, hidden, moe_gain),
        [
            pltpu.VMEM(routes.T.shape, jnp.int32),
            pltpu.VMEM(routes.T.shape, F32),
            pltpu.VMEM(hidden.shape, BF16),
            pltpu.VMEM((1, width), F32),
            pltpu.VMEM((slots, tokens), BF16),
            pltpu.VMEM((2 * CAP, width), F32),
            pltpu.SemaphoreType.DMA((3 + chunks,)),
        ],
        flops=4 * slots * tokens * width,
        hbm=(0, 1, 2, 3),
    )
    hidden_share = lax.dynamic_slice_in_dim(hidden, lax.axis_index("tp") * share, share, 1)
    rows, mix, at = call(
        functools.partial(seats_kernel, n_tp, seat_cap),
        [
            struct((n_tp * seats, share), BF16),
            struct((n_tp * seats, slots), BF16),
            struct((seats, 1), F32),
        ],
        (owners[None, :], positions[None, :], combine, hidden_share),
        flops=2 * n_tp * seats * tokens * (share + slots),
    )
    freqs = ROPE_BASE ** (-jnp.arange(half, dtype=F32) / half)
    angles = at * freqs[None, :]
    cosine, sine = jnp.cos(angles), jnp.sin(angles)

    from_core = swap(to_core, "ep", 1)
    arrived = []
    for d in range(1, n_z):
        at_rows = slice((d - 1) * CAP, d * CAP)
        both = jnp.concatenate([far[at_rows], from_core[at_rows]], axis=0)
        arrived.append(swap(both, "ep", 2 * d))
    mine = jnp.concatenate(arrived, axis=0)
    others = [swap(mine, "tp", d) for d in range(1, n_tp)]
    gate_w, up_w, down_w = gate_weight[0], up_weight[0], down_weight[0]
    *loaded, gate_sum, up_sum = call(
        functools.partial(first_kernel, n_tp),
        [struct(w.shape, BF16) for w in (gate_w, up_w, down_w)] + [struct((slots, ff), F32)] * 2,
        (own, from_core, mine, gate_w, up_w, down_w),
        [pltpu.VMEM((2 * CAP, width), BF16), pltpu.SemaphoreType.DMA((3,))],
        flops=2 * slots * width * ff,
        hbm=(3, 4, 5),
    )
    terms = call(
        functools.partial(expert_kernel, n_tp),
        [struct((slots, share), BF16)] * n_tp,
        (*others, *loaded, gate_sum, up_sum),
        flops=2 * slots * width * ff * 3,
    )
    terms = [terms[0]] + [swap(terms[d], "tp", d) for d in range(1, n_tp)]
    done = call(
        functools.partial(sum_kernel, n_tp),
        [struct((2 * CAP, share), BF16)] * n_z,
        terms,
    )
    back = [done[0]] + [swap(done[d], "ep", 2 * d) for d in range(1, n_z)]
    crossed = swap(jnp.concatenate([piece[CAP:] for piece in back], axis=0), "ep", 1)
    partial = call(
        functools.partial(cache_kernel, n_z, n_tp, cache_width),
        [struct((seats, wide), BF16)] * n_tp,
        (*back, crossed, mix, rows, attn_gain[None, :], latent_weight.T),
        [pltpu.VMEM((slots, share), BF16)],
        flops=2 * n_tp * seats * share * (slots + cache_width),
    )
    partial = [partial[0]] + [swap(partial[d], "tp", d) for d in range(1, n_tp)]
    return tuple(
        call(
            functools.partial(finish_kernel, n_tp, width, rank_width),
            [struct((seats, rank_width), BF16), struct((seats, 2 * half), BF16)],
            (*partial, latent_gain[None, :], cosine, sine),
        )
    )


def solution(mesh):
    placed = (
        P(("groups", "ep"), None),
        P(),
        P(("groups", "ep"), None),
        P(("groups", "ep"), None),
        P("ep", None, "tp"),
        P("ep", None, "tp"),
        P("ep", "tp", None),
        P("tp"),
        P("tp", None),
        P(),
        P(("groups", "ep")),
        P(("groups", "ep")),
    )
    return jax.shard_map(
        on_device,
        mesh=mesh,
        in_specs=placed,
        out_specs=(P(("groups", "ep", "tp"), None), P(("groups", "ep", "tp"), None)),
        check_vma=False,
    )
```

```python
import functools

import jax
import jax.numpy as jnp
from jax import lax
from jax.experimental import pallas as pl
from jax.experimental.pallas import tpu as pltpu
from jax.sharding import PartitionSpec as P

CAP = 16
EPS = 1e-06
ROUTE_SCALE = 2.5
ROPE_BASE = 10000.0
BF16 = jnp.bfloat16
F32 = jnp.float32
VMEM_LIMIT = 40 * 1024 * 1024


def columns_of(ref, index, count, share):
    if share % 128 == 0:
        return ref[:, pl.ds(pl.multiple_of(index * share, 128), share)]
    out = ref[:, 0:share]
    for q in range(1, count):
        out = jnp.where(index == q, ref[:, q * share : (q + 1) * share], out)
    return out


def dispatch_kernel(
    n_ep,
    n_tp,
    routes_hbm,
    logits_hbm,
    hidden_hbm,
    gain_hbm,
    own_ref,
    core_ref,
    far_ref,
    combine_ref,
    routes_ref,
    logits_ref,
    hidden_ref,
    gain_ref,
    pick_ref,
    head_ref,
    sems,
):
    me = lax.axis_index("ep")
    part = lax.axis_index("tp")
    tokens, width = hidden_ref.shape
    share = width // n_tp
    step = 512 if width % 512 == 0 else width
    starts = range(0, width, step)
    small = [
        pltpu.make_async_copy(routes_hbm, routes_ref, sems.at[0]),
        pltpu.make_async_copy(logits_hbm, logits_ref, sems.at[1]),
        pltpu.make_async_copy(gain_hbm, gain_ref.at[0], sems.at[2]),
    ]
    large = [
        pltpu.make_async_copy(
            hidden_hbm.at[:, c : c + step], hidden_ref.at[:, c : c + step], sems.at[3 + i]
        )
        for i, c in enumerate(starts)
    ]
    for copy in small + large:
        copy.start()
    small[0].wait()
    small[1].wait()
    routes = routes_ref[...]
    affinity = jax.nn.sigmoid(logits_ref[...])
    weight = ROUTE_SCALE * affinity / jnp.sum(affinity, axis=0, keepdims=True)
    weight = weight.astype(BF16).astype(F32)
    expert = lax.broadcasted_iota(jnp.int32, (n_ep, tokens), 0) ^ me
    hit = jnp.zeros((n_ep, tokens), F32)
    gain_of = jnp.zeros((n_ep, tokens), F32)
    for k in range(routes.shape[0]):
        same = routes[k : k + 1, :] == expert
        hit = jnp.where(same, 1.0, hit)
        gain_of = jnp.where(same, weight[k : k + 1, :], gain_of)
    earlier = lax.broadcasted_iota(jnp.int32, (tokens, tokens), 0) < lax.broadcasted_iota(
        jnp.int32, (tokens, tokens), 1
    )
    rank = jnp.dot(hit.astype(BF16), earlier.astype(F32).astype(BF16), preferred_element_type=F32)
    rank = jnp.where(hit > 0, rank, -1.0)
    place = lax.broadcasted_iota(jnp.int32, (CAP, tokens), 0).astype(F32)
    order = [0, 1, *range(2, n_ep, 2), *range(3, n_ep, 2)]
    for i, d in enumerate(order):
        match = rank[d : d + 1, :] == place
        pick_ref[i * CAP : (i + 1) * CAP, :] = jnp.where(match, 1.0, 0.0).astype(BF16)
        combine_ref[d * CAP : (d + 1) * CAP, :] = jnp.where(
            match, gain_of[d : d + 1, :], 0.0
        ).astype(BF16)
    pick = pick_ref[...]
    head = 2 * CAP
    square = jnp.zeros((n_ep * CAP, 1), F32)
    for copy in large:
        copy.wait()
    for c in starts:
        got = jnp.dot(pick, hidden_ref[:, c : c + step], preferred_element_type=F32)
        square = square + jnp.sum(got * got, axis=1, keepdims=True)
        head_ref[:, c : c + step] = got[:head]
    small[2].wait()
    scale = lax.rsqrt(square / width + EPS)
    near = (head_ref[...] * scale[:head] * gain_ref[...]).astype(BF16)
    got = jnp.dot(pick[head:], columns_of(hidden_ref, part, n_tp, share), preferred_element_type=F32)
    far = (got * scale[head:] * columns_of(gain_ref, part, n_tp, share)).astype(BF16)
    count = far_ref.shape[0]
    own_ref[...] = near[:CAP]
    far_ref[...] = far[:count]
    core_ref[:count, :] = far[count:]
    for q in range(n_tp):
        core_ref[count + q * CAP : count + (q + 1) * CAP, :] = near[
            CAP:, q * share : (q + 1) * share
        ]


def first_kernel(
    n_tp,
    own_ref,
    core_ref,
    mine_ref,
    gate_hbm,
    up_hbm,
    down_hbm,
    gate_ref,
    up_ref,
    down_ref,
    gate_sum_ref,
    up_sum_ref,
    head_ref,
    sems,
):
    part = lax.axis_index("tp")
    share = mine_ref.shape[1]
    count = core_ref.shape[0] - n_tp * CAP
    copies = [
        pltpu.make_async_copy(gate_hbm, gate_ref, sems.at[0]),
        pltpu.make_async_copy(up_hbm, up_ref, sems.at[1]),
        pltpu.make_async_copy(down_hbm, down_ref, sems.at[2]),
    ]
    for copy in copies:
        copy.start()
    head_ref[:CAP, :] = own_ref[...]
    for q in range(n_tp):
        head_ref[CAP:, q * share : (q + 1) * share] = core_ref[
            count + q * CAP : count + (q + 1) * CAP, :
        ]
    depth = pl.ds(pl.multiple_of(part * share, CAP), share)
    head = 2 * CAP
    for copy, weight_ref, sum_ref in zip(
        copies, (gate_ref, up_ref), (gate_sum_ref, up_sum_ref)
    ):
        copy.wait()
        sum_ref[:head, :] = jnp.dot(head_ref[...], weight_ref[...], preferred_element_type=F32)
        sum_ref[head:, :] = jnp.dot(
            mine_ref[...], weight_ref[depth, :], preferred_element_type=F32
        )
    copies[2].wait()


def expert_kernel(n_tp, *refs):
    rows = refs[: n_tp - 1]
    gate_ref, up_ref, down_ref, gate_sum_ref, up_sum_ref = refs[n_tp - 1 : n_tp + 4]
    out_ref = refs[n_tp + 4]
    part = lax.axis_index("tp")
    count, share = rows[0].shape
    head = gate_sum_ref.shape[0] - count
    gate = gate_sum_ref[head:, :]
    upper = up_sum_ref[head:, :]
    for d in range(1, n_tp):
        value = rows[d - 1][...]
        depth = pl.ds(pl.multiple_of((part ^ d) * share, CAP), share)
        gate = gate + jnp.dot(value, gate_ref[depth, :], preferred_element_type=F32)
        upper = upper + jnp.dot(value, up_ref[depth, :], preferred_element_type=F32)
    gate = jnp.concatenate([gate_sum_ref[:head, :], gate], axis=0)
    upper = jnp.concatenate([up_sum_ref[:head, :], upper], axis=0)
    inner = (gate / (1.0 + jnp.exp(-gate)) * upper).astype(BF16)
    for q in range(n_tp):
        down = down_ref[:, q * share : (q + 1) * share]
        out_ref[q] = jnp.dot(inner, down, preferred_element_type=F32).astype(BF16)


def sum_kernel(parts_ref, *outs):
    size = outs[0].shape[0]
    for d, out in enumerate(outs):
        rows = slice(d * size, (d + 1) * size)
        total = parts_ref[0, rows, :].astype(F32)
        for q in range(1, parts_ref.shape[0]):
            total = total + parts_ref[q, rows, :].astype(F32)
        out[...] = total.astype(BF16)


def seats_kernel(
    n_tp, seat_cap, owners_ref, positions_ref, combine_ref, hidden_ref, rows_ref, mix_ref, at_ref
):
    part = lax.axis_index("tp")
    tokens = owners_ref.shape[1]
    source_rows = tokens // n_tp
    owners = owners_ref[...]
    owner = lax.broadcasted_iota(jnp.int32, (n_tp, tokens), 0)
    hot = jnp.where(owners == owner, 1.0, 0.0)
    first = lax.broadcasted_iota(jnp.int32, (tokens, tokens), 0)
    second = lax.broadcasted_iota(jnp.int32, (tokens, tokens), 1)
    earlier = jnp.where((first < second) & (first // source_rows == second // source_rows), 1.0, 0.0)
    before = jnp.dot(hot.astype(BF16), earlier.astype(BF16), preferred_element_type=F32)
    seat = jnp.sum(before * hot, axis=0, keepdims=True).astype(jnp.int32)
    source = lax.broadcasted_iota(jnp.int32, (1, tokens), 1) // source_rows
    code = owners * (n_tp * seat_cap) + source * seat_cap + seat
    seats = n_tp * seat_cap
    held = lax.broadcasted_iota(jnp.int32, (n_tp * seats, tokens), 0) == code
    pick = jnp.where(held, 1.0, 0.0).astype(BF16)
    rows_ref[...] = jnp.dot(pick, hidden_ref[...], preferred_element_type=F32).astype(BF16)
    mix_ref[...] = lax.dot_general(
        pick, combine_ref[...], (((1,), (1,)), ((), ())), preferred_element_type=F32
    ).astype(BF16)
    mine = lax.broadcasted_iota(jnp.int32, (seats, tokens), 0) + part * seats
    place = jnp.where(mine == code, positions_ref[...].astype(F32), 0.0)
    at_ref[...] = jnp.sum(place, axis=1, keepdims=True)


def cache_kernel(n_z, n_tp, cache_width, *refs):
    pieces, core_ref = refs[:n_z], refs[n_z]
    mix_ref, rows_ref, gain_ref, weight_ref = refs[n_z + 1 : n_z + 5]
    out_ref, back_ref = refs[n_z + 5 :]
    for d in range(n_z):
        at = 2 * d * CAP
        back_ref[at : at + CAP, :] = pieces[d][:CAP, :]
        back_ref[at + CAP : at + 2 * CAP, :] = core_ref[d * CAP : (d + 1) * CAP, :]
    mixed = jnp.dot(mix_ref[...], back_ref[...], preferred_element_type=F32)
    state = rows_ref[...].astype(F32) + mixed
    square = jnp.sum(state * state, axis=1, keepdims=True)
    scaled = (state * gain_ref[...]).astype(BF16)
    value = lax.dot_general(
        scaled, weight_ref[...], (((1,), (1,)), ((), ())), preferred_element_type=F32
    ).astype(BF16)
    high = square.astype(BF16).astype(F32)
    rest = square - high
    middle = rest.astype(BF16).astype(F32)
    low = rest - middle
    seats, wide = out_ref.shape[1:]
    lane = lax.broadcasted_iota(jnp.int32, (square.shape[0], wide - cache_width), 1)
    extra = jnp.where(lane == 0, high, jnp.where(lane == 1, middle, jnp.where(lane == 2, low, 0.0)))
    extra = extra.astype(BF16)
    for d in range(n_tp):
        out_ref[d, :, :cache_width] = value[d * seats : (d + 1) * seats]
        out_ref[d, :, cache_width:] = extra[d * seats : (d + 1) * seats]


def finish_kernel(
    width, rank_width, parts_ref, gain_ref, cos_ref, sin_ref, latent_ref, rotary_ref
):
    total = parts_ref[0].astype(F32)
    for q in range(1, parts_ref.shape[0]):
        total = total + parts_ref[q].astype(F32)
    half = cos_ref.shape[1]
    cache_width = rank_width + 2 * half
    square = jnp.sum(total[:, cache_width : cache_width + 3], axis=1, keepdims=True)
    cache = total[:, :cache_width] * lax.rsqrt(square / width + EPS)
    latent = cache[:, :rank_width]
    scale = lax.rsqrt(jnp.mean(latent * latent, axis=1, keepdims=True) + EPS)
    latent_ref[...] = (latent * scale * gain_ref[...]).astype(BF16)
    first = cache[:, rank_width : rank_width + half]
    second = cache[:, rank_width + half :]
    cosine, sine = cos_ref[...], sin_ref[...]
    rotary_ref[:, :half] = (first * cosine - second * sine).astype(BF16)
    rotary_ref[:, half:] = (second * cosine + first * sine).astype(BF16)


def call(kernel, out_shape, args, scratch=(), flops=0, hbm=()):
    moved = sum(a.size * a.dtype.itemsize for a in args)
    vmem = pl.BlockSpec(memory_space=pltpu.VMEM)
    args = [
        pltpu.with_memory_space_constraint(a, pltpu.HBM) if i in hbm else a
        for i, a in enumerate(args)
    ]
    return pl.pallas_call(
        kernel,
        out_shape=out_shape,
        in_specs=[
            pl.BlockSpec(memory_space=pltpu.HBM) if i in hbm else vmem for i in range(len(args))
        ],
        out_specs=[vmem] * len(out_shape),
        scratch_shapes=list(scratch),
        compiler_params=pltpu.CompilerParams(vmem_limit_bytes=VMEM_LIMIT),
        cost_estimate=pl.CostEstimate(flops=flops, bytes_accessed=moved, transcendentals=0),
    )(*args)


def swap(value, axis, d):
    return lax.ppermute(value, axis, [(i, i ^ d) for i in range(lax.axis_size(axis))])


def on_device(
    hidden,
    moe_gain,
    route_logits,
    routes,
    gate_weight,
    up_weight,
    down_weight,
    attn_gain,
    latent_weight,
    latent_gain,
    positions,
    owners,
):
    n_ep = lax.axis_size("ep")
    n_tp = lax.axis_size("tp")
    n_z = n_ep // 2
    tokens, width = hidden.shape
    share = width // n_tp
    ff = gate_weight.shape[2]
    slots = n_ep * CAP
    far_rows = (n_z - 1) * CAP
    seat_cap = max(2, tokens // n_tp // 4)
    seats = n_tp * seat_cap
    rank_width = latent_gain.shape[0]
    cache_width = latent_weight.shape[1]
    half = (cache_width - rank_width) // 2
    wide = (cache_width + 3 + 127) // 128 * 128
    struct = jax.ShapeDtypeStruct
    chunks = width // 512 if width % 512 == 0 else 1

    own, to_core, far, combine = call(
        functools.partial(dispatch_kernel, n_ep, n_tp),
        [
            struct((CAP, width), BF16),
            struct((far_rows + n_tp * CAP, share), BF16),
            struct((far_rows, share), BF16),
            struct((slots, tokens), BF16),
        ],
        (routes.T, route_logits.T, hidden, moe_gain),
        [
            pltpu.VMEM(routes.T.shape, jnp.int32),
            pltpu.VMEM(routes.T.shape, F32),
            pltpu.VMEM(hidden.shape, BF16),
            pltpu.VMEM((1, width), F32),
            pltpu.VMEM((slots, tokens), BF16),
            pltpu.VMEM((2 * CAP, width), F32),
            pltpu.SemaphoreType.DMA((3 + chunks,)),
        ],
        flops=4 * slots * tokens * width,
        hbm=(0, 1, 2, 3),
    )
    hidden_share = lax.dynamic_slice_in_dim(hidden, lax.axis_index("tp") * share, share, 1)
    rows, mix, at = call(
        functools.partial(seats_kernel, n_tp, seat_cap),
        [
            struct((n_tp * seats, share), BF16),
            struct((n_tp * seats, slots), BF16),
            struct((seats, 1), F32),
        ],
        (owners[None, :], positions[None, :], combine, hidden_share),
        flops=2 * n_tp * seats * tokens * (share + slots),
    )
    freqs = ROPE_BASE ** (-jnp.arange(half, dtype=F32) / half)
    angles = at * freqs[None, :]
    cosine, sine = jnp.cos(angles), jnp.sin(angles)

    from_core = swap(to_core, "ep", 1)
    arrived = []
    for d in range(1, n_z):
        at_rows = slice((d - 1) * CAP, d * CAP)
        both = jnp.concatenate([far[at_rows], from_core[at_rows]], axis=0)
        arrived.append(swap(both, "ep", 2 * d))
    mine = jnp.concatenate(arrived, axis=0)
    others = [swap(mine, "tp", d) for d in range(1, n_tp)]
    gate_w, up_w, down_w = gate_weight[0], up_weight[0], down_weight[0]
    *loaded, gate_sum, up_sum = call(
        functools.partial(first_kernel, n_tp),
        [struct(w.shape, BF16) for w in (gate_w, up_w, down_w)] + [struct((slots, ff), F32)] * 2,
        (own, from_core, mine, gate_w, up_w, down_w),
        [pltpu.VMEM((2 * CAP, width), BF16), pltpu.SemaphoreType.DMA((3,))],
        flops=2 * slots * width * ff,
        hbm=(3, 4, 5),
    )
    (terms,) = call(
        functools.partial(expert_kernel, n_tp),
        [struct((n_tp, slots, share), BF16)],
        (*others, *loaded, gate_sum, up_sum),
        flops=2 * slots * width * ff * 3,
    )
    terms = lax.all_to_all(terms, "tp", 0, 0, tiled=True)
    done = call(sum_kernel, [struct((2 * CAP, share), BF16)] * n_z, (terms,))
    back = [done[0]] + [swap(done[d], "ep", 2 * d) for d in range(1, n_z)]
    crossed = swap(jnp.concatenate([piece[CAP:] for piece in back], axis=0), "ep", 1)
    (partial,) = call(
        functools.partial(cache_kernel, n_z, n_tp, cache_width),
        [struct((n_tp, seats, wide), BF16)],
        (*back, crossed, mix, rows, attn_gain[None, :], latent_weight.T),
        [pltpu.VMEM((slots, share), BF16)],
        flops=2 * n_tp * seats * share * (slots + cache_width),
    )
    partial = lax.all_to_all(partial, "tp", 0, 0, tiled=True)
    return tuple(
        call(
            functools.partial(finish_kernel, width, rank_width),
            [struct((seats, rank_width), BF16), struct((seats, 2 * half), BF16)],
            (partial, latent_gain[None, :], cosine, sine),
        )
    )


def solution(mesh):
    placed = (
        P(("groups", "ep"), None),
        P(),
        P(("groups", "ep"), None),
        P(("groups", "ep"), None),
        P("ep", None, "tp"),
        P("ep", None, "tp"),
        P("ep", "tp", None),
        P("tp"),
        P("tp", None),
        P(),
        P(("groups", "ep")),
        P(("groups", "ep")),
    )
    return jax.shard_map(
        on_device,
        mesh=mesh,
        in_specs=placed,
        out_specs=(P(("groups", "ep", "tp"), None), P(("groups", "ep", "tp"), None)),
        check_vma=False,
    )
```

```python
import functools

import jax
import jax.numpy as jnp
from jax import lax
from jax.experimental import pallas as pl
from jax.experimental.pallas import tpu as pltpu
from jax.sharding import PartitionSpec as P

CAP = 16
EPS = 1e-06
ROUTE_SCALE = 2.5
ROPE_BASE = 10000.0
BF16 = jnp.bfloat16
F32 = jnp.float32
VMEM_LIMIT = 40 * 1024 * 1024


def columns_of(ref, index, count, share):
    if share % 128 == 0:
        return ref[:, pl.ds(pl.multiple_of(index * share, 128), share)]
    out = ref[:, 0:share]
    for q in range(1, count):
        out = jnp.where(index == q, ref[:, q * share : (q + 1) * share], out)
    return out


def dispatch_kernel(n_ep, n_tp, routes_hbm, logits_hbm, hidden_hbm, gain_hbm, *refs):
    own_ref, core_ref = refs[:2]
    outs, combine_ref = refs[2 : n_ep // 2 + 2], refs[n_ep // 2 + 2]
    routes_ref, logits_ref, hidden_ref, gain_ref, pick_ref, head_ref, sems = refs[n_ep // 2 + 3 :]
    me = lax.axis_index("ep")
    part = lax.axis_index("tp")
    tokens, width = hidden_ref.shape
    share = width // n_tp
    step = 512 if width % 512 == 0 else width
    starts = range(0, width, step)
    small = [
        pltpu.make_async_copy(routes_hbm, routes_ref, sems.at[0]),
        pltpu.make_async_copy(logits_hbm, logits_ref, sems.at[1]),
        pltpu.make_async_copy(gain_hbm, gain_ref.at[0], sems.at[2]),
    ]
    large = [
        pltpu.make_async_copy(
            hidden_hbm.at[:, c : c + step], hidden_ref.at[:, c : c + step], sems.at[3 + i]
        )
        for i, c in enumerate(starts)
    ]
    for copy in small + large:
        copy.start()
    small[0].wait()
    small[1].wait()
    routes = routes_ref[...]
    affinity = jax.nn.sigmoid(logits_ref[...])
    weight = ROUTE_SCALE * affinity / jnp.sum(affinity, axis=0, keepdims=True)
    weight = weight.astype(BF16).astype(F32)
    expert = lax.broadcasted_iota(jnp.int32, (n_ep, tokens), 0) ^ me
    hit = jnp.zeros((n_ep, tokens), F32)
    gain_of = jnp.zeros((n_ep, tokens), F32)
    for k in range(routes.shape[0]):
        same = routes[k : k + 1, :] == expert
        hit = jnp.where(same, 1.0, hit)
        gain_of = jnp.where(same, weight[k : k + 1, :], gain_of)
    earlier = lax.broadcasted_iota(jnp.int32, (tokens, tokens), 0) < lax.broadcasted_iota(
        jnp.int32, (tokens, tokens), 1
    )
    rank = jnp.dot(hit.astype(BF16), earlier.astype(F32).astype(BF16), preferred_element_type=F32)
    rank = jnp.where(hit > 0, rank, -1.0)
    place = lax.broadcasted_iota(jnp.int32, (CAP, tokens), 0).astype(F32)
    for d in range(n_ep):
        match = rank[d : d + 1, :] == place
        rows = slice(d * CAP, (d + 1) * CAP)
        pick_ref[rows, :] = jnp.where(match, 1.0, 0.0).astype(BF16)
        combine_ref[rows, :] = jnp.where(match, gain_of[d : d + 1, :], 0.0).astype(BF16)
    pick = pick_ref[...]
    head = 2 * CAP
    square = jnp.zeros((n_ep * CAP, 1), F32)
    for copy in large:
        copy.wait()
    for c in starts:
        got = jnp.dot(pick, hidden_ref[:, c : c + step], preferred_element_type=F32)
        square = square + jnp.sum(got * got, axis=1, keepdims=True)
        head_ref[:, c : c + step] = got[:head]
    small[2].wait()
    scale = lax.rsqrt(square / width + EPS)
    got = jnp.dot(pick[head:], columns_of(hidden_ref, part, n_tp, share), preferred_element_type=F32)
    rest = (got * scale[head:] * columns_of(gain_ref, part, n_tp, share)).astype(BF16)
    at = 0
    for out in outs:
        out[...] = rest[at : at + out.shape[0]]
        at += out.shape[0]
    near = (head_ref[...] * scale[:head] * gain_ref[...]).astype(BF16)
    own_ref[...] = near[:CAP]
    for q in range(n_tp):
        core_ref[q * CAP : (q + 1) * CAP, :] = near[CAP:, q * share : (q + 1) * share]


def first_kernel(n_tp, own_ref, core_ref, *refs):
    near, mine_ref = refs[:n_tp], refs[n_tp]
    hbm = refs[n_tp + 1 : n_tp + 4]
    loaded = refs[n_tp + 4 : n_tp + 7]
    inner_ref, gate_sum_ref, up_sum_ref, head_ref, sems = refs[n_tp + 7 :]
    part = lax.axis_index("tp")
    share = mine_ref.shape[1]
    copies = [
        pltpu.make_async_copy(source, target, sems.at[i])
        for i, (source, target) in enumerate(zip(hbm, loaded))
    ]
    for copy in copies:
        copy.start()
    head_ref[:CAP, :] = own_ref[...]
    for q in range(n_tp):
        columns = slice(q * share, (q + 1) * share)
        head_ref[CAP : 2 * CAP, columns] = core_ref[q * CAP : (q + 1) * CAP, :]
    sums = []
    for copy, weight_ref, sum_ref in zip(copies, loaded, (gate_sum_ref, up_sum_ref)):
        copy.wait()
        total = jnp.dot(head_ref[...], weight_ref[...], preferred_element_type=F32)
        other = None
        for d in range(n_tp):
            depth = pl.ds(pl.multiple_of((part ^ d) * share, CAP), share)
            term = jnp.dot(near[d][...], weight_ref[depth, :], preferred_element_type=F32)
            other = term if other is None else other + term
        sums.append(jnp.concatenate([total, other], axis=0))
        depth = pl.ds(pl.multiple_of(part * share, CAP), share)
        sum_ref[...] = jnp.dot(mine_ref[...], weight_ref[depth, :], preferred_element_type=F32)
    gate, upper = sums
    inner_ref[...] = (gate / (1.0 + jnp.exp(-gate)) * upper).astype(BF16)
    copies[2].wait()


def expert_kernel(n_tp, *refs):
    rows = refs[: n_tp - 1]
    gate_ref, up_ref, down_ref, near_ref, gate_sum_ref, up_sum_ref = refs[n_tp - 1 : n_tp + 5]
    far_outs = refs[n_tp + 5 : 2 * n_tp + 5]
    near_outs = refs[2 * n_tp + 5 :]
    part = lax.axis_index("tp")
    share = rows[0].shape[1]
    gate = gate_sum_ref[...]
    upper = up_sum_ref[...]
    for d in range(1, n_tp):
        value = rows[d - 1][...]
        depth = pl.ds(pl.multiple_of((part ^ d) * share, CAP), share)
        gate = gate + jnp.dot(value, gate_ref[depth, :], preferred_element_type=F32)
        upper = upper + jnp.dot(value, up_ref[depth, :], preferred_element_type=F32)
    far = (gate / (1.0 + jnp.exp(-gate)) * upper).astype(BF16)
    inner = jnp.concatenate([far, near_ref[...]], axis=0)
    count = far.shape[0]
    for d in range(n_tp):
        down = columns_of(down_ref, part ^ d, n_tp, share)
        out = jnp.dot(inner, down, preferred_element_type=F32).astype(BF16)
        far_outs[d][...] = out[:count]
        near_outs[d][...] = out[count:]


def sum_kernel(n_tp, *refs):
    parts, outs = refs[:n_tp], refs[n_tp:]
    at = 0
    for out in outs:
        rows = slice(at, at + out.shape[0])
        total = parts[0][rows, :].astype(F32)
        for other in parts[1:]:
            total = total + other[rows, :].astype(F32)
        out[...] = total.astype(BF16)
        at += out.shape[0]


def seats_kernel(
    n_tp,
    seat_cap,
    owners_ref,
    positions_ref,
    combine_ref,
    hidden_hbm,
    rows_ref,
    mix_ref,
    at_ref,
    hidden_ref,
    sem,
):
    part = lax.axis_index("tp")
    tokens, share = hidden_ref.shape
    if hidden_hbm.shape[1] != share:
        hidden_hbm = hidden_hbm.at[:, pl.ds(pl.multiple_of(part * share, 128), share)]
    copy = pltpu.make_async_copy(hidden_hbm, hidden_ref, sem)
    copy.start()
    source_rows = tokens // n_tp
    owners = owners_ref[...] ^ part
    owner = lax.broadcasted_iota(jnp.int32, (n_tp, tokens), 0)
    hot = jnp.where(owners == owner, 1.0, 0.0)
    first = lax.broadcasted_iota(jnp.int32, (tokens, tokens), 0)
    second = lax.broadcasted_iota(jnp.int32, (tokens, tokens), 1)
    earlier = jnp.where((first < second) & (first // source_rows == second // source_rows), 1.0, 0.0)
    before = jnp.dot(hot.astype(BF16), earlier.astype(BF16), preferred_element_type=F32)
    seat = jnp.sum(before * hot, axis=0, keepdims=True).astype(jnp.int32)
    source = lax.broadcasted_iota(jnp.int32, (1, tokens), 1) // source_rows
    code = owners * (n_tp * seat_cap) + source * seat_cap + seat
    seats = n_tp * seat_cap
    held = lax.broadcasted_iota(jnp.int32, (n_tp * seats, tokens), 0) == code
    pick = jnp.where(held, 1.0, 0.0).astype(BF16)
    mix_ref[...] = lax.dot_general(
        pick, combine_ref[...], (((1,), (1,)), ((), ())), preferred_element_type=F32
    ).astype(BF16)
    place = jnp.where(held[:seats], positions_ref[...].astype(F32), 0.0)
    at_ref[...] = jnp.sum(place, axis=1, keepdims=True)
    copy.wait()
    rows_ref[...] = jnp.dot(pick, hidden_ref[...], preferred_element_type=F32).astype(BF16)


def cache_kernel(n_z, n_tp, cache_width, *refs):
    near, far, core_ref = refs[:4], refs[4 : n_z + 2], refs[n_z + 2]
    mix_ref, rows_ref, gain_ref, weight_ref = refs[n_z + 3 : n_z + 7]
    outs, back_ref = refs[n_z + 7 : n_z + 7 + n_tp], refs[n_z + 7 + n_tp]
    for d in range(4):
        back_ref[d * CAP : (d + 1) * CAP, :] = near[d][...]
    for d in range(n_z - 2):
        at = (2 * d + 4) * CAP
        back_ref[at : at + CAP, :] = far[d][:CAP, :]
        back_ref[at + CAP : at + 2 * CAP, :] = core_ref[d * CAP : (d + 1) * CAP, :]
    mixed = jnp.dot(mix_ref[...], back_ref[...], preferred_element_type=F32)
    state = rows_ref[...].astype(F32) + mixed
    square = jnp.sum(state * state, axis=1, keepdims=True)
    scaled = (state * gain_ref[...]).astype(BF16)
    value = lax.dot_general(
        scaled, weight_ref[...], (((1,), (1,)), ((), ())), preferred_element_type=F32
    ).astype(BF16)
    high = square.astype(BF16).astype(F32)
    rest = square - high
    middle = rest.astype(BF16).astype(F32)
    low = rest - middle
    seats, wide = outs[0].shape
    lane = lax.broadcasted_iota(jnp.int32, (square.shape[0], wide - cache_width), 1)
    extra = jnp.where(lane == 0, high, jnp.where(lane == 1, middle, jnp.where(lane == 2, low, 0.0)))
    extra = extra.astype(BF16)
    for d in range(n_tp):
        outs[d][:, :cache_width] = value[d * seats : (d + 1) * seats]
        outs[d][:, cache_width:] = extra[d * seats : (d + 1) * seats]


def finish_kernel(n_tp, width, rank_width, *refs):
    parts = refs[:n_tp]
    gain_ref, cos_ref, sin_ref, latent_ref, rotary_ref = refs[n_tp:]
    total = parts[0][...].astype(F32)
    for other in parts[1:]:
        total = total + other[...].astype(F32)
    half = cos_ref.shape[1]
    cache_width = rank_width + 2 * half
    square = jnp.sum(total[:, cache_width : cache_width + 3], axis=1, keepdims=True)
    cache = total[:, :cache_width] * lax.rsqrt(square / width + EPS)
    latent = cache[:, :rank_width]
    scale = lax.rsqrt(jnp.mean(latent * latent, axis=1, keepdims=True) + EPS)
    latent_ref[...] = (latent * scale * gain_ref[...]).astype(BF16)
    first = cache[:, rank_width : rank_width + half]
    second = cache[:, rank_width + half :]
    cosine, sine = cos_ref[...], sin_ref[...]
    rotary_ref[:, :half] = (first * cosine - second * sine).astype(BF16)
    rotary_ref[:, half:] = (second * cosine + first * sine).astype(BF16)


def call(kernel, out_shape, args, scratch=(), flops=0, hbm=()):
    moved = sum(a.size * a.dtype.itemsize for a in args)
    vmem = pl.BlockSpec(memory_space=pltpu.VMEM)
    args = [
        pltpu.with_memory_space_constraint(a, pltpu.HBM) if i in hbm else a
        for i, a in enumerate(args)
    ]
    return pl.pallas_call(
        kernel,
        out_shape=out_shape,
        in_specs=[
            pl.BlockSpec(memory_space=pltpu.HBM) if i in hbm else vmem for i in range(len(args))
        ],
        out_specs=[vmem] * len(out_shape),
        scratch_shapes=list(scratch),
        compiler_params=pltpu.CompilerParams(vmem_limit_bytes=VMEM_LIMIT),
        cost_estimate=pl.CostEstimate(flops=flops, bytes_accessed=moved, transcendentals=0),
    )(*args)


def swap(value, axis, d):
    return lax.ppermute(value, axis, [(i, i ^ d) for i in range(lax.axis_size(axis))])


def spread(value, n_tp):
    return [swap(value, "tp", d) for d in reversed(range(1, n_tp))][::-1]


def collect(values):
    got = [swap(values[d], "tp", d) for d in reversed(range(1, len(values)))]
    return [values[0]] + got[::-1]


def on_device(
    hidden,
    moe_gain,
    route_logits,
    routes,
    gate_weight,
    up_weight,
    down_weight,
    attn_gain,
    latent_weight,
    latent_gain,
    positions,
    owners,
):
    n_ep = lax.axis_size("ep")
    n_tp = lax.axis_size("tp")
    n_z = n_ep // 2
    tokens, width = hidden.shape
    share = width // n_tp
    ff = gate_weight.shape[2]
    slots = n_ep * CAP
    seat_cap = max(2, tokens // n_tp // 4)
    seats = n_tp * seat_cap
    rank_width = latent_gain.shape[0]
    cache_width = latent_weight.shape[1]
    half = (cache_width - rank_width) // 2
    wide = (cache_width + 3 + 127) // 128 * 128
    struct = jax.ShapeDtypeStruct
    chunks = width // 512 if width % 512 == 0 else 1

    own, to_core, *outgoing, combine = call(
        functools.partial(dispatch_kernel, n_ep, n_tp),
        [struct((CAP, width), BF16), struct((n_tp * CAP, share), BF16)]
        + [struct((CAP, share), BF16)] * 2
        + [struct((2 * CAP, share), BF16)] * (n_z - 2)
        + [struct((slots, tokens), BF16)],
        (routes.T, route_logits.T, hidden, moe_gain),
        [
            pltpu.VMEM(routes.T.shape, jnp.int32),
            pltpu.VMEM(routes.T.shape, F32),
            pltpu.VMEM(hidden.shape, BF16),
            pltpu.VMEM((1, width), F32),
            pltpu.VMEM((slots, tokens), BF16),
            pltpu.VMEM((2 * CAP, width), F32),
            pltpu.SemaphoreType.DMA((3 + chunks,)),
        ],
        flops=4 * slots * tokens * width,
        hbm=(0, 1, 2, 3),
    )
    share_of = hidden
    if share % 128:
        share_of = lax.dynamic_slice_in_dim(hidden, lax.axis_index("tp") * share, share, 1)
    rows, mix, at = call(
        functools.partial(seats_kernel, n_tp, seat_cap),
        [
            struct((n_tp * seats, share), BF16),
            struct((n_tp * seats, slots), BF16),
            struct((seats, 1), F32),
        ],
        (owners[None, :], positions[None, :], combine, share_of),
        [pltpu.VMEM((tokens, share), BF16), pltpu.SemaphoreType.DMA(())],
        flops=2 * n_tp * seats * tokens * (share + slots),
        hbm=(3,),
    )
    freqs = ROPE_BASE ** (-jnp.arange(half, dtype=F32) / half)
    angles = at * freqs[None, :]
    cosine, sine = jnp.cos(angles), jnp.sin(angles)

    near_out, far_out = outgoing[:2], outgoing[2:]
    far = [swap(far_out[d - 2], "ep", 2 * d) for d in range(2, n_z)]
    near = [swap(near_out[d - 2], "ep", d) for d in (2, 3)]
    from_core = swap(to_core, "ep", 1)
    near_mine = jnp.concatenate(near, axis=0)
    near_shares = [near_mine] + spread(near_mine, n_tp)
    crossed = swap(jnp.concatenate([piece[CAP:] for piece in far], axis=0), "ep", 1)
    far_mine = jnp.concatenate(
        [
            block
            for d, piece in enumerate(far)
            for block in (piece[:CAP], crossed[d * CAP : (d + 1) * CAP])
        ],
        axis=0,
    )
    far_shares = spread(far_mine, n_tp)
    own, rows, mix, at = lax.optimization_barrier((own, rows, mix, at))
    gate_w, up_w, down_w = gate_weight[0], up_weight[0], down_weight[0]
    near_rows, far_rows = 4 * CAP, slots - 4 * CAP
    *loaded, inner, gate_sum, up_sum = call(
        functools.partial(first_kernel, n_tp),
        [struct(w.shape, BF16) for w in (gate_w, up_w, down_w)]
        + [struct((near_rows, ff), BF16)]
        + [struct((far_rows, ff), F32)] * 2,
        (own, from_core, *near_shares, far_mine, gate_w, up_w, down_w),
        [pltpu.VMEM((2 * CAP, width), BF16), pltpu.SemaphoreType.DMA((3,))],
        flops=2 * slots * width * ff,
        hbm=tuple(range(n_tp + 3, n_tp + 6)),
    )
    terms = call(
        functools.partial(expert_kernel, n_tp),
        [struct((far_rows, share), BF16)] * n_tp + [struct((near_rows, share), BF16)] * n_tp,
        (*far_shares, *loaded, inner, gate_sum, up_sum),
        flops=2 * slots * width * ff * 3,
    )
    far_terms = collect(terms[:n_tp])
    near_terms = collect(terms[n_tp:])
    far_done = call(
        functools.partial(sum_kernel, n_tp),
        [struct((2 * CAP, share), BF16)] * (n_z - 2),
        far_terms,
    )
    far_back = [swap(far_done[d - 2], "ep", 2 * d) for d in range(2, n_z)]
    near_done = call(
        functools.partial(sum_kernel, n_tp), [struct((CAP, share), BF16)] * 4, near_terms
    )
    near_back = [near_done[0]] + [swap(near_done[d], "ep", d) for d in (1, 2, 3)]
    crossed = swap(jnp.concatenate([piece[CAP:] for piece in far_back], axis=0), "ep", 1)
    partial = call(
        functools.partial(cache_kernel, n_z, n_tp, cache_width),
        [struct((seats, wide), BF16)] * n_tp,
        (*near_back, *far_back, crossed, mix, rows, attn_gain[None, :], latent_weight.T),
        [pltpu.VMEM((slots, share), BF16)],
        flops=2 * n_tp * seats * share * (slots + cache_width),
    )
    return tuple(
        call(
            functools.partial(finish_kernel, n_tp, width, rank_width),
            [struct((seats, rank_width), BF16), struct((seats, 2 * half), BF16)],
            (*collect(partial), latent_gain[None, :], cosine, sine),
        )
    )


def solution(mesh):
    placed = (
        P(("groups", "ep"), None),
        P(),
        P(("groups", "ep"), None),
        P(("groups", "ep"), None),
        P("ep", None, "tp"),
        P("ep", None, "tp"),
        P("ep", "tp", None),
        P("tp"),
        P("tp", None),
        P(),
        P(("groups", "ep")),
        P(("groups", "ep")),
    )
    return jax.shard_map(
        on_device,
        mesh=mesh,
        in_specs=placed,
        out_specs=(P(("groups", "ep", "tp"), None), P(("groups", "ep", "tp"), None)),
        check_vma=False,
    )
```

```python
import functools

import jax
import jax.numpy as jnp
from jax import lax
from jax.experimental import pallas as pl
from jax.experimental.pallas import tpu as pltpu
from jax.sharding import PartitionSpec as P

CAP = 16
EPS = 1e-06
ROUTE_SCALE = 2.5
ROPE_BASE = 10000.0
BF16 = jnp.bfloat16
F32 = jnp.float32
VMEM_LIMIT = 40 * 1024 * 1024


def columns_of(ref, index, count, share):
    if share % 128 == 0:
        return ref[:, pl.ds(pl.multiple_of(index * share, 128), share)]
    out = ref[:, 0:share]
    for q in range(1, count):
        out = jnp.where(index == q, ref[:, q * share : (q + 1) * share], out)
    return out


def dispatch_kernel(n_ep, n_tp, routes_hbm, logits_hbm, hidden_hbm, gain_hbm, *refs):
    own_ref, core_ref = refs[:2]
    outs, combine_ref = refs[2 : n_ep // 2 + 2], refs[n_ep // 2 + 2]
    routes_ref, logits_ref, hidden_ref, gain_ref, pick_ref, head_ref, sems = refs[n_ep // 2 + 3 :]
    me = lax.axis_index("ep")
    part = lax.axis_index("tp")
    tokens, width = hidden_ref.shape
    share = width // n_tp
    step = 512 if width % 512 == 0 else width
    starts = range(0, width, step)
    small = [
        pltpu.make_async_copy(routes_hbm, routes_ref, sems.at[0]),
        pltpu.make_async_copy(logits_hbm, logits_ref, sems.at[1]),
        pltpu.make_async_copy(gain_hbm, gain_ref.at[0], sems.at[2]),
    ]
    large = [
        pltpu.make_async_copy(
            hidden_hbm.at[:, c : c + step], hidden_ref.at[:, c : c + step], sems.at[3 + i]
        )
        for i, c in enumerate(starts)
    ]
    for copy in small + large:
        copy.start()
    small[0].wait()
    small[1].wait()
    routes = routes_ref[...]
    affinity = jax.nn.sigmoid(logits_ref[...])
    weight = ROUTE_SCALE * affinity / jnp.sum(affinity, axis=0, keepdims=True)
    weight = weight.astype(BF16).astype(F32)
    expert = lax.broadcasted_iota(jnp.int32, (n_ep, tokens), 0) ^ me
    hit = jnp.zeros((n_ep, tokens), F32)
    gain_of = jnp.zeros((n_ep, tokens), F32)
    for k in range(routes.shape[0]):
        same = routes[k : k + 1, :] == expert
        hit = jnp.where(same, 1.0, hit)
        gain_of = jnp.where(same, weight[k : k + 1, :], gain_of)
    earlier = lax.broadcasted_iota(jnp.int32, (tokens, tokens), 0) < lax.broadcasted_iota(
        jnp.int32, (tokens, tokens), 1
    )
    rank = jnp.dot(hit.astype(BF16), earlier.astype(F32).astype(BF16), preferred_element_type=F32)
    rank = jnp.where(hit > 0, rank, -1.0)
    place = lax.broadcasted_iota(jnp.int32, (CAP, tokens), 0).astype(F32)
    for d in range(n_ep):
        match = rank[d : d + 1, :] == place
        rows = slice(d * CAP, (d + 1) * CAP)
        pick_ref[rows, :] = jnp.where(match, 1.0, 0.0).astype(BF16)
        combine_ref[rows, :] = jnp.where(match, gain_of[d : d + 1, :], 0.0).astype(BF16)
    pick = pick_ref[...]
    head = 2 * CAP
    square = jnp.zeros((n_ep * CAP, 1), F32)
    for copy in large:
        copy.wait()
    for c in starts:
        got = jnp.dot(pick, hidden_ref[:, c : c + step], preferred_element_type=F32)
        square = square + jnp.sum(got * got, axis=1, keepdims=True)
        head_ref[:, c : c + step] = got[:head]
    small[2].wait()
    scale = lax.rsqrt(square / width + EPS)
    got = jnp.dot(pick[head:], columns_of(hidden_ref, part, n_tp, share), preferred_element_type=F32)
    rest = (got * scale[head:] * columns_of(gain_ref, part, n_tp, share)).astype(BF16)
    at = 0
    for out in outs:
        out[...] = rest[at : at + out.shape[0]]
        at += out.shape[0]
    near = (head_ref[...] * scale[:head] * gain_ref[...]).astype(BF16)
    own_ref[...] = near[:CAP]
    for q in range(n_tp):
        core_ref[q * CAP : (q + 1) * CAP, :] = near[CAP:, q * share : (q + 1) * share]


def first_kernel(n_tp, own_ref, core_ref, *refs):
    near, mine_ref = refs[:n_tp], refs[n_tp]
    hbm = refs[n_tp + 1 : n_tp + 4]
    loaded = refs[n_tp + 4 : n_tp + 7]
    inner_ref, gate_sum_ref, up_sum_ref, head_ref, sems = refs[n_tp + 7 :]
    part = lax.axis_index("tp")
    share = mine_ref.shape[1]
    copies = [
        pltpu.make_async_copy(source, target, sems.at[i])
        for i, (source, target) in enumerate(zip(hbm, loaded))
    ]
    for copy in copies:
        copy.start()
    head_ref[:CAP, :] = own_ref[...]
    for q in range(n_tp):
        columns = slice(q * share, (q + 1) * share)
        head_ref[CAP : 2 * CAP, columns] = core_ref[q * CAP : (q + 1) * CAP, :]
    sums = []
    for copy, weight_ref, sum_ref in zip(copies, loaded, (gate_sum_ref, up_sum_ref)):
        copy.wait()
        total = jnp.dot(head_ref[...], weight_ref[...], preferred_element_type=F32)
        other = None
        for d in range(n_tp):
            depth = pl.ds(pl.multiple_of((part ^ d) * share, CAP), share)
            term = jnp.dot(near[d][...], weight_ref[depth, :], preferred_element_type=F32)
            other = term if other is None else other + term
        sums.append(jnp.concatenate([total, other], axis=0))
        depth = pl.ds(pl.multiple_of(part * share, CAP), share)
        sum_ref[...] = jnp.dot(mine_ref[...], weight_ref[depth, :], preferred_element_type=F32)
    gate, upper = sums
    inner_ref[...] = (gate / (1.0 + jnp.exp(-gate)) * upper).astype(BF16)
    copies[2].wait()


def expert_kernel(n_tp, *refs):
    rows = refs[: n_tp - 1]
    gate_ref, up_ref, down_ref, near_ref, gate_sum_ref, up_sum_ref = refs[n_tp - 1 : n_tp + 5]
    far_outs = refs[n_tp + 5 : 2 * n_tp + 5]
    near_outs = refs[2 * n_tp + 5 :]
    part = lax.axis_index("tp")
    share = rows[0].shape[1]
    gate = gate_sum_ref[...]
    upper = up_sum_ref[...]
    for d in range(1, n_tp):
        value = rows[d - 1][...]
        depth = pl.ds(pl.multiple_of((part ^ d) * share, CAP), share)
        gate = gate + jnp.dot(value, gate_ref[depth, :], preferred_element_type=F32)
        upper = upper + jnp.dot(value, up_ref[depth, :], preferred_element_type=F32)
    far = (gate / (1.0 + jnp.exp(-gate)) * upper).astype(BF16)
    inner = jnp.concatenate([far, near_ref[...]], axis=0)
    count = far.shape[0]
    for d in range(n_tp):
        down = columns_of(down_ref, part ^ d, n_tp, share)
        out = jnp.dot(inner, down, preferred_element_type=F32).astype(BF16)
        far_outs[d][...] = out[:count]
        near_outs[d][...] = out[count:]


def sum_kernel(n_tp, *refs):
    parts, outs = refs[:n_tp], refs[n_tp:]
    at = 0
    for out in outs:
        rows = slice(at, at + out.shape[0])
        total = parts[0][rows, :].astype(F32)
        for other in parts[1:]:
            total = total + other[rows, :].astype(F32)
        out[...] = total.astype(BF16)
        at += out.shape[0]


def seats_kernel(
    n_tp,
    seat_cap,
    owners_ref,
    positions_ref,
    combine_ref,
    hidden_hbm,
    rows_ref,
    mix_ref,
    at_ref,
    hidden_ref,
    sem,
):
    part = lax.axis_index("tp")
    tokens, share = hidden_ref.shape
    if hidden_hbm.shape[1] != share:
        hidden_hbm = hidden_hbm.at[:, pl.ds(pl.multiple_of(part * share, 128), share)]
    copy = pltpu.make_async_copy(hidden_hbm, hidden_ref, sem)
    copy.start()
    source_rows = tokens // n_tp
    owners = owners_ref[...] ^ part
    owner = lax.broadcasted_iota(jnp.int32, (n_tp, tokens), 0)
    hot = jnp.where(owners == owner, 1.0, 0.0)
    first = lax.broadcasted_iota(jnp.int32, (tokens, tokens), 0)
    second = lax.broadcasted_iota(jnp.int32, (tokens, tokens), 1)
    earlier = jnp.where((first < second) & (first // source_rows == second // source_rows), 1.0, 0.0)
    before = jnp.dot(hot.astype(BF16), earlier.astype(BF16), preferred_element_type=F32)
    seat = jnp.sum(before * hot, axis=0, keepdims=True).astype(jnp.int32)
    source = lax.broadcasted_iota(jnp.int32, (1, tokens), 1) // source_rows
    code = owners * (n_tp * seat_cap) + source * seat_cap + seat
    seats = n_tp * seat_cap
    held = lax.broadcasted_iota(jnp.int32, (n_tp * seats, tokens), 0) == code
    pick = jnp.where(held, 1.0, 0.0).astype(BF16)
    mix_ref[...] = lax.dot_general(
        pick, combine_ref[...], (((1,), (1,)), ((), ())), preferred_element_type=F32
    ).astype(BF16)
    place = jnp.where(held[:seats], positions_ref[...].astype(F32), 0.0)
    at_ref[...] = jnp.sum(place, axis=1, keepdims=True)
    copy.wait()
    rows_ref[...] = jnp.dot(pick, hidden_ref[...], preferred_element_type=F32).astype(BF16)


def cache_kernel(n_z, n_tp, cache_width, *refs):
    near, far, core_ref = refs[:4], refs[4 : n_z + 2], refs[n_z + 2]
    mix_ref, rows_ref, gain_ref, weight_ref = refs[n_z + 3 : n_z + 7]
    outs, back_ref = refs[n_z + 7 : n_z + 7 + n_tp], refs[n_z + 7 + n_tp]
    for d in range(4):
        back_ref[d * CAP : (d + 1) * CAP, :] = near[d][...]
    for d in range(n_z - 2):
        at = (2 * d + 4) * CAP
        back_ref[at : at + CAP, :] = far[d][:CAP, :]
        back_ref[at + CAP : at + 2 * CAP, :] = core_ref[d * CAP : (d + 1) * CAP, :]
    mixed = jnp.dot(mix_ref[...], back_ref[...], preferred_element_type=F32)
    state = rows_ref[...].astype(F32) + mixed
    square = jnp.sum(state * state, axis=1, keepdims=True)
    scaled = (state * gain_ref[...]).astype(BF16)
    value = lax.dot_general(
        scaled, weight_ref[...], (((1,), (1,)), ((), ())), preferred_element_type=F32
    ).astype(BF16)
    high = square.astype(BF16).astype(F32)
    rest = square - high
    middle = rest.astype(BF16).astype(F32)
    low = rest - middle
    seats, wide = outs[0].shape
    lane = lax.broadcasted_iota(jnp.int32, (square.shape[0], wide - cache_width), 1)
    extra = jnp.where(lane == 0, high, jnp.where(lane == 1, middle, jnp.where(lane == 2, low, 0.0)))
    extra = extra.astype(BF16)
    for d in range(n_tp):
        outs[d][:, :cache_width] = value[d * seats : (d + 1) * seats]
        outs[d][:, cache_width:] = extra[d * seats : (d + 1) * seats]


def finish_kernel(n_tp, width, rank_width, *refs):
    parts = refs[:n_tp]
    gain_ref, cos_ref, sin_ref, latent_ref, rotary_ref = refs[n_tp:]
    total = parts[0][...].astype(F32)
    for other in parts[1:]:
        total = total + other[...].astype(F32)
    half = cos_ref.shape[1]
    cache_width = rank_width + 2 * half
    square = jnp.sum(total[:, cache_width : cache_width + 3], axis=1, keepdims=True)
    cache = total[:, :cache_width] * lax.rsqrt(square / width + EPS)
    latent = cache[:, :rank_width]
    scale = lax.rsqrt(jnp.mean(latent * latent, axis=1, keepdims=True) + EPS)
    latent_ref[...] = (latent * scale * gain_ref[...]).astype(BF16)
    first = cache[:, rank_width : rank_width + half]
    second = cache[:, rank_width + half :]
    cosine, sine = cos_ref[...], sin_ref[...]
    rotary_ref[:, :half] = (first * cosine - second * sine).astype(BF16)
    rotary_ref[:, half:] = (second * cosine + first * sine).astype(BF16)


def call(kernel, out_shape, args, scratch=(), flops=0, hbm=()):
    moved = sum(a.size * a.dtype.itemsize for a in args)
    vmem = pl.BlockSpec(memory_space=pltpu.VMEM)
    args = [
        pltpu.with_memory_space_constraint(a, pltpu.HBM) if i in hbm else a
        for i, a in enumerate(args)
    ]
    return pl.pallas_call(
        kernel,
        out_shape=out_shape,
        in_specs=[
            pl.BlockSpec(memory_space=pltpu.HBM) if i in hbm else vmem for i in range(len(args))
        ],
        out_specs=[vmem] * len(out_shape),
        scratch_shapes=list(scratch),
        compiler_params=pltpu.CompilerParams(vmem_limit_bytes=VMEM_LIMIT),
        cost_estimate=pl.CostEstimate(flops=flops, bytes_accessed=moved, transcendentals=0),
    )(*args)


def swap(value, axis, d):
    return lax.ppermute(value, axis, [(i, i ^ d) for i in range(lax.axis_size(axis))])


def spread(value, n_tp):
    return [swap(value, "tp", d) for d in reversed(range(1, n_tp))][::-1]


def collect(values):
    got = [swap(values[d], "tp", d) for d in reversed(range(1, len(values)))]
    return [values[0]] + got[::-1]


def on_device(
    hidden,
    moe_gain,
    route_logits,
    routes,
    gate_weight,
    up_weight,
    down_weight,
    attn_gain,
    latent_weight,
    latent_gain,
    positions,
    owners,
):
    n_ep = lax.axis_size("ep")
    n_tp = lax.axis_size("tp")
    n_z = n_ep // 2
    tokens, width = hidden.shape
    share = width // n_tp
    ff = gate_weight.shape[2]
    slots = n_ep * CAP
    seat_cap = max(2, tokens // n_tp // 4)
    seats = n_tp * seat_cap
    rank_width = latent_gain.shape[0]
    cache_width = latent_weight.shape[1]
    half = (cache_width - rank_width) // 2
    wide = (cache_width + 3 + 127) // 128 * 128
    struct = jax.ShapeDtypeStruct
    chunks = width // 512 if width % 512 == 0 else 1

    own, to_core, *outgoing, combine = call(
        functools.partial(dispatch_kernel, n_ep, n_tp),
        [struct((CAP, width), BF16), struct((n_tp * CAP, share), BF16)]
        + [struct((CAP, share), BF16)] * 2
        + [struct((2 * CAP, share), BF16)] * (n_z - 2)
        + [struct((slots, tokens), BF16)],
        (routes.T, route_logits.T, hidden, moe_gain),
        [
            pltpu.VMEM(routes.T.shape, jnp.int32),
            pltpu.VMEM(routes.T.shape, F32),
            pltpu.VMEM(hidden.shape, BF16),
            pltpu.VMEM((1, width), F32),
            pltpu.VMEM((slots, tokens), BF16),
            pltpu.VMEM((2 * CAP, width), F32),
            pltpu.SemaphoreType.DMA((3 + chunks,)),
        ],
        flops=4 * slots * tokens * width,
        hbm=(0, 1, 2, 3),
    )
    share_of = hidden
    if share % 128:
        share_of = lax.dynamic_slice_in_dim(hidden, lax.axis_index("tp") * share, share, 1)
    rows, mix, at = call(
        functools.partial(seats_kernel, n_tp, seat_cap),
        [
            struct((n_tp * seats, share), BF16),
            struct((n_tp * seats, slots), BF16),
            struct((seats, 1), F32),
        ],
        (owners[None, :], positions[None, :], combine, share_of),
        [pltpu.VMEM((tokens, share), BF16), pltpu.SemaphoreType.DMA(())],
        flops=2 * n_tp * seats * tokens * (share + slots),
        hbm=(3,),
    )

    near_out, far_out = outgoing[:2], outgoing[2:]
    far = [swap(far_out[d - 2], "ep", 2 * d) for d in range(2, n_z)]
    near = [swap(near_out[d - 2], "ep", d) for d in (2, 3)]
    from_core = swap(to_core, "ep", 1)
    near_mine = jnp.concatenate(near, axis=0)
    near_shares = [near_mine] + spread(near_mine, n_tp)
    far, near_shares, rows, mix, at = lax.optimization_barrier((far, near_shares, rows, mix, at))
    crossed = swap(jnp.concatenate([piece[CAP:] for piece in far], axis=0), "ep", 1)
    far_mine = jnp.concatenate(
        [
            block
            for d, piece in enumerate(far)
            for block in (piece[:CAP], crossed[d * CAP : (d + 1) * CAP])
        ],
        axis=0,
    )
    far_shares = spread(far_mine, n_tp)
    gate_w, up_w, down_w = gate_weight[0], up_weight[0], down_weight[0]
    near_rows, far_rows = 4 * CAP, slots - 4 * CAP
    *loaded, inner, gate_sum, up_sum = call(
        functools.partial(first_kernel, n_tp),
        [struct(w.shape, BF16) for w in (gate_w, up_w, down_w)]
        + [struct((near_rows, ff), BF16)]
        + [struct((far_rows, ff), F32)] * 2,
        (own, from_core, *near_shares, far_mine, gate_w, up_w, down_w),
        [pltpu.VMEM((2 * CAP, width), BF16), pltpu.SemaphoreType.DMA((3,))],
        flops=2 * slots * width * ff,
        hbm=tuple(range(n_tp + 3, n_tp + 6)),
    )
    freqs = ROPE_BASE ** (-jnp.arange(half, dtype=F32) / half)
    angles = at * freqs[None, :]
    cosine, sine = jnp.cos(angles), jnp.sin(angles)
    terms = call(
        functools.partial(expert_kernel, n_tp),
        [struct((far_rows, share), BF16)] * n_tp + [struct((near_rows, share), BF16)] * n_tp,
        (*far_shares, *loaded, inner, gate_sum, up_sum),
        flops=2 * slots * width * ff * 3,
    )
    far_terms = collect(terms[:n_tp])
    near_terms = collect(terms[n_tp:])
    far_done = call(
        functools.partial(sum_kernel, n_tp),
        [struct((2 * CAP, share), BF16)] * (n_z - 2),
        far_terms,
    )
    far_back = [swap(far_done[d - 2], "ep", 2 * d) for d in range(2, n_z)]
    near_done = call(
        functools.partial(sum_kernel, n_tp), [struct((CAP, share), BF16)] * 4, near_terms
    )
    near_back = [near_done[0]] + [swap(near_done[d], "ep", d) for d in (1, 2, 3)]
    crossed = swap(jnp.concatenate([piece[CAP:] for piece in far_back], axis=0), "ep", 1)
    partial = call(
        functools.partial(cache_kernel, n_z, n_tp, cache_width),
        [struct((seats, wide), BF16)] * n_tp,
        (*near_back, *far_back, crossed, mix, rows, attn_gain[None, :], latent_weight.T),
        [pltpu.VMEM((slots, share), BF16)],
        flops=2 * n_tp * seats * share * (slots + cache_width),
    )
    return tuple(
        call(
            functools.partial(finish_kernel, n_tp, width, rank_width),
            [struct((seats, rank_width), BF16), struct((seats, 2 * half), BF16)],
            (*collect(partial), latent_gain[None, :], cosine, sine),
        )
    )


def solution(mesh):
    placed = (
        P(("groups", "ep"), None),
        P(),
        P(("groups", "ep"), None),
        P(("groups", "ep"), None),
        P("ep", None, "tp"),
        P("ep", None, "tp"),
        P("ep", "tp", None),
        P("tp"),
        P("tp", None),
        P(),
        P(("groups", "ep")),
        P(("groups", "ep")),
    )
    return jax.shard_map(
        on_device,
        mesh=mesh,
        in_specs=placed,
        out_specs=(P(("groups", "ep", "tp"), None), P(("groups", "ep", "tp"), None)),
        check_vma=False,
    )
```

```python
import functools

import jax
import jax.numpy as jnp
from jax import lax
from jax.experimental import pallas as pl
from jax.experimental.pallas import tpu as pltpu
from jax.sharding import PartitionSpec as P

CAP = 16
EPS = 1e-06
ROUTE_SCALE = 2.5
ROPE_BASE = 10000.0
BF16 = jnp.bfloat16
F32 = jnp.float32
VMEM_LIMIT = 40 * 1024 * 1024


def columns_of(ref, index, count, share):
    if share % 128 == 0:
        return ref[:, pl.ds(pl.multiple_of(index * share, 128), share)]
    out = ref[:, 0:share]
    for q in range(1, count):
        out = jnp.where(index == q, ref[:, q * share : (q + 1) * share], out)
    return out


def dispatch_kernel(n_ep, n_tp, routes_hbm, logits_hbm, hidden_hbm, gain_hbm, *refs):
    own_ref, core_ref = refs[:2]
    outs, combine_ref = refs[2 : n_ep // 2 + 1], refs[n_ep // 2 + 1]
    routes_ref, logits_ref, hidden_ref, gain_ref, pick_ref, head_ref, sems = refs[n_ep // 2 + 2 :]
    me = lax.axis_index("ep")
    part = lax.axis_index("tp")
    tokens, width = hidden_ref.shape
    share = width // n_tp
    step = 512 if width % 512 == 0 else width
    starts = range(0, width, step)
    small = [
        pltpu.make_async_copy(routes_hbm, routes_ref, sems.at[0]),
        pltpu.make_async_copy(logits_hbm, logits_ref, sems.at[1]),
        pltpu.make_async_copy(gain_hbm, gain_ref.at[0], sems.at[2]),
    ]
    large = [
        pltpu.make_async_copy(
            hidden_hbm.at[:, c : c + step], hidden_ref.at[:, c : c + step], sems.at[3 + i]
        )
        for i, c in enumerate(starts)
    ]
    for copy in small + large:
        copy.start()
    small[0].wait()
    small[1].wait()
    routes = routes_ref[...]
    affinity = jax.nn.sigmoid(logits_ref[...])
    weight = ROUTE_SCALE * affinity / jnp.sum(affinity, axis=0, keepdims=True)
    weight = weight.astype(BF16).astype(F32)
    expert = lax.broadcasted_iota(jnp.int32, (n_ep, tokens), 0) ^ me
    hit = jnp.zeros((n_ep, tokens), F32)
    gain_of = jnp.zeros((n_ep, tokens), F32)
    for k in range(routes.shape[0]):
        same = routes[k : k + 1, :] == expert
        hit = jnp.where(same, 1.0, hit)
        gain_of = jnp.where(same, weight[k : k + 1, :], gain_of)
    earlier = lax.broadcasted_iota(jnp.int32, (tokens, tokens), 0) < lax.broadcasted_iota(
        jnp.int32, (tokens, tokens), 1
    )
    rank = jnp.dot(hit.astype(BF16), earlier.astype(F32).astype(BF16), preferred_element_type=F32)
    rank = jnp.where(hit > 0, rank, -1.0)
    place = lax.broadcasted_iota(jnp.int32, (CAP, tokens), 0).astype(F32)
    for d in range(n_ep):
        match = rank[d : d + 1, :] == place
        rows = slice(d * CAP, (d + 1) * CAP)
        pick_ref[rows, :] = jnp.where(match, 1.0, 0.0).astype(BF16)
        combine_ref[rows, :] = jnp.where(match, gain_of[d : d + 1, :], 0.0).astype(BF16)
    pick = pick_ref[...]
    head = 2 * CAP
    square = jnp.zeros((n_ep * CAP, 1), F32)
    for copy in large:
        copy.wait()
    for c in starts:
        got = jnp.dot(pick, hidden_ref[:, c : c + step], preferred_element_type=F32)
        square = square + jnp.sum(got * got, axis=1, keepdims=True)
        head_ref[:, c : c + step] = got[:head]
    small[2].wait()
    scale = lax.rsqrt(square / width + EPS)
    got = jnp.dot(pick[head:], columns_of(hidden_ref, part, n_tp, share), preferred_element_type=F32)
    rest = (got * scale[head:] * columns_of(gain_ref, part, n_tp, share)).astype(BF16)
    at = 0
    for out in outs:
        out[...] = rest[at : at + out.shape[0]]
        at += out.shape[0]
    near = (head_ref[...] * scale[:head] * gain_ref[...]).astype(BF16)
    own_ref[...] = near[:CAP]
    for q in range(n_tp):
        core_ref[q * CAP : (q + 1) * CAP, :] = near[CAP:, q * share : (q + 1) * share]


def load_kernel(after_ref, *refs):
    count = (len(refs) - 2) // 2
    mark_ref, sems = refs[-2:]
    copies = [
        pltpu.make_async_copy(refs[i], refs[count + i], sems.at[i]) for i in range(count)
    ]
    for copy in copies:
        copy.start()
    mark_ref[...] = jnp.zeros(mark_ref.shape, F32)
    for copy in copies:
        copy.wait()


def first_kernel(n_tp, own_ref, core_ref, *refs):
    shares, mine_ref = refs[:n_tp], refs[n_tp]
    gate_ref, up_ref, _, inner_ref, gate_sum_ref, up_sum_ref, head_ref = refs[n_tp + 1 :]
    part = lax.axis_index("tp")
    share = mine_ref.shape[1]
    head_ref[:CAP, :] = own_ref[...]
    for q in range(n_tp):
        columns = slice(q * share, (q + 1) * share)
        head_ref[CAP : 2 * CAP, columns] = core_ref[q * CAP : (q + 1) * CAP, :]
    sums = []
    for weight_ref, sum_ref in zip((gate_ref, up_ref), (gate_sum_ref, up_sum_ref)):
        total = jnp.dot(head_ref[...], weight_ref[...], preferred_element_type=F32)
        other = None
        for d in range(n_tp):
            depth = pl.ds(pl.multiple_of((part ^ d) * share, CAP), share)
            term = jnp.dot(shares[d][...], weight_ref[depth, :], preferred_element_type=F32)
            other = term if other is None else other + term
        sums.append(jnp.concatenate([total, other], axis=0))
        depth = pl.ds(pl.multiple_of(part * share, CAP), share)
        sum_ref[...] = jnp.dot(mine_ref[...], weight_ref[depth, :], preferred_element_type=F32)
    gate, upper = sums
    inner_ref[...] = (gate / (1.0 + jnp.exp(-gate)) * upper).astype(BF16)


def expert_kernel(n_tp, *refs):
    rows = refs[: n_tp - 1]
    gate_ref, up_ref, down_ref, first_ref, gate_sum_ref, up_sum_ref = refs[n_tp - 1 : n_tp + 5]
    far_outs = refs[n_tp + 5 : 2 * n_tp + 5]
    near_outs = refs[2 * n_tp + 5 :]
    part = lax.axis_index("tp")
    share = rows[0].shape[1]
    gate = gate_sum_ref[...]
    upper = up_sum_ref[...]
    for d in range(1, n_tp):
        value = rows[d - 1][...]
        depth = pl.ds(pl.multiple_of((part ^ d) * share, CAP), share)
        gate = gate + jnp.dot(value, gate_ref[depth, :], preferred_element_type=F32)
        upper = upper + jnp.dot(value, up_ref[depth, :], preferred_element_type=F32)
    second = (gate / (1.0 + jnp.exp(-gate)) * upper).astype(BF16)
    first = first_ref[...]
    groups = [first[:CAP], first[CAP : 2 * CAP]]
    for at in range(0, second.shape[0], CAP):
        groups += [first[2 * CAP + at : 3 * CAP + at], second[at : at + CAP]]
    inner = jnp.concatenate(groups[4:] + groups[:4], axis=0)
    count = (len(groups) - 4) * CAP
    for d in range(n_tp):
        down = columns_of(down_ref, part ^ d, n_tp, share)
        out = jnp.dot(inner, down, preferred_element_type=F32).astype(BF16)
        far_outs[d][...] = out[:count]
        near_outs[d][...] = out[count:]


def sum_kernel(n_tp, *refs):
    parts, outs = refs[:n_tp], refs[n_tp:]
    at = 0
    for out in outs:
        rows = slice(at, at + out.shape[0])
        total = parts[0][rows, :].astype(F32)
        for other in parts[1:]:
            total = total + other[rows, :].astype(F32)
        out[...] = total.astype(BF16)
        at += out.shape[0]


def seats_kernel(
    n_tp,
    seat_cap,
    owners_ref,
    positions_ref,
    combine_ref,
    hidden_hbm,
    rows_ref,
    mix_ref,
    at_ref,
    hidden_ref,
    sem,
):
    part = lax.axis_index("tp")
    tokens, share = hidden_ref.shape
    if hidden_hbm.shape[1] != share:
        hidden_hbm = hidden_hbm.at[:, pl.ds(pl.multiple_of(part * share, 128), share)]
    copy = pltpu.make_async_copy(hidden_hbm, hidden_ref, sem)
    copy.start()
    source_rows = tokens // n_tp
    owners = owners_ref[...] ^ part
    owner = lax.broadcasted_iota(jnp.int32, (n_tp, tokens), 0)
    hot = jnp.where(owners == owner, 1.0, 0.0)
    first = lax.broadcasted_iota(jnp.int32, (tokens, tokens), 0)
    second = lax.broadcasted_iota(jnp.int32, (tokens, tokens), 1)
    earlier = jnp.where((first < second) & (first // source_rows == second // source_rows), 1.0, 0.0)
    before = jnp.dot(hot.astype(BF16), earlier.astype(BF16), preferred_element_type=F32)
    seat = jnp.sum(before * hot, axis=0, keepdims=True).astype(jnp.int32)
    source = lax.broadcasted_iota(jnp.int32, (1, tokens), 1) // source_rows
    code = owners * (n_tp * seat_cap) + source * seat_cap + seat
    seats = n_tp * seat_cap
    held = lax.broadcasted_iota(jnp.int32, (n_tp * seats, tokens), 0) == code
    pick = jnp.where(held, 1.0, 0.0).astype(BF16)
    mix_ref[...] = lax.dot_general(
        pick, combine_ref[...], (((1,), (1,)), ((), ())), preferred_element_type=F32
    ).astype(BF16)
    place = jnp.where(held[:seats], positions_ref[...].astype(F32), 0.0)
    at_ref[...] = jnp.sum(place, axis=1, keepdims=True)
    copy.wait()
    rows_ref[...] = jnp.dot(pick, hidden_ref[...], preferred_element_type=F32).astype(BF16)


def cache_kernel(n_z, n_tp, cache_width, *refs):
    near, far, core_ref = refs[:4], refs[4 : n_z + 2], refs[n_z + 2]
    mix_ref, rows_ref, gain_ref, weight_ref = refs[n_z + 3 : n_z + 7]
    outs, back_ref = refs[n_z + 7 : n_z + 7 + n_tp], refs[n_z + 7 + n_tp]
    for d in range(4):
        back_ref[d * CAP : (d + 1) * CAP, :] = near[d][...]
    for d in range(n_z - 2):
        at = (2 * d + 4) * CAP
        back_ref[at : at + CAP, :] = far[d][:CAP, :]
        back_ref[at + CAP : at + 2 * CAP, :] = core_ref[d * CAP : (d + 1) * CAP, :]
    mixed = jnp.dot(mix_ref[...], back_ref[...], preferred_element_type=F32)
    state = rows_ref[...].astype(F32) + mixed
    square = jnp.sum(state * state, axis=1, keepdims=True)
    scaled = (state * gain_ref[...]).astype(BF16)
    value = lax.dot_general(
        scaled, weight_ref[...], (((1,), (1,)), ((), ())), preferred_element_type=F32
    ).astype(BF16)
    high = square.astype(BF16).astype(F32)
    rest = square - high
    middle = rest.astype(BF16).astype(F32)
    low = rest - middle
    seats, wide = outs[0].shape
    lane = lax.broadcasted_iota(jnp.int32, (square.shape[0], wide - cache_width), 1)
    extra = jnp.where(lane == 0, high, jnp.where(lane == 1, middle, jnp.where(lane == 2, low, 0.0)))
    extra = extra.astype(BF16)
    for d in range(n_tp):
        outs[d][:, :cache_width] = value[d * seats : (d + 1) * seats]
        outs[d][:, cache_width:] = extra[d * seats : (d + 1) * seats]


def finish_kernel(n_tp, width, rank_width, *refs):
    parts = refs[:n_tp]
    gain_ref, cos_ref, sin_ref, latent_ref, rotary_ref = refs[n_tp:]
    total = parts[0][...].astype(F32)
    for other in parts[1:]:
        total = total + other[...].astype(F32)
    half = cos_ref.shape[1]
    cache_width = rank_width + 2 * half
    square = jnp.sum(total[:, cache_width : cache_width + 3], axis=1, keepdims=True)
    cache = total[:, :cache_width] * lax.rsqrt(square / width + EPS)
    latent = cache[:, :rank_width]
    scale = lax.rsqrt(jnp.mean(latent * latent, axis=1, keepdims=True) + EPS)
    latent_ref[...] = (latent * scale * gain_ref[...]).astype(BF16)
    first = cache[:, rank_width : rank_width + half]
    second = cache[:, rank_width + half :]
    cosine, sine = cos_ref[...], sin_ref[...]
    rotary_ref[:, :half] = (first * cosine - second * sine).astype(BF16)
    rotary_ref[:, half:] = (second * cosine + first * sine).astype(BF16)


def call(kernel, out_shape, args, scratch=(), flops=0, hbm=()):
    moved = sum(a.size * a.dtype.itemsize for a in args)
    vmem = pl.BlockSpec(memory_space=pltpu.VMEM)
    args = [
        pltpu.with_memory_space_constraint(a, pltpu.HBM) if i in hbm else a
        for i, a in enumerate(args)
    ]
    return pl.pallas_call(
        kernel,
        out_shape=out_shape,
        in_specs=[
            pl.BlockSpec(memory_space=pltpu.HBM) if i in hbm else vmem for i in range(len(args))
        ],
        out_specs=[vmem] * len(out_shape),
        scratch_shapes=list(scratch),
        compiler_params=pltpu.CompilerParams(vmem_limit_bytes=VMEM_LIMIT),
        cost_estimate=pl.CostEstimate(flops=flops, bytes_accessed=moved, transcendentals=0),
    )(*args)


def swap(value, axis, d):
    return lax.ppermute(value, axis, [(i, i ^ d) for i in range(lax.axis_size(axis))])


def spread(value, n_tp):
    return [swap(value, "tp", d) for d in reversed(range(1, n_tp))][::-1]


def collect(values):
    got = [swap(values[d], "tp", d) for d in reversed(range(1, len(values)))]
    return [values[0]] + got[::-1]


def on_device(
    hidden,
    moe_gain,
    route_logits,
    routes,
    gate_weight,
    up_weight,
    down_weight,
    attn_gain,
    latent_weight,
    latent_gain,
    positions,
    owners,
):
    n_ep = lax.axis_size("ep")
    n_tp = lax.axis_size("tp")
    n_z = n_ep // 2
    tokens, width = hidden.shape
    share = width // n_tp
    ff = gate_weight.shape[2]
    slots = n_ep * CAP
    seat_cap = max(2, tokens // n_tp // 4)
    seats = n_tp * seat_cap
    rank_width = latent_gain.shape[0]
    cache_width = latent_weight.shape[1]
    half = (cache_width - rank_width) // 2
    wide = (cache_width + 3 + 127) // 128 * 128
    struct = jax.ShapeDtypeStruct
    chunks = width // 512 if width % 512 == 0 else 1

    own, to_core, *outgoing, combine = call(
        functools.partial(dispatch_kernel, n_ep, n_tp),
        [struct((CAP, width), BF16), struct((n_tp * CAP, share), BF16)]
        + [struct((2 * CAP, share), BF16)] * (n_z - 1)
        + [struct((slots, tokens), BF16)],
        (routes.T, route_logits.T, hidden, moe_gain),
        [
            pltpu.VMEM(routes.T.shape, jnp.int32),
            pltpu.VMEM(routes.T.shape, F32),
            pltpu.VMEM(hidden.shape, BF16),
            pltpu.VMEM((1, width), F32),
            pltpu.VMEM((slots, tokens), BF16),
            pltpu.VMEM((2 * CAP, width), F32),
            pltpu.SemaphoreType.DMA((3 + chunks,)),
        ],
        flops=4 * slots * tokens * width,
        hbm=(0, 1, 2, 3),
    )
    arrived = [swap(outgoing[d - 1], "ep", 2 * d) for d in reversed(range(1, n_z))][::-1]
    from_core = swap(to_core, "ep", 1)
    gate_w, up_w, down_w = gate_weight[0], up_weight[0], down_weight[0]
    *loaded, mark = call(
        load_kernel,
        [struct(w.shape, BF16) for w in (gate_w, up_w, down_w)] + [struct((8, 128), F32)],
        (combine, gate_w, up_w, down_w),
        [pltpu.SemaphoreType.DMA((3,))],
        hbm=(1, 2, 3),
    )
    arrived, mark = lax.optimization_barrier((arrived, mark))
    crossed = swap(jnp.concatenate([piece[CAP:] for piece in arrived], axis=0), "ep", 1)
    direct = jnp.concatenate([piece[:CAP] for piece in arrived], axis=0)
    direct_shares = [direct] + spread(direct, n_tp)
    crossed_shares = spread(crossed, n_tp)
    half_rows = (n_z - 1) * CAP
    near_rows, far_rows = 4 * CAP, slots - 4 * CAP
    inner, gate_sum, up_sum = call(
        functools.partial(first_kernel, n_tp),
        [struct((2 * CAP + half_rows, ff), BF16)] + [struct((half_rows, ff), F32)] * 2,
        (own, from_core, *direct_shares, crossed, *loaded[:2], mark),
        [pltpu.VMEM((2 * CAP, width), BF16)],
        flops=2 * slots * width * ff,
    )
    terms = call(
        functools.partial(expert_kernel, n_tp),
        [struct((far_rows, share), BF16)] * n_tp + [struct((near_rows, share), BF16)] * n_tp,
        (*crossed_shares, *loaded, inner, gate_sum, up_sum),
        flops=2 * slots * width * ff * 3,
    )
    combine, _ = lax.optimization_barrier((combine, terms[0]))
    share_of = hidden
    if share % 128:
        share_of = lax.dynamic_slice_in_dim(hidden, lax.axis_index("tp") * share, share, 1)
    rows, mix, at = call(
        functools.partial(seats_kernel, n_tp, seat_cap),
        [
            struct((n_tp * seats, share), BF16),
            struct((n_tp * seats, slots), BF16),
            struct((seats, 1), F32),
        ],
        (owners[None, :], positions[None, :], combine, share_of),
        [pltpu.VMEM((tokens, share), BF16), pltpu.SemaphoreType.DMA(())],
        flops=2 * n_tp * seats * tokens * (share + slots),
        hbm=(3,),
    )
    freqs = ROPE_BASE ** (-jnp.arange(half, dtype=F32) / half)
    angles = at * freqs[None, :]
    cosine, sine = jnp.cos(angles), jnp.sin(angles)

    far_terms = collect(terms[:n_tp])
    far_terms, rows, mix = lax.optimization_barrier((far_terms, rows, mix))
    near_terms = collect(terms[n_tp:])
    far_done = call(
        functools.partial(sum_kernel, n_tp),
        [struct((2 * CAP, share), BF16)] * (n_z - 2),
        far_terms,
    )
    far_back = [swap(far_done[d - 2], "ep", 2 * d) for d in range(2, n_z)]
    near_done = call(
        functools.partial(sum_kernel, n_tp), [struct((CAP, share), BF16)] * 4, near_terms
    )
    near_back = [near_done[0]] + [swap(near_done[d], "ep", d) for d in (1, 2, 3)]
    crossed = swap(jnp.concatenate([piece[CAP:] for piece in far_back], axis=0), "ep", 1)
    partial = call(
        functools.partial(cache_kernel, n_z, n_tp, cache_width),
        [struct((seats, wide), BF16)] * n_tp,
        (*near_back, *far_back, crossed, mix, rows, attn_gain[None, :], latent_weight.T),
        [pltpu.VMEM((slots, share), BF16)],
        flops=2 * n_tp * seats * share * (slots + cache_width),
    )
    return tuple(
        call(
            functools.partial(finish_kernel, n_tp, width, rank_width),
            [struct((seats, rank_width), BF16), struct((seats, 2 * half), BF16)],
            (*collect(partial), latent_gain[None, :], cosine, sine),
        )
    )


def solution(mesh):
    placed = (
        P(("groups", "ep"), None),
        P(),
        P(("groups", "ep"), None),
        P(("groups", "ep"), None),
        P("ep", None, "tp"),
        P("ep", None, "tp"),
        P("ep", "tp", None),
        P("tp"),
        P("tp", None),
        P(),
        P(("groups", "ep")),
        P(("groups", "ep")),
    )
    return jax.shard_map(
        on_device,
        mesh=mesh,
        in_specs=placed,
        out_specs=(P(("groups", "ep", "tp"), None), P(("groups", "ep", "tp"), None)),
        check_vma=False,
    )
```

```python
import functools

import jax
import jax.numpy as jnp
from jax import lax
from jax.experimental import pallas as pl
from jax.experimental.pallas import tpu as pltpu
from jax.sharding import PartitionSpec as P

CAP = 16
EPS = 1e-06
ROUTE_SCALE = 2.5
ROPE_BASE = 10000.0
BF16 = jnp.bfloat16
F32 = jnp.float32
VMEM_LIMIT = 40 * 1024 * 1024


def columns_of(ref, index, count, share):
    if share % 128 == 0:
        return ref[:, pl.ds(pl.multiple_of(index * share, 128), share)]
    out = ref[:, 0:share]
    for q in range(1, count):
        out = jnp.where(index == q, ref[:, q * share : (q + 1) * share], out)
    return out


def offset_of(label, n_tp, core):
    steps = n_tp.bit_length() - 1
    reverse = sum(((label >> p) & 1) << (steps - 1 - p) for p in range(steps))
    return label if label == reverse else jnp.where(core == 0, label, reverse)


def halves(n_tp):
    labels = [0]
    for bit in reversed(range(1, n_tp.bit_length() - 1)):
        labels = labels + [label | (1 << bit) for label in labels]
    return labels


def dispatch_kernel(n_ep, n_tp, routes_hbm, logits_hbm, hidden_hbm, gain_hbm, *refs):
    own_ref, core_ref = refs[:2]
    outs, combine_ref = refs[2 : n_ep // 2 + 1], refs[n_ep // 2 + 1]
    routes_ref, logits_ref, hidden_ref, gain_ref, pick_ref, head_ref, sems = refs[n_ep // 2 + 2 :]
    me = lax.axis_index("ep")
    part = lax.axis_index("tp")
    tokens, width = hidden_ref.shape
    share = width // n_tp
    step = 512 if width % 512 == 0 else width
    starts = range(0, width, step)
    small = [
        pltpu.make_async_copy(routes_hbm, routes_ref, sems.at[0]),
        pltpu.make_async_copy(logits_hbm, logits_ref, sems.at[1]),
        pltpu.make_async_copy(gain_hbm, gain_ref.at[0], sems.at[2]),
    ]
    large = [
        pltpu.make_async_copy(
            hidden_hbm.at[:, c : c + step], hidden_ref.at[:, c : c + step], sems.at[3 + i]
        )
        for i, c in enumerate(starts)
    ]
    for copy in small + large:
        copy.start()
    small[0].wait()
    small[1].wait()
    routes = routes_ref[...]
    affinity = jax.nn.sigmoid(logits_ref[...])
    weight = ROUTE_SCALE * affinity / jnp.sum(affinity, axis=0, keepdims=True)
    weight = weight.astype(BF16).astype(F32)
    expert = lax.broadcasted_iota(jnp.int32, (n_ep, tokens), 0) ^ me
    hit = jnp.zeros((n_ep, tokens), F32)
    gain_of = jnp.zeros((n_ep, tokens), F32)
    for k in range(routes.shape[0]):
        same = routes[k : k + 1, :] == expert
        hit = jnp.where(same, 1.0, hit)
        gain_of = jnp.where(same, weight[k : k + 1, :], gain_of)
    earlier = lax.broadcasted_iota(jnp.int32, (tokens, tokens), 0) < lax.broadcasted_iota(
        jnp.int32, (tokens, tokens), 1
    )
    rank = jnp.dot(hit.astype(BF16), earlier.astype(F32).astype(BF16), preferred_element_type=F32)
    rank = jnp.where(hit > 0, rank, -1.0)
    place = lax.broadcasted_iota(jnp.int32, (CAP, tokens), 0).astype(F32)
    for d in range(n_ep):
        match = rank[d : d + 1, :] == place
        rows = slice(d * CAP, (d + 1) * CAP)
        pick_ref[rows, :] = jnp.where(match, 1.0, 0.0).astype(BF16)
        combine_ref[rows, :] = jnp.where(match, gain_of[d : d + 1, :], 0.0).astype(BF16)
    pick = pick_ref[...]
    head = 2 * CAP
    square = jnp.zeros((n_ep * CAP, 1), F32)
    for copy in large:
        copy.wait()
    for c in starts:
        got = jnp.dot(pick, hidden_ref[:, c : c + step], preferred_element_type=F32)
        square = square + jnp.sum(got * got, axis=1, keepdims=True)
        head_ref[:, c : c + step] = got[:head]
    small[2].wait()
    scale = lax.rsqrt(square / width + EPS)
    got = jnp.dot(pick[head:], columns_of(hidden_ref, part, n_tp, share), preferred_element_type=F32)
    rest = (got * scale[head:] * columns_of(gain_ref, part, n_tp, share)).astype(BF16)
    at = 0
    for out in outs:
        out[...] = rest[at : at + out.shape[0]]
        at += out.shape[0]
    near = (head_ref[...] * scale[:head] * gain_ref[...]).astype(BF16)
    own_ref[...] = near[:CAP]
    for q in range(n_tp):
        core_ref[q * CAP : (q + 1) * CAP, :] = near[CAP:, q * share : (q + 1) * share]


def load_kernel(after_ref, *refs):
    count = (len(refs) - 2) // 2
    mark_ref, sems = refs[-2:]
    copies = [
        pltpu.make_async_copy(refs[i], refs[count + i], sems.at[i]) for i in range(count)
    ]
    for copy in copies:
        copy.start()
    mark_ref[...] = jnp.zeros(mark_ref.shape, F32)
    for copy in copies:
        copy.wait()


def gathered(refs, n_tp):
    count = refs[0].shape[0]
    return [
        ref.at[at : at + count]
        for ref in refs
        for at in range(0, ref.shape[0], count)
    ]


def first_kernel(n_tp, own_ref, core_ref, *refs):
    steps = n_tp.bit_length()
    shares, mine_ref = gathered(refs[:steps], n_tp), refs[steps]
    gate_ref, up_ref, _, inner_ref, gate_sum_ref, up_sum_ref, head_ref = refs[steps + 1 :]
    core = lax.axis_index("ep") % 2
    part = lax.axis_index("tp")
    share = mine_ref.shape[1]
    head_ref[:CAP, :] = own_ref[...]
    for q in range(n_tp):
        columns = slice(q * share, (q + 1) * share)
        head_ref[CAP : 2 * CAP, columns] = core_ref[q * CAP : (q + 1) * CAP, :]
    sums = []
    for weight_ref, sum_ref in zip((gate_ref, up_ref), (gate_sum_ref, up_sum_ref)):
        total = jnp.dot(head_ref[...], weight_ref[...], preferred_element_type=F32)
        other = None
        for label in range(n_tp):
            d = offset_of(label, n_tp, core)
            depth = pl.ds(pl.multiple_of((part ^ d) * share, CAP), share)
            term = jnp.dot(shares[label][...], weight_ref[depth, :], preferred_element_type=F32)
            other = term if other is None else other + term
        sums.append(jnp.concatenate([total, other], axis=0))
        depth = pl.ds(pl.multiple_of(part * share, CAP), share)
        sum_ref[...] = jnp.dot(mine_ref[...], weight_ref[depth, :], preferred_element_type=F32)
    gate, upper = sums
    inner_ref[...] = (gate / (1.0 + jnp.exp(-gate)) * upper).astype(BF16)


def expert_kernel(n_tp, *refs):
    steps = n_tp.bit_length() - 1
    rows = gathered(refs[:steps], n_tp)
    gate_ref, up_ref, down_ref, first_ref, gate_sum_ref, up_sum_ref = refs[steps : steps + 6]
    far_send, far_keep, near_send, near_keep = refs[steps + 6 :]
    core = lax.axis_index("ep") % 2
    part = lax.axis_index("tp")
    share = rows[0].shape[1]
    gate = gate_sum_ref[...]
    upper = up_sum_ref[...]
    for label in range(1, n_tp):
        value = rows[label - 1][...]
        d = offset_of(label, n_tp, core)
        depth = pl.ds(pl.multiple_of((part ^ d) * share, CAP), share)
        gate = gate + jnp.dot(value, gate_ref[depth, :], preferred_element_type=F32)
        upper = upper + jnp.dot(value, up_ref[depth, :], preferred_element_type=F32)
    second = (gate / (1.0 + jnp.exp(-gate)) * upper).astype(BF16)
    first = first_ref[...]
    groups = [first[:CAP], first[CAP : 2 * CAP]]
    for at in range(0, second.shape[0], CAP):
        groups += [first[2 * CAP + at : 3 * CAP + at], second[at : at + CAP]]
    inner = jnp.concatenate(groups[4:] + groups[:4], axis=0)
    far, near = (len(groups) - 4) * CAP, 4 * CAP
    for odd, far_ref, near_ref in ((1, far_send, near_send), (0, far_keep, near_keep)):
        for i, label in enumerate(halves(n_tp)):
            down = columns_of(down_ref, part ^ offset_of(label + odd, n_tp, core), n_tp, share)
            out = jnp.dot(inner, down, preferred_element_type=F32).astype(BF16)
            far_ref[i * far : (i + 1) * far, :] = out[:far]
            near_ref[i * near : (i + 1) * near, :] = out[far:]


def fold_kernel(*refs):
    terms, out = refs[:-1], refs[-1]
    count = out.shape[0]
    total = terms[0][count : 2 * count, :].astype(F32)
    for other in terms[1:]:
        total = total + other[count : 2 * count, :].astype(F32)
    out[...] = total.astype(BF16)


def sum_kernel(count, *refs):
    parts, outs = refs[:count], refs[count:]
    at = 0
    for out in outs:
        rows = slice(at, at + out.shape[0])
        total = parts[0][rows, :].astype(F32)
        for other in parts[1:]:
            total = total + other[rows, :].astype(F32)
        out[...] = total.astype(BF16)
        at += out.shape[0]


def seats_kernel(
    n_tp,
    seat_cap,
    owners_ref,
    positions_ref,
    combine_ref,
    hidden_hbm,
    rows_ref,
    mix_ref,
    at_ref,
    hidden_ref,
    sem,
):
    part = lax.axis_index("tp")
    tokens, share = hidden_ref.shape
    if hidden_hbm.shape[1] != share:
        hidden_hbm = hidden_hbm.at[:, pl.ds(pl.multiple_of(part * share, 128), share)]
    copy = pltpu.make_async_copy(hidden_hbm, hidden_ref, sem)
    copy.start()
    source_rows = tokens // n_tp
    owners = owners_ref[...] ^ part
    owner = lax.broadcasted_iota(jnp.int32, (n_tp, tokens), 0)
    hot = jnp.where(owners == owner, 1.0, 0.0)
    first = lax.broadcasted_iota(jnp.int32, (tokens, tokens), 0)
    second = lax.broadcasted_iota(jnp.int32, (tokens, tokens), 1)
    earlier = jnp.where((first < second) & (first // source_rows == second // source_rows), 1.0, 0.0)
    before = jnp.dot(hot.astype(BF16), earlier.astype(BF16), preferred_element_type=F32)
    seat = jnp.sum(before * hot, axis=0, keepdims=True).astype(jnp.int32)
    source = lax.broadcasted_iota(jnp.int32, (1, tokens), 1) // source_rows
    code = owners * (n_tp * seat_cap) + source * seat_cap + seat
    seats = n_tp * seat_cap
    held = lax.broadcasted_iota(jnp.int32, (n_tp * seats, tokens), 0) == code
    pick = jnp.where(held, 1.0, 0.0).astype(BF16)
    mix_ref[...] = lax.dot_general(
        pick, combine_ref[...], (((1,), (1,)), ((), ())), preferred_element_type=F32
    ).astype(BF16)
    place = jnp.where(held[:seats], positions_ref[...].astype(F32), 0.0)
    at_ref[...] = jnp.sum(place, axis=1, keepdims=True)
    copy.wait()
    rows_ref[...] = jnp.dot(pick, hidden_ref[...], preferred_element_type=F32).astype(BF16)


def cache_kernel(n_z, n_tp, cache_width, *refs):
    near, far, core_ref = refs[:4], refs[4 : n_z + 2], refs[n_z + 2]
    mix_ref, rows_ref, gain_ref, weight_ref = refs[n_z + 3 : n_z + 7]
    outs, back_ref = refs[n_z + 7 : n_z + 7 + n_tp], refs[n_z + 7 + n_tp]
    for d in range(4):
        back_ref[d * CAP : (d + 1) * CAP, :] = near[d][...]
    for d in range(n_z - 2):
        at = (2 * d + 4) * CAP
        back_ref[at : at + CAP, :] = far[d][:CAP, :]
        back_ref[at + CAP : at + 2 * CAP, :] = core_ref[d * CAP : (d + 1) * CAP, :]
    mixed = jnp.dot(mix_ref[...], back_ref[...], preferred_element_type=F32)
    state = rows_ref[...].astype(F32) + mixed
    square = jnp.sum(state * state, axis=1, keepdims=True)
    scaled = (state * gain_ref[...]).astype(BF16)
    value = lax.dot_general(
        scaled, weight_ref[...], (((1,), (1,)), ((), ())), preferred_element_type=F32
    ).astype(BF16)
    high = square.astype(BF16).astype(F32)
    rest = square - high
    middle = rest.astype(BF16).astype(F32)
    low = rest - middle
    seats, wide = outs[0].shape
    lane = lax.broadcasted_iota(jnp.int32, (square.shape[0], wide - cache_width), 1)
    extra = jnp.where(lane == 0, high, jnp.where(lane == 1, middle, jnp.where(lane == 2, low, 0.0)))
    extra = extra.astype(BF16)
    for d in range(n_tp):
        outs[d][:, :cache_width] = value[d * seats : (d + 1) * seats]
        outs[d][:, cache_width:] = extra[d * seats : (d + 1) * seats]


def finish_kernel(n_tp, width, rank_width, *refs):
    parts = refs[:n_tp]
    gain_ref, cos_ref, sin_ref, latent_ref, rotary_ref = refs[n_tp:]
    total = parts[0][...].astype(F32)
    for other in parts[1:]:
        total = total + other[...].astype(F32)
    half = cos_ref.shape[1]
    cache_width = rank_width + 2 * half
    square = jnp.sum(total[:, cache_width : cache_width + 3], axis=1, keepdims=True)
    cache = total[:, :cache_width] * lax.rsqrt(square / width + EPS)
    latent = cache[:, :rank_width]
    scale = lax.rsqrt(jnp.mean(latent * latent, axis=1, keepdims=True) + EPS)
    latent_ref[...] = (latent * scale * gain_ref[...]).astype(BF16)
    first = cache[:, rank_width : rank_width + half]
    second = cache[:, rank_width + half :]
    cosine, sine = cos_ref[...], sin_ref[...]
    rotary_ref[:, :half] = (first * cosine - second * sine).astype(BF16)
    rotary_ref[:, half:] = (second * cosine + first * sine).astype(BF16)


def call(kernel, out_shape, args, scratch=(), flops=0, hbm=()):
    moved = sum(a.size * a.dtype.itemsize for a in args)
    vmem = pl.BlockSpec(memory_space=pltpu.VMEM)
    args = [
        pltpu.with_memory_space_constraint(a, pltpu.HBM) if i in hbm else a
        for i, a in enumerate(args)
    ]
    return pl.pallas_call(
        kernel,
        out_shape=out_shape,
        in_specs=[
            pl.BlockSpec(memory_space=pltpu.HBM) if i in hbm else vmem for i in range(len(args))
        ],
        out_specs=[vmem] * len(out_shape),
        scratch_shapes=list(scratch),
        compiler_params=pltpu.CompilerParams(vmem_limit_bytes=VMEM_LIMIT),
        cost_estimate=pl.CostEstimate(flops=flops, bytes_accessed=moved, transcendentals=0),
    )(*args)


def swap(value, axis, d):
    return lax.ppermute(value, axis, [(i, i ^ d) for i in range(lax.axis_size(axis))])


def step_swap(value, step):
    n_ep, n_tp = lax.axis_size("ep"), lax.axis_size("tp")
    last = n_tp.bit_length() - 2
    pairs = []
    for e in range(n_ep):
        bit = 1 << (last - step if e % 2 else step)
        pairs += [(e * n_tp + t, e * n_tp + (t ^ bit)) for t in range(n_tp)]
    return lax.ppermute(value, ("ep", "tp"), pairs)


def double(value, n_tp):
    held = [value]
    for step in range(n_tp.bit_length() - 1):
        whole = held[0] if step == 0 else jnp.concatenate(held, axis=0)
        held.append(step_swap(whole, step))
    return held


def halve(send, keep, n_tp):
    terms = [keep, step_swap(send, 0)]
    for step in range(1, n_tp.bit_length() - 1):
        count = keep.shape[0] >> step
        (out,) = call(fold_kernel, [jax.ShapeDtypeStruct((count, keep.shape[1]), BF16)], terms)
        terms.append(step_swap(out, step))
    return terms


def collect(values):
    got = [swap(values[d], "tp", d) for d in reversed(range(1, len(values)))]
    return [values[0]] + got[::-1]


def on_device(
    hidden,
    moe_gain,
    route_logits,
    routes,
    gate_weight,
    up_weight,
    down_weight,
    attn_gain,
    latent_weight,
    latent_gain,
    positions,
    owners,
):
    n_ep = lax.axis_size("ep")
    n_tp = lax.axis_size("tp")
    n_z = n_ep // 2
    tokens, width = hidden.shape
    share = width // n_tp
    ff = gate_weight.shape[2]
    slots = n_ep * CAP
    seat_cap = max(2, tokens // n_tp // 4)
    seats = n_tp * seat_cap
    rank_width = latent_gain.shape[0]
    cache_width = latent_weight.shape[1]
    half = (cache_width - rank_width) // 2
    wide = (cache_width + 3 + 127) // 128 * 128
    struct = jax.ShapeDtypeStruct
    chunks = width // 512 if width % 512 == 0 else 1

    own, to_core, *outgoing, combine = call(
        functools.partial(dispatch_kernel, n_ep, n_tp),
        [struct((CAP, width), BF16), struct((n_tp * CAP, share), BF16)]
        + [struct((2 * CAP, share), BF16)] * (n_z - 1)
        + [struct((slots, tokens), BF16)],
        (routes.T, route_logits.T, hidden, moe_gain),
        [
            pltpu.VMEM(routes.T.shape, jnp.int32),
            pltpu.VMEM(routes.T.shape, F32),
            pltpu.VMEM(hidden.shape, BF16),
            pltpu.VMEM((1, width), F32),
            pltpu.VMEM((slots, tokens), BF16),
            pltpu.VMEM((2 * CAP, width), F32),
            pltpu.SemaphoreType.DMA((3 + chunks,)),
        ],
        flops=4 * slots * tokens * width,
        hbm=(0, 1, 2, 3),
    )
    arrived = [swap(outgoing[d - 1], "ep", 2 * d) for d in reversed(range(1, n_z))][::-1]
    from_core = swap(to_core, "ep", 1)
    gate_w, up_w, down_w = gate_weight[0], up_weight[0], down_weight[0]
    *loaded, mark = call(
        load_kernel,
        [struct(w.shape, BF16) for w in (gate_w, up_w, down_w)] + [struct((8, 128), F32)],
        (combine, gate_w, up_w, down_w),
        [pltpu.SemaphoreType.DMA((3,))],
        hbm=(1, 2, 3),
    )
    arrived, mark, from_core = lax.optimization_barrier((arrived, mark, from_core))
    crossed = swap(jnp.concatenate([piece[CAP:] for piece in arrived], axis=0), "ep", 1)
    direct = jnp.concatenate([piece[:CAP] for piece in arrived], axis=0)
    direct_shares = double(direct, n_tp)
    crossed_shares = double(crossed, n_tp)[1:]
    half_rows = (n_z - 1) * CAP
    near_rows, far_rows = 4 * CAP, slots - 4 * CAP
    inner, gate_sum, up_sum = call(
        functools.partial(first_kernel, n_tp),
        [struct((2 * CAP + half_rows, ff), BF16)] + [struct((half_rows, ff), F32)] * 2,
        (own, from_core, *direct_shares, crossed, *loaded[:2], mark),
        [pltpu.VMEM((2 * CAP, width), BF16)],
        flops=2 * slots * width * ff,
    )
    far_send, far_keep, near_send, near_keep = call(
        functools.partial(expert_kernel, n_tp),
        [struct((n_tp // 2 * far_rows, share), BF16)] * 2
        + [struct((n_tp // 2 * near_rows, share), BF16)] * 2,
        (*crossed_shares, *loaded, inner, gate_sum, up_sum),
        flops=2 * slots * width * ff * 3,
    )
    combine, far_keep = lax.optimization_barrier((combine, far_keep))
    share_of = hidden
    if share % 128:
        share_of = lax.dynamic_slice_in_dim(hidden, lax.axis_index("tp") * share, share, 1)
    rows, mix, at = call(
        functools.partial(seats_kernel, n_tp, seat_cap),
        [
            struct((n_tp * seats, share), BF16),
            struct((n_tp * seats, slots), BF16),
            struct((seats, 1), F32),
        ],
        (owners[None, :], positions[None, :], combine, share_of),
        [pltpu.VMEM((tokens, share), BF16), pltpu.SemaphoreType.DMA(())],
        flops=2 * n_tp * seats * tokens * (share + slots),
        hbm=(3,),
    )
    freqs = ROPE_BASE ** (-jnp.arange(half, dtype=F32) / half)
    angles = at * freqs[None, :]
    cosine, sine = jnp.cos(angles), jnp.sin(angles)

    far_terms = halve(far_send, far_keep, n_tp)
    far_terms, rows, mix = lax.optimization_barrier((far_terms, rows, mix))
    near_terms = halve(near_send, near_keep, n_tp)
    far_done = call(
        functools.partial(sum_kernel, len(far_terms)),
        [struct((2 * CAP, share), BF16)] * (n_z - 2),
        far_terms,
    )
    far_back = [swap(far_done[d - 2], "ep", 2 * d) for d in range(2, n_z)]
    near_done = call(
        functools.partial(sum_kernel, len(near_terms)),
        [struct((CAP, share), BF16)] * 4,
        near_terms,
    )
    near_back = [near_done[0]] + [swap(near_done[d], "ep", d) for d in (1, 2, 3)]
    crossed = swap(jnp.concatenate([piece[CAP:] for piece in far_back], axis=0), "ep", 1)
    partial = call(
        functools.partial(cache_kernel, n_z, n_tp, cache_width),
        [struct((seats, wide), BF16)] * n_tp,
        (*near_back, *far_back, crossed, mix, rows, attn_gain[None, :], latent_weight.T),
        [pltpu.VMEM((slots, share), BF16)],
        flops=2 * n_tp * seats * share * (slots + cache_width),
    )
    return tuple(
        call(
            functools.partial(finish_kernel, n_tp, width, rank_width),
            [struct((seats, rank_width), BF16), struct((seats, 2 * half), BF16)],
            (*collect(partial), latent_gain[None, :], cosine, sine),
        )
    )


def solution(mesh):
    placed = (
        P(("groups", "ep"), None),
        P(),
        P(("groups", "ep"), None),
        P(("groups", "ep"), None),
        P("ep", None, "tp"),
        P("ep", None, "tp"),
        P("ep", "tp", None),
        P("tp"),
        P("tp", None),
        P(),
        P(("groups", "ep")),
        P(("groups", "ep")),
    )
    return jax.shard_map(
        on_device,
        mesh=mesh,
        in_specs=placed,
        out_specs=(P(("groups", "ep", "tp"), None), P(("groups", "ep", "tp"), None)),
        check_vma=False,
    )
```

```python
import functools

import jax
import jax.numpy as jnp
from jax import lax
from jax.experimental import pallas as pl
from jax.experimental.pallas import tpu as pltpu
from jax.sharding import PartitionSpec as P

CAP = 16
EPS = 1e-06
ROUTE_SCALE = 2.5
ROPE_BASE = 10000.0
BF16 = jnp.bfloat16
F32 = jnp.float32
VMEM_LIMIT = 40 * 1024 * 1024


def columns_of(ref, index, count, share):
    if share % 128 == 0:
        return ref[:, pl.ds(pl.multiple_of(index * share, 128), share)]
    out = ref[:, 0:share]
    for q in range(1, count):
        out = jnp.where(index == q, ref[:, q * share : (q + 1) * share], out)
    return out


def dispatch_kernel(n_ep, n_tp, routes_hbm, logits_hbm, hidden_hbm, gain_hbm, *refs):
    own_ref, core_ref = refs[:2]
    outs, combine_ref = refs[2 : n_ep // 2 + 1], refs[n_ep // 2 + 1]
    routes_ref, logits_ref, hidden_ref, gain_ref, pick_ref, head_ref, sems = refs[n_ep // 2 + 2 :]
    me = lax.axis_index("ep")
    part = lax.axis_index("tp")
    tokens, width = hidden_ref.shape
    share = width // n_tp
    step = 512 if width % 512 == 0 else width
    starts = range(0, width, step)
    small = [
        pltpu.make_async_copy(routes_hbm, routes_ref, sems.at[0]),
        pltpu.make_async_copy(logits_hbm, logits_ref, sems.at[1]),
        pltpu.make_async_copy(gain_hbm, gain_ref.at[0], sems.at[2]),
    ]
    large = [
        pltpu.make_async_copy(
            hidden_hbm.at[:, c : c + step], hidden_ref.at[:, c : c + step], sems.at[3 + i]
        )
        for i, c in enumerate(starts)
    ]
    for copy in small + large:
        copy.start()
    small[0].wait()
    small[1].wait()
    routes = routes_ref[...]
    affinity = jax.nn.sigmoid(logits_ref[...])
    weight = ROUTE_SCALE * affinity / jnp.sum(affinity, axis=0, keepdims=True)
    weight = weight.astype(BF16).astype(F32)
    expert = lax.broadcasted_iota(jnp.int32, (n_ep, tokens), 0) ^ me
    hit = jnp.zeros((n_ep, tokens), F32)
    gain_of = jnp.zeros((n_ep, tokens), F32)
    for k in range(routes.shape[0]):
        same = routes[k : k + 1, :] == expert
        hit = jnp.where(same, 1.0, hit)
        gain_of = jnp.where(same, weight[k : k + 1, :], gain_of)
    earlier = lax.broadcasted_iota(jnp.int32, (tokens, tokens), 0) < lax.broadcasted_iota(
        jnp.int32, (tokens, tokens), 1
    )
    rank = jnp.dot(hit.astype(BF16), earlier.astype(F32).astype(BF16), preferred_element_type=F32)
    rank = jnp.where(hit > 0, rank, -1.0)
    place = lax.broadcasted_iota(jnp.int32, (CAP, tokens), 0).astype(F32)
    for d in range(n_ep):
        match = rank[d : d + 1, :] == place
        rows = slice(d * CAP, (d + 1) * CAP)
        pick_ref[rows, :] = jnp.where(match, 1.0, 0.0).astype(BF16)
        combine_ref[rows, :] = jnp.where(match, gain_of[d : d + 1, :], 0.0).astype(BF16)
    pick = pick_ref[...]
    head = 2 * CAP
    square = jnp.zeros((n_ep * CAP, 1), F32)
    for copy in large:
        copy.wait()
    for c in starts:
        got = jnp.dot(pick, hidden_ref[:, c : c + step], preferred_element_type=F32)
        square = square + jnp.sum(got * got, axis=1, keepdims=True)
        head_ref[:, c : c + step] = got[:head]
    small[2].wait()
    scale = lax.rsqrt(square / width + EPS)
    got = jnp.dot(pick[head:], columns_of(hidden_ref, part, n_tp, share), preferred_element_type=F32)
    rest = (got * scale[head:] * columns_of(gain_ref, part, n_tp, share)).astype(BF16)
    at = 0
    for out in outs:
        out[...] = rest[at : at + out.shape[0]]
        at += out.shape[0]
    near = (head_ref[...] * scale[:head] * gain_ref[...]).astype(BF16)
    own_ref[...] = near[:CAP]
    for q in range(n_tp):
        core_ref[q * CAP : (q + 1) * CAP, :] = near[CAP:, q * share : (q + 1) * share]


def load_kernel(after_ref, *refs):
    count = (len(refs) - 2) // 2
    mark_ref, sems = refs[-2:]
    copies = [
        pltpu.make_async_copy(refs[i], refs[count + i], sems.at[i]) for i in range(count)
    ]
    for copy in copies:
        copy.start()
    mark_ref[...] = jnp.zeros(mark_ref.shape, F32)
    for copy in copies:
        copy.wait()


def first_kernel(n_tp, own_ref, core_ref, *refs):
    shares, mine_ref = refs[:n_tp], refs[n_tp]
    gate_ref, up_ref, _, inner_ref, gate_sum_ref, up_sum_ref, head_ref = refs[n_tp + 1 :]
    part = lax.axis_index("tp")
    share = mine_ref.shape[1]
    head_ref[:CAP, :] = own_ref[...]
    for q in range(n_tp):
        columns = slice(q * share, (q + 1) * share)
        head_ref[CAP : 2 * CAP, columns] = core_ref[q * CAP : (q + 1) * CAP, :]
    sums = []
    for weight_ref, sum_ref in zip((gate_ref, up_ref), (gate_sum_ref, up_sum_ref)):
        total = jnp.dot(head_ref[...], weight_ref[...], preferred_element_type=F32)
        other = None
        for d in range(n_tp):
            depth = pl.ds(pl.multiple_of((part ^ d) * share, CAP), share)
            term = jnp.dot(shares[d][...], weight_ref[depth, :], preferred_element_type=F32)
            other = term if other is None else other + term
        sums.append(jnp.concatenate([total, other], axis=0))
        depth = pl.ds(pl.multiple_of(part * share, CAP), share)
        sum_ref[...] = jnp.dot(mine_ref[...], weight_ref[depth, :], preferred_element_type=F32)
    gate, upper = sums
    inner_ref[...] = (gate / (1.0 + jnp.exp(-gate)) * upper).astype(BF16)


def expert_kernel(n_tp, *refs):
    rows = refs[: n_tp - 1]
    gate_ref, up_ref, down_ref, first_ref, gate_sum_ref, up_sum_ref = refs[n_tp - 1 : n_tp + 5]
    far_outs = refs[n_tp + 5 : 2 * n_tp + 5]
    near_outs = refs[2 * n_tp + 5 :]
    part = lax.axis_index("tp")
    share = rows[0].shape[1]
    gate = gate_sum_ref[...]
    upper = up_sum_ref[...]
    for d in range(1, n_tp):
        value = rows[d - 1][...]
        depth = pl.ds(pl.multiple_of((part ^ d) * share, CAP), share)
        gate = gate + jnp.dot(value, gate_ref[depth, :], preferred_element_type=F32)
        upper = upper + jnp.dot(value, up_ref[depth, :], preferred_element_type=F32)
    second = (gate / (1.0 + jnp.exp(-gate)) * upper).astype(BF16)
    first = first_ref[...]
    groups = [first[:CAP], first[CAP : 2 * CAP]]
    for at in range(0, second.shape[0], CAP):
        groups += [first[2 * CAP + at : 3 * CAP + at], second[at : at + CAP]]
    inner = jnp.concatenate(groups[2:] + groups[:2], axis=0)
    count = (len(groups) - 2) * CAP
    for d in range(n_tp):
        down = columns_of(down_ref, part ^ d, n_tp, share)
        out = jnp.dot(inner, down, preferred_element_type=F32).astype(BF16)
        far_outs[d][...] = out[:count]
        near_outs[d][...] = out[count:]


def sum_kernel(n_tp, *refs):
    parts, outs = refs[:n_tp], refs[n_tp:]
    at = 0
    for out in outs:
        rows = slice(at, at + out.shape[0])
        total = parts[0][rows, :].astype(F32)
        for other in parts[1:]:
            total = total + other[rows, :].astype(F32)
        out[...] = total.astype(BF16)
        at += out.shape[0]


def seats_kernel(
    n_tp,
    seat_cap,
    owners_ref,
    positions_ref,
    combine_ref,
    hidden_hbm,
    rows_ref,
    mix_ref,
    at_ref,
    hidden_ref,
    sem,
):
    part = lax.axis_index("tp")
    tokens, share = hidden_ref.shape
    if hidden_hbm.shape[1] != share:
        hidden_hbm = hidden_hbm.at[:, pl.ds(pl.multiple_of(part * share, 128), share)]
    copy = pltpu.make_async_copy(hidden_hbm, hidden_ref, sem)
    copy.start()
    source_rows = tokens // n_tp
    owners = owners_ref[...] ^ part
    owner = lax.broadcasted_iota(jnp.int32, (n_tp, tokens), 0)
    hot = jnp.where(owners == owner, 1.0, 0.0)
    first = lax.broadcasted_iota(jnp.int32, (tokens, tokens), 0)
    second = lax.broadcasted_iota(jnp.int32, (tokens, tokens), 1)
    earlier = jnp.where((first < second) & (first // source_rows == second // source_rows), 1.0, 0.0)
    before = jnp.dot(hot.astype(BF16), earlier.astype(BF16), preferred_element_type=F32)
    seat = jnp.sum(before * hot, axis=0, keepdims=True).astype(jnp.int32)
    source = lax.broadcasted_iota(jnp.int32, (1, tokens), 1) // source_rows
    code = owners * (n_tp * seat_cap) + source * seat_cap + seat
    seats = n_tp * seat_cap
    held = lax.broadcasted_iota(jnp.int32, (n_tp * seats, tokens), 0) == code
    pick = jnp.where(held, 1.0, 0.0).astype(BF16)
    mix_ref[...] = lax.dot_general(
        pick, combine_ref[...], (((1,), (1,)), ((), ())), preferred_element_type=F32
    ).astype(BF16)
    place = jnp.where(held[:seats], positions_ref[...].astype(F32), 0.0)
    at_ref[...] = jnp.sum(place, axis=1, keepdims=True)
    copy.wait()
    rows_ref[...] = jnp.dot(pick, hidden_ref[...], preferred_element_type=F32).astype(BF16)


def cache_kernel(n_z, n_tp, cache_width, *refs):
    pieces, core_ref = refs[:n_z], refs[n_z]
    mix_ref, rows_ref, gain_ref, weight_ref = refs[n_z + 1 : n_z + 5]
    outs, back_ref = refs[n_z + 5 : n_z + 5 + n_tp], refs[n_z + 5 + n_tp]
    for d in range(n_z):
        at = 2 * d * CAP
        back_ref[at : at + CAP, :] = pieces[d][:CAP, :]
        back_ref[at + CAP : at + 2 * CAP, :] = core_ref[d * CAP : (d + 1) * CAP, :]
    mixed = jnp.dot(mix_ref[...], back_ref[...], preferred_element_type=F32)
    state = rows_ref[...].astype(F32) + mixed
    square = jnp.sum(state * state, axis=1, keepdims=True)
    scaled = (state * gain_ref[...]).astype(BF16)
    value = lax.dot_general(
        scaled, weight_ref[...], (((1,), (1,)), ((), ())), preferred_element_type=F32
    ).astype(BF16)
    high = square.astype(BF16).astype(F32)
    rest = square - high
    middle = rest.astype(BF16).astype(F32)
    low = rest - middle
    seats, wide = outs[0].shape
    lane = lax.broadcasted_iota(jnp.int32, (square.shape[0], wide - cache_width), 1)
    extra = jnp.where(lane == 0, high, jnp.where(lane == 1, middle, jnp.where(lane == 2, low, 0.0)))
    extra = extra.astype(BF16)
    for d in range(n_tp):
        outs[d][:, :cache_width] = value[d * seats : (d + 1) * seats]
        outs[d][:, cache_width:] = extra[d * seats : (d + 1) * seats]


def finish_kernel(n_tp, width, rank_width, *refs):
    parts = refs[:n_tp]
    gain_ref, cos_ref, sin_ref, latent_ref, rotary_ref = refs[n_tp:]
    total = parts[0][...].astype(F32)
    for other in parts[1:]:
        total = total + other[...].astype(F32)
    half = cos_ref.shape[1]
    cache_width = rank_width + 2 * half
    square = jnp.sum(total[:, cache_width : cache_width + 3], axis=1, keepdims=True)
    cache = total[:, :cache_width] * lax.rsqrt(square / width + EPS)
    latent = cache[:, :rank_width]
    scale = lax.rsqrt(jnp.mean(latent * latent, axis=1, keepdims=True) + EPS)
    latent_ref[...] = (latent * scale * gain_ref[...]).astype(BF16)
    first = cache[:, rank_width : rank_width + half]
    second = cache[:, rank_width + half :]
    cosine, sine = cos_ref[...], sin_ref[...]
    rotary_ref[:, :half] = (first * cosine - second * sine).astype(BF16)
    rotary_ref[:, half:] = (second * cosine + first * sine).astype(BF16)


def call(kernel, out_shape, args, scratch=(), flops=0, hbm=()):
    moved = sum(a.size * a.dtype.itemsize for a in args)
    vmem = pl.BlockSpec(memory_space=pltpu.VMEM)
    args = [
        pltpu.with_memory_space_constraint(a, pltpu.HBM) if i in hbm else a
        for i, a in enumerate(args)
    ]
    return pl.pallas_call(
        kernel,
        out_shape=out_shape,
        in_specs=[
            pl.BlockSpec(memory_space=pltpu.HBM) if i in hbm else vmem for i in range(len(args))
        ],
        out_specs=[vmem] * len(out_shape),
        scratch_shapes=list(scratch),
        compiler_params=pltpu.CompilerParams(vmem_limit_bytes=VMEM_LIMIT),
        cost_estimate=pl.CostEstimate(flops=flops, bytes_accessed=moved, transcendentals=0),
    )(*args)


def swap(value, axis, d):
    return lax.ppermute(value, axis, [(i, i ^ d) for i in range(lax.axis_size(axis))])


def spread(value, n_tp):
    return [swap(value, "tp", d) for d in reversed(range(1, n_tp))][::-1]


def collect(values):
    got = [swap(values[d], "tp", d) for d in reversed(range(1, len(values)))]
    return [values[0]] + got[::-1]


def on_device(
    hidden,
    moe_gain,
    route_logits,
    routes,
    gate_weight,
    up_weight,
    down_weight,
    attn_gain,
    latent_weight,
    latent_gain,
    positions,
    owners,
):
    n_ep = lax.axis_size("ep")
    n_tp = lax.axis_size("tp")
    n_z = n_ep // 2
    tokens, width = hidden.shape
    share = width // n_tp
    ff = gate_weight.shape[2]
    slots = n_ep * CAP
    seat_cap = max(2, tokens // n_tp // 4)
    seats = n_tp * seat_cap
    rank_width = latent_gain.shape[0]
    cache_width = latent_weight.shape[1]
    half = (cache_width - rank_width) // 2
    wide = (cache_width + 3 + 127) // 128 * 128
    struct = jax.ShapeDtypeStruct
    chunks = width // 512 if width % 512 == 0 else 1

    own, to_core, *outgoing, combine = call(
        functools.partial(dispatch_kernel, n_ep, n_tp),
        [struct((CAP, width), BF16), struct((n_tp * CAP, share), BF16)]
        + [struct((2 * CAP, share), BF16)] * (n_z - 1)
        + [struct((slots, tokens), BF16)],
        (routes.T, route_logits.T, hidden, moe_gain),
        [
            pltpu.VMEM(routes.T.shape, jnp.int32),
            pltpu.VMEM(routes.T.shape, F32),
            pltpu.VMEM(hidden.shape, BF16),
            pltpu.VMEM((1, width), F32),
            pltpu.VMEM((slots, tokens), BF16),
            pltpu.VMEM((2 * CAP, width), F32),
            pltpu.SemaphoreType.DMA((3 + chunks,)),
        ],
        flops=4 * slots * tokens * width,
        hbm=(0, 1, 2, 3),
    )
    arrived = [swap(outgoing[d - 1], "ep", 2 * d) for d in reversed(range(1, n_z))][::-1]
    from_core = swap(to_core, "ep", 1)
    gate_w, up_w, down_w = gate_weight[0], up_weight[0], down_weight[0]
    *loaded, mark = call(
        load_kernel,
        [struct(w.shape, BF16) for w in (gate_w, up_w, down_w)] + [struct((8, 128), F32)],
        (combine, gate_w, up_w, down_w),
        [pltpu.SemaphoreType.DMA((3,))],
        hbm=(1, 2, 3),
    )
    arrived, mark = lax.optimization_barrier((arrived, mark))
    crossed = swap(jnp.concatenate([piece[CAP:] for piece in arrived], axis=0), "ep", 1)
    direct = jnp.concatenate([piece[:CAP] for piece in arrived], axis=0)
    direct_shares = [direct] + spread(direct, n_tp)
    crossed_shares = spread(crossed, n_tp)
    half_rows = (n_z - 1) * CAP
    near_rows, far_rows = 2 * CAP, slots - 2 * CAP
    inner, gate_sum, up_sum = call(
        functools.partial(first_kernel, n_tp),
        [struct((2 * CAP + half_rows, ff), BF16)] + [struct((half_rows, ff), F32)] * 2,
        (own, from_core, *direct_shares, crossed, *loaded[:2], mark),
        [pltpu.VMEM((2 * CAP, width), BF16)],
        flops=2 * slots * width * ff,
    )
    terms = call(
        functools.partial(expert_kernel, n_tp),
        [struct((far_rows, share), BF16)] * n_tp + [struct((near_rows, share), BF16)] * n_tp,
        (*crossed_shares, *loaded, inner, gate_sum, up_sum),
        flops=2 * slots * width * ff * 3,
    )
    combine, _ = lax.optimization_barrier((combine, terms[0]))
    share_of = hidden
    if share % 128:
        share_of = lax.dynamic_slice_in_dim(hidden, lax.axis_index("tp") * share, share, 1)
    rows, mix, at = call(
        functools.partial(seats_kernel, n_tp, seat_cap),
        [
            struct((n_tp * seats, share), BF16),
            struct((n_tp * seats, slots), BF16),
            struct((seats, 1), F32),
        ],
        (owners[None, :], positions[None, :], combine, share_of),
        [pltpu.VMEM((tokens, share), BF16), pltpu.SemaphoreType.DMA(())],
        flops=2 * n_tp * seats * tokens * (share + slots),
        hbm=(3,),
    )
    freqs = ROPE_BASE ** (-jnp.arange(half, dtype=F32) / half)
    angles = at * freqs[None, :]
    cosine, sine = jnp.cos(angles), jnp.sin(angles)

    far_terms = collect(terms[:n_tp])
    far_terms, rows, mix = lax.optimization_barrier((far_terms, rows, mix))
    near_terms = collect(terms[n_tp:])
    far_done = call(
        functools.partial(sum_kernel, n_tp),
        [struct((2 * CAP, share), BF16)] * (n_z - 1),
        far_terms,
    )
    far_back = [swap(far_done[d - 1], "ep", 2 * d) for d in reversed(range(1, n_z))][::-1]
    near_done = call(
        functools.partial(sum_kernel, n_tp), [struct((2 * CAP, share), BF16)], near_terms
    )
    back = [*near_done, *far_back]
    crossed = swap(jnp.concatenate([piece[CAP:] for piece in back], axis=0), "ep", 1)
    partial = call(
        functools.partial(cache_kernel, n_z, n_tp, cache_width),
        [struct((seats, wide), BF16)] * n_tp,
        (*back, crossed, mix, rows, attn_gain[None, :], latent_weight.T),
        [pltpu.VMEM((slots, share), BF16)],
        flops=2 * n_tp * seats * share * (slots + cache_width),
    )
    return tuple(
        call(
            functools.partial(finish_kernel, n_tp, width, rank_width),
            [struct((seats, rank_width), BF16), struct((seats, 2 * half), BF16)],
            (*collect(partial), latent_gain[None, :], cosine, sine),
        )
    )


def solution(mesh):
    placed = (
        P(("groups", "ep"), None),
        P(),
        P(("groups", "ep"), None),
        P(("groups", "ep"), None),
        P("ep", None, "tp"),
        P("ep", None, "tp"),
        P("ep", "tp", None),
        P("tp"),
        P("tp", None),
        P(),
        P(("groups", "ep")),
        P(("groups", "ep")),
    )
    return jax.shard_map(
        on_device,
        mesh=mesh,
        in_specs=placed,
        out_specs=(P(("groups", "ep", "tp"), None), P(("groups", "ep", "tp"), None)),
        check_vma=False,
    )
```

```python
import functools

import jax
import jax.numpy as jnp
from jax import lax
from jax.experimental import pallas as pl
from jax.experimental.pallas import tpu as pltpu
from jax.sharding import PartitionSpec as P

CAP = 16
EPS = 1e-06
ROUTE_SCALE = 2.5
ROPE_BASE = 10000.0
BF16 = jnp.bfloat16
F32 = jnp.float32
VMEM_LIMIT = 40 * 1024 * 1024


def columns_of(ref, index, count, share):
    if share % 128 == 0:
        return ref[:, pl.ds(pl.multiple_of(index * share, 128), share)]
    out = ref[:, 0:share]
    for q in range(1, count):
        out = jnp.where(index == q, ref[:, q * share : (q + 1) * share], out)
    return out


def dispatch_kernel(n_ep, n_tp, routes_hbm, logits_hbm, hidden_hbm, gain_hbm, *refs):
    own_ref, core_ref, near_ref = refs[:3]
    outs, combine_ref = refs[3 : n_ep // 2 + 1], refs[n_ep // 2 + 1]
    routes_ref, logits_ref, hidden_ref, gain_ref, pick_ref, head_ref, sems = refs[n_ep // 2 + 2 :]
    me = lax.axis_index("ep")
    part = lax.axis_index("tp")
    tokens, width = hidden_ref.shape
    share = width // n_tp
    step = 512 if width % 512 == 0 else width
    starts = range(0, width, step)
    small = [
        pltpu.make_async_copy(routes_hbm, routes_ref, sems.at[0]),
        pltpu.make_async_copy(logits_hbm, logits_ref, sems.at[1]),
        pltpu.make_async_copy(gain_hbm, gain_ref.at[0], sems.at[2]),
    ]
    large = [
        pltpu.make_async_copy(
            hidden_hbm.at[:, c : c + step], hidden_ref.at[:, c : c + step], sems.at[3 + i]
        )
        for i, c in enumerate(starts)
    ]
    for copy in small + large:
        copy.start()
    small[0].wait()
    small[1].wait()
    routes = routes_ref[...]
    affinity = jax.nn.sigmoid(logits_ref[...])
    weight = ROUTE_SCALE * affinity / jnp.sum(affinity, axis=0, keepdims=True)
    weight = weight.astype(BF16).astype(F32)
    expert = lax.broadcasted_iota(jnp.int32, (n_ep, tokens), 0) ^ me
    hit = jnp.zeros((n_ep, tokens), F32)
    gain_of = jnp.zeros((n_ep, tokens), F32)
    for k in range(routes.shape[0]):
        same = routes[k : k + 1, :] == expert
        hit = jnp.where(same, 1.0, hit)
        gain_of = jnp.where(same, weight[k : k + 1, :], gain_of)
    earlier = lax.broadcasted_iota(jnp.int32, (tokens, tokens), 0) < lax.broadcasted_iota(
        jnp.int32, (tokens, tokens), 1
    )
    rank = jnp.dot(hit.astype(BF16), earlier.astype(F32).astype(BF16), preferred_element_type=F32)
    rank = jnp.where(hit > 0, rank, -1.0)
    place = lax.broadcasted_iota(jnp.int32, (CAP, tokens), 0).astype(F32)
    for d in range(n_ep):
        match = rank[d : d + 1, :] == place
        rows = slice(d * CAP, (d + 1) * CAP)
        pick_ref[rows, :] = jnp.where(match, 1.0, 0.0).astype(BF16)
        combine_ref[rows, :] = jnp.where(match, gain_of[d : d + 1, :], 0.0).astype(BF16)
    pick = pick_ref[...]
    head = 4 * CAP
    square = jnp.zeros((n_ep * CAP, 1), F32)
    for copy in large:
        copy.wait()
    for c in starts:
        got = jnp.dot(pick, hidden_ref[:, c : c + step], preferred_element_type=F32)
        square = square + jnp.sum(got * got, axis=1, keepdims=True)
        head_ref[:, c : c + step] = got[:head]
    small[2].wait()
    scale = lax.rsqrt(square / width + EPS)
    got = jnp.dot(pick[head:], columns_of(hidden_ref, part, n_tp, share), preferred_element_type=F32)
    rest = (got * scale[head:] * columns_of(gain_ref, part, n_tp, share)).astype(BF16)
    at = 0
    for out in outs:
        out[...] = rest[at : at + out.shape[0]]
        at += out.shape[0]
    whole = (head_ref[...] * scale[:head] * gain_ref[...]).astype(BF16)
    own_ref[...] = whole[:CAP]
    for q in range(n_tp):
        columns = slice(q * share, (q + 1) * share)
        core_ref[q * CAP : (q + 1) * CAP, :] = whole[CAP : 2 * CAP, columns]
        near_ref[q * CAP : (q + 1) * CAP, :] = whole[2 * CAP : 3 * CAP, columns]
        near_ref[(n_tp + q) * CAP : (n_tp + q + 1) * CAP, :] = whole[3 * CAP :, columns]


def load_kernel(after_ref, *refs):
    count = (len(refs) - 2) // 2
    mark_ref, sems = refs[-2:]
    copies = [
        pltpu.make_async_copy(refs[i], refs[count + i], sems.at[i]) for i in range(count)
    ]
    for copy in copies:
        copy.start()
    mark_ref[...] = jnp.zeros(mark_ref.shape, F32)
    for copy in copies:
        copy.wait()


def first_kernel(
    n_tp,
    own_ref,
    core_ref,
    near_ref,
    cross_ref,
    mine_ref,
    gate_ref,
    up_ref,
    mark_ref,
    inner_ref,
    gate_sum_ref,
    up_sum_ref,
    head_ref,
):
    part = lax.axis_index("tp")
    share = mine_ref.shape[1]
    head_ref[:CAP, :] = own_ref[...]
    for i, ref in enumerate((core_ref, near_ref, cross_ref)):
        for q in range(n_tp):
            rows = slice((i + 1) * CAP, (i + 2) * CAP)
            head_ref[rows, q * share : (q + 1) * share] = ref[q * CAP : (q + 1) * CAP, :]
    depth = pl.ds(pl.multiple_of(part * share, CAP), share)
    gate, upper = (
        jnp.dot(head_ref[...], ref[...], preferred_element_type=F32) for ref in (gate_ref, up_ref)
    )
    for weight_ref, sum_ref in zip((gate_ref, up_ref), (gate_sum_ref, up_sum_ref)):
        sum_ref[...] = jnp.dot(mine_ref[...], weight_ref[depth, :], preferred_element_type=F32)
    inner_ref[...] = (gate / (1.0 + jnp.exp(-gate)) * upper).astype(BF16)


def expert_kernel(n_tp, *refs):
    rows = refs[: n_tp - 1]
    gate_ref, up_ref, down_ref, near_ref, gate_sum_ref, up_sum_ref = refs[n_tp - 1 : n_tp + 5]
    far_outs = refs[n_tp + 5 : 2 * n_tp + 5]
    near_outs = refs[2 * n_tp + 5 :]
    part = lax.axis_index("tp")
    share = rows[0].shape[1]
    gate = gate_sum_ref[...]
    upper = up_sum_ref[...]
    for d in range(1, n_tp):
        value = rows[d - 1][...]
        depth = pl.ds(pl.multiple_of((part ^ d) * share, CAP), share)
        gate = gate + jnp.dot(value, gate_ref[depth, :], preferred_element_type=F32)
        upper = upper + jnp.dot(value, up_ref[depth, :], preferred_element_type=F32)
    far = (gate / (1.0 + jnp.exp(-gate)) * upper).astype(BF16)
    inner = jnp.concatenate([far, near_ref[...]], axis=0)
    count = far.shape[0]
    for d in range(n_tp):
        down = columns_of(down_ref, part ^ d, n_tp, share)
        out = jnp.dot(inner, down, preferred_element_type=F32).astype(BF16)
        far_outs[d][...] = out[:count]
        near_outs[d][...] = out[count:]


def sum_kernel(n_tp, *refs):
    parts, outs = refs[:n_tp], refs[n_tp:]
    at = 0
    for out in outs:
        rows = slice(at, at + out.shape[0])
        total = parts[0][rows, :].astype(F32)
        for other in parts[1:]:
            total = total + other[rows, :].astype(F32)
        out[...] = total.astype(BF16)
        at += out.shape[0]


def seats_kernel(
    n_tp,
    seat_cap,
    owners_ref,
    positions_ref,
    combine_ref,
    hidden_hbm,
    rows_ref,
    mix_ref,
    at_ref,
    hidden_ref,
    sem,
):
    part = lax.axis_index("tp")
    tokens, share = hidden_ref.shape
    if hidden_hbm.shape[1] != share:
        hidden_hbm = hidden_hbm.at[:, pl.ds(pl.multiple_of(part * share, 128), share)]
    copy = pltpu.make_async_copy(hidden_hbm, hidden_ref, sem)
    copy.start()
    source_rows = tokens // n_tp
    owners = owners_ref[...] ^ part
    owner = lax.broadcasted_iota(jnp.int32, (n_tp, tokens), 0)
    hot = jnp.where(owners == owner, 1.0, 0.0)
    first = lax.broadcasted_iota(jnp.int32, (tokens, tokens), 0)
    second = lax.broadcasted_iota(jnp.int32, (tokens, tokens), 1)
    earlier = jnp.where((first < second) & (first // source_rows == second // source_rows), 1.0, 0.0)
    before = jnp.dot(hot.astype(BF16), earlier.astype(BF16), preferred_element_type=F32)
    seat = jnp.sum(before * hot, axis=0, keepdims=True).astype(jnp.int32)
    source = lax.broadcasted_iota(jnp.int32, (1, tokens), 1) // source_rows
    code = owners * (n_tp * seat_cap) + source * seat_cap + seat
    seats = n_tp * seat_cap
    held = lax.broadcasted_iota(jnp.int32, (n_tp * seats, tokens), 0) == code
    pick = jnp.where(held, 1.0, 0.0).astype(BF16)
    mix_ref[...] = lax.dot_general(
        pick, combine_ref[...], (((1,), (1,)), ((), ())), preferred_element_type=F32
    ).astype(BF16)
    place = jnp.where(held[:seats], positions_ref[...].astype(F32), 0.0)
    at_ref[...] = jnp.sum(place, axis=1, keepdims=True)
    copy.wait()
    rows_ref[...] = jnp.dot(pick, hidden_ref[...], preferred_element_type=F32).astype(BF16)


def cache_kernel(n_z, n_tp, cache_width, *refs):
    near, far, core_ref = refs[:4], refs[4 : n_z + 2], refs[n_z + 2]
    mix_ref, rows_ref, gain_ref, weight_ref = refs[n_z + 3 : n_z + 7]
    outs, back_ref = refs[n_z + 7 : n_z + 7 + n_tp], refs[n_z + 7 + n_tp]
    for d in range(4):
        back_ref[d * CAP : (d + 1) * CAP, :] = near[d][...]
    for d in range(n_z - 2):
        at = (2 * d + 4) * CAP
        back_ref[at : at + CAP, :] = far[d][:CAP, :]
        back_ref[at + CAP : at + 2 * CAP, :] = core_ref[d * CAP : (d + 1) * CAP, :]
    mixed = jnp.dot(mix_ref[...], back_ref[...], preferred_element_type=F32)
    state = rows_ref[...].astype(F32) + mixed
    square = jnp.sum(state * state, axis=1, keepdims=True)
    scaled = (state * gain_ref[...]).astype(BF16)
    value = lax.dot_general(
        scaled, weight_ref[...], (((1,), (1,)), ((), ())), preferred_element_type=F32
    ).astype(BF16)
    high = square.astype(BF16).astype(F32)
    rest = square - high
    middle = rest.astype(BF16).astype(F32)
    low = rest - middle
    seats, wide = outs[0].shape
    lane = lax.broadcasted_iota(jnp.int32, (square.shape[0], wide - cache_width), 1)
    extra = jnp.where(lane == 0, high, jnp.where(lane == 1, middle, jnp.where(lane == 2, low, 0.0)))
    extra = extra.astype(BF16)
    for d in range(n_tp):
        outs[d][:, :cache_width] = value[d * seats : (d + 1) * seats]
        outs[d][:, cache_width:] = extra[d * seats : (d + 1) * seats]


def finish_kernel(n_tp, width, rank_width, *refs):
    parts = refs[:n_tp]
    gain_ref, cos_ref, sin_ref, latent_ref, rotary_ref = refs[n_tp:]
    total = parts[0][...].astype(F32)
    for other in parts[1:]:
        total = total + other[...].astype(F32)
    half = cos_ref.shape[1]
    cache_width = rank_width + 2 * half
    square = jnp.sum(total[:, cache_width : cache_width + 3], axis=1, keepdims=True)
    cache = total[:, :cache_width] * lax.rsqrt(square / width + EPS)
    latent = cache[:, :rank_width]
    scale = lax.rsqrt(jnp.mean(latent * latent, axis=1, keepdims=True) + EPS)
    latent_ref[...] = (latent * scale * gain_ref[...]).astype(BF16)
    first = cache[:, rank_width : rank_width + half]
    second = cache[:, rank_width + half :]
    cosine, sine = cos_ref[...], sin_ref[...]
    rotary_ref[:, :half] = (first * cosine - second * sine).astype(BF16)
    rotary_ref[:, half:] = (second * cosine + first * sine).astype(BF16)


def call(kernel, out_shape, args, scratch=(), flops=0, hbm=()):
    moved = sum(a.size * a.dtype.itemsize for a in args)
    vmem = pl.BlockSpec(memory_space=pltpu.VMEM)
    args = [
        pltpu.with_memory_space_constraint(a, pltpu.HBM) if i in hbm else a
        for i, a in enumerate(args)
    ]
    return pl.pallas_call(
        kernel,
        out_shape=out_shape,
        in_specs=[
            pl.BlockSpec(memory_space=pltpu.HBM) if i in hbm else vmem for i in range(len(args))
        ],
        out_specs=[vmem] * len(out_shape),
        scratch_shapes=list(scratch),
        compiler_params=pltpu.CompilerParams(vmem_limit_bytes=VMEM_LIMIT),
        cost_estimate=pl.CostEstimate(flops=flops, bytes_accessed=moved, transcendentals=0),
    )(*args)


def swap(value, axis, d):
    return lax.ppermute(value, axis, [(i, i ^ d) for i in range(lax.axis_size(axis))])


def spread(value, n_tp):
    return [swap(value, "tp", d) for d in reversed(range(1, n_tp))][::-1]


def collect(values):
    got = [swap(values[d], "tp", d) for d in reversed(range(1, len(values)))]
    return [values[0]] + got[::-1]


def on_device(
    hidden,
    moe_gain,
    route_logits,
    routes,
    gate_weight,
    up_weight,
    down_weight,
    attn_gain,
    latent_weight,
    latent_gain,
    positions,
    owners,
):
    n_ep = lax.axis_size("ep")
    n_tp = lax.axis_size("tp")
    n_z = n_ep // 2
    tokens, width = hidden.shape
    share = width // n_tp
    ff = gate_weight.shape[2]
    slots = n_ep * CAP
    seat_cap = max(2, tokens // n_tp // 4)
    seats = n_tp * seat_cap
    rank_width = latent_gain.shape[0]
    cache_width = latent_weight.shape[1]
    half = (cache_width - rank_width) // 2
    wide = (cache_width + 3 + 127) // 128 * 128
    struct = jax.ShapeDtypeStruct
    chunks = width // 512 if width % 512 == 0 else 1

    own, to_core, to_near, *outgoing, combine = call(
        functools.partial(dispatch_kernel, n_ep, n_tp),
        [struct((CAP, width), BF16), struct((n_tp * CAP, share), BF16)]
        + [struct((2 * n_tp * CAP, share), BF16)]
        + [struct((2 * CAP, share), BF16)] * (n_z - 2)
        + [struct((slots, tokens), BF16)],
        (routes.T, route_logits.T, hidden, moe_gain),
        [
            pltpu.VMEM(routes.T.shape, jnp.int32),
            pltpu.VMEM(routes.T.shape, F32),
            pltpu.VMEM(hidden.shape, BF16),
            pltpu.VMEM((1, width), F32),
            pltpu.VMEM((slots, tokens), BF16),
            pltpu.VMEM((4 * CAP, width), F32),
            pltpu.SemaphoreType.DMA((3 + chunks,)),
        ],
        flops=4 * slots * tokens * width,
        hbm=(0, 1, 2, 3),
    )
    arrived = [swap(outgoing[d - 2], "ep", 2 * d) for d in reversed(range(2, n_z))][::-1]
    near = swap(to_near, "ep", 2)
    from_core = swap(to_core, "ep", 1)
    gate_w, up_w, down_w = gate_weight[0], up_weight[0], down_weight[0]
    *loaded, mark = call(
        load_kernel,
        [struct(w.shape, BF16) for w in (gate_w, up_w, down_w)] + [struct((8, 128), F32)],
        (combine, gate_w, up_w, down_w),
        [pltpu.SemaphoreType.DMA((3,))],
        hbm=(1, 2, 3),
    )
    arrived, near, mark, from_core = lax.optimization_barrier((arrived, near, mark, from_core))
    crossed = swap(jnp.concatenate([piece[CAP:] for piece in arrived], axis=0), "ep", 1)
    mine = jnp.concatenate(
        [
            block
            for d, piece in enumerate(arrived)
            for block in (piece[:CAP], crossed[d * CAP : (d + 1) * CAP])
        ],
        axis=0,
    )
    shares = spread(mine, n_tp)
    near_crossed = swap(near[n_tp * CAP :], "ep", 1)
    near_rows, far_rows = 4 * CAP, slots - 4 * CAP
    inner, gate_sum, up_sum = call(
        functools.partial(first_kernel, n_tp),
        [struct((near_rows, ff), BF16)] + [struct((far_rows, ff), F32)] * 2,
        (own, from_core, near[: n_tp * CAP], near_crossed, mine, *loaded[:2], mark),
        [pltpu.VMEM((4 * CAP, width), BF16)],
        flops=2 * slots * width * ff,
    )
    terms = call(
        functools.partial(expert_kernel, n_tp),
        [struct((far_rows, share), BF16)] * n_tp + [struct((near_rows, share), BF16)] * n_tp,
        (*shares, *loaded, inner, gate_sum, up_sum),
        flops=2 * slots * width * ff * 3,
    )
    combine, _ = lax.optimization_barrier((combine, terms[0]))
    share_of = hidden
    if share % 128:
        share_of = lax.dynamic_slice_in_dim(hidden, lax.axis_index("tp") * share, share, 1)
    rows, mix, at = call(
        functools.partial(seats_kernel, n_tp, seat_cap),
        [
            struct((n_tp * seats, share), BF16),
            struct((n_tp * seats, slots), BF16),
            struct((seats, 1), F32),
        ],
        (owners[None, :], positions[None, :], combine, share_of),
        [pltpu.VMEM((tokens, share), BF16), pltpu.SemaphoreType.DMA(())],
        flops=2 * n_tp * seats * tokens * (share + slots),
        hbm=(3,),
    )
    freqs = ROPE_BASE ** (-jnp.arange(half, dtype=F32) / half)
    angles = at * freqs[None, :]
    cosine, sine = jnp.cos(angles), jnp.sin(angles)

    far_terms = collect(terms[:n_tp])
    far_terms, rows, mix = lax.optimization_barrier((far_terms, rows, mix))
    near_terms = collect(terms[n_tp:])
    far_done = call(
        functools.partial(sum_kernel, n_tp),
        [struct((2 * CAP, share), BF16)] * (n_z - 2),
        far_terms,
    )
    far_back = [swap(far_done[d - 2], "ep", 2 * d) for d in range(2, n_z)]
    near_done = call(
        functools.partial(sum_kernel, n_tp), [struct((CAP, share), BF16)] * 4, near_terms
    )
    near_back = [near_done[0]] + [swap(near_done[d], "ep", d) for d in (1, 2, 3)]
    crossed = swap(jnp.concatenate([piece[CAP:] for piece in far_back], axis=0), "ep", 1)
    partial = call(
        functools.partial(cache_kernel, n_z, n_tp, cache_width),
        [struct((seats, wide), BF16)] * n_tp,
        (*near_back, *far_back, crossed, mix, rows, attn_gain[None, :], latent_weight.T),
        [pltpu.VMEM((slots, share), BF16)],
        flops=2 * n_tp * seats * share * (slots + cache_width),
    )
    return tuple(
        call(
            functools.partial(finish_kernel, n_tp, width, rank_width),
            [struct((seats, rank_width), BF16), struct((seats, 2 * half), BF16)],
            (*collect(partial), latent_gain[None, :], cosine, sine),
        )
    )


def solution(mesh):
    placed = (
        P(("groups", "ep"), None),
        P(),
        P(("groups", "ep"), None),
        P(("groups", "ep"), None),
        P("ep", None, "tp"),
        P("ep", None, "tp"),
        P("ep", "tp", None),
        P("tp"),
        P("tp", None),
        P(),
        P(("groups", "ep")),
        P(("groups", "ep")),
    )
    return jax.shard_map(
        on_device,
        mesh=mesh,
        in_specs=placed,
        out_specs=(P(("groups", "ep", "tp"), None), P(("groups", "ep", "tp"), None)),
        check_vma=False,
    )
```

```python
import functools

import jax
import jax.numpy as jnp
from jax import lax
from jax.experimental import pallas as pl
from jax.experimental.pallas import tpu as pltpu
from jax.sharding import PartitionSpec as P

CAP = 16
EPS = 1e-06
ROUTE_SCALE = 2.5
ROPE_BASE = 10000.0
BF16 = jnp.bfloat16
F32 = jnp.float32
VMEM_LIMIT = 40 * 1024 * 1024


def columns_of(ref, index, count, share):
    if share % 128 == 0:
        return ref[:, pl.ds(pl.multiple_of(index * share, 128), share)]
    out = ref[:, 0:share]
    for q in range(1, count):
        out = jnp.where(index == q, ref[:, q * share : (q + 1) * share], out)
    return out


def dispatch_kernel(n_ep, n_tp, routes_hbm, logits_hbm, hidden_hbm, gain_hbm, *refs):
    own_ref, core_ref, near_ref = refs[:3]
    outs, combine_ref = refs[3 : n_ep // 2 + 1], refs[n_ep // 2 + 1]
    routes_ref, logits_ref, hidden_ref, gain_ref, pick_ref, head_ref, sems = refs[n_ep // 2 + 2 :]
    me = lax.axis_index("ep")
    part = lax.axis_index("tp")
    tokens, width = hidden_ref.shape
    share = width // n_tp
    step = 512 if width % 512 == 0 else width
    starts = range(0, width, step)
    small = [
        pltpu.make_async_copy(routes_hbm, routes_ref, sems.at[0]),
        pltpu.make_async_copy(logits_hbm, logits_ref, sems.at[1]),
        pltpu.make_async_copy(gain_hbm, gain_ref.at[0], sems.at[2]),
    ]
    large = [
        pltpu.make_async_copy(
            hidden_hbm.at[:, c : c + step], hidden_ref.at[:, c : c + step], sems.at[3 + i]
        )
        for i, c in enumerate(starts)
    ]
    for copy in small + large:
        copy.start()
    small[0].wait()
    small[1].wait()
    routes = routes_ref[...]
    affinity = jax.nn.sigmoid(logits_ref[...])
    weight = ROUTE_SCALE * affinity / jnp.sum(affinity, axis=0, keepdims=True)
    weight = weight.astype(BF16).astype(F32)
    expert = lax.broadcasted_iota(jnp.int32, (n_ep, tokens), 0) ^ me
    hit = jnp.zeros((n_ep, tokens), F32)
    gain_of = jnp.zeros((n_ep, tokens), F32)
    for k in range(routes.shape[0]):
        same = routes[k : k + 1, :] == expert
        hit = jnp.where(same, 1.0, hit)
        gain_of = jnp.where(same, weight[k : k + 1, :], gain_of)
    earlier = lax.broadcasted_iota(jnp.int32, (tokens, tokens), 0) < lax.broadcasted_iota(
        jnp.int32, (tokens, tokens), 1
    )
    rank = jnp.dot(hit.astype(BF16), earlier.astype(F32).astype(BF16), preferred_element_type=F32)
    rank = jnp.where(hit > 0, rank, -1.0)
    place = lax.broadcasted_iota(jnp.int32, (CAP, tokens), 0).astype(F32)
    for d in range(n_ep):
        match = rank[d : d + 1, :] == place
        rows = slice(d * CAP, (d + 1) * CAP)
        pick_ref[rows, :] = jnp.where(match, 1.0, 0.0).astype(BF16)
        combine_ref[rows, :] = jnp.where(match, gain_of[d : d + 1, :], 0.0).astype(BF16)
    pick = pick_ref[...]
    head = 4 * CAP
    square = jnp.zeros((n_ep * CAP, 1), F32)
    for copy in large:
        copy.wait()
    for c in starts:
        got = jnp.dot(pick, hidden_ref[:, c : c + step], preferred_element_type=F32)
        square = square + jnp.sum(got * got, axis=1, keepdims=True)
        head_ref[:, c : c + step] = got[:head]
    small[2].wait()
    scale = lax.rsqrt(square / width + EPS)
    got = jnp.dot(pick[head:], columns_of(hidden_ref, part, n_tp, share), preferred_element_type=F32)
    rest = (got * scale[head:] * columns_of(gain_ref, part, n_tp, share)).astype(BF16)
    at = 0
    for out in outs:
        out[...] = rest[at : at + out.shape[0]]
        at += out.shape[0]
    whole = (head_ref[...] * scale[:head] * gain_ref[...]).astype(BF16)
    own_ref[...] = whole[:CAP]
    for q in range(n_tp):
        columns = slice(q * share, (q + 1) * share)
        core_ref[q * CAP : (q + 1) * CAP, :] = whole[CAP : 2 * CAP, columns]
        near_ref[q * CAP : (q + 1) * CAP, :] = whole[2 * CAP : 3 * CAP, columns]
        near_ref[(n_tp + q) * CAP : (n_tp + q + 1) * CAP, :] = whole[3 * CAP :, columns]


def load_kernel(after_ref, *refs):
    count = (len(refs) - 2) // 2
    mark_ref, sems = refs[-2:]
    copies = [
        pltpu.make_async_copy(refs[i], refs[count + i], sems.at[i]) for i in range(count)
    ]
    for copy in copies:
        copy.start()
    mark_ref[...] = jnp.zeros(mark_ref.shape, F32)
    for copy in copies:
        copy.wait()


def first_kernel(
    n_tp,
    own_ref,
    core_ref,
    near_ref,
    cross_ref,
    mine_ref,
    gate_ref,
    up_ref,
    mark_ref,
    inner_ref,
    gate_sum_ref,
    up_sum_ref,
    head_ref,
):
    part = lax.axis_index("tp")
    share = mine_ref.shape[1]
    head_ref[:CAP, :] = own_ref[...]
    for i, ref in enumerate((core_ref, near_ref, cross_ref)):
        for q in range(n_tp):
            rows = slice((i + 1) * CAP, (i + 2) * CAP)
            head_ref[rows, q * share : (q + 1) * share] = ref[q * CAP : (q + 1) * CAP, :]
    depth = pl.ds(pl.multiple_of(part * share, CAP), share)
    gate, upper = (
        jnp.dot(head_ref[...], ref[...], preferred_element_type=F32) for ref in (gate_ref, up_ref)
    )
    for weight_ref, sum_ref in zip((gate_ref, up_ref), (gate_sum_ref, up_sum_ref)):
        sum_ref[...] = jnp.dot(mine_ref[...], weight_ref[depth, :], preferred_element_type=F32)
    inner_ref[...] = (gate / (1.0 + jnp.exp(-gate)) * upper).astype(BF16)


def expert_kernel(n_tp, *refs):
    rows = refs[: n_tp - 1]
    gate_ref, up_ref, down_ref, near_ref, gate_sum_ref, up_sum_ref = refs[n_tp - 1 : n_tp + 5]
    far_outs = refs[n_tp + 5 : 2 * n_tp + 5]
    near_outs = refs[2 * n_tp + 5 :]
    part = lax.axis_index("tp")
    share = rows[0].shape[1]
    gate = gate_sum_ref[...]
    upper = up_sum_ref[...]
    for d in range(1, n_tp):
        value = rows[n_tp - 1 - d][...]
        depth = pl.ds(pl.multiple_of((part ^ d) * share, CAP), share)
        gate = gate + jnp.dot(value, gate_ref[depth, :], preferred_element_type=F32)
        upper = upper + jnp.dot(value, up_ref[depth, :], preferred_element_type=F32)
    far = (gate / (1.0 + jnp.exp(-gate)) * upper).astype(BF16)
    inner = jnp.concatenate([far, near_ref[...]], axis=0)
    count = far.shape[0]
    for d in range(n_tp):
        down = columns_of(down_ref, part ^ d, n_tp, share)
        out = jnp.dot(inner, down, preferred_element_type=F32).astype(BF16)
        far_outs[d][...] = out[:count]
        near_outs[d][...] = out[count:]


def sum_kernel(n_tp, *refs):
    parts, outs = refs[:n_tp], refs[n_tp:]
    at = 0
    for out in outs:
        rows = slice(at, at + out.shape[0])
        total = parts[0][rows, :].astype(F32)
        for other in parts[1:]:
            total = total + other[rows, :].astype(F32)
        out[...] = total.astype(BF16)
        at += out.shape[0]


def seats_kernel(
    n_tp,
    seat_cap,
    owners_ref,
    positions_ref,
    combine_ref,
    hidden_hbm,
    rows_ref,
    mix_ref,
    at_ref,
    hidden_ref,
    sem,
):
    part = lax.axis_index("tp")
    tokens, share = hidden_ref.shape
    if hidden_hbm.shape[1] != share:
        hidden_hbm = hidden_hbm.at[:, pl.ds(pl.multiple_of(part * share, 128), share)]
    copy = pltpu.make_async_copy(hidden_hbm, hidden_ref, sem)
    copy.start()
    source_rows = tokens // n_tp
    owners = owners_ref[...] ^ part
    owner = lax.broadcasted_iota(jnp.int32, (n_tp, tokens), 0)
    hot = jnp.where(owners == owner, 1.0, 0.0)
    first = lax.broadcasted_iota(jnp.int32, (tokens, tokens), 0)
    second = lax.broadcasted_iota(jnp.int32, (tokens, tokens), 1)
    earlier = jnp.where((first < second) & (first // source_rows == second // source_rows), 1.0, 0.0)
    before = jnp.dot(hot.astype(BF16), earlier.astype(BF16), preferred_element_type=F32)
    seat = jnp.sum(before * hot, axis=0, keepdims=True).astype(jnp.int32)
    source = lax.broadcasted_iota(jnp.int32, (1, tokens), 1) // source_rows
    code = owners * (n_tp * seat_cap) + source * seat_cap + seat
    seats = n_tp * seat_cap
    held = lax.broadcasted_iota(jnp.int32, (n_tp * seats, tokens), 0) == code
    pick = jnp.where(held, 1.0, 0.0).astype(BF16)
    mix_ref[...] = lax.dot_general(
        pick, combine_ref[...], (((1,), (1,)), ((), ())), preferred_element_type=F32
    ).astype(BF16)
    place = jnp.where(held[:seats], positions_ref[...].astype(F32), 0.0)
    at_ref[...] = jnp.sum(place, axis=1, keepdims=True)
    copy.wait()
    rows_ref[...] = jnp.dot(pick, hidden_ref[...], preferred_element_type=F32).astype(BF16)


def cache_kernel(n_z, n_tp, cache_width, *refs):
    near, far, core_ref = refs[:4], refs[4 : n_z + 2], refs[n_z + 2]
    mix_ref, rows_ref, gain_ref, weight_ref = refs[n_z + 3 : n_z + 7]
    outs, back_ref = refs[n_z + 7 : n_z + 7 + n_tp], refs[n_z + 7 + n_tp]
    for d in range(4):
        back_ref[d * CAP : (d + 1) * CAP, :] = near[d][...]
    for d in range(n_z - 2):
        at = (2 * d + 4) * CAP
        back_ref[at : at + CAP, :] = far[d][:CAP, :]
        back_ref[at + CAP : at + 2 * CAP, :] = core_ref[d * CAP : (d + 1) * CAP, :]
    mixed = jnp.dot(mix_ref[...], back_ref[...], preferred_element_type=F32)
    state = rows_ref[...].astype(F32) + mixed
    square = jnp.sum(state * state, axis=1, keepdims=True)
    scaled = (state * gain_ref[...]).astype(BF16)
    value = lax.dot_general(
        scaled, weight_ref[...], (((1,), (1,)), ((), ())), preferred_element_type=F32
    ).astype(BF16)
    high = square.astype(BF16).astype(F32)
    rest = square - high
    middle = rest.astype(BF16).astype(F32)
    low = rest - middle
    seats, wide = outs[0].shape
    lane = lax.broadcasted_iota(jnp.int32, (square.shape[0], wide - cache_width), 1)
    extra = jnp.where(lane == 0, high, jnp.where(lane == 1, middle, jnp.where(lane == 2, low, 0.0)))
    extra = extra.astype(BF16)
    for d in range(n_tp):
        outs[d][:, :cache_width] = value[d * seats : (d + 1) * seats]
        outs[d][:, cache_width:] = extra[d * seats : (d + 1) * seats]


def finish_kernel(n_tp, width, rank_width, *refs):
    parts = refs[:n_tp]
    gain_ref, cos_ref, sin_ref, latent_ref, rotary_ref = refs[n_tp:]
    total = parts[0][...].astype(F32)
    for other in parts[1:]:
        total = total + other[...].astype(F32)
    half = cos_ref.shape[1]
    cache_width = rank_width + 2 * half
    square = jnp.sum(total[:, cache_width : cache_width + 3], axis=1, keepdims=True)
    cache = total[:, :cache_width] * lax.rsqrt(square / width + EPS)
    latent = cache[:, :rank_width]
    scale = lax.rsqrt(jnp.mean(latent * latent, axis=1, keepdims=True) + EPS)
    latent_ref[...] = (latent * scale * gain_ref[...]).astype(BF16)
    first = cache[:, rank_width : rank_width + half]
    second = cache[:, rank_width + half :]
    cosine, sine = cos_ref[...], sin_ref[...]
    rotary_ref[:, :half] = (first * cosine - second * sine).astype(BF16)
    rotary_ref[:, half:] = (second * cosine + first * sine).astype(BF16)


def call(kernel, out_shape, args, scratch=(), flops=0, hbm=()):
    moved = sum(a.size * a.dtype.itemsize for a in args)
    vmem = pl.BlockSpec(memory_space=pltpu.VMEM)
    args = [
        pltpu.with_memory_space_constraint(a, pltpu.HBM) if i in hbm else a
        for i, a in enumerate(args)
    ]
    return pl.pallas_call(
        kernel,
        out_shape=out_shape,
        in_specs=[
            pl.BlockSpec(memory_space=pltpu.HBM) if i in hbm else vmem for i in range(len(args))
        ],
        out_specs=[vmem] * len(out_shape),
        scratch_shapes=list(scratch),
        compiler_params=pltpu.CompilerParams(vmem_limit_bytes=VMEM_LIMIT),
        cost_estimate=pl.CostEstimate(flops=flops, bytes_accessed=moved, transcendentals=0),
    )(*args)


def swap(value, axis, d):
    return lax.ppermute(value, axis, [(i, i ^ d) for i in range(lax.axis_size(axis))])


def spread(value, n_tp):
    return [swap(value, "tp", d) for d in reversed(range(1, n_tp))]


def collect(values):
    return [swap(values[d], "tp", d) for d in reversed(range(1, len(values)))] + [values[0]]


def on_device(
    hidden,
    moe_gain,
    route_logits,
    routes,
    gate_weight,
    up_weight,
    down_weight,
    attn_gain,
    latent_weight,
    latent_gain,
    positions,
    owners,
):
    n_ep = lax.axis_size("ep")
    n_tp = lax.axis_size("tp")
    n_z = n_ep // 2
    tokens, width = hidden.shape
    share = width // n_tp
    ff = gate_weight.shape[2]
    slots = n_ep * CAP
    seat_cap = max(2, tokens // n_tp // 4)
    seats = n_tp * seat_cap
    rank_width = latent_gain.shape[0]
    cache_width = latent_weight.shape[1]
    half = (cache_width - rank_width) // 2
    wide = (cache_width + 3 + 127) // 128 * 128
    struct = jax.ShapeDtypeStruct
    chunks = width // 512 if width % 512 == 0 else 1

    own, to_core, to_near, *outgoing, combine = call(
        functools.partial(dispatch_kernel, n_ep, n_tp),
        [struct((CAP, width), BF16), struct((n_tp * CAP, share), BF16)]
        + [struct((2 * n_tp * CAP, share), BF16)]
        + [struct((2 * CAP, share), BF16)] * (n_z - 2)
        + [struct((slots, tokens), BF16)],
        (routes.T, route_logits.T, hidden, moe_gain),
        [
            pltpu.VMEM(routes.T.shape, jnp.int32),
            pltpu.VMEM(routes.T.shape, F32),
            pltpu.VMEM(hidden.shape, BF16),
            pltpu.VMEM((1, width), F32),
            pltpu.VMEM((slots, tokens), BF16),
            pltpu.VMEM((4 * CAP, width), F32),
            pltpu.SemaphoreType.DMA((3 + chunks,)),
        ],
        flops=4 * slots * tokens * width,
        hbm=(0, 1, 2, 3),
    )
    arrived = [swap(outgoing[d - 2], "ep", 2 * d) for d in reversed(range(2, n_z))][::-1]
    near = swap(to_near, "ep", 2)
    from_core = swap(to_core, "ep", 1)
    gate_w, up_w, down_w = gate_weight[0], up_weight[0], down_weight[0]
    *loaded, mark = call(
        load_kernel,
        [struct(w.shape, BF16) for w in (gate_w, up_w, down_w)] + [struct((8, 128), F32)],
        (combine, gate_w, up_w, down_w),
        [pltpu.SemaphoreType.DMA((3,))],
        hbm=(1, 2, 3),
    )
    arrived, near, mark, from_core = lax.optimization_barrier((arrived, near, mark, from_core))
    crossed = swap(jnp.concatenate([piece[CAP:] for piece in arrived], axis=0), "ep", 1)
    mine = jnp.concatenate(
        [
            block
            for d, piece in enumerate(arrived)
            for block in (piece[:CAP], crossed[d * CAP : (d + 1) * CAP])
        ],
        axis=0,
    )
    shares = spread(mine, n_tp)
    near_crossed = swap(near[n_tp * CAP :], "ep", 1)
    near_rows, far_rows = 4 * CAP, slots - 4 * CAP
    inner, gate_sum, up_sum = call(
        functools.partial(first_kernel, n_tp),
        [struct((near_rows, ff), BF16)] + [struct((far_rows, ff), F32)] * 2,
        (own, from_core, near[: n_tp * CAP], near_crossed, mine, *loaded[:2], mark),
        [pltpu.VMEM((4 * CAP, width), BF16)],
        flops=2 * slots * width * ff,
    )
    terms = call(
        functools.partial(expert_kernel, n_tp),
        [struct((far_rows, share), BF16)] * n_tp + [struct((near_rows, share), BF16)] * n_tp,
        (*shares, *loaded, inner, gate_sum, up_sum),
        flops=2 * slots * width * ff * 3,
    )
    combine, _ = lax.optimization_barrier((combine, terms[0]))
    share_of = hidden
    if share % 128:
        share_of = lax.dynamic_slice_in_dim(hidden, lax.axis_index("tp") * share, share, 1)
    rows, mix, at = call(
        functools.partial(seats_kernel, n_tp, seat_cap),
        [
            struct((n_tp * seats, share), BF16),
            struct((n_tp * seats, slots), BF16),
            struct((seats, 1), F32),
        ],
        (owners[None, :], positions[None, :], combine, share_of),
        [pltpu.VMEM((tokens, share), BF16), pltpu.SemaphoreType.DMA(())],
        flops=2 * n_tp * seats * tokens * (share + slots),
        hbm=(3,),
    )
    freqs = ROPE_BASE ** (-jnp.arange(half, dtype=F32) / half)
    angles = at * freqs[None, :]
    cosine, sine = jnp.cos(angles), jnp.sin(angles)

    far_terms = collect(terms[:n_tp])
    far_terms, rows, mix = lax.optimization_barrier((far_terms, rows, mix))
    *ahead, last, here = collect(terms[n_tp:])
    near_terms = [last, *ahead, here]
    far_done = call(
        functools.partial(sum_kernel, n_tp),
        [struct((2 * CAP, share), BF16)] * (n_z - 2),
        far_terms,
    )
    far_back = [swap(far_done[d - 2], "ep", 2 * d) for d in range(2, n_z)]
    near_done = call(
        functools.partial(sum_kernel, n_tp), [struct((CAP, share), BF16)] * 4, near_terms
    )
    near_back = [near_done[0]] + [swap(near_done[d], "ep", d) for d in (1, 2, 3)]
    crossed = swap(jnp.concatenate([piece[CAP:] for piece in far_back], axis=0), "ep", 1)
    partial = call(
        functools.partial(cache_kernel, n_z, n_tp, cache_width),
        [struct((seats, wide), BF16)] * n_tp,
        (*near_back, *far_back, crossed, mix, rows, attn_gain[None, :], latent_weight.T),
        [pltpu.VMEM((slots, share), BF16)],
        flops=2 * n_tp * seats * share * (slots + cache_width),
    )
    return tuple(
        call(
            functools.partial(finish_kernel, n_tp, width, rank_width),
            [struct((seats, rank_width), BF16), struct((seats, 2 * half), BF16)],
            (*collect(partial), latent_gain[None, :], cosine, sine),
        )
    )


def solution(mesh):
    placed = (
        P(("groups", "ep"), None),
        P(),
        P(("groups", "ep"), None),
        P(("groups", "ep"), None),
        P("ep", None, "tp"),
        P("ep", None, "tp"),
        P("ep", "tp", None),
        P("tp"),
        P("tp", None),
        P(),
        P(("groups", "ep")),
        P(("groups", "ep")),
    )
    return jax.shard_map(
        on_device,
        mesh=mesh,
        in_specs=placed,
        out_specs=(P(("groups", "ep", "tp"), None), P(("groups", "ep", "tp"), None)),
        check_vma=False,
    )
```

```python
import functools

import jax
import jax.numpy as jnp
from jax import lax
from jax.experimental import pallas as pl
from jax.experimental.pallas import tpu as pltpu
from jax.sharding import PartitionSpec as P

CAP = 16
EPS = 1e-06
ROUTE_SCALE = 2.5
ROPE_BASE = 10000.0
BF16 = jnp.bfloat16
F32 = jnp.float32
VMEM_LIMIT = 40 * 1024 * 1024


def columns_of(ref, index, count, share):
    if share % 128 == 0:
        return ref[:, pl.ds(pl.multiple_of(index * share, 128), share)]
    out = ref[:, 0:share]
    for q in range(1, count):
        out = jnp.where(index == q, ref[:, q * share : (q + 1) * share], out)
    return out


def dispatch_kernel(n_ep, n_tp, routes_hbm, logits_hbm, hidden_hbm, gain_hbm, *refs):
    own_ref, core_ref, near_ref = refs[:3]
    outs, combine_ref = refs[3 : n_ep - 1], refs[n_ep - 1]
    routes_ref, logits_ref, hidden_ref, gain_ref, pick_ref, head_ref, sems = refs[n_ep:]
    me = lax.axis_index("ep")
    part = lax.axis_index("tp")
    tokens, width = hidden_ref.shape
    share = width // n_tp
    step = 512 if width % 512 == 0 else width
    starts = range(0, width, step)
    small = [
        pltpu.make_async_copy(routes_hbm, routes_ref, sems.at[0]),
        pltpu.make_async_copy(logits_hbm, logits_ref, sems.at[1]),
        pltpu.make_async_copy(gain_hbm, gain_ref.at[0], sems.at[2]),
    ]
    large = [
        pltpu.make_async_copy(
            hidden_hbm.at[:, c : c + step], hidden_ref.at[:, c : c + step], sems.at[3 + i]
        )
        for i, c in enumerate(starts)
    ]
    for copy in small + large:
        copy.start()
    small[0].wait()
    small[1].wait()
    routes = routes_ref[...]
    affinity = jax.nn.sigmoid(logits_ref[...])
    weight = ROUTE_SCALE * affinity / jnp.sum(affinity, axis=0, keepdims=True)
    weight = weight.astype(BF16).astype(F32)
    expert = lax.broadcasted_iota(jnp.int32, (n_ep, tokens), 0) ^ me
    hit = jnp.zeros((n_ep, tokens), F32)
    gain_of = jnp.zeros((n_ep, tokens), F32)
    for k in range(routes.shape[0]):
        same = routes[k : k + 1, :] == expert
        hit = jnp.where(same, 1.0, hit)
        gain_of = jnp.where(same, weight[k : k + 1, :], gain_of)
    earlier = lax.broadcasted_iota(jnp.int32, (tokens, tokens), 0) < lax.broadcasted_iota(
        jnp.int32, (tokens, tokens), 1
    )
    rank = jnp.dot(hit.astype(BF16), earlier.astype(F32).astype(BF16), preferred_element_type=F32)
    rank = jnp.where(hit > 0, rank, -1.0)
    place = lax.broadcasted_iota(jnp.int32, (CAP, tokens), 0).astype(F32)
    for d in range(n_ep):
        match = rank[d : d + 1, :] == place
        rows = slice(d * CAP, (d + 1) * CAP)
        pick_ref[rows, :] = jnp.where(match, 1.0, 0.0).astype(BF16)
        combine_ref[rows, :] = jnp.where(match, gain_of[d : d + 1, :], 0.0).astype(BF16)
    pick = pick_ref[...]
    head = 4 * CAP
    square = jnp.zeros((n_ep * CAP, 1), F32)
    middle = len(large) // 2
    for i, c in enumerate(starts):
        if i == 0 or i == middle:
            for copy in large[:middle] if i < middle else large[i:]:
                copy.wait()
        got = jnp.dot(pick, hidden_ref[:, c : c + step], preferred_element_type=F32)
        square = square + jnp.sum(got * got, axis=1, keepdims=True)
        head_ref[:, c : c + step] = got[:head]
    small[2].wait()
    scale = lax.rsqrt(square / width + EPS)
    got = jnp.dot(pick[head:], columns_of(hidden_ref, part, n_tp, share), preferred_element_type=F32)
    rest = (got * scale[head:] * columns_of(gain_ref, part, n_tp, share)).astype(BF16)
    at = 0
    for out in outs:
        out[...] = rest[at : at + out.shape[0]]
        at += out.shape[0]
    whole = (head_ref[...] * scale[:head] * gain_ref[...]).astype(BF16)
    own_ref[...] = whole[:CAP]
    for q in range(n_tp):
        columns = slice(q * share, (q + 1) * share)
        core_ref[q * CAP : (q + 1) * CAP, :] = whole[CAP : 2 * CAP, columns]
        near_ref[q * CAP : (q + 1) * CAP, :] = whole[2 * CAP : 3 * CAP, columns]
        near_ref[(n_tp + q) * CAP : (n_tp + q + 1) * CAP, :] = whole[3 * CAP :, columns]


def load_kernel(after_ref, *refs):
    count = (len(refs) - 2) // 2
    mark_ref, sems = refs[-2:]
    copies = [
        pltpu.make_async_copy(refs[i], refs[count + i], sems.at[i]) for i in range(count)
    ]
    for copy in copies:
        copy.start()
    mark_ref[...] = jnp.zeros(mark_ref.shape, F32)
    for copy in copies:
        copy.wait()


def first_kernel(
    n_tp,
    own_ref,
    core_ref,
    near_ref,
    cross_ref,
    mine_ref,
    gate_ref,
    up_ref,
    mark_ref,
    inner_ref,
    gate_sum_ref,
    up_sum_ref,
    head_ref,
):
    part = lax.axis_index("tp")
    share = mine_ref.shape[1]
    head_ref[:CAP, :] = own_ref[...]
    for i, ref in enumerate((core_ref, near_ref, cross_ref)):
        for q in range(n_tp):
            rows = slice((i + 1) * CAP, (i + 2) * CAP)
            head_ref[rows, q * share : (q + 1) * share] = ref[q * CAP : (q + 1) * CAP, :]
    depth = pl.ds(pl.multiple_of(part * share, CAP), share)
    gate, upper = (
        jnp.dot(head_ref[...], ref[...], preferred_element_type=F32) for ref in (gate_ref, up_ref)
    )
    for weight_ref, sum_ref in zip((gate_ref, up_ref), (gate_sum_ref, up_sum_ref)):
        sum_ref[...] = jnp.dot(mine_ref[...], weight_ref[depth, :], preferred_element_type=F32)
    inner_ref[...] = (gate / (1.0 + jnp.exp(-gate)) * upper).astype(BF16)


def expert_kernel(n_tp, *refs):
    rows = refs[: n_tp - 1]
    gate_ref, up_ref, down_ref, near_ref, gate_sum_ref, up_sum_ref = refs[n_tp - 1 : n_tp + 5]
    far_outs = refs[n_tp + 5 : 2 * n_tp + 5]
    near_outs = refs[2 * n_tp + 5 :]
    part = lax.axis_index("tp")
    share = rows[0].shape[1]
    gate = gate_sum_ref[...]
    upper = up_sum_ref[...]
    for d in range(1, n_tp):
        value = rows[n_tp - 1 - d][...]
        depth = pl.ds(pl.multiple_of((part ^ d) * share, CAP), share)
        gate = gate + jnp.dot(value, gate_ref[depth, :], preferred_element_type=F32)
        upper = upper + jnp.dot(value, up_ref[depth, :], preferred_element_type=F32)
    far = (gate / (1.0 + jnp.exp(-gate)) * upper).astype(BF16)
    inner = jnp.concatenate([far, near_ref[...]], axis=0)
    count = far.shape[0]
    for d in range(n_tp):
        down = columns_of(down_ref, part ^ d, n_tp, share)
        out = jnp.dot(inner, down, preferred_element_type=F32).astype(BF16)
        far_outs[d][...] = out[:count]
        near_outs[d][...] = out[count:]


def sum_kernel(n_tp, *refs):
    parts, outs = refs[:n_tp], refs[n_tp:]
    at = 0
    for out in outs:
        rows = slice(at, at + out.shape[0])
        total = parts[0][rows, :].astype(F32)
        for other in parts[1:]:
            total = total + other[rows, :].astype(F32)
        out[...] = total.astype(BF16)
        at += out.shape[0]


def seats_kernel(
    n_tp,
    seat_cap,
    owners_ref,
    positions_ref,
    combine_ref,
    hidden_hbm,
    rows_ref,
    mix_ref,
    at_ref,
    hidden_ref,
    sem,
):
    part = lax.axis_index("tp")
    tokens, share = hidden_ref.shape
    if hidden_hbm.shape[1] != share:
        hidden_hbm = hidden_hbm.at[:, pl.ds(pl.multiple_of(part * share, 128), share)]
    copy = pltpu.make_async_copy(hidden_hbm, hidden_ref, sem)
    copy.start()
    source_rows = tokens // n_tp
    owners = owners_ref[...] ^ part
    owner = lax.broadcasted_iota(jnp.int32, (n_tp, tokens), 0)
    hot = jnp.where(owners == owner, 1.0, 0.0)
    first = lax.broadcasted_iota(jnp.int32, (tokens, tokens), 0)
    second = lax.broadcasted_iota(jnp.int32, (tokens, tokens), 1)
    earlier = jnp.where((first < second) & (first // source_rows == second // source_rows), 1.0, 0.0)
    before = jnp.dot(hot.astype(BF16), earlier.astype(BF16), preferred_element_type=F32)
    seat = jnp.sum(before * hot, axis=0, keepdims=True).astype(jnp.int32)
    source = lax.broadcasted_iota(jnp.int32, (1, tokens), 1) // source_rows
    code = owners * (n_tp * seat_cap) + source * seat_cap + seat
    seats = n_tp * seat_cap
    held = lax.broadcasted_iota(jnp.int32, (n_tp * seats, tokens), 0) == code
    pick = jnp.where(held, 1.0, 0.0).astype(BF16)
    mix_ref[...] = lax.dot_general(
        pick, combine_ref[...], (((1,), (1,)), ((), ())), preferred_element_type=F32
    ).astype(BF16)
    place = jnp.where(held[:seats], positions_ref[...].astype(F32), 0.0)
    at_ref[...] = jnp.sum(place, axis=1, keepdims=True)
    copy.wait()
    rows_ref[...] = jnp.dot(pick, hidden_ref[...], preferred_element_type=F32).astype(BF16)


def cache_kernel(n_z, n_tp, cache_width, *refs):
    near, far, core_ref = refs[:4], refs[4 : n_z + 2], refs[n_z + 2]
    mix_ref, rows_ref, gain_ref, weight_ref = refs[n_z + 3 : n_z + 7]
    outs, back_ref = refs[n_z + 7 : n_z + 7 + n_tp], refs[n_z + 7 + n_tp]
    for d in range(4):
        back_ref[d * CAP : (d + 1) * CAP, :] = near[d][...]
    for d in range(n_z - 2):
        at = (2 * d + 4) * CAP
        back_ref[at : at + CAP, :] = far[d][:CAP, :]
        back_ref[at + CAP : at + 2 * CAP, :] = core_ref[d * CAP : (d + 1) * CAP, :]
    mixed = jnp.dot(mix_ref[...], back_ref[...], preferred_element_type=F32)
    state = rows_ref[...].astype(F32) + mixed
    square = jnp.sum(state * state, axis=1, keepdims=True)
    scaled = (state * gain_ref[...]).astype(BF16)
    value = lax.dot_general(
        scaled, weight_ref[...], (((1,), (1,)), ((), ())), preferred_element_type=F32
    ).astype(BF16)
    high = square.astype(BF16).astype(F32)
    rest = square - high
    middle = rest.astype(BF16).astype(F32)
    low = rest - middle
    seats, wide = outs[0].shape
    lane = lax.broadcasted_iota(jnp.int32, (square.shape[0], wide - cache_width), 1)
    extra = jnp.where(lane == 0, high, jnp.where(lane == 1, middle, jnp.where(lane == 2, low, 0.0)))
    extra = extra.astype(BF16)
    for d in range(n_tp):
        outs[d][:, :cache_width] = value[d * seats : (d + 1) * seats]
        outs[d][:, cache_width:] = extra[d * seats : (d + 1) * seats]


def finish_kernel(n_tp, width, rank_width, *refs):
    parts = refs[:n_tp]
    gain_ref, cos_ref, sin_ref, latent_ref, rotary_ref = refs[n_tp:]
    total = parts[0][...].astype(F32)
    for other in parts[1:]:
        total = total + other[...].astype(F32)
    half = cos_ref.shape[1]
    cache_width = rank_width + 2 * half
    square = jnp.sum(total[:, cache_width : cache_width + 3], axis=1, keepdims=True)
    cache = total[:, :cache_width] * lax.rsqrt(square / width + EPS)
    latent = cache[:, :rank_width]
    scale = lax.rsqrt(jnp.mean(latent * latent, axis=1, keepdims=True) + EPS)
    latent_ref[...] = (latent * scale * gain_ref[...]).astype(BF16)
    first = cache[:, rank_width : rank_width + half]
    second = cache[:, rank_width + half :]
    cosine, sine = cos_ref[...], sin_ref[...]
    rotary_ref[:, :half] = (first * cosine - second * sine).astype(BF16)
    rotary_ref[:, half:] = (second * cosine + first * sine).astype(BF16)


def call(kernel, out_shape, args, scratch=(), flops=0, hbm=()):
    moved = sum(a.size * a.dtype.itemsize for a in args)
    vmem = pl.BlockSpec(memory_space=pltpu.VMEM)
    args = [
        pltpu.with_memory_space_constraint(a, pltpu.HBM) if i in hbm else a
        for i, a in enumerate(args)
    ]
    return pl.pallas_call(
        kernel,
        out_shape=out_shape,
        in_specs=[
            pl.BlockSpec(memory_space=pltpu.HBM) if i in hbm else vmem for i in range(len(args))
        ],
        out_specs=[vmem] * len(out_shape),
        scratch_shapes=list(scratch),
        compiler_params=pltpu.CompilerParams(vmem_limit_bytes=VMEM_LIMIT),
        cost_estimate=pl.CostEstimate(flops=flops, bytes_accessed=moved, transcendentals=0),
    )(*args)


def swap(value, axis, d):
    return lax.ppermute(value, axis, [(i, i ^ d) for i in range(lax.axis_size(axis))])


def spread(value, n_tp):
    return [swap(value, "tp", d) for d in reversed(range(1, n_tp))]


def collect(values):
    return [swap(values[d], "tp", d) for d in reversed(range(1, len(values)))] + [values[0]]


def on_device(
    hidden,
    moe_gain,
    route_logits,
    routes,
    gate_weight,
    up_weight,
    down_weight,
    attn_gain,
    latent_weight,
    latent_gain,
    positions,
    owners,
):
    n_ep = lax.axis_size("ep")
    n_tp = lax.axis_size("tp")
    n_z = n_ep // 2
    tokens, width = hidden.shape
    share = width // n_tp
    ff = gate_weight.shape[2]
    slots = n_ep * CAP
    seat_cap = max(2, tokens // n_tp // 4)
    seats = n_tp * seat_cap
    rank_width = latent_gain.shape[0]
    cache_width = latent_weight.shape[1]
    half = (cache_width - rank_width) // 2
    wide = (cache_width + 3 + 127) // 128 * 128
    struct = jax.ShapeDtypeStruct
    chunks = width // 512 if width % 512 == 0 else 1

    own, to_core, to_near, *outgoing, combine = call(
        functools.partial(dispatch_kernel, n_ep, n_tp),
        [struct((CAP, width), BF16), struct((n_tp * CAP, share), BF16)]
        + [struct((2 * n_tp * CAP, share), BF16)]
        + [struct((CAP, share), BF16)] * (n_ep - 4)
        + [struct((slots, tokens), BF16)],
        (routes.T, route_logits.T, hidden, moe_gain),
        [
            pltpu.VMEM(routes.T.shape, jnp.int32),
            pltpu.VMEM(routes.T.shape, F32),
            pltpu.VMEM(hidden.shape, BF16),
            pltpu.VMEM((1, width), F32),
            pltpu.VMEM((slots, tokens), BF16),
            pltpu.VMEM((4 * CAP, width), F32),
            pltpu.SemaphoreType.DMA((3 + chunks,)),
        ],
        flops=4 * slots * tokens * width,
        hbm=(0, 1, 2, 3),
    )
    arrived = [swap(outgoing[d - 4], "ep", d) for d in range(4, n_ep)]
    near = swap(to_near, "ep", 2)
    from_core = swap(to_core, "ep", 1)
    gate_w, up_w, down_w = gate_weight[0], up_weight[0], down_weight[0]
    *loaded, mark = call(
        load_kernel,
        [struct(w.shape, BF16) for w in (gate_w, up_w, down_w)] + [struct((8, 128), F32)],
        (combine, gate_w, up_w, down_w),
        [pltpu.SemaphoreType.DMA((3,))],
        hbm=(1, 2, 3),
    )
    arrived, near, mark = lax.optimization_barrier((arrived, near, mark))
    mine = jnp.concatenate(arrived, axis=0)
    shares = spread(mine, n_tp)
    near_crossed = swap(near[n_tp * CAP :], "ep", 1)
    near_rows, far_rows = 4 * CAP, slots - 4 * CAP
    inner, gate_sum, up_sum = call(
        functools.partial(first_kernel, n_tp),
        [struct((near_rows, ff), BF16)] + [struct((far_rows, ff), F32)] * 2,
        (own, from_core, near[: n_tp * CAP], near_crossed, mine, *loaded[:2], mark),
        [pltpu.VMEM((4 * CAP, width), BF16)],
        flops=2 * slots * width * ff,
    )
    combine, inner = lax.optimization_barrier((combine, inner))
    share_of = hidden
    if share % 128:
        share_of = lax.dynamic_slice_in_dim(hidden, lax.axis_index("tp") * share, share, 1)
    rows, mix, at = call(
        functools.partial(seats_kernel, n_tp, seat_cap),
        [
            struct((n_tp * seats, share), BF16),
            struct((n_tp * seats, slots), BF16),
            struct((seats, 1), F32),
        ],
        (owners[None, :], positions[None, :], combine, share_of),
        [pltpu.VMEM((tokens, share), BF16), pltpu.SemaphoreType.DMA(())],
        flops=2 * n_tp * seats * tokens * (share + slots),
        hbm=(3,),
    )
    gate_sum, rows, mix = lax.optimization_barrier((gate_sum, rows, mix))
    terms = call(
        functools.partial(expert_kernel, n_tp),
        [struct((far_rows, share), BF16)] * n_tp + [struct((near_rows, share), BF16)] * n_tp,
        (*shares, *loaded, inner, gate_sum, up_sum),
        flops=2 * slots * width * ff * 3,
    )
    freqs = ROPE_BASE ** (-jnp.arange(half, dtype=F32) / half)
    angles = at * freqs[None, :]
    cosine, sine = jnp.cos(angles), jnp.sin(angles)

    far_terms = collect(terms[:n_tp])
    near_terms = collect(terms[n_tp:])
    far_done = call(
        functools.partial(sum_kernel, n_tp),
        [struct((2 * CAP, share), BF16)] * (n_z - 2),
        far_terms,
    )
    far_back = [swap(far_done[d - 2], "ep", 2 * d) for d in range(2, n_z)]
    near_done = call(
        functools.partial(sum_kernel, n_tp), [struct((CAP, share), BF16)] * 4, near_terms
    )
    near_back = [near_done[0]] + [swap(near_done[d], "ep", d) for d in (1, 2, 3)]
    crossed = swap(jnp.concatenate([piece[CAP:] for piece in far_back], axis=0), "ep", 1)
    partial = call(
        functools.partial(cache_kernel, n_z, n_tp, cache_width),
        [struct((seats, wide), BF16)] * n_tp,
        (*near_back, *far_back, crossed, mix, rows, attn_gain[None, :], latent_weight.T),
        [pltpu.VMEM((slots, share), BF16)],
        flops=2 * n_tp * seats * share * (slots + cache_width),
    )
    return tuple(
        call(
            functools.partial(finish_kernel, n_tp, width, rank_width),
            [struct((seats, rank_width), BF16), struct((seats, 2 * half), BF16)],
            (*collect(partial), latent_gain[None, :], cosine, sine),
        )
    )


def solution(mesh):
    placed = (
        P(("groups", "ep"), None),
        P(),
        P(("groups", "ep"), None),
        P(("groups", "ep"), None),
        P("ep", None, "tp"),
        P("ep", None, "tp"),
        P("ep", "tp", None),
        P("tp"),
        P("tp", None),
        P(),
        P(("groups", "ep")),
        P(("groups", "ep")),
    )
    return jax.shard_map(
        on_device,
        mesh=mesh,
        in_specs=placed,
        out_specs=(P(("groups", "ep", "tp"), None), P(("groups", "ep", "tp"), None)),
        check_vma=False,
    )
```

```python
import functools

import jax
import jax.numpy as jnp
from jax import lax
from jax.experimental import pallas as pl
from jax.experimental.pallas import tpu as pltpu
from jax.sharding import PartitionSpec as P

CAP = 16
EPS = 1e-06
ROUTE_SCALE = 2.5
ROPE_BASE = 10000.0
BF16 = jnp.bfloat16
F32 = jnp.float32
VMEM_LIMIT = 40 * 1024 * 1024


def columns_of(ref, index, count, share):
    if share % 128 == 0:
        return ref[:, pl.ds(pl.multiple_of(index * share, 128), share)]
    out = ref[:, 0:share]
    for q in range(1, count):
        out = jnp.where(index == q, ref[:, q * share : (q + 1) * share], out)
    return out


def dispatch_kernel(n_ep, n_tp, routes_hbm, logits_hbm, hidden_hbm, gain_hbm, *refs):
    own_ref, core_ref, near_ref = refs[:3]
    outs, combine_ref = refs[3 : n_ep - 1], refs[n_ep - 1]
    routes_ref, logits_ref, hidden_ref, gain_ref, pick_ref, head_ref, sems = refs[n_ep:]
    me = lax.axis_index("ep")
    part = lax.axis_index("tp")
    tokens, width = hidden_ref.shape
    share = width // n_tp
    step = 512 if width % 512 == 0 else width
    starts = range(0, width, step)
    small = [
        pltpu.make_async_copy(routes_hbm, routes_ref, sems.at[0]),
        pltpu.make_async_copy(logits_hbm, logits_ref, sems.at[1]),
        pltpu.make_async_copy(gain_hbm, gain_ref.at[0], sems.at[2]),
    ]
    large = [
        pltpu.make_async_copy(
            hidden_hbm.at[:, c : c + step], hidden_ref.at[:, c : c + step], sems.at[3 + i]
        )
        for i, c in enumerate(starts)
    ]
    for copy in small + large:
        copy.start()
    small[0].wait()
    small[1].wait()
    routes = routes_ref[...]
    affinity = jax.nn.sigmoid(logits_ref[...])
    weight = ROUTE_SCALE * affinity / jnp.sum(affinity, axis=0, keepdims=True)
    weight = weight.astype(BF16).astype(F32)
    expert = lax.broadcasted_iota(jnp.int32, (n_ep, tokens), 0) ^ me
    hit = jnp.zeros((n_ep, tokens), F32)
    gain_of = jnp.zeros((n_ep, tokens), F32)
    for k in range(routes.shape[0]):
        same = routes[k : k + 1, :] == expert
        hit = jnp.where(same, 1.0, hit)
        gain_of = jnp.where(same, weight[k : k + 1, :], gain_of)
    earlier = lax.broadcasted_iota(jnp.int32, (tokens, tokens), 0) < lax.broadcasted_iota(
        jnp.int32, (tokens, tokens), 1
    )
    rank = jnp.dot(hit.astype(BF16), earlier.astype(F32).astype(BF16), preferred_element_type=F32)
    rank = jnp.where(hit > 0, rank, -1.0)
    place = lax.broadcasted_iota(jnp.int32, (CAP, tokens), 0).astype(F32)
    for d in range(n_ep):
        match = rank[d : d + 1, :] == place
        rows = slice(d * CAP, (d + 1) * CAP)
        pick_ref[rows, :] = jnp.where(match, 1.0, 0.0).astype(BF16)
        combine_ref[rows, :] = jnp.where(match, gain_of[d : d + 1, :], 0.0).astype(BF16)
    pick = pick_ref[...]
    head = 4 * CAP
    square = jnp.zeros((n_ep * CAP, 1), F32)
    middle = len(large) // 2
    for i, c in enumerate(starts):
        if i == 0 or i == middle:
            for copy in large[:middle] if i < middle else large[i:]:
                copy.wait()
        got = jnp.dot(pick, hidden_ref[:, c : c + step], preferred_element_type=F32)
        square = square + jnp.sum(got * got, axis=1, keepdims=True)
        head_ref[:, c : c + step] = got[:head]
    small[2].wait()
    scale = lax.rsqrt(square / width + EPS)
    got = jnp.dot(pick[head:], columns_of(hidden_ref, part, n_tp, share), preferred_element_type=F32)
    rest = (got * scale[head:] * columns_of(gain_ref, part, n_tp, share)).astype(BF16)
    at = 0
    for out in outs:
        out[...] = rest[at : at + out.shape[0]]
        at += out.shape[0]
    whole = (head_ref[...] * scale[:head] * gain_ref[...]).astype(BF16)
    own_ref[...] = whole[:CAP]
    for q in range(n_tp):
        columns = slice(q * share, (q + 1) * share)
        core_ref[q * CAP : (q + 1) * CAP, :] = whole[CAP : 2 * CAP, columns]
        near_ref[q * CAP : (q + 1) * CAP, :] = whole[2 * CAP : 3 * CAP, columns]
        near_ref[(n_tp + q) * CAP : (n_tp + q + 1) * CAP, :] = whole[3 * CAP :, columns]


def load_kernel(after_ref, *refs):
    count = (len(refs) - 2) // 2
    mark_ref, sems = refs[-2:]
    copies = [
        pltpu.make_async_copy(refs[i], refs[count + i], sems.at[i]) for i in range(count)
    ]
    for copy in copies:
        copy.start()
    mark_ref[...] = jnp.zeros(mark_ref.shape, F32)
    for copy in copies:
        copy.wait()


def first_kernel(
    n_tp,
    own_ref,
    core_ref,
    near_ref,
    cross_ref,
    mine_ref,
    gate_ref,
    up_ref,
    mark_ref,
    inner_ref,
    gate_sum_ref,
    up_sum_ref,
    head_ref,
):
    part = lax.axis_index("tp")
    share = mine_ref.shape[1]
    head_ref[:CAP, :] = own_ref[...]
    for i, ref in enumerate((core_ref, near_ref, cross_ref)):
        for q in range(n_tp):
            rows = slice((i + 1) * CAP, (i + 2) * CAP)
            head_ref[rows, q * share : (q + 1) * share] = ref[q * CAP : (q + 1) * CAP, :]
    depth = pl.ds(pl.multiple_of(part * share, CAP), share)
    gate, upper = (
        jnp.dot(head_ref[...], ref[...], preferred_element_type=F32) for ref in (gate_ref, up_ref)
    )
    for weight_ref, sum_ref in zip((gate_ref, up_ref), (gate_sum_ref, up_sum_ref)):
        sum_ref[...] = jnp.dot(mine_ref[...], weight_ref[depth, :], preferred_element_type=F32)
    inner_ref[...] = (gate / (1.0 + jnp.exp(-gate)) * upper).astype(BF16)


def expert_kernel(n_tp, *refs):
    rows = refs[: n_tp - 1]
    gate_ref, up_ref, down_ref, near_ref, gate_sum_ref, up_sum_ref = refs[n_tp - 1 : n_tp + 5]
    far_outs = refs[n_tp + 5 : 2 * n_tp + 5]
    near_outs = refs[2 * n_tp + 5 :]
    part = lax.axis_index("tp")
    share = rows[0].shape[1]
    gate = gate_sum_ref[...]
    upper = up_sum_ref[...]
    for d in range(1, n_tp):
        value = rows[n_tp - 1 - d][...]
        depth = pl.ds(pl.multiple_of((part ^ d) * share, CAP), share)
        gate = gate + jnp.dot(value, gate_ref[depth, :], preferred_element_type=F32)
        upper = upper + jnp.dot(value, up_ref[depth, :], preferred_element_type=F32)
    far = (gate / (1.0 + jnp.exp(-gate)) * upper).astype(BF16)
    inner = jnp.concatenate([far, near_ref[...]], axis=0)
    count = far.shape[0]
    for d in range(n_tp):
        down = columns_of(down_ref, part ^ d, n_tp, share)
        out = jnp.dot(inner, down, preferred_element_type=F32).astype(BF16)
        far_outs[d][...] = out[:count]
        near_outs[d][...] = out[count:]


def sum_kernel(n_tp, *refs):
    parts, outs = refs[:n_tp], refs[n_tp:]
    at = 0
    for out in outs:
        rows = slice(at, at + out.shape[0])
        total = parts[0][rows, :].astype(F32)
        for other in parts[1:]:
            total = total + other[rows, :].astype(F32)
        out[...] = total.astype(BF16)
        at += out.shape[0]


def seats_kernel(
    n_tp,
    seat_cap,
    owners_ref,
    positions_ref,
    combine_ref,
    hidden_hbm,
    rows_ref,
    mix_ref,
    at_ref,
    hidden_ref,
    sem,
):
    part = lax.axis_index("tp")
    tokens, share = hidden_ref.shape
    if hidden_hbm.shape[1] != share:
        hidden_hbm = hidden_hbm.at[:, pl.ds(pl.multiple_of(part * share, 128), share)]
    copy = pltpu.make_async_copy(hidden_hbm, hidden_ref, sem)
    copy.start()
    source_rows = tokens // n_tp
    owners = owners_ref[...] ^ part
    owner = lax.broadcasted_iota(jnp.int32, (n_tp, tokens), 0)
    hot = jnp.where(owners == owner, 1.0, 0.0)
    first = lax.broadcasted_iota(jnp.int32, (tokens, tokens), 0)
    second = lax.broadcasted_iota(jnp.int32, (tokens, tokens), 1)
    earlier = jnp.where((first < second) & (first // source_rows == second // source_rows), 1.0, 0.0)
    before = jnp.dot(hot.astype(BF16), earlier.astype(BF16), preferred_element_type=F32)
    seat = jnp.sum(before * hot, axis=0, keepdims=True).astype(jnp.int32)
    source = lax.broadcasted_iota(jnp.int32, (1, tokens), 1) // source_rows
    code = owners * (n_tp * seat_cap) + source * seat_cap + seat
    seats = n_tp * seat_cap
    held = lax.broadcasted_iota(jnp.int32, (n_tp * seats, tokens), 0) == code
    pick = jnp.where(held, 1.0, 0.0).astype(BF16)
    mix_ref[...] = lax.dot_general(
        pick, combine_ref[...], (((1,), (1,)), ((), ())), preferred_element_type=F32
    ).astype(BF16)
    place = jnp.where(held[:seats], positions_ref[...].astype(F32), 0.0)
    at_ref[...] = jnp.sum(place, axis=1, keepdims=True)
    copy.wait()
    rows_ref[...] = jnp.dot(pick, hidden_ref[...], preferred_element_type=F32).astype(BF16)


def cache_kernel(n_z, n_tp, cache_width, *refs):
    near, far, core_ref = refs[:4], refs[4 : n_z + 2], refs[n_z + 2]
    mix_ref, rows_ref, gain_ref, weight_ref = refs[n_z + 3 : n_z + 7]
    outs, back_ref = refs[n_z + 7 : n_z + 7 + n_tp], refs[n_z + 7 + n_tp]
    for d in range(4):
        back_ref[d * CAP : (d + 1) * CAP, :] = near[d][...]
    for d in range(n_z - 2):
        at = (2 * d + 4) * CAP
        back_ref[at : at + CAP, :] = far[d][:CAP, :]
        back_ref[at + CAP : at + 2 * CAP, :] = core_ref[d * CAP : (d + 1) * CAP, :]
    mixed = jnp.dot(mix_ref[...], back_ref[...], preferred_element_type=F32)
    state = rows_ref[...].astype(F32) + mixed
    square = jnp.sum(state * state, axis=1, keepdims=True)
    scaled = (state * gain_ref[...]).astype(BF16)
    value = lax.dot_general(
        scaled, weight_ref[...], (((1,), (1,)), ((), ())), preferred_element_type=F32
    ).astype(BF16)
    high = square.astype(BF16).astype(F32)
    rest = square - high
    middle = rest.astype(BF16).astype(F32)
    low = rest - middle
    seats, wide = outs[0].shape
    lane = lax.broadcasted_iota(jnp.int32, (square.shape[0], wide - cache_width), 1)
    extra = jnp.where(lane == 0, high, jnp.where(lane == 1, middle, jnp.where(lane == 2, low, 0.0)))
    extra = extra.astype(BF16)
    for d in range(n_tp):
        outs[d][:, :cache_width] = value[d * seats : (d + 1) * seats]
        outs[d][:, cache_width:] = extra[d * seats : (d + 1) * seats]


def finish_kernel(n_tp, width, rank_width, *refs):
    parts = refs[:n_tp]
    gain_ref, cos_ref, sin_ref, latent_ref, rotary_ref = refs[n_tp:]
    total = parts[0][...].astype(F32)
    for other in parts[1:]:
        total = total + other[...].astype(F32)
    half = cos_ref.shape[1]
    cache_width = rank_width + 2 * half
    square = jnp.sum(total[:, cache_width : cache_width + 3], axis=1, keepdims=True)
    cache = total[:, :cache_width] * lax.rsqrt(square / width + EPS)
    latent = cache[:, :rank_width]
    scale = lax.rsqrt(jnp.mean(latent * latent, axis=1, keepdims=True) + EPS)
    latent_ref[...] = (latent * scale * gain_ref[...]).astype(BF16)
    first = cache[:, rank_width : rank_width + half]
    second = cache[:, rank_width + half :]
    cosine, sine = cos_ref[...], sin_ref[...]
    rotary_ref[:, :half] = (first * cosine - second * sine).astype(BF16)
    rotary_ref[:, half:] = (second * cosine + first * sine).astype(BF16)


def call(kernel, out_shape, args, scratch=(), flops=0, hbm=()):
    moved = sum(a.size * a.dtype.itemsize for a in args)
    vmem = pl.BlockSpec(memory_space=pltpu.VMEM)
    args = [
        pltpu.with_memory_space_constraint(a, pltpu.HBM) if i in hbm else a
        for i, a in enumerate(args)
    ]
    return pl.pallas_call(
        kernel,
        out_shape=out_shape,
        in_specs=[
            pl.BlockSpec(memory_space=pltpu.HBM) if i in hbm else vmem for i in range(len(args))
        ],
        out_specs=[vmem] * len(out_shape),
        scratch_shapes=list(scratch),
        compiler_params=pltpu.CompilerParams(vmem_limit_bytes=VMEM_LIMIT),
        cost_estimate=pl.CostEstimate(flops=flops, bytes_accessed=moved, transcendentals=0),
    )(*args)


def swap(value, axis, d):
    return lax.ppermute(value, axis, [(i, i ^ d) for i in range(lax.axis_size(axis))])


def spread(value, n_tp):
    return [swap(value, "tp", d) for d in reversed(range(1, n_tp))]


def collect(values):
    return [swap(values[d], "tp", d) for d in reversed(range(1, len(values)))] + [values[0]]


def on_device(
    hidden,
    moe_gain,
    route_logits,
    routes,
    gate_weight,
    up_weight,
    down_weight,
    attn_gain,
    latent_weight,
    latent_gain,
    positions,
    owners,
):
    n_ep = lax.axis_size("ep")
    n_tp = lax.axis_size("tp")
    n_z = n_ep // 2
    tokens, width = hidden.shape
    share = width // n_tp
    ff = gate_weight.shape[2]
    slots = n_ep * CAP
    seat_cap = max(2, tokens // n_tp // 4)
    seats = n_tp * seat_cap
    rank_width = latent_gain.shape[0]
    cache_width = latent_weight.shape[1]
    half = (cache_width - rank_width) // 2
    wide = (cache_width + 3 + 127) // 128 * 128
    struct = jax.ShapeDtypeStruct
    chunks = width // 512 if width % 512 == 0 else 1

    own, to_core, to_near, *outgoing, combine = call(
        functools.partial(dispatch_kernel, n_ep, n_tp),
        [struct((CAP, width), BF16), struct((n_tp * CAP, share), BF16)]
        + [struct((2 * n_tp * CAP, share), BF16)]
        + [struct((CAP, share), BF16)] * (n_ep - 4)
        + [struct((slots, tokens), BF16)],
        (routes.T, route_logits.T, hidden, moe_gain),
        [
            pltpu.VMEM(routes.T.shape, jnp.int32),
            pltpu.VMEM(routes.T.shape, F32),
            pltpu.VMEM(hidden.shape, BF16),
            pltpu.VMEM((1, width), F32),
            pltpu.VMEM((slots, tokens), BF16),
            pltpu.VMEM((4 * CAP, width), F32),
            pltpu.SemaphoreType.DMA((3 + chunks,)),
        ],
        flops=4 * slots * tokens * width,
        hbm=(0, 1, 2, 3),
    )
    order = [*range(4, n_ep, 2), *range(5, n_ep, 2)]
    arrived = [swap(outgoing[d - 4], "ep", d) for d in order]
    near = swap(to_near, "ep", 2)
    from_core = swap(to_core, "ep", 1)
    gate_w, up_w, down_w = gate_weight[0], up_weight[0], down_weight[0]
    *loaded, mark = call(
        load_kernel,
        [struct(w.shape, BF16) for w in (gate_w, up_w, down_w)] + [struct((8, 128), F32)],
        (combine, gate_w, up_w, down_w),
        [pltpu.SemaphoreType.DMA((3,))],
        hbm=(1, 2, 3),
    )
    arrived, near, mark = lax.optimization_barrier((arrived, near, mark))
    mine = jnp.concatenate([arrived[order.index(d)] for d in range(4, n_ep)], axis=0)
    shares = spread(mine, n_tp)
    near_crossed = swap(near[n_tp * CAP :], "ep", 1)
    near_rows, far_rows = 4 * CAP, slots - 4 * CAP
    inner, gate_sum, up_sum = call(
        functools.partial(first_kernel, n_tp),
        [struct((near_rows, ff), BF16)] + [struct((far_rows, ff), F32)] * 2,
        (own, from_core, near[: n_tp * CAP], near_crossed, mine, *loaded[:2], mark),
        [pltpu.VMEM((4 * CAP, width), BF16)],
        flops=2 * slots * width * ff,
    )
    terms = call(
        functools.partial(expert_kernel, n_tp),
        [struct((far_rows, share), BF16)] * n_tp + [struct((near_rows, share), BF16)] * n_tp,
        (*shares, *loaded, inner, gate_sum, up_sum),
        flops=2 * slots * width * ff * 3,
    )
    terms = list(terms)
    combine, terms[0] = lax.optimization_barrier((combine, terms[0]))
    share_of = hidden
    if share % 128:
        share_of = lax.dynamic_slice_in_dim(hidden, lax.axis_index("tp") * share, share, 1)
    rows, mix, at = call(
        functools.partial(seats_kernel, n_tp, seat_cap),
        [
            struct((n_tp * seats, share), BF16),
            struct((n_tp * seats, slots), BF16),
            struct((seats, 1), F32),
        ],
        (owners[None, :], positions[None, :], combine, share_of),
        [pltpu.VMEM((tokens, share), BF16), pltpu.SemaphoreType.DMA(())],
        flops=2 * n_tp * seats * tokens * (share + slots),
        hbm=(3,),
    )
    near_pieces, rows, mix = lax.optimization_barrier((list(terms[n_tp:]), rows, mix))
    freqs = ROPE_BASE ** (-jnp.arange(half, dtype=F32) / half)
    angles = at * freqs[None, :]
    cosine, sine = jnp.cos(angles), jnp.sin(angles)

    far_terms = collect(terms[:n_tp])
    near_terms = collect(near_pieces)
    far_done = call(
        functools.partial(sum_kernel, n_tp),
        [struct((2 * CAP, share), BF16)] * (n_z - 2),
        far_terms,
    )
    far_back = [swap(far_done[d - 2], "ep", 2 * d) for d in range(2, n_z)]
    near_done = call(
        functools.partial(sum_kernel, n_tp), [struct((CAP, share), BF16)] * 4, near_terms
    )
    near_back = [near_done[0]] + [swap(near_done[d], "ep", d) for d in (1, 2, 3)]
    crossed = swap(jnp.concatenate([piece[CAP:] for piece in far_back], axis=0), "ep", 1)
    partial = call(
        functools.partial(cache_kernel, n_z, n_tp, cache_width),
        [struct((seats, wide), BF16)] * n_tp,
        (*near_back, *far_back, crossed, mix, rows, attn_gain[None, :], latent_weight.T),
        [pltpu.VMEM((slots, share), BF16)],
        flops=2 * n_tp * seats * share * (slots + cache_width),
    )
    return tuple(
        call(
            functools.partial(finish_kernel, n_tp, width, rank_width),
            [struct((seats, rank_width), BF16), struct((seats, 2 * half), BF16)],
            (*collect(partial), latent_gain[None, :], cosine, sine),
        )
    )


def solution(mesh):
    placed = (
        P(("groups", "ep"), None),
        P(),
        P(("groups", "ep"), None),
        P(("groups", "ep"), None),
        P("ep", None, "tp"),
        P("ep", None, "tp"),
        P("ep", "tp", None),
        P("tp"),
        P("tp", None),
        P(),
        P(("groups", "ep")),
        P(("groups", "ep")),
    )
    return jax.shard_map(
        on_device,
        mesh=mesh,
        in_specs=placed,
        out_specs=(P(("groups", "ep", "tp"), None), P(("groups", "ep", "tp"), None)),
        check_vma=False,
    )
```

```python
import functools

import jax
import jax.numpy as jnp
from jax import lax
from jax.experimental import pallas as pl
from jax.experimental.pallas import tpu as pltpu
from jax.sharding import PartitionSpec as P

CAP = 16
EPS = 1e-06
ROUTE_SCALE = 2.5
ROPE_BASE = 10000.0
BF16 = jnp.bfloat16
F32 = jnp.float32
VMEM_LIMIT = 40 * 1024 * 1024


def columns_of(ref, index, count, share):
    if share % 128 == 0:
        return ref[:, pl.ds(pl.multiple_of(index * share, 128), share)]
    out = ref[:, 0:share]
    for q in range(1, count):
        out = jnp.where(index == q, ref[:, q * share : (q + 1) * share], out)
    return out


def dispatch_kernel(n_ep, n_tp, routes_hbm, logits_hbm, hidden_hbm, gain_hbm, *refs):
    own_ref, core_ref, near_ref = refs[:3]
    outs, combine_ref = refs[3 : n_ep - 1], refs[n_ep - 1]
    routes_ref, logits_ref, hidden_ref, gain_ref, pick_ref, head_ref, sems = refs[n_ep:]
    me = lax.axis_index("ep")
    part = lax.axis_index("tp")
    tokens, width = hidden_ref.shape
    share = width // n_tp
    step = 512 if width % 512 == 0 else width
    starts = range(0, width, step)
    small = [
        pltpu.make_async_copy(routes_hbm, routes_ref, sems.at[0]),
        pltpu.make_async_copy(logits_hbm, logits_ref, sems.at[1]),
        pltpu.make_async_copy(gain_hbm, gain_ref.at[0], sems.at[2]),
    ]
    large = [
        pltpu.make_async_copy(
            hidden_hbm.at[:, c : c + step], hidden_ref.at[:, c : c + step], sems.at[3 + i]
        )
        for i, c in enumerate(starts)
    ]
    for copy in small + large:
        copy.start()
    small[0].wait()
    small[1].wait()
    routes = routes_ref[...]
    affinity = jax.nn.sigmoid(logits_ref[...])
    weight = ROUTE_SCALE * affinity / jnp.sum(affinity, axis=0, keepdims=True)
    weight = weight.astype(BF16).astype(F32)
    expert = lax.broadcasted_iota(jnp.int32, (n_ep, tokens), 0) ^ me
    hit = jnp.zeros((n_ep, tokens), F32)
    gain_of = jnp.zeros((n_ep, tokens), F32)
    for k in range(routes.shape[0]):
        same = routes[k : k + 1, :] == expert
        hit = jnp.where(same, 1.0, hit)
        gain_of = jnp.where(same, weight[k : k + 1, :], gain_of)
    earlier = lax.broadcasted_iota(jnp.int32, (tokens, tokens), 0) < lax.broadcasted_iota(
        jnp.int32, (tokens, tokens), 1
    )
    rank = jnp.dot(hit.astype(BF16), earlier.astype(F32).astype(BF16), preferred_element_type=F32)
    rank = jnp.where(hit > 0, rank, -1.0)
    place = lax.broadcasted_iota(jnp.int32, (CAP, tokens), 0).astype(F32)
    for d in range(n_ep):
        match = rank[d : d + 1, :] == place
        rows = slice(d * CAP, (d + 1) * CAP)
        pick_ref[rows, :] = jnp.where(match, 1.0, 0.0).astype(BF16)
        combine_ref[rows, :] = jnp.where(match, gain_of[d : d + 1, :], 0.0).astype(BF16)
    pick = pick_ref[...]
    head = 4 * CAP
    square = jnp.zeros((n_ep * CAP, 1), F32)
    middle = len(large) // 2
    for i, c in enumerate(starts):
        if i == 0 or i == middle:
            for copy in large[:middle] if i < middle else large[i:]:
                copy.wait()
        got = jnp.dot(pick, hidden_ref[:, c : c + step], preferred_element_type=F32)
        square = square + jnp.sum(got * got, axis=1, keepdims=True)
        head_ref[:, c : c + step] = got[:head]
    small[2].wait()
    scale = lax.rsqrt(square / width + EPS)
    got = jnp.dot(pick[head:], columns_of(hidden_ref, part, n_tp, share), preferred_element_type=F32)
    rest = (got * scale[head:] * columns_of(gain_ref, part, n_tp, share)).astype(BF16)
    at = 0
    for out in outs:
        out[...] = rest[at : at + out.shape[0]]
        at += out.shape[0]
    whole = (head_ref[...] * scale[:head] * gain_ref[...]).astype(BF16)
    own_ref[...] = whole[:CAP]
    for q in range(n_tp):
        columns = slice(q * share, (q + 1) * share)
        core_ref[q * CAP : (q + 1) * CAP, :] = whole[CAP : 2 * CAP, columns]
        near_ref[q * CAP : (q + 1) * CAP, :] = whole[2 * CAP : 3 * CAP, columns]
        near_ref[(n_tp + q) * CAP : (n_tp + q + 1) * CAP, :] = whole[3 * CAP :, columns]


def load_kernel(after_ref, *refs):
    count = (len(refs) - 2) // 2
    mark_ref, sems = refs[-2:]
    copies = [
        pltpu.make_async_copy(refs[i], refs[count + i], sems.at[i]) for i in range(count)
    ]
    for copy in copies:
        copy.start()
    mark_ref[...] = jnp.zeros(mark_ref.shape, F32)
    for copy in copies:
        copy.wait()


def first_kernel(
    n_tp,
    own_ref,
    core_ref,
    near_ref,
    cross_ref,
    mine_ref,
    gate_ref,
    up_ref,
    mark_ref,
    inner_ref,
    gate_sum_ref,
    up_sum_ref,
    head_ref,
):
    part = lax.axis_index("tp")
    share = mine_ref.shape[1]
    head_ref[:CAP, :] = own_ref[...]
    for i, ref in enumerate((core_ref, near_ref, cross_ref)):
        for q in range(n_tp):
            rows = slice((i + 1) * CAP, (i + 2) * CAP)
            head_ref[rows, q * share : (q + 1) * share] = ref[q * CAP : (q + 1) * CAP, :]
    depth = pl.ds(pl.multiple_of(part * share, CAP), share)
    gate, upper = (
        jnp.dot(head_ref[...], ref[...], preferred_element_type=F32) for ref in (gate_ref, up_ref)
    )
    for weight_ref, sum_ref in zip((gate_ref, up_ref), (gate_sum_ref, up_sum_ref)):
        sum_ref[...] = jnp.dot(mine_ref[...], weight_ref[depth, :], preferred_element_type=F32)
    inner_ref[...] = (gate / (1.0 + jnp.exp(-gate)) * upper).astype(BF16)


def expert_kernel(n_tp, *refs):
    rows = refs[: n_tp - 1]
    gate_ref, up_ref, down_ref, near_ref, gate_sum_ref, up_sum_ref = refs[n_tp - 1 : n_tp + 5]
    far_outs = refs[n_tp + 5 : 2 * n_tp + 5]
    near_outs = refs[2 * n_tp + 5 :]
    part = lax.axis_index("tp")
    share = rows[0].shape[1]
    gate = gate_sum_ref[...]
    upper = up_sum_ref[...]
    for d in range(1, n_tp):
        value = rows[n_tp - 1 - d][...]
        depth = pl.ds(pl.multiple_of((part ^ d) * share, CAP), share)
        gate = gate + jnp.dot(value, gate_ref[depth, :], preferred_element_type=F32)
        upper = upper + jnp.dot(value, up_ref[depth, :], preferred_element_type=F32)
    far = (gate / (1.0 + jnp.exp(-gate)) * upper).astype(BF16)
    inner = jnp.concatenate([far, near_ref[...]], axis=0)
    count = far.shape[0]
    for d in range(n_tp):
        down = columns_of(down_ref, part ^ d, n_tp, share)
        out = jnp.dot(inner, down, preferred_element_type=F32).astype(BF16)
        far_outs[d][...] = out[:count]
        near_outs[d][...] = out[count:]


def sum_kernel(n_tp, *refs):
    parts, outs = refs[:n_tp], refs[n_tp:]
    at = 0
    for out in outs:
        rows = slice(at, at + out.shape[0])
        total = parts[0][rows, :].astype(F32)
        for other in parts[1:]:
            total = total + other[rows, :].astype(F32)
        out[...] = total.astype(BF16)
        at += out.shape[0]


def seats_kernel(
    n_tp,
    seat_cap,
    owners_ref,
    positions_ref,
    combine_ref,
    hidden_hbm,
    rows_ref,
    mix_ref,
    at_ref,
    hidden_ref,
    sem,
):
    part = lax.axis_index("tp")
    tokens, share = hidden_ref.shape
    if hidden_hbm.shape[1] != share:
        hidden_hbm = hidden_hbm.at[:, pl.ds(pl.multiple_of(part * share, 128), share)]
    copy = pltpu.make_async_copy(hidden_hbm, hidden_ref, sem)
    copy.start()
    source_rows = tokens // n_tp
    owners = owners_ref[...] ^ part
    owner = lax.broadcasted_iota(jnp.int32, (n_tp, tokens), 0)
    hot = jnp.where(owners == owner, 1.0, 0.0)
    first = lax.broadcasted_iota(jnp.int32, (tokens, tokens), 0)
    second = lax.broadcasted_iota(jnp.int32, (tokens, tokens), 1)
    earlier = jnp.where((first < second) & (first // source_rows == second // source_rows), 1.0, 0.0)
    before = jnp.dot(hot.astype(BF16), earlier.astype(BF16), preferred_element_type=F32)
    seat = jnp.sum(before * hot, axis=0, keepdims=True).astype(jnp.int32)
    source = lax.broadcasted_iota(jnp.int32, (1, tokens), 1) // source_rows
    code = owners * (n_tp * seat_cap) + source * seat_cap + seat
    seats = n_tp * seat_cap
    held = lax.broadcasted_iota(jnp.int32, (n_tp * seats, tokens), 0) == code
    pick = jnp.where(held, 1.0, 0.0).astype(BF16)
    mix_ref[...] = lax.dot_general(
        pick, combine_ref[...], (((1,), (1,)), ((), ())), preferred_element_type=F32
    ).astype(BF16)
    place = jnp.where(held[:seats], positions_ref[...].astype(F32), 0.0)
    at_ref[...] = jnp.sum(place, axis=1, keepdims=True)
    copy.wait()
    rows_ref[...] = jnp.dot(pick, hidden_ref[...], preferred_element_type=F32).astype(BF16)


def cache_kernel(n_z, n_tp, cache_width, *refs):
    near, far, core_ref = refs[:4], refs[4 : n_z + 2], refs[n_z + 2]
    mix_ref, rows_ref, gain_ref, weight_ref = refs[n_z + 3 : n_z + 7]
    outs, back_ref = refs[n_z + 7 : n_z + 7 + n_tp], refs[n_z + 7 + n_tp]
    for d in range(4):
        back_ref[d * CAP : (d + 1) * CAP, :] = near[d][...]
    for d in range(n_z - 2):
        at = (2 * d + 4) * CAP
        back_ref[at : at + CAP, :] = far[d][:CAP, :]
        back_ref[at + CAP : at + 2 * CAP, :] = core_ref[d * CAP : (d + 1) * CAP, :]
    mixed = jnp.dot(mix_ref[...], back_ref[...], preferred_element_type=F32)
    state = rows_ref[...].astype(F32) + mixed
    square = jnp.sum(state * state, axis=1, keepdims=True)
    scaled = (state * gain_ref[...]).astype(BF16)
    value = lax.dot_general(
        scaled, weight_ref[...], (((1,), (1,)), ((), ())), preferred_element_type=F32
    ).astype(BF16)
    high = square.astype(BF16).astype(F32)
    rest = square - high
    middle = rest.astype(BF16).astype(F32)
    low = rest - middle
    seats, wide = outs[0].shape
    lane = lax.broadcasted_iota(jnp.int32, (square.shape[0], wide - cache_width), 1)
    extra = jnp.where(lane == 0, high, jnp.where(lane == 1, middle, jnp.where(lane == 2, low, 0.0)))
    extra = extra.astype(BF16)
    for d in range(n_tp):
        outs[d][:, :cache_width] = value[d * seats : (d + 1) * seats]
        outs[d][:, cache_width:] = extra[d * seats : (d + 1) * seats]


def finish_kernel(n_tp, width, rank_width, *refs):
    parts = refs[:n_tp]
    gain_ref, cos_ref, sin_ref, latent_ref, rotary_ref = refs[n_tp:]
    total = parts[0][...].astype(F32)
    for other in parts[1:]:
        total = total + other[...].astype(F32)
    half = cos_ref.shape[1]
    cache_width = rank_width + 2 * half
    square = jnp.sum(total[:, cache_width : cache_width + 3], axis=1, keepdims=True)
    cache = total[:, :cache_width] * lax.rsqrt(square / width + EPS)
    latent = cache[:, :rank_width]
    scale = lax.rsqrt(jnp.mean(latent * latent, axis=1, keepdims=True) + EPS)
    latent_ref[...] = (latent * scale * gain_ref[...]).astype(BF16)
    first = cache[:, rank_width : rank_width + half]
    second = cache[:, rank_width + half :]
    cosine, sine = cos_ref[...], sin_ref[...]
    rotary_ref[:, :half] = (first * cosine - second * sine).astype(BF16)
    rotary_ref[:, half:] = (second * cosine + first * sine).astype(BF16)


def call(kernel, out_shape, args, scratch=(), flops=0, hbm=()):
    moved = sum(a.size * a.dtype.itemsize for a in args)
    vmem = pl.BlockSpec(memory_space=pltpu.VMEM)
    args = [
        pltpu.with_memory_space_constraint(a, pltpu.HBM) if i in hbm else a
        for i, a in enumerate(args)
    ]
    return pl.pallas_call(
        kernel,
        out_shape=out_shape,
        in_specs=[
            pl.BlockSpec(memory_space=pltpu.HBM) if i in hbm else vmem for i in range(len(args))
        ],
        out_specs=[vmem] * len(out_shape),
        scratch_shapes=list(scratch),
        compiler_params=pltpu.CompilerParams(vmem_limit_bytes=VMEM_LIMIT),
        cost_estimate=pl.CostEstimate(flops=flops, bytes_accessed=moved, transcendentals=0),
    )(*args)


def swap(value, axis, d):
    return lax.ppermute(value, axis, [(i, i ^ d) for i in range(lax.axis_size(axis))])


def spread(value, n_tp):
    return [swap(value, "tp", d) for d in reversed(range(1, n_tp))]


def collect(values):
    return [swap(values[d], "tp", d) for d in reversed(range(1, len(values)))] + [values[0]]


def on_device(
    hidden,
    moe_gain,
    route_logits,
    routes,
    gate_weight,
    up_weight,
    down_weight,
    attn_gain,
    latent_weight,
    latent_gain,
    positions,
    owners,
):
    n_ep = lax.axis_size("ep")
    n_tp = lax.axis_size("tp")
    n_z = n_ep // 2
    tokens, width = hidden.shape
    share = width // n_tp
    ff = gate_weight.shape[2]
    slots = n_ep * CAP
    seat_cap = max(2, tokens // n_tp // 4)
    seats = n_tp * seat_cap
    rank_width = latent_gain.shape[0]
    cache_width = latent_weight.shape[1]
    half = (cache_width - rank_width) // 2
    wide = (cache_width + 3 + 127) // 128 * 128
    struct = jax.ShapeDtypeStruct
    chunks = width // 512 if width % 512 == 0 else 1

    own, to_core, to_near, *outgoing, combine = call(
        functools.partial(dispatch_kernel, n_ep, n_tp),
        [struct((CAP, width), BF16), struct((n_tp * CAP, share), BF16)]
        + [struct((2 * n_tp * CAP, share), BF16)]
        + [struct((CAP, share), BF16)] * (n_ep - 4)
        + [struct((slots, tokens), BF16)],
        (routes.T, route_logits.T, hidden, moe_gain),
        [
            pltpu.VMEM(routes.T.shape, jnp.int32),
            pltpu.VMEM(routes.T.shape, F32),
            pltpu.VMEM(hidden.shape, BF16),
            pltpu.VMEM((1, width), F32),
            pltpu.VMEM((slots, tokens), BF16),
            pltpu.VMEM((4 * CAP, width), F32),
            pltpu.SemaphoreType.DMA((3 + chunks,)),
        ],
        flops=4 * slots * tokens * width,
        hbm=(0, 1, 2, 3),
    )
    order = [*range(4, n_ep, 2), *range(5, n_ep, 2)]
    arrived = [swap(outgoing[d - 4], "ep", d) for d in order]
    near = swap(to_near[: n_tp * CAP], "ep", 2)
    near_crossed = swap(to_near[n_tp * CAP :], "ep", 3)
    from_core = swap(to_core, "ep", 1)
    gate_w, up_w, down_w = gate_weight[0], up_weight[0], down_weight[0]
    *loaded, mark = call(
        load_kernel,
        [struct(w.shape, BF16) for w in (gate_w, up_w, down_w)] + [struct((8, 128), F32)],
        (combine, gate_w, up_w, down_w),
        [pltpu.SemaphoreType.DMA((3,))],
        hbm=(1, 2, 3),
    )
    mine = jnp.concatenate([arrived[order.index(d)] for d in range(4, n_ep)], axis=0)
    shares = spread(mine, n_tp)
    near_rows, far_rows = 4 * CAP, slots - 4 * CAP
    inner, gate_sum, up_sum = call(
        functools.partial(first_kernel, n_tp),
        [struct((near_rows, ff), BF16)] + [struct((far_rows, ff), F32)] * 2,
        (own, from_core, near, near_crossed, mine, *loaded[:2], mark),
        [pltpu.VMEM((4 * CAP, width), BF16)],
        flops=2 * slots * width * ff,
    )
    terms = call(
        functools.partial(expert_kernel, n_tp),
        [struct((far_rows, share), BF16)] * n_tp + [struct((near_rows, share), BF16)] * n_tp,
        (*shares, *loaded, inner, gate_sum, up_sum),
        flops=2 * slots * width * ff * 3,
    )
    terms = list(terms)
    combine, terms[0] = lax.optimization_barrier((combine, terms[0]))
    share_of = hidden
    if share % 128:
        share_of = lax.dynamic_slice_in_dim(hidden, lax.axis_index("tp") * share, share, 1)
    rows, mix, at = call(
        functools.partial(seats_kernel, n_tp, seat_cap),
        [
            struct((n_tp * seats, share), BF16),
            struct((n_tp * seats, slots), BF16),
            struct((seats, 1), F32),
        ],
        (owners[None, :], positions[None, :], combine, share_of),
        [pltpu.VMEM((tokens, share), BF16), pltpu.SemaphoreType.DMA(())],
        flops=2 * n_tp * seats * tokens * (share + slots),
        hbm=(3,),
    )
    near_pieces, rows, mix = lax.optimization_barrier((list(terms[n_tp:]), rows, mix))
    freqs = ROPE_BASE ** (-jnp.arange(half, dtype=F32) / half)
    angles = at * freqs[None, :]
    cosine, sine = jnp.cos(angles), jnp.sin(angles)

    far_terms = collect(terms[:n_tp])
    near_terms = collect(near_pieces)
    far_done = call(
        functools.partial(sum_kernel, n_tp),
        [struct((2 * CAP, share), BF16)] * (n_z - 2),
        far_terms,
    )
    far_back = [swap(far_done[d - 2], "ep", 2 * d) for d in range(2, n_z)]
    near_done = call(
        functools.partial(sum_kernel, n_tp), [struct((CAP, share), BF16)] * 4, near_terms
    )
    near_back = [near_done[0]] + [swap(near_done[d], "ep", d) for d in (1, 2, 3)]
    crossed = swap(jnp.concatenate([piece[CAP:] for piece in far_back], axis=0), "ep", 1)
    partial = call(
        functools.partial(cache_kernel, n_z, n_tp, cache_width),
        [struct((seats, wide), BF16)] * n_tp,
        (*near_back, *far_back, crossed, mix, rows, attn_gain[None, :], latent_weight.T),
        [pltpu.VMEM((slots, share), BF16)],
        flops=2 * n_tp * seats * share * (slots + cache_width),
    )
    return tuple(
        call(
            functools.partial(finish_kernel, n_tp, width, rank_width),
            [struct((seats, rank_width), BF16), struct((seats, 2 * half), BF16)],
            (*collect(partial), latent_gain[None, :], cosine, sine),
        )
    )


def solution(mesh):
    placed = (
        P(("groups", "ep"), None),
        P(),
        P(("groups", "ep"), None),
        P(("groups", "ep"), None),
        P("ep", None, "tp"),
        P("ep", None, "tp"),
        P("ep", "tp", None),
        P("tp"),
        P("tp", None),
        P(),
        P(("groups", "ep")),
        P(("groups", "ep")),
    )
    return jax.shard_map(
        on_device,
        mesh=mesh,
        in_specs=placed,
        out_specs=(P(("groups", "ep", "tp"), None), P(("groups", "ep", "tp"), None)),
        check_vma=False,
    )
```

```python
import functools

import jax
import jax.numpy as jnp
from jax import lax
from jax.experimental import pallas as pl
from jax.experimental.pallas import tpu as pltpu
from jax.sharding import PartitionSpec as P

CAP = 16
EPS = 1e-06
ROUTE_SCALE = 2.5
ROPE_BASE = 10000.0
BF16 = jnp.bfloat16
F32 = jnp.float32
VMEM_LIMIT = 40 * 1024 * 1024


def columns_of(ref, index, count, share):
    if share % 128 == 0:
        return ref[:, pl.ds(pl.multiple_of(index * share, 128), share)]
    out = ref[:, 0:share]
    for q in range(1, count):
        out = jnp.where(index == q, ref[:, q * share : (q + 1) * share], out)
    return out


def dispatch_kernel(n_ep, n_tp, routes_hbm, logits_hbm, hidden_hbm, gain_hbm, *refs):
    own_ref, core_ref, near_ref = refs[:3]
    outs, combine_ref = refs[3 : n_ep - 1], refs[n_ep - 1]
    routes_ref, logits_ref, hidden_ref, gain_ref, pick_ref, head_ref, sems = refs[n_ep:]
    me = lax.axis_index("ep")
    part = lax.axis_index("tp")
    tokens, width = hidden_ref.shape
    share = width // n_tp
    step = 512 if width % 512 == 0 else width
    starts = range(0, width, step)
    small = [
        pltpu.make_async_copy(routes_hbm, routes_ref, sems.at[0]),
        pltpu.make_async_copy(logits_hbm, logits_ref, sems.at[1]),
        pltpu.make_async_copy(gain_hbm, gain_ref.at[0], sems.at[2]),
    ]
    large = [
        pltpu.make_async_copy(
            hidden_hbm.at[:, c : c + step], hidden_ref.at[:, c : c + step], sems.at[3 + i]
        )
        for i, c in enumerate(starts)
    ]
    for copy in small + large:
        copy.start()
    small[0].wait()
    small[1].wait()
    routes = routes_ref[...]
    affinity = jax.nn.sigmoid(logits_ref[...])
    weight = ROUTE_SCALE * affinity / jnp.sum(affinity, axis=0, keepdims=True)
    weight = weight.astype(BF16).astype(F32)
    expert = lax.broadcasted_iota(jnp.int32, (n_ep, tokens), 0) ^ me
    hit = jnp.zeros((n_ep, tokens), F32)
    gain_of = jnp.zeros((n_ep, tokens), F32)
    for k in range(routes.shape[0]):
        same = routes[k : k + 1, :] == expert
        hit = jnp.where(same, 1.0, hit)
        gain_of = jnp.where(same, weight[k : k + 1, :], gain_of)
    earlier = lax.broadcasted_iota(jnp.int32, (tokens, tokens), 0) < lax.broadcasted_iota(
        jnp.int32, (tokens, tokens), 1
    )
    rank = jnp.dot(hit.astype(BF16), earlier.astype(F32).astype(BF16), preferred_element_type=F32)
    rank = jnp.where(hit > 0, rank, -1.0)
    place = lax.broadcasted_iota(jnp.int32, (CAP, tokens), 0).astype(F32)
    for d in range(n_ep):
        match = rank[d : d + 1, :] == place
        rows = slice(d * CAP, (d + 1) * CAP)
        pick_ref[rows, :] = jnp.where(match, 1.0, 0.0).astype(BF16)
        combine_ref[rows, :] = jnp.where(match, gain_of[d : d + 1, :], 0.0).astype(BF16)
    pick = pick_ref[...]
    head = 4 * CAP
    square = jnp.zeros((n_ep * CAP, 1), F32)
    middle = len(large) // 2
    for i, c in enumerate(starts):
        if i == 0 or i == middle:
            for copy in large[:middle] if i < middle else large[i:]:
                copy.wait()
        got = jnp.dot(pick, hidden_ref[:, c : c + step], preferred_element_type=F32)
        square = square + jnp.sum(got * got, axis=1, keepdims=True)
        head_ref[:, c : c + step] = got[:head]
    small[2].wait()
    scale = lax.rsqrt(square / width + EPS)
    got = jnp.dot(pick[head:], columns_of(hidden_ref, part, n_tp, share), preferred_element_type=F32)
    rest = (got * scale[head:] * columns_of(gain_ref, part, n_tp, share)).astype(BF16)
    at = 0
    for out in outs:
        out[...] = rest[at : at + out.shape[0]]
        at += out.shape[0]
    whole = (head_ref[...] * scale[:head] * gain_ref[...]).astype(BF16)
    own_ref[...] = whole[:CAP]
    for q in range(n_tp):
        columns = slice(q * share, (q + 1) * share)
        core_ref[q * CAP : (q + 1) * CAP, :] = whole[CAP : 2 * CAP, columns]
        near_ref[q * CAP : (q + 1) * CAP, :] = whole[2 * CAP : 3 * CAP, columns]
        near_ref[(n_tp + q) * CAP : (n_tp + q + 1) * CAP, :] = whole[3 * CAP :, columns]


def load_kernel(after_ref, *refs):
    count = (len(refs) - 2) // 2
    mark_ref, sems = refs[-2:]
    copies = [
        pltpu.make_async_copy(refs[i], refs[count + i], sems.at[i]) for i in range(count)
    ]
    for copy in copies:
        copy.start()
    mark_ref[...] = jnp.zeros(mark_ref.shape, F32)
    for copy in copies:
        copy.wait()


def first_kernel(
    n_tp,
    own_ref,
    core_ref,
    near_ref,
    cross_ref,
    mine_ref,
    gate_ref,
    up_ref,
    mark_ref,
    inner_ref,
    gate_sum_ref,
    up_sum_ref,
    head_ref,
):
    part = lax.axis_index("tp")
    share = mine_ref.shape[1]
    head_ref[:CAP, :] = own_ref[...]
    for i, ref in enumerate((core_ref, near_ref, cross_ref)):
        for q in range(n_tp):
            rows = slice((i + 1) * CAP, (i + 2) * CAP)
            head_ref[rows, q * share : (q + 1) * share] = ref[q * CAP : (q + 1) * CAP, :]
    depth = pl.ds(pl.multiple_of(part * share, CAP), share)
    gate, upper = (
        jnp.dot(head_ref[...], ref[...], preferred_element_type=F32) for ref in (gate_ref, up_ref)
    )
    for weight_ref, sum_ref in zip((gate_ref, up_ref), (gate_sum_ref, up_sum_ref)):
        sum_ref[...] = jnp.dot(mine_ref[...], weight_ref[depth, :], preferred_element_type=F32)
    inner_ref[...] = (gate / (1.0 + jnp.exp(-gate)) * upper).astype(BF16)


def expert_kernel(n_tp, *refs):
    rows = refs[: n_tp - 1]
    gate_ref, up_ref, down_ref, near_ref, gate_sum_ref, up_sum_ref = refs[n_tp - 1 : n_tp + 5]
    far_outs = refs[n_tp + 5 : 2 * n_tp + 5]
    near_outs = refs[2 * n_tp + 5 :]
    part = lax.axis_index("tp")
    share = rows[0].shape[1]
    gate = gate_sum_ref[...]
    upper = up_sum_ref[...]
    for d in range(1, n_tp):
        value = rows[n_tp - 1 - d][...]
        depth = pl.ds(pl.multiple_of((part ^ d) * share, CAP), share)
        gate = gate + jnp.dot(value, gate_ref[depth, :], preferred_element_type=F32)
        upper = upper + jnp.dot(value, up_ref[depth, :], preferred_element_type=F32)
    far = (gate / (1.0 + jnp.exp(-gate)) * upper).astype(BF16)
    count = far.shape[0]
    groups = [
        far[start : start + CAP]
        for at in range(0, count // 2, CAP)
        for start in (at, count // 2 + at)
    ]
    inner = jnp.concatenate([*groups, near_ref[...]], axis=0)
    for d in range(n_tp):
        down = columns_of(down_ref, part ^ d, n_tp, share)
        out = jnp.dot(inner, down, preferred_element_type=F32).astype(BF16)
        far_outs[d][...] = out[:count]
        near_outs[d][...] = out[count:]


def sum_kernel(n_tp, *refs):
    parts, outs = refs[:n_tp], refs[n_tp:]
    at = 0
    for out in outs:
        rows = slice(at, at + out.shape[0])
        total = parts[0][rows, :].astype(F32)
        for other in parts[1:]:
            total = total + other[rows, :].astype(F32)
        out[...] = total.astype(BF16)
        at += out.shape[0]


def seats_kernel(
    n_tp,
    seat_cap,
    owners_ref,
    positions_ref,
    combine_ref,
    hidden_hbm,
    rows_ref,
    mix_ref,
    at_ref,
    hidden_ref,
    sem,
):
    part = lax.axis_index("tp")
    tokens, share = hidden_ref.shape
    if hidden_hbm.shape[1] != share:
        hidden_hbm = hidden_hbm.at[:, pl.ds(pl.multiple_of(part * share, 128), share)]
    copy = pltpu.make_async_copy(hidden_hbm, hidden_ref, sem)
    copy.start()
    source_rows = tokens // n_tp
    owners = owners_ref[...] ^ part
    owner = lax.broadcasted_iota(jnp.int32, (n_tp, tokens), 0)
    hot = jnp.where(owners == owner, 1.0, 0.0)
    first = lax.broadcasted_iota(jnp.int32, (tokens, tokens), 0)
    second = lax.broadcasted_iota(jnp.int32, (tokens, tokens), 1)
    earlier = jnp.where((first < second) & (first // source_rows == second // source_rows), 1.0, 0.0)
    before = jnp.dot(hot.astype(BF16), earlier.astype(BF16), preferred_element_type=F32)
    seat = jnp.sum(before * hot, axis=0, keepdims=True).astype(jnp.int32)
    source = lax.broadcasted_iota(jnp.int32, (1, tokens), 1) // source_rows
    code = owners * (n_tp * seat_cap) + source * seat_cap + seat
    seats = n_tp * seat_cap
    held = lax.broadcasted_iota(jnp.int32, (n_tp * seats, tokens), 0) == code
    pick = jnp.where(held, 1.0, 0.0).astype(BF16)
    mix_ref[...] = lax.dot_general(
        pick, combine_ref[...], (((1,), (1,)), ((), ())), preferred_element_type=F32
    ).astype(BF16)
    place = jnp.where(held[:seats], positions_ref[...].astype(F32), 0.0)
    at_ref[...] = jnp.sum(place, axis=1, keepdims=True)
    copy.wait()
    rows_ref[...] = jnp.dot(pick, hidden_ref[...], preferred_element_type=F32).astype(BF16)


def cache_kernel(n_z, n_tp, cache_width, *refs):
    near, far, core_ref = refs[:4], refs[4 : n_z + 2], refs[n_z + 2]
    mix_ref, rows_ref, gain_ref, weight_ref = refs[n_z + 3 : n_z + 7]
    outs, back_ref = refs[n_z + 7 : n_z + 7 + n_tp], refs[n_z + 7 + n_tp]
    for d in range(4):
        back_ref[d * CAP : (d + 1) * CAP, :] = near[d][...]
    for d in range(n_z - 2):
        at = (2 * d + 4) * CAP
        back_ref[at : at + CAP, :] = far[d][:CAP, :]
        back_ref[at + CAP : at + 2 * CAP, :] = core_ref[d * CAP : (d + 1) * CAP, :]
    mixed = jnp.dot(mix_ref[...], back_ref[...], preferred_element_type=F32)
    state = rows_ref[...].astype(F32) + mixed
    square = jnp.sum(state * state, axis=1, keepdims=True)
    scaled = (state * gain_ref[...]).astype(BF16)
    value = lax.dot_general(
        scaled, weight_ref[...], (((1,), (1,)), ((), ())), preferred_element_type=F32
    ).astype(BF16)
    high = square.astype(BF16).astype(F32)
    rest = square - high
    middle = rest.astype(BF16).astype(F32)
    low = rest - middle
    seats, wide = outs[0].shape
    lane = lax.broadcasted_iota(jnp.int32, (square.shape[0], wide - cache_width), 1)
    extra = jnp.where(lane == 0, high, jnp.where(lane == 1, middle, jnp.where(lane == 2, low, 0.0)))
    extra = extra.astype(BF16)
    for d in range(n_tp):
        outs[d][:, :cache_width] = value[d * seats : (d + 1) * seats]
        outs[d][:, cache_width:] = extra[d * seats : (d + 1) * seats]


def finish_kernel(n_tp, width, rank_width, *refs):
    parts = refs[:n_tp]
    gain_ref, cos_ref, sin_ref, latent_ref, rotary_ref = refs[n_tp:]
    total = parts[0][...].astype(F32)
    for other in parts[1:]:
        total = total + other[...].astype(F32)
    half = cos_ref.shape[1]
    cache_width = rank_width + 2 * half
    square = jnp.sum(total[:, cache_width : cache_width + 3], axis=1, keepdims=True)
    cache = total[:, :cache_width] * lax.rsqrt(square / width + EPS)
    latent = cache[:, :rank_width]
    scale = lax.rsqrt(jnp.mean(latent * latent, axis=1, keepdims=True) + EPS)
    latent_ref[...] = (latent * scale * gain_ref[...]).astype(BF16)
    first = cache[:, rank_width : rank_width + half]
    second = cache[:, rank_width + half :]
    cosine, sine = cos_ref[...], sin_ref[...]
    rotary_ref[:, :half] = (first * cosine - second * sine).astype(BF16)
    rotary_ref[:, half:] = (second * cosine + first * sine).astype(BF16)


def call(kernel, out_shape, args, scratch=(), flops=0, hbm=()):
    moved = sum(a.size * a.dtype.itemsize for a in args)
    vmem = pl.BlockSpec(memory_space=pltpu.VMEM)
    args = [
        pltpu.with_memory_space_constraint(a, pltpu.HBM) if i in hbm else a
        for i, a in enumerate(args)
    ]
    return pl.pallas_call(
        kernel,
        out_shape=out_shape,
        in_specs=[
            pl.BlockSpec(memory_space=pltpu.HBM) if i in hbm else vmem for i in range(len(args))
        ],
        out_specs=[vmem] * len(out_shape),
        scratch_shapes=list(scratch),
        compiler_params=pltpu.CompilerParams(vmem_limit_bytes=VMEM_LIMIT),
        cost_estimate=pl.CostEstimate(flops=flops, bytes_accessed=moved, transcendentals=0),
    )(*args)


def swap(value, axis, d):
    return lax.ppermute(value, axis, [(i, i ^ d) for i in range(lax.axis_size(axis))])


def spread(value, n_tp):
    return [swap(value, "tp", d) for d in reversed(range(1, n_tp))]


def collect(values):
    return [swap(values[d], "tp", d) for d in reversed(range(1, len(values)))] + [values[0]]


def on_device(
    hidden,
    moe_gain,
    route_logits,
    routes,
    gate_weight,
    up_weight,
    down_weight,
    attn_gain,
    latent_weight,
    latent_gain,
    positions,
    owners,
):
    n_ep = lax.axis_size("ep")
    n_tp = lax.axis_size("tp")
    n_z = n_ep // 2
    tokens, width = hidden.shape
    share = width // n_tp
    ff = gate_weight.shape[2]
    slots = n_ep * CAP
    seat_cap = max(2, tokens // n_tp // 4)
    seats = n_tp * seat_cap
    rank_width = latent_gain.shape[0]
    cache_width = latent_weight.shape[1]
    half = (cache_width - rank_width) // 2
    wide = (cache_width + 3 + 127) // 128 * 128
    struct = jax.ShapeDtypeStruct
    chunks = width // 512 if width % 512 == 0 else 1

    own, to_core, to_near, *outgoing, combine = call(
        functools.partial(dispatch_kernel, n_ep, n_tp),
        [struct((CAP, width), BF16), struct((n_tp * CAP, share), BF16)]
        + [struct((2 * n_tp * CAP, share), BF16)]
        + [struct((CAP, share), BF16)] * (n_ep - 4)
        + [struct((slots, tokens), BF16)],
        (routes.T, route_logits.T, hidden, moe_gain),
        [
            pltpu.VMEM(routes.T.shape, jnp.int32),
            pltpu.VMEM(routes.T.shape, F32),
            pltpu.VMEM(hidden.shape, BF16),
            pltpu.VMEM((1, width), F32),
            pltpu.VMEM((slots, tokens), BF16),
            pltpu.VMEM((4 * CAP, width), F32),
            pltpu.SemaphoreType.DMA((3 + chunks,)),
        ],
        flops=4 * slots * tokens * width,
        hbm=(0, 1, 2, 3),
    )
    order = [*range(4, n_ep, 2), *range(5, n_ep, 2)]
    arrived = [swap(outgoing[d - 4], "ep", d) for d in order]
    near = swap(to_near[: n_tp * CAP], "ep", 2)
    near_crossed = swap(to_near[n_tp * CAP :], "ep", 3)
    from_core = swap(to_core, "ep", 1)
    gate_w, up_w, down_w = gate_weight[0], up_weight[0], down_weight[0]
    *loaded, mark = call(
        load_kernel,
        [struct(w.shape, BF16) for w in (gate_w, up_w, down_w)] + [struct((8, 128), F32)],
        (combine, gate_w, up_w, down_w),
        [pltpu.SemaphoreType.DMA((3,))],
        hbm=(1, 2, 3),
    )
    mine = jnp.concatenate(arrived, axis=0)
    shares = spread(mine, n_tp)
    near_rows, far_rows = 4 * CAP, slots - 4 * CAP
    inner, gate_sum, up_sum = call(
        functools.partial(first_kernel, n_tp),
        [struct((near_rows, ff), BF16)] + [struct((far_rows, ff), F32)] * 2,
        (own, from_core, near, near_crossed, mine, *loaded[:2], mark),
        [pltpu.VMEM((4 * CAP, width), BF16)],
        flops=2 * slots * width * ff,
    )
    terms = call(
        functools.partial(expert_kernel, n_tp),
        [struct((far_rows, share), BF16)] * n_tp + [struct((near_rows, share), BF16)] * n_tp,
        (*shares, *loaded, inner, gate_sum, up_sum),
        flops=2 * slots * width * ff * 3,
    )
    terms = list(terms)
    combine, terms[0] = lax.optimization_barrier((combine, terms[0]))
    share_of = hidden
    if share % 128:
        share_of = lax.dynamic_slice_in_dim(hidden, lax.axis_index("tp") * share, share, 1)
    rows, mix, at = call(
        functools.partial(seats_kernel, n_tp, seat_cap),
        [
            struct((n_tp * seats, share), BF16),
            struct((n_tp * seats, slots), BF16),
            struct((seats, 1), F32),
        ],
        (owners[None, :], positions[None, :], combine, share_of),
        [pltpu.VMEM((tokens, share), BF16), pltpu.SemaphoreType.DMA(())],
        flops=2 * n_tp * seats * tokens * (share + slots),
        hbm=(3,),
    )
    near_pieces, rows, mix = lax.optimization_barrier((list(terms[n_tp:]), rows, mix))
    freqs = ROPE_BASE ** (-jnp.arange(half, dtype=F32) / half)
    angles = at * freqs[None, :]
    cosine, sine = jnp.cos(angles), jnp.sin(angles)

    far_terms = collect(terms[:n_tp])
    near_terms = collect(near_pieces)
    far_done = call(
        functools.partial(sum_kernel, n_tp),
        [struct((2 * CAP, share), BF16)] * (n_z - 2),
        far_terms,
    )
    far_back = [swap(far_done[d - 2], "ep", 2 * d) for d in range(2, n_z)]
    near_done = call(
        functools.partial(sum_kernel, n_tp), [struct((CAP, share), BF16)] * 4, near_terms
    )
    near_back = [near_done[0]] + [swap(near_done[d], "ep", d) for d in (1, 2, 3)]
    crossed = swap(jnp.concatenate([piece[CAP:] for piece in far_back], axis=0), "ep", 1)
    partial = call(
        functools.partial(cache_kernel, n_z, n_tp, cache_width),
        [struct((seats, wide), BF16)] * n_tp,
        (*near_back, *far_back, crossed, mix, rows, attn_gain[None, :], latent_weight.T),
        [pltpu.VMEM((slots, share), BF16)],
        flops=2 * n_tp * seats * share * (slots + cache_width),
    )
    return tuple(
        call(
            functools.partial(finish_kernel, n_tp, width, rank_width),
            [struct((seats, rank_width), BF16), struct((seats, 2 * half), BF16)],
            (*collect(partial), latent_gain[None, :], cosine, sine),
        )
    )


def solution(mesh):
    placed = (
        P(("groups", "ep"), None),
        P(),
        P(("groups", "ep"), None),
        P(("groups", "ep"), None),
        P("ep", None, "tp"),
        P("ep", None, "tp"),
        P("ep", "tp", None),
        P("tp"),
        P("tp", None),
        P(),
        P(("groups", "ep")),
        P(("groups", "ep")),
    )
    return jax.shard_map(
        on_device,
        mesh=mesh,
        in_specs=placed,
        out_specs=(P(("groups", "ep", "tp"), None), P(("groups", "ep", "tp"), None)),
        check_vma=False,
    )
```

```python
import functools

import jax
import jax.numpy as jnp
from jax import lax
from jax.experimental import pallas as pl
from jax.experimental.pallas import tpu as pltpu
from jax.sharding import PartitionSpec as P

CAP = 16
EPS = 1e-06
ROUTE_SCALE = 2.5
ROPE_BASE = 10000.0
BF16 = jnp.bfloat16
F32 = jnp.float32
VMEM_LIMIT = 40 * 1024 * 1024


def columns_of(ref, index, count, share):
    if share % 128 == 0:
        return ref[:, pl.ds(pl.multiple_of(index * share, 128), share)]
    out = ref[:, 0:share]
    for q in range(1, count):
        out = jnp.where(index == q, ref[:, q * share : (q + 1) * share], out)
    return out


def dispatch_kernel(n_ep, n_tp, routes_hbm, logits_hbm, hidden_hbm, gain_hbm, *refs):
    own_ref, core_ref, near_ref = refs[:3]
    outs, combine_ref = refs[3 : n_ep - 1], refs[n_ep - 1]
    routes_ref, logits_ref, hidden_ref, gain_ref, pick_ref, head_ref, sems = refs[n_ep:]
    me = lax.axis_index("ep")
    part = lax.axis_index("tp")
    tokens, width = hidden_ref.shape
    share = width // n_tp
    step = 512 if width % 512 == 0 else width
    starts = range(0, width, step)
    small = [
        pltpu.make_async_copy(routes_hbm, routes_ref, sems.at[0]),
        pltpu.make_async_copy(logits_hbm, logits_ref, sems.at[1]),
        pltpu.make_async_copy(gain_hbm, gain_ref.at[0], sems.at[2]),
    ]
    large = [
        pltpu.make_async_copy(
            hidden_hbm.at[:, c : c + step], hidden_ref.at[:, c : c + step], sems.at[3 + i]
        )
        for i, c in enumerate(starts)
    ]
    for copy in small + large:
        copy.start()
    small[0].wait()
    small[1].wait()
    routes = routes_ref[...]
    affinity = jax.nn.sigmoid(logits_ref[...])
    weight = ROUTE_SCALE * affinity / jnp.sum(affinity, axis=0, keepdims=True)
    weight = weight.astype(BF16).astype(F32)
    expert = lax.broadcasted_iota(jnp.int32, (n_ep, tokens), 0) ^ me
    hit = jnp.zeros((n_ep, tokens), F32)
    gain_of = jnp.zeros((n_ep, tokens), F32)
    for k in range(routes.shape[0]):
        same = routes[k : k + 1, :] == expert
        hit = jnp.where(same, 1.0, hit)
        gain_of = jnp.where(same, weight[k : k + 1, :], gain_of)
    earlier = lax.broadcasted_iota(jnp.int32, (tokens, tokens), 0) < lax.broadcasted_iota(
        jnp.int32, (tokens, tokens), 1
    )
    rank = jnp.dot(hit.astype(BF16), earlier.astype(F32).astype(BF16), preferred_element_type=F32)
    rank = jnp.where(hit > 0, rank, -1.0)
    place = lax.broadcasted_iota(jnp.int32, (CAP, tokens), 0).astype(F32)
    for d in range(n_ep):
        match = rank[d : d + 1, :] == place
        rows = slice(d * CAP, (d + 1) * CAP)
        pick_ref[rows, :] = jnp.where(match, 1.0, 0.0).astype(BF16)
        combine_ref[rows, :] = jnp.where(match, gain_of[d : d + 1, :], 0.0).astype(BF16)
    pick = pick_ref[...]
    head = 4 * CAP
    square = jnp.zeros((n_ep * CAP, 1), F32)
    middle = len(large) // 2
    for i, c in enumerate(starts):
        if i == 0 or i == middle:
            for copy in large[:middle] if i < middle else large[i:]:
                copy.wait()
        got = jnp.dot(pick, hidden_ref[:, c : c + step], preferred_element_type=F32)
        square = square + jnp.sum(got * got, axis=1, keepdims=True)
        head_ref[:, c : c + step] = got[:head]
    small[2].wait()
    scale = lax.rsqrt(square / width + EPS)
    got = jnp.dot(pick[head:], columns_of(hidden_ref, part, n_tp, share), preferred_element_type=F32)
    rest = (got * scale[head:] * columns_of(gain_ref, part, n_tp, share)).astype(BF16)
    at = 0
    for out in outs:
        out[...] = rest[at : at + out.shape[0]]
        at += out.shape[0]
    whole = (head_ref[...] * scale[:head] * gain_ref[...]).astype(BF16)
    own_ref[...] = whole[:CAP]
    for q in range(n_tp):
        columns = slice(q * share, (q + 1) * share)
        core_ref[q * CAP : (q + 1) * CAP, :] = whole[CAP : 2 * CAP, columns]
        near_ref[q * CAP : (q + 1) * CAP, :] = whole[2 * CAP : 3 * CAP, columns]
        near_ref[(n_tp + q) * CAP : (n_tp + q + 1) * CAP, :] = whole[3 * CAP :, columns]


def load_kernel(after_ref, *refs):
    count = (len(refs) - 2) // 2
    mark_ref, sems = refs[-2:]
    copies = [
        pltpu.make_async_copy(refs[i], refs[count + i], sems.at[i]) for i in range(count)
    ]
    for copy in copies:
        copy.start()
    mark_ref[...] = jnp.zeros(mark_ref.shape, F32)
    for copy in copies:
        copy.wait()


def first_kernel(n_tp, own_ref, core_ref, near_ref, cross_ref, mine_ref, *refs):
    gate_ref, up_ref, down_ref, _ = refs[:4]
    outs, (gate_sum_ref, up_sum_ref, head_ref) = refs[4 : n_tp + 4], refs[n_tp + 4 :]
    part = lax.axis_index("tp")
    share = mine_ref.shape[1]
    head_ref[:CAP, :] = own_ref[...]
    for i, ref in enumerate((core_ref, near_ref, cross_ref)):
        for q in range(n_tp):
            rows = slice((i + 1) * CAP, (i + 2) * CAP)
            head_ref[rows, q * share : (q + 1) * share] = ref[q * CAP : (q + 1) * CAP, :]
    depth = pl.ds(pl.multiple_of(part * share, CAP), share)
    gate, upper = (
        jnp.dot(head_ref[...], ref[...], preferred_element_type=F32) for ref in (gate_ref, up_ref)
    )
    for weight_ref, sum_ref in zip((gate_ref, up_ref), (gate_sum_ref, up_sum_ref)):
        sum_ref[...] = jnp.dot(mine_ref[...], weight_ref[depth, :], preferred_element_type=F32)
    inner = (gate / (1.0 + jnp.exp(-gate)) * upper).astype(BF16)
    for d in range(n_tp):
        down = columns_of(down_ref, part ^ d, n_tp, share)
        outs[d][...] = jnp.dot(inner, down, preferred_element_type=F32).astype(BF16)


def expert_kernel(n_tp, *refs):
    rows = refs[: n_tp - 1]
    gate_ref, up_ref, down_ref, gate_sum_ref, up_sum_ref = refs[n_tp - 1 : n_tp + 4]
    outs = refs[n_tp + 4 :]
    part = lax.axis_index("tp")
    share = rows[0].shape[1]
    gate = gate_sum_ref[...]
    upper = up_sum_ref[...]
    for d in range(1, n_tp):
        value = rows[n_tp - 1 - d][...]
        depth = pl.ds(pl.multiple_of((part ^ d) * share, CAP), share)
        gate = gate + jnp.dot(value, gate_ref[depth, :], preferred_element_type=F32)
        upper = upper + jnp.dot(value, up_ref[depth, :], preferred_element_type=F32)
    far = (gate / (1.0 + jnp.exp(-gate)) * upper).astype(BF16)
    count = far.shape[0]
    groups = [
        far[start : start + CAP]
        for at in range(0, count // 2, CAP)
        for start in (at, count // 2 + at)
    ]
    inner = jnp.concatenate(groups, axis=0)
    for d in range(n_tp):
        down = columns_of(down_ref, part ^ d, n_tp, share)
        outs[d][...] = jnp.dot(inner, down, preferred_element_type=F32).astype(BF16)


def sum_kernel(n_tp, *refs):
    parts, outs = refs[:n_tp], refs[n_tp:]
    at = 0
    for out in outs:
        rows = slice(at, at + out.shape[0])
        total = parts[0][rows, :].astype(F32)
        for other in parts[1:]:
            total = total + other[rows, :].astype(F32)
        out[...] = total.astype(BF16)
        at += out.shape[0]


def seats_kernel(
    n_tp,
    seat_cap,
    owners_ref,
    positions_ref,
    combine_ref,
    hidden_hbm,
    rows_ref,
    mix_ref,
    at_ref,
    hidden_ref,
    sem,
):
    part = lax.axis_index("tp")
    tokens, share = hidden_ref.shape
    if hidden_hbm.shape[1] != share:
        hidden_hbm = hidden_hbm.at[:, pl.ds(pl.multiple_of(part * share, 128), share)]
    copy = pltpu.make_async_copy(hidden_hbm, hidden_ref, sem)
    copy.start()
    source_rows = tokens // n_tp
    owners = owners_ref[...] ^ part
    owner = lax.broadcasted_iota(jnp.int32, (n_tp, tokens), 0)
    hot = jnp.where(owners == owner, 1.0, 0.0)
    first = lax.broadcasted_iota(jnp.int32, (tokens, tokens), 0)
    second = lax.broadcasted_iota(jnp.int32, (tokens, tokens), 1)
    earlier = jnp.where((first < second) & (first // source_rows == second // source_rows), 1.0, 0.0)
    before = jnp.dot(hot.astype(BF16), earlier.astype(BF16), preferred_element_type=F32)
    seat = jnp.sum(before * hot, axis=0, keepdims=True).astype(jnp.int32)
    source = lax.broadcasted_iota(jnp.int32, (1, tokens), 1) // source_rows
    code = owners * (n_tp * seat_cap) + source * seat_cap + seat
    seats = n_tp * seat_cap
    held = lax.broadcasted_iota(jnp.int32, (n_tp * seats, tokens), 0) == code
    pick = jnp.where(held, 1.0, 0.0).astype(BF16)
    mix_ref[...] = lax.dot_general(
        pick, combine_ref[...], (((1,), (1,)), ((), ())), preferred_element_type=F32
    ).astype(BF16)
    place = jnp.where(held[:seats], positions_ref[...].astype(F32), 0.0)
    at_ref[...] = jnp.sum(place, axis=1, keepdims=True)
    copy.wait()
    rows_ref[...] = jnp.dot(pick, hidden_ref[...], preferred_element_type=F32).astype(BF16)


def cache_kernel(n_z, n_tp, cache_width, *refs):
    near, far, core_ref = refs[:4], refs[4 : n_z + 2], refs[n_z + 2]
    mix_ref, rows_ref, gain_ref, weight_ref = refs[n_z + 3 : n_z + 7]
    outs, back_ref = refs[n_z + 7 : n_z + 7 + n_tp], refs[n_z + 7 + n_tp]
    for d in range(4):
        back_ref[d * CAP : (d + 1) * CAP, :] = near[d][...]
    for d in range(n_z - 2):
        at = (2 * d + 4) * CAP
        back_ref[at : at + CAP, :] = far[d][:CAP, :]
        back_ref[at + CAP : at + 2 * CAP, :] = core_ref[d * CAP : (d + 1) * CAP, :]
    mixed = jnp.dot(mix_ref[...], back_ref[...], preferred_element_type=F32)
    state = rows_ref[...].astype(F32) + mixed
    square = jnp.sum(state * state, axis=1, keepdims=True)
    scaled = (state * gain_ref[...]).astype(BF16)
    value = lax.dot_general(
        scaled, weight_ref[...], (((1,), (1,)), ((), ())), preferred_element_type=F32
    ).astype(BF16)
    high = square.astype(BF16).astype(F32)
    rest = square - high
    middle = rest.astype(BF16).astype(F32)
    low = rest - middle
    seats, wide = outs[0].shape
    lane = lax.broadcasted_iota(jnp.int32, (square.shape[0], wide - cache_width), 1)
    extra = jnp.where(lane == 0, high, jnp.where(lane == 1, middle, jnp.where(lane == 2, low, 0.0)))
    extra = extra.astype(BF16)
    for d in range(n_tp):
        outs[d][:, :cache_width] = value[d * seats : (d + 1) * seats]
        outs[d][:, cache_width:] = extra[d * seats : (d + 1) * seats]


def finish_kernel(n_tp, width, rank_width, *refs):
    parts = refs[:n_tp]
    gain_ref, cos_ref, sin_ref, latent_ref, rotary_ref = refs[n_tp:]
    total = parts[0][...].astype(F32)
    for other in parts[1:]:
        total = total + other[...].astype(F32)
    half = cos_ref.shape[1]
    cache_width = rank_width + 2 * half
    square = jnp.sum(total[:, cache_width : cache_width + 3], axis=1, keepdims=True)
    cache = total[:, :cache_width] * lax.rsqrt(square / width + EPS)
    latent = cache[:, :rank_width]
    scale = lax.rsqrt(jnp.mean(latent * latent, axis=1, keepdims=True) + EPS)
    latent_ref[...] = (latent * scale * gain_ref[...]).astype(BF16)
    first = cache[:, rank_width : rank_width + half]
    second = cache[:, rank_width + half :]
    cosine, sine = cos_ref[...], sin_ref[...]
    rotary_ref[:, :half] = (first * cosine - second * sine).astype(BF16)
    rotary_ref[:, half:] = (second * cosine + first * sine).astype(BF16)


def call(kernel, out_shape, args, scratch=(), flops=0, hbm=()):
    moved = sum(a.size * a.dtype.itemsize for a in args)
    vmem = pl.BlockSpec(memory_space=pltpu.VMEM)
    args = [
        pltpu.with_memory_space_constraint(a, pltpu.HBM) if i in hbm else a
        for i, a in enumerate(args)
    ]
    return pl.pallas_call(
        kernel,
        out_shape=out_shape,
        in_specs=[
            pl.BlockSpec(memory_space=pltpu.HBM) if i in hbm else vmem for i in range(len(args))
        ],
        out_specs=[vmem] * len(out_shape),
        scratch_shapes=list(scratch),
        compiler_params=pltpu.CompilerParams(vmem_limit_bytes=VMEM_LIMIT),
        cost_estimate=pl.CostEstimate(flops=flops, bytes_accessed=moved, transcendentals=0),
    )(*args)


def swap(value, axis, d):
    return lax.ppermute(value, axis, [(i, i ^ d) for i in range(lax.axis_size(axis))])


def spread(value, n_tp):
    return [swap(value, "tp", d) for d in reversed(range(1, n_tp))]


def collect(values):
    return [swap(values[d], "tp", d) for d in reversed(range(1, len(values)))] + [values[0]]


def on_device(
    hidden,
    moe_gain,
    route_logits,
    routes,
    gate_weight,
    up_weight,
    down_weight,
    attn_gain,
    latent_weight,
    latent_gain,
    positions,
    owners,
):
    n_ep = lax.axis_size("ep")
    n_tp = lax.axis_size("tp")
    n_z = n_ep // 2
    tokens, width = hidden.shape
    share = width // n_tp
    ff = gate_weight.shape[2]
    slots = n_ep * CAP
    seat_cap = max(2, tokens // n_tp // 4)
    seats = n_tp * seat_cap
    rank_width = latent_gain.shape[0]
    cache_width = latent_weight.shape[1]
    half = (cache_width - rank_width) // 2
    wide = (cache_width + 3 + 127) // 128 * 128
    struct = jax.ShapeDtypeStruct
    chunks = width // 512 if width % 512 == 0 else 1

    own, to_core, to_near, *outgoing, combine = call(
        functools.partial(dispatch_kernel, n_ep, n_tp),
        [struct((CAP, width), BF16), struct((n_tp * CAP, share), BF16)]
        + [struct((2 * n_tp * CAP, share), BF16)]
        + [struct((CAP, share), BF16)] * (n_ep - 4)
        + [struct((slots, tokens), BF16)],
        (routes.T, route_logits.T, hidden, moe_gain),
        [
            pltpu.VMEM(routes.T.shape, jnp.int32),
            pltpu.VMEM(routes.T.shape, F32),
            pltpu.VMEM(hidden.shape, BF16),
            pltpu.VMEM((1, width), F32),
            pltpu.VMEM((slots, tokens), BF16),
            pltpu.VMEM((4 * CAP, width), F32),
            pltpu.SemaphoreType.DMA((3 + chunks,)),
        ],
        flops=4 * slots * tokens * width,
        hbm=(0, 1, 2, 3),
    )
    order = [*range(4, n_ep, 2), *range(5, n_ep, 2)]
    arrived = [swap(outgoing[d - 4], "ep", d) for d in order]
    near = swap(to_near[: n_tp * CAP], "ep", 2)
    near_crossed = swap(to_near[n_tp * CAP :], "ep", 3)
    from_core = swap(to_core, "ep", 1)
    gate_w, up_w, down_w = gate_weight[0], up_weight[0], down_weight[0]
    *loaded, mark = call(
        load_kernel,
        [struct(w.shape, BF16) for w in (gate_w, up_w, down_w)] + [struct((8, 128), F32)],
        (combine, gate_w, up_w, down_w),
        [pltpu.SemaphoreType.DMA((3,))],
        hbm=(1, 2, 3),
    )
    arrived, from_core = lax.optimization_barrier((arrived, from_core))
    mine = jnp.concatenate(arrived, axis=0)
    shares = spread(mine, n_tp)
    near_rows, far_rows = 4 * CAP, slots - 4 * CAP
    *near_pieces, gate_sum, up_sum = call(
        functools.partial(first_kernel, n_tp),
        [struct((near_rows, share), BF16)] * n_tp + [struct((far_rows, ff), F32)] * 2,
        (own, from_core, near, near_crossed, mine, *loaded, mark),
        [pltpu.VMEM((4 * CAP, width), BF16)],
        flops=2 * slots * width * ff,
    )
    terms = call(
        functools.partial(expert_kernel, n_tp),
        [struct((far_rows, share), BF16)] * n_tp,
        (*shares, *loaded, gate_sum, up_sum),
        flops=2 * slots * width * ff * 3,
    )
    terms = list(terms)
    combine, terms[0] = lax.optimization_barrier((combine, terms[0]))
    share_of = hidden
    if share % 128:
        share_of = lax.dynamic_slice_in_dim(hidden, lax.axis_index("tp") * share, share, 1)
    rows, mix, at = call(
        functools.partial(seats_kernel, n_tp, seat_cap),
        [
            struct((n_tp * seats, share), BF16),
            struct((n_tp * seats, slots), BF16),
            struct((seats, 1), F32),
        ],
        (owners[None, :], positions[None, :], combine, share_of),
        [pltpu.VMEM((tokens, share), BF16), pltpu.SemaphoreType.DMA(())],
        flops=2 * n_tp * seats * tokens * (share + slots),
        hbm=(3,),
    )
    near_pieces, rows, mix = lax.optimization_barrier((near_pieces, rows, mix))
    freqs = ROPE_BASE ** (-jnp.arange(half, dtype=F32) / half)
    angles = at * freqs[None, :]
    cosine, sine = jnp.cos(angles), jnp.sin(angles)

    far_terms = collect(terms)
    near_terms = collect(near_pieces)
    far_done = call(
        functools.partial(sum_kernel, n_tp),
        [struct((2 * CAP, share), BF16)] * (n_z - 2),
        far_terms,
    )
    far_back = [swap(far_done[d - 2], "ep", 2 * d) for d in range(2, n_z)]
    near_done = call(
        functools.partial(sum_kernel, n_tp), [struct((CAP, share), BF16)] * 4, near_terms
    )
    near_back = [near_done[0]] + [swap(near_done[d], "ep", d) for d in (1, 2, 3)]
    crossed = swap(jnp.concatenate([piece[CAP:] for piece in far_back], axis=0), "ep", 1)
    partial = call(
        functools.partial(cache_kernel, n_z, n_tp, cache_width),
        [struct((seats, wide), BF16)] * n_tp,
        (*near_back, *far_back, crossed, mix, rows, attn_gain[None, :], latent_weight.T),
        [pltpu.VMEM((slots, share), BF16)],
        flops=2 * n_tp * seats * share * (slots + cache_width),
    )
    return tuple(
        call(
            functools.partial(finish_kernel, n_tp, width, rank_width),
            [struct((seats, rank_width), BF16), struct((seats, 2 * half), BF16)],
            (*collect(partial), latent_gain[None, :], cosine, sine),
        )
    )


def solution(mesh):
    placed = (
        P(("groups", "ep"), None),
        P(),
        P(("groups", "ep"), None),
        P(("groups", "ep"), None),
        P("ep", None, "tp"),
        P("ep", None, "tp"),
        P("ep", "tp", None),
        P("tp"),
        P("tp", None),
        P(),
        P(("groups", "ep")),
        P(("groups", "ep")),
    )
    return jax.shard_map(
        on_device,
        mesh=mesh,
        in_specs=placed,
        out_specs=(P(("groups", "ep", "tp"), None), P(("groups", "ep", "tp"), None)),
        check_vma=False,
    )
```

```python
import functools

import jax
import jax.numpy as jnp
from jax import lax
from jax.experimental import pallas as pl
from jax.experimental.pallas import tpu as pltpu
from jax.sharding import PartitionSpec as P

CAP = 16
EPS = 1e-06
ROUTE_SCALE = 2.5
ROPE_BASE = 10000.0
BF16 = jnp.bfloat16
F32 = jnp.float32
VMEM_LIMIT = 40 * 1024 * 1024


def columns_of(ref, index, count, share):
    if share % 128 == 0:
        return ref[:, pl.ds(pl.multiple_of(index * share, 128), share)]
    out = ref[:, 0:share]
    for q in range(1, count):
        out = jnp.where(index == q, ref[:, q * share : (q + 1) * share], out)
    return out


def dispatch_kernel(n_ep, n_tp, routes_hbm, logits_hbm, hidden_hbm, gain_hbm, *refs):
    outs = refs[: n_ep - 4]
    pick_ref, combine_ref, hidden_ref, gain_ref, routes_ref, logits_ref, sems = refs[n_ep - 4 :]
    me = lax.axis_index("ep")
    part = lax.axis_index("tp")
    tokens, width = hidden_ref.shape
    share = width // n_tp
    step = 512 if width % 512 == 0 else width
    starts = range(0, width, step)
    small = [
        pltpu.make_async_copy(routes_hbm, routes_ref, sems.at[0]),
        pltpu.make_async_copy(logits_hbm, logits_ref, sems.at[1]),
        pltpu.make_async_copy(gain_hbm, gain_ref.at[0], sems.at[2]),
    ]
    large = [
        pltpu.make_async_copy(
            hidden_hbm.at[:, c : c + step], hidden_ref.at[:, c : c + step], sems.at[3 + i]
        )
        for i, c in enumerate(starts)
    ]
    for copy in small + large:
        copy.start()
    small[0].wait()
    small[1].wait()
    routes = routes_ref[...]
    affinity = jax.nn.sigmoid(logits_ref[...])
    weight = ROUTE_SCALE * affinity / jnp.sum(affinity, axis=0, keepdims=True)
    weight = weight.astype(BF16).astype(F32)
    expert = lax.broadcasted_iota(jnp.int32, (n_ep, tokens), 0) ^ me
    hit = jnp.zeros((n_ep, tokens), F32)
    gain_of = jnp.zeros((n_ep, tokens), F32)
    for k in range(routes.shape[0]):
        same = routes[k : k + 1, :] == expert
        hit = jnp.where(same, 1.0, hit)
        gain_of = jnp.where(same, weight[k : k + 1, :], gain_of)
    earlier = lax.broadcasted_iota(jnp.int32, (tokens, tokens), 0) < lax.broadcasted_iota(
        jnp.int32, (tokens, tokens), 1
    )
    rank = jnp.dot(hit.astype(BF16), earlier.astype(F32).astype(BF16), preferred_element_type=F32)
    rank = jnp.where(hit > 0, rank, -1.0)
    place = lax.broadcasted_iota(jnp.int32, (CAP, tokens), 0).astype(F32)
    for d in range(n_ep):
        match = rank[d : d + 1, :] == place
        rows = slice(d * CAP, (d + 1) * CAP)
        pick_ref[rows, :] = jnp.where(match, 1.0, 0.0).astype(BF16)
        combine_ref[rows, :] = jnp.where(match, gain_of[d : d + 1, :], 0.0).astype(BF16)
    pick = pick_ref[4 * CAP :, :]
    square = jnp.zeros((pick.shape[0], 1), F32)
    middle = len(large) // 2
    for i, c in enumerate(starts):
        if i == 0 or i == middle:
            for copy in large[:middle] if i < middle else large[i:]:
                copy.wait()
        got = jnp.dot(pick, hidden_ref[:, c : c + step], preferred_element_type=F32)
        square = square + jnp.sum(got * got, axis=1, keepdims=True)
    small[2].wait()
    scale = lax.rsqrt(square / width + EPS)
    got = jnp.dot(pick, columns_of(hidden_ref, part, n_tp, share), preferred_element_type=F32)
    rows = (got * scale * columns_of(gain_ref, part, n_tp, share)).astype(BF16)
    for i, out in enumerate(outs):
        out[...] = rows[i * CAP : (i + 1) * CAP]


def near_kernel(n_tp, pick_ref, hidden_ref, gain_ref, own_ref, core_ref, near_ref):
    share = hidden_ref.shape[1] // n_tp
    got = jnp.dot(pick_ref[: 4 * CAP, :], hidden_ref[...], preferred_element_type=F32)
    scale = lax.rsqrt(jnp.mean(got * got, axis=1, keepdims=True) + EPS)
    whole = (got * scale * gain_ref[...]).astype(BF16)
    own_ref[...] = whole[:CAP]
    for q in range(n_tp):
        columns = slice(q * share, (q + 1) * share)
        core_ref[q * CAP : (q + 1) * CAP, :] = whole[CAP : 2 * CAP, columns]
        near_ref[q * CAP : (q + 1) * CAP, :] = whole[2 * CAP : 3 * CAP, columns]
        near_ref[(n_tp + q) * CAP : (n_tp + q + 1) * CAP, :] = whole[3 * CAP :, columns]


def load_kernel(after_ref, *refs):
    count = (len(refs) - 2) // 2
    mark_ref, sems = refs[-2:]
    copies = [
        pltpu.make_async_copy(refs[i], refs[count + i], sems.at[i]) for i in range(count)
    ]
    for copy in copies:
        copy.start()
    mark_ref[...] = jnp.zeros(mark_ref.shape, F32)
    for copy in copies:
        copy.wait()


def first_kernel(n_tp, own_ref, core_ref, near_ref, cross_ref, mine_ref, *refs):
    gate_ref, up_ref, down_ref, _ = refs[:4]
    outs, (gate_sum_ref, up_sum_ref, head_ref) = refs[4 : n_tp + 4], refs[n_tp + 4 :]
    part = lax.axis_index("tp")
    share = mine_ref.shape[1]
    head_ref[:CAP, :] = own_ref[...]
    for i, ref in enumerate((core_ref, near_ref, cross_ref)):
        for q in range(n_tp):
            rows = slice((i + 1) * CAP, (i + 2) * CAP)
            head_ref[rows, q * share : (q + 1) * share] = ref[q * CAP : (q + 1) * CAP, :]
    depth = pl.ds(pl.multiple_of(part * share, CAP), share)
    gate, upper = (
        jnp.dot(head_ref[...], ref[...], preferred_element_type=F32) for ref in (gate_ref, up_ref)
    )
    for weight_ref, sum_ref in zip((gate_ref, up_ref), (gate_sum_ref, up_sum_ref)):
        sum_ref[...] = jnp.dot(mine_ref[...], weight_ref[depth, :], preferred_element_type=F32)
    inner = (gate / (1.0 + jnp.exp(-gate)) * upper).astype(BF16)
    for d in range(n_tp):
        down = columns_of(down_ref, part ^ d, n_tp, share)
        outs[d][...] = jnp.dot(inner, down, preferred_element_type=F32).astype(BF16)


def expert_kernel(n_tp, *refs):
    rows = refs[: n_tp - 1]
    gate_ref, up_ref, down_ref, gate_sum_ref, up_sum_ref = refs[n_tp - 1 : n_tp + 4]
    outs = refs[n_tp + 4 :]
    part = lax.axis_index("tp")
    share = rows[0].shape[1]
    gate = gate_sum_ref[...]
    upper = up_sum_ref[...]
    for d in range(1, n_tp):
        value = rows[n_tp - 1 - d][...]
        depth = pl.ds(pl.multiple_of((part ^ d) * share, CAP), share)
        gate = gate + jnp.dot(value, gate_ref[depth, :], preferred_element_type=F32)
        upper = upper + jnp.dot(value, up_ref[depth, :], preferred_element_type=F32)
    far = (gate / (1.0 + jnp.exp(-gate)) * upper).astype(BF16)
    count = far.shape[0]
    groups = [
        far[start : start + CAP]
        for at in range(0, count // 2, CAP)
        for start in (at, count // 2 + at)
    ]
    inner = jnp.concatenate(groups, axis=0)
    for d in range(n_tp):
        down = columns_of(down_ref, part ^ d, n_tp, share)
        outs[d][...] = jnp.dot(inner, down, preferred_element_type=F32).astype(BF16)


def sum_kernel(n_tp, *refs):
    parts, outs = refs[:n_tp], refs[n_tp:]
    at = 0
    for out in outs:
        rows = slice(at, at + out.shape[0])
        total = parts[0][rows, :].astype(F32)
        for other in parts[1:]:
            total = total + other[rows, :].astype(F32)
        out[...] = total.astype(BF16)
        at += out.shape[0]


def seats_kernel(
    n_tp,
    seat_cap,
    owners_ref,
    positions_ref,
    combine_ref,
    hidden_ref,
    rows_ref,
    mix_ref,
    at_ref,
):
    part = lax.axis_index("tp")
    tokens, width = hidden_ref.shape
    source_rows = tokens // n_tp
    owners = owners_ref[...] ^ part
    owner = lax.broadcasted_iota(jnp.int32, (n_tp, tokens), 0)
    hot = jnp.where(owners == owner, 1.0, 0.0)
    first = lax.broadcasted_iota(jnp.int32, (tokens, tokens), 0)
    second = lax.broadcasted_iota(jnp.int32, (tokens, tokens), 1)
    earlier = jnp.where((first < second) & (first // source_rows == second // source_rows), 1.0, 0.0)
    before = jnp.dot(hot.astype(BF16), earlier.astype(BF16), preferred_element_type=F32)
    seat = jnp.sum(before * hot, axis=0, keepdims=True).astype(jnp.int32)
    source = lax.broadcasted_iota(jnp.int32, (1, tokens), 1) // source_rows
    code = owners * (n_tp * seat_cap) + source * seat_cap + seat
    seats = n_tp * seat_cap
    held = lax.broadcasted_iota(jnp.int32, (n_tp * seats, tokens), 0) == code
    pick = jnp.where(held, 1.0, 0.0).astype(BF16)
    mix_ref[...] = lax.dot_general(
        pick, combine_ref[...], (((1,), (1,)), ((), ())), preferred_element_type=F32
    ).astype(BF16)
    place = jnp.where(held[:seats], positions_ref[...].astype(F32), 0.0)
    at_ref[...] = jnp.sum(place, axis=1, keepdims=True)
    hidden = columns_of(hidden_ref, part, n_tp, width // n_tp)
    rows_ref[...] = jnp.dot(pick, hidden, preferred_element_type=F32).astype(BF16)


def cache_kernel(n_z, n_tp, cache_width, *refs):
    near, far, core_ref = refs[:4], refs[4 : n_z + 2], refs[n_z + 2]
    mix_ref, rows_ref, gain_ref, weight_ref = refs[n_z + 3 : n_z + 7]
    outs, back_ref = refs[n_z + 7 : n_z + 7 + n_tp], refs[n_z + 7 + n_tp]
    for d in range(4):
        back_ref[d * CAP : (d + 1) * CAP, :] = near[d][...]
    for d in range(n_z - 2):
        at = (2 * d + 4) * CAP
        back_ref[at : at + CAP, :] = far[d][:CAP, :]
        last = (n_z - 3 - d) * CAP
        back_ref[at + CAP : at + 2 * CAP, :] = core_ref[last : last + CAP, :]
    mixed = jnp.dot(mix_ref[...], back_ref[...], preferred_element_type=F32)
    state = rows_ref[...].astype(F32) + mixed
    square = jnp.sum(state * state, axis=1, keepdims=True)
    scaled = (state * gain_ref[...]).astype(BF16)
    value = lax.dot_general(
        scaled, weight_ref[...], (((1,), (1,)), ((), ())), preferred_element_type=F32
    ).astype(BF16)
    high = square.astype(BF16).astype(F32)
    rest = square - high
    middle = rest.astype(BF16).astype(F32)
    low = rest - middle
    seats, wide = outs[0].shape
    lane = lax.broadcasted_iota(jnp.int32, (square.shape[0], wide - cache_width), 1)
    extra = jnp.where(lane == 0, high, jnp.where(lane == 1, middle, jnp.where(lane == 2, low, 0.0)))
    extra = extra.astype(BF16)
    for d in range(n_tp):
        outs[d][:, :cache_width] = value[d * seats : (d + 1) * seats]
        outs[d][:, cache_width:] = extra[d * seats : (d + 1) * seats]


def finish_kernel(n_tp, width, rank_width, *refs):
    parts = refs[:n_tp]
    gain_ref, cos_ref, sin_ref, latent_ref, rotary_ref = refs[n_tp:]
    total = parts[0][...].astype(F32)
    for other in parts[1:]:
        total = total + other[...].astype(F32)
    half = cos_ref.shape[1]
    cache_width = rank_width + 2 * half
    square = jnp.sum(total[:, cache_width : cache_width + 3], axis=1, keepdims=True)
    cache = total[:, :cache_width] * lax.rsqrt(square / width + EPS)
    latent = cache[:, :rank_width]
    scale = lax.rsqrt(jnp.mean(latent * latent, axis=1, keepdims=True) + EPS)
    latent_ref[...] = (latent * scale * gain_ref[...]).astype(BF16)
    first = cache[:, rank_width : rank_width + half]
    second = cache[:, rank_width + half :]
    cosine, sine = cos_ref[...], sin_ref[...]
    rotary_ref[:, :half] = (first * cosine - second * sine).astype(BF16)
    rotary_ref[:, half:] = (second * cosine + first * sine).astype(BF16)


def call(kernel, out_shape, args, scratch=(), flops=0, hbm=()):
    moved = sum(a.size * a.dtype.itemsize for a in args)
    vmem = pl.BlockSpec(memory_space=pltpu.VMEM)
    args = [
        pltpu.with_memory_space_constraint(a, pltpu.HBM) if i in hbm else a
        for i, a in enumerate(args)
    ]
    return pl.pallas_call(
        kernel,
        out_shape=out_shape,
        in_specs=[
            pl.BlockSpec(memory_space=pltpu.HBM) if i in hbm else vmem for i in range(len(args))
        ],
        out_specs=[vmem] * len(out_shape),
        scratch_shapes=list(scratch),
        compiler_params=pltpu.CompilerParams(vmem_limit_bytes=VMEM_LIMIT),
        cost_estimate=pl.CostEstimate(flops=flops, bytes_accessed=moved, transcendentals=0),
    )(*args)


def swap(value, axis, d):
    return lax.ppermute(value, axis, [(i, i ^ d) for i in range(lax.axis_size(axis))])


def spread(value, n_tp):
    return [swap(value, "tp", d) for d in reversed(range(1, n_tp))]


def collect(values):
    return [swap(values[d], "tp", d) for d in reversed(range(1, len(values)))] + [values[0]]


def on_device(
    hidden,
    moe_gain,
    route_logits,
    routes,
    gate_weight,
    up_weight,
    down_weight,
    attn_gain,
    latent_weight,
    latent_gain,
    positions,
    owners,
):
    n_ep = lax.axis_size("ep")
    n_tp = lax.axis_size("tp")
    n_z = n_ep // 2
    tokens, width = hidden.shape
    share = width // n_tp
    ff = gate_weight.shape[2]
    slots = n_ep * CAP
    seat_cap = max(2, tokens // n_tp // 4)
    seats = n_tp * seat_cap
    rank_width = latent_gain.shape[0]
    cache_width = latent_weight.shape[1]
    half = (cache_width - rank_width) // 2
    wide = (cache_width + 3 + 127) // 128 * 128
    struct = jax.ShapeDtypeStruct
    chunks = width // 512 if width % 512 == 0 else 1

    *outgoing, pick, combine, hidden, gain = call(
        functools.partial(dispatch_kernel, n_ep, n_tp),
        [struct((CAP, share), BF16)] * (n_ep - 4)
        + [struct((slots, tokens), BF16)] * 2
        + [struct(hidden.shape, BF16), struct((1, width), F32)],
        (routes.T, route_logits.T, hidden, moe_gain),
        [
            pltpu.VMEM(routes.T.shape, jnp.int32),
            pltpu.VMEM(routes.T.shape, F32),
            pltpu.SemaphoreType.DMA((3 + chunks,)),
        ],
        flops=2 * slots * tokens * width,
        hbm=(0, 1, 2, 3),
    )
    own, to_core, to_near = call(
        functools.partial(near_kernel, n_tp),
        [struct((CAP, width), BF16), struct((n_tp * CAP, share), BF16)]
        + [struct((2 * n_tp * CAP, share), BF16)],
        (pick, hidden, gain),
        flops=8 * CAP * tokens * width,
    )
    order = [*range(4, n_ep, 2), *range(5, n_ep, 2)]
    arrived = [swap(outgoing[d - 4], "ep", d) for d in order]
    near = swap(to_near[: n_tp * CAP], "ep", 2)
    near_crossed = swap(to_near[n_tp * CAP :], "ep", 3)
    from_core = swap(to_core, "ep", 1)
    gate_w, up_w, down_w = gate_weight[0], up_weight[0], down_weight[0]
    *loaded, mark = call(
        load_kernel,
        [struct(w.shape, BF16) for w in (gate_w, up_w, down_w)] + [struct((8, 128), F32)],
        (combine, gate_w, up_w, down_w),
        [pltpu.SemaphoreType.DMA((3,))],
        hbm=(1, 2, 3),
    )
    arrived, from_core = lax.optimization_barrier((arrived, from_core))
    mine = jnp.concatenate(arrived, axis=0)
    shares = spread(mine, n_tp)
    near_rows, far_rows = 4 * CAP, slots - 4 * CAP
    *near_pieces, gate_sum, up_sum = call(
        functools.partial(first_kernel, n_tp),
        [struct((near_rows, share), BF16)] * n_tp + [struct((far_rows, ff), F32)] * 2,
        (own, from_core, near, near_crossed, mine, *loaded, mark),
        [pltpu.VMEM((4 * CAP, width), BF16)],
        flops=2 * slots * width * ff,
    )
    terms = call(
        functools.partial(expert_kernel, n_tp),
        [struct((far_rows, share), BF16)] * n_tp,
        (*shares, *loaded, gate_sum, up_sum),
        flops=2 * slots * width * ff * 3,
    )
    terms = list(terms)
    combine, terms[0] = lax.optimization_barrier((combine, terms[0]))
    rows, mix, at = call(
        functools.partial(seats_kernel, n_tp, seat_cap),
        [
            struct((n_tp * seats, share), BF16),
            struct((n_tp * seats, slots), BF16),
            struct((seats, 1), F32),
        ],
        (owners[None, :], positions[None, :], combine, hidden),
        flops=2 * n_tp * seats * tokens * (share + slots),
    )
    near_pieces, rows, mix = lax.optimization_barrier((near_pieces, rows, mix))
    freqs = ROPE_BASE ** (-jnp.arange(half, dtype=F32) / half)
    angles = at * freqs[None, :]
    cosine, sine = jnp.cos(angles), jnp.sin(angles)

    far_terms = collect(terms)
    near_terms = collect(near_pieces)
    far_done = call(
        functools.partial(sum_kernel, n_tp),
        [struct((2 * CAP, share), BF16)] * (n_z - 2),
        far_terms,
    )
    far_back = [swap(far_done[d - 2], "ep", 2 * d) for d in range(2, n_z)]
    near_done = call(
        functools.partial(sum_kernel, n_tp), [struct((CAP, share), BF16)] * 4, near_terms
    )
    near_back = [near_done[0]] + [swap(near_done[d], "ep", d) for d in (1, 2, 3)]
    crossed = swap(jnp.concatenate([piece[CAP:] for piece in far_back[::-1]], axis=0), "ep", 1)
    partial = call(
        functools.partial(cache_kernel, n_z, n_tp, cache_width),
        [struct((seats, wide), BF16)] * n_tp,
        (*near_back, *far_back, crossed, mix, rows, attn_gain[None, :], latent_weight.T),
        [pltpu.VMEM((slots, share), BF16)],
        flops=2 * n_tp * seats * share * (slots + cache_width),
    )
    return tuple(
        call(
            functools.partial(finish_kernel, n_tp, width, rank_width),
            [struct((seats, rank_width), BF16), struct((seats, 2 * half), BF16)],
            (*collect(partial), latent_gain[None, :], cosine, sine),
        )
    )


def solution(mesh):
    placed = (
        P(("groups", "ep"), None),
        P(),
        P(("groups", "ep"), None),
        P(("groups", "ep"), None),
        P("ep", None, "tp"),
        P("ep", None, "tp"),
        P("ep", "tp", None),
        P("tp"),
        P("tp", None),
        P(),
        P(("groups", "ep")),
        P(("groups", "ep")),
    )
    return jax.shard_map(
        on_device,
        mesh=mesh,
        in_specs=placed,
        out_specs=(P(("groups", "ep", "tp"), None), P(("groups", "ep", "tp"), None)),
        check_vma=False,
    )
```

```python
import functools

import jax
import jax.numpy as jnp
from jax import lax
from jax.experimental import pallas as pl
from jax.experimental.pallas import tpu as pltpu
from jax.sharding import PartitionSpec as P

CAP = 16
EPS = 1e-06
ROUTE_SCALE = 2.5
ROPE_BASE = 10000.0
BF16 = jnp.bfloat16
F32 = jnp.float32
VMEM_LIMIT = 40 * 1024 * 1024


def columns_of(ref, index, count, share):
    if share % 128 == 0:
        return ref[:, pl.ds(pl.multiple_of(index * share, 128), share)]
    out = ref[:, 0:share]
    for q in range(1, count):
        out = jnp.where(index == q, ref[:, q * share : (q + 1) * share], out)
    return out


def dispatch_kernel(n_ep, n_tp, routes_hbm, logits_hbm, hidden_hbm, gain_hbm, *refs):
    outs = refs[: n_ep - 4]
    pick_ref, combine_ref, hidden_ref, gain_ref, routes_ref, logits_ref, sems = refs[n_ep - 4 :]
    me = lax.axis_index("ep")
    part = lax.axis_index("tp")
    tokens, width = hidden_ref.shape
    share = width // n_tp
    step = 512 if width % 512 == 0 else width
    starts = range(0, width, step)
    small = [
        pltpu.make_async_copy(routes_hbm, routes_ref, sems.at[0]),
        pltpu.make_async_copy(logits_hbm, logits_ref, sems.at[1]),
        pltpu.make_async_copy(gain_hbm, gain_ref.at[0], sems.at[2]),
    ]
    large = [
        pltpu.make_async_copy(
            hidden_hbm.at[:, c : c + step], hidden_ref.at[:, c : c + step], sems.at[3 + i]
        )
        for i, c in enumerate(starts)
    ]
    for copy in small + large:
        copy.start()
    small[0].wait()
    small[1].wait()
    routes = routes_ref[...]
    affinity = jax.nn.sigmoid(logits_ref[...])
    weight = ROUTE_SCALE * affinity / jnp.sum(affinity, axis=0, keepdims=True)
    weight = weight.astype(BF16).astype(F32)
    expert = lax.broadcasted_iota(jnp.int32, (n_ep, tokens), 0) ^ me
    hit = jnp.zeros((n_ep, tokens), F32)
    gain_of = jnp.zeros((n_ep, tokens), F32)
    for k in range(routes.shape[0]):
        same = routes[k : k + 1, :] == expert
        hit = jnp.where(same, 1.0, hit)
        gain_of = jnp.where(same, weight[k : k + 1, :], gain_of)
    earlier = lax.broadcasted_iota(jnp.int32, (tokens, tokens), 0) < lax.broadcasted_iota(
        jnp.int32, (tokens, tokens), 1
    )
    rank = jnp.dot(hit.astype(BF16), earlier.astype(F32).astype(BF16), preferred_element_type=F32)
    rank = jnp.where(hit > 0, rank, -1.0)
    place = lax.broadcasted_iota(jnp.int32, (CAP, tokens), 0).astype(F32)
    for d in range(n_ep):
        match = rank[d : d + 1, :] == place
        rows = slice(d * CAP, (d + 1) * CAP)
        pick_ref[rows, :] = jnp.where(match, 1.0, 0.0).astype(BF16)
        combine_ref[rows, :] = jnp.where(match, gain_of[d : d + 1, :], 0.0).astype(BF16)
    pick = pick_ref[4 * CAP :, :]
    square = jnp.zeros((pick.shape[0], 1), F32)
    middle = len(large) // 2
    for i, c in enumerate(starts):
        if i == 0 or i == middle:
            for copy in large[:middle] if i < middle else large[i:]:
                copy.wait()
        got = jnp.dot(pick, hidden_ref[:, c : c + step], preferred_element_type=F32)
        square = square + jnp.sum(got * got, axis=1, keepdims=True)
    small[2].wait()
    scale = lax.rsqrt(square / width + EPS)
    got = jnp.dot(pick, columns_of(hidden_ref, part, n_tp, share), preferred_element_type=F32)
    rows = (got * scale * columns_of(gain_ref, part, n_tp, share)).astype(BF16)
    for i, out in enumerate(outs):
        out[...] = rows[i * CAP : (i + 1) * CAP]


def near_kernel(n_tp, pick_ref, hidden_ref, gain_ref, own_ref, core_ref, near_ref):
    share = hidden_ref.shape[1] // n_tp
    got = jnp.dot(pick_ref[: 4 * CAP, :], hidden_ref[...], preferred_element_type=F32)
    scale = lax.rsqrt(jnp.mean(got * got, axis=1, keepdims=True) + EPS)
    whole = (got * scale * gain_ref[...]).astype(BF16)
    own_ref[...] = whole[:CAP]
    for q in range(n_tp):
        columns = slice(q * share, (q + 1) * share)
        core_ref[q * CAP : (q + 1) * CAP, :] = whole[CAP : 2 * CAP, columns]
        near_ref[q * CAP : (q + 1) * CAP, :] = whole[2 * CAP : 3 * CAP, columns]
        near_ref[(n_tp + q) * CAP : (n_tp + q + 1) * CAP, :] = whole[3 * CAP :, columns]


def load_kernel(after_ref, *refs):
    count = (len(refs) - 2) // 2
    mark_ref, sems = refs[-2:]
    copies = [
        pltpu.make_async_copy(refs[i], refs[count + i], sems.at[i]) for i in range(count)
    ]
    for copy in copies:
        copy.start()
    mark_ref[...] = jnp.zeros(mark_ref.shape, F32)
    for copy in copies:
        copy.wait()


def first_kernel(n_tp, own_ref, core_ref, near_ref, cross_ref, mine_ref, *refs):
    gate_ref, up_ref, down_ref, _ = refs[:4]
    outs, (gate_sum_ref, up_sum_ref, head_ref) = refs[4 : n_tp + 4], refs[n_tp + 4 :]
    part = lax.axis_index("tp")
    share = mine_ref.shape[1]
    head_ref[:CAP, :] = own_ref[...]
    for i, ref in enumerate((core_ref, near_ref, cross_ref)):
        for q in range(n_tp):
            rows = slice((i + 1) * CAP, (i + 2) * CAP)
            head_ref[rows, q * share : (q + 1) * share] = ref[q * CAP : (q + 1) * CAP, :]
    depth = pl.ds(pl.multiple_of(part * share, CAP), share)
    gate, upper = (
        jnp.dot(head_ref[...], ref[...], preferred_element_type=F32) for ref in (gate_ref, up_ref)
    )
    for weight_ref, sum_ref in zip((gate_ref, up_ref), (gate_sum_ref, up_sum_ref)):
        sum_ref[...] = jnp.dot(mine_ref[...], weight_ref[depth, :], preferred_element_type=F32)
    inner = (gate / (1.0 + jnp.exp(-gate)) * upper).astype(BF16)
    for d in range(n_tp):
        down = columns_of(down_ref, part ^ d, n_tp, share)
        outs[d][...] = jnp.dot(inner, down, preferred_element_type=F32).astype(BF16)


def expert_kernel(n_tp, *refs):
    rows = refs[: n_tp - 1]
    gate_ref, up_ref, down_ref, gate_sum_ref, up_sum_ref = refs[n_tp - 1 : n_tp + 4]
    outs = refs[n_tp + 4 :]
    part = lax.axis_index("tp")
    share = rows[0].shape[1]
    gate = gate_sum_ref[...]
    upper = up_sum_ref[...]
    for d in range(1, n_tp):
        value = rows[n_tp - 1 - d][...]
        depth = pl.ds(pl.multiple_of((part ^ d) * share, CAP), share)
        gate = gate + jnp.dot(value, gate_ref[depth, :], preferred_element_type=F32)
        upper = upper + jnp.dot(value, up_ref[depth, :], preferred_element_type=F32)
    far = (gate / (1.0 + jnp.exp(-gate)) * upper).astype(BF16)
    count = far.shape[0]
    groups = [
        far[start : start + CAP]
        for at in range(0, count // 2, CAP)
        for start in (at, count // 2 + at)
    ]
    inner = jnp.concatenate(groups, axis=0)
    for d in range(n_tp):
        down = columns_of(down_ref, part ^ d, n_tp, share)
        outs[d][...] = jnp.dot(inner, down, preferred_element_type=F32).astype(BF16)


def sum_kernel(n_tp, *refs):
    parts, outs = refs[:n_tp], refs[n_tp:]
    at = 0
    for out in outs:
        rows = slice(at, at + out.shape[0])
        total = parts[0][rows, :].astype(F32)
        for other in parts[1:]:
            total = total + other[rows, :].astype(F32)
        out[...] = total.astype(BF16)
        at += out.shape[0]


def seats_kernel(
    n_tp,
    seat_cap,
    owners_ref,
    positions_ref,
    combine_ref,
    hidden_ref,
    rows_ref,
    mix_ref,
    at_ref,
):
    part = lax.axis_index("tp")
    tokens, width = hidden_ref.shape
    source_rows = tokens // n_tp
    owners = owners_ref[...] ^ part
    owner = lax.broadcasted_iota(jnp.int32, (n_tp, tokens), 0)
    hot = jnp.where(owners == owner, 1.0, 0.0)
    first = lax.broadcasted_iota(jnp.int32, (tokens, tokens), 0)
    second = lax.broadcasted_iota(jnp.int32, (tokens, tokens), 1)
    earlier = jnp.where((first < second) & (first // source_rows == second // source_rows), 1.0, 0.0)
    before = jnp.dot(hot.astype(BF16), earlier.astype(BF16), preferred_element_type=F32)
    seat = jnp.sum(before * hot, axis=0, keepdims=True).astype(jnp.int32)
    source = lax.broadcasted_iota(jnp.int32, (1, tokens), 1) // source_rows
    code = owners * (n_tp * seat_cap) + source * seat_cap + seat
    seats = n_tp * seat_cap
    held = lax.broadcasted_iota(jnp.int32, (n_tp * seats, tokens), 0) == code
    pick = jnp.where(held, 1.0, 0.0).astype(BF16)
    mix_ref[...] = lax.dot_general(
        pick, combine_ref[...], (((1,), (1,)), ((), ())), preferred_element_type=F32
    ).astype(BF16)
    place = jnp.where(held[:seats], positions_ref[...].astype(F32), 0.0)
    at_ref[...] = jnp.sum(place, axis=1, keepdims=True)
    hidden = columns_of(hidden_ref, part, n_tp, width // n_tp)
    rows_ref[...] = jnp.dot(pick, hidden, preferred_element_type=F32).astype(BF16)


def cache_kernel(order, n_tp, cache_width, *refs):
    count = len(order)
    mix_ref, rows_ref, gain_ref, weight_ref = refs[count : count + 4]
    outs, back_ref = refs[count + 4 : count + 4 + n_tp], refs[count + 4 + n_tp]
    for piece, d in zip(refs, order):
        back_ref[d * CAP : (d + 1) * CAP, :] = piece[...]
    mixed = jnp.dot(mix_ref[...], back_ref[...], preferred_element_type=F32)
    state = rows_ref[...].astype(F32) + mixed
    square = jnp.sum(state * state, axis=1, keepdims=True)
    scaled = (state * gain_ref[...]).astype(BF16)
    value = lax.dot_general(
        scaled, weight_ref[...], (((1,), (1,)), ((), ())), preferred_element_type=F32
    ).astype(BF16)
    high = square.astype(BF16).astype(F32)
    rest = square - high
    middle = rest.astype(BF16).astype(F32)
    low = rest - middle
    seats, wide = outs[0].shape
    lane = lax.broadcasted_iota(jnp.int32, (square.shape[0], wide - cache_width), 1)
    extra = jnp.where(lane == 0, high, jnp.where(lane == 1, middle, jnp.where(lane == 2, low, 0.0)))
    extra = extra.astype(BF16)
    for d in range(n_tp):
        outs[d][:, :cache_width] = value[d * seats : (d + 1) * seats]
        outs[d][:, cache_width:] = extra[d * seats : (d + 1) * seats]


def finish_kernel(n_tp, width, rank_width, *refs):
    parts = refs[:n_tp]
    gain_ref, cos_ref, sin_ref, latent_ref, rotary_ref = refs[n_tp:]
    total = parts[0][...].astype(F32)
    for other in parts[1:]:
        total = total + other[...].astype(F32)
    half = cos_ref.shape[1]
    cache_width = rank_width + 2 * half
    square = jnp.sum(total[:, cache_width : cache_width + 3], axis=1, keepdims=True)
    cache = total[:, :cache_width] * lax.rsqrt(square / width + EPS)
    latent = cache[:, :rank_width]
    scale = lax.rsqrt(jnp.mean(latent * latent, axis=1, keepdims=True) + EPS)
    latent_ref[...] = (latent * scale * gain_ref[...]).astype(BF16)
    first = cache[:, rank_width : rank_width + half]
    second = cache[:, rank_width + half :]
    cosine, sine = cos_ref[...], sin_ref[...]
    rotary_ref[:, :half] = (first * cosine - second * sine).astype(BF16)
    rotary_ref[:, half:] = (second * cosine + first * sine).astype(BF16)


def call(kernel, out_shape, args, scratch=(), flops=0, hbm=()):
    moved = sum(a.size * a.dtype.itemsize for a in args)
    vmem = pl.BlockSpec(memory_space=pltpu.VMEM)
    args = [
        pltpu.with_memory_space_constraint(a, pltpu.HBM) if i in hbm else a
        for i, a in enumerate(args)
    ]
    return pl.pallas_call(
        kernel,
        out_shape=out_shape,
        in_specs=[
            pl.BlockSpec(memory_space=pltpu.HBM) if i in hbm else vmem for i in range(len(args))
        ],
        out_specs=[vmem] * len(out_shape),
        scratch_shapes=list(scratch),
        compiler_params=pltpu.CompilerParams(vmem_limit_bytes=VMEM_LIMIT),
        cost_estimate=pl.CostEstimate(flops=flops, bytes_accessed=moved, transcendentals=0),
    )(*args)


def swap(value, axis, d):
    return lax.ppermute(value, axis, [(i, i ^ d) for i in range(lax.axis_size(axis))])


def spread(value, n_tp):
    return [swap(value, "tp", d) for d in reversed(range(1, n_tp))]


def collect(values):
    return [swap(values[d], "tp", d) for d in reversed(range(1, len(values)))] + [values[0]]


def on_device(
    hidden,
    moe_gain,
    route_logits,
    routes,
    gate_weight,
    up_weight,
    down_weight,
    attn_gain,
    latent_weight,
    latent_gain,
    positions,
    owners,
):
    n_ep = lax.axis_size("ep")
    n_tp = lax.axis_size("tp")
    n_z = n_ep // 2
    tokens, width = hidden.shape
    share = width // n_tp
    ff = gate_weight.shape[2]
    slots = n_ep * CAP
    seat_cap = max(2, tokens // n_tp // 4)
    seats = n_tp * seat_cap
    rank_width = latent_gain.shape[0]
    cache_width = latent_weight.shape[1]
    half = (cache_width - rank_width) // 2
    wide = (cache_width + 3 + 127) // 128 * 128
    struct = jax.ShapeDtypeStruct
    chunks = width // 512 if width % 512 == 0 else 1

    *outgoing, pick, combine, hidden, gain = call(
        functools.partial(dispatch_kernel, n_ep, n_tp),
        [struct((CAP, share), BF16)] * (n_ep - 4)
        + [struct((slots, tokens), BF16)] * 2
        + [struct(hidden.shape, BF16), struct((1, width), F32)],
        (routes.T, route_logits.T, hidden, moe_gain),
        [
            pltpu.VMEM(routes.T.shape, jnp.int32),
            pltpu.VMEM(routes.T.shape, F32),
            pltpu.SemaphoreType.DMA((3 + chunks,)),
        ],
        flops=2 * slots * tokens * width,
        hbm=(0, 1, 2, 3),
    )
    own, to_core, to_near = call(
        functools.partial(near_kernel, n_tp),
        [struct((CAP, width), BF16), struct((n_tp * CAP, share), BF16)]
        + [struct((2 * n_tp * CAP, share), BF16)],
        (pick, hidden, gain),
        flops=8 * CAP * tokens * width,
    )
    order = [*range(4, n_ep, 2), *range(5, n_ep, 2)]
    arrived = [swap(outgoing[d - 4], "ep", d) for d in order]
    near = swap(to_near[: n_tp * CAP], "ep", 2)
    near_crossed = swap(to_near[n_tp * CAP :], "ep", 3)
    from_core = swap(to_core, "ep", 1)
    gate_w, up_w, down_w = gate_weight[0], up_weight[0], down_weight[0]
    *loaded, mark = call(
        load_kernel,
        [struct(w.shape, BF16) for w in (gate_w, up_w, down_w)] + [struct((8, 128), F32)],
        (combine, gate_w, up_w, down_w),
        [pltpu.SemaphoreType.DMA((3,))],
        hbm=(1, 2, 3),
    )
    arrived, from_core = lax.optimization_barrier((arrived, from_core))
    mine = jnp.concatenate(arrived, axis=0)
    shares = spread(mine, n_tp)
    near_rows, far_rows = 4 * CAP, slots - 4 * CAP
    *near_pieces, gate_sum, up_sum = call(
        functools.partial(first_kernel, n_tp),
        [struct((near_rows, share), BF16)] * n_tp + [struct((far_rows, ff), F32)] * 2,
        (own, from_core, near, near_crossed, mine, *loaded, mark),
        [pltpu.VMEM((4 * CAP, width), BF16)],
        flops=2 * slots * width * ff,
    )
    terms = call(
        functools.partial(expert_kernel, n_tp),
        [struct((far_rows, share), BF16)] * n_tp,
        (*shares, *loaded, gate_sum, up_sum),
        flops=2 * slots * width * ff * 3,
    )
    terms = list(terms)
    combine, terms[0] = lax.optimization_barrier((combine, terms[0]))
    rows, mix, at = call(
        functools.partial(seats_kernel, n_tp, seat_cap),
        [
            struct((n_tp * seats, share), BF16),
            struct((n_tp * seats, slots), BF16),
            struct((seats, 1), F32),
        ],
        (owners[None, :], positions[None, :], combine, hidden),
        flops=2 * n_tp * seats * tokens * (share + slots),
    )
    freqs = ROPE_BASE ** (-jnp.arange(half, dtype=F32) / half)
    angles = at * freqs[None, :]
    cosine, sine = jnp.cos(angles), jnp.sin(angles)

    near_terms = collect(near_pieces)
    near_done = call(
        functools.partial(sum_kernel, n_tp), [struct((CAP, share), BF16)] * 4, near_terms
    )
    near_back = [near_done[0]] + [swap(near_done[d], "ep", d) for d in (1, 2, 3)]
    far_done = call(
        functools.partial(sum_kernel, n_tp),
        [struct((CAP, share), BF16)] * (n_ep - 4),
        collect(terms),
    )
    near_back, far_done, rows, mix = lax.optimization_barrier((near_back, far_done, rows, mix))
    far_back = [swap(far_done[d - 4], "ep", d) for d in order]
    partial = call(
        functools.partial(cache_kernel, [0, 1, 2, 3, *order], n_tp, cache_width),
        [struct((seats, wide), BF16)] * n_tp,
        (*near_back, *far_back, mix, rows, attn_gain[None, :], latent_weight.T),
        [pltpu.VMEM((slots, share), BF16)],
        flops=2 * n_tp * seats * share * (slots + cache_width),
    )
    return tuple(
        call(
            functools.partial(finish_kernel, n_tp, width, rank_width),
            [struct((seats, rank_width), BF16), struct((seats, 2 * half), BF16)],
            (*collect(partial), latent_gain[None, :], cosine, sine),
        )
    )


def solution(mesh):
    placed = (
        P(("groups", "ep"), None),
        P(),
        P(("groups", "ep"), None),
        P(("groups", "ep"), None),
        P("ep", None, "tp"),
        P("ep", None, "tp"),
        P("ep", "tp", None),
        P("tp"),
        P("tp", None),
        P(),
        P(("groups", "ep")),
        P(("groups", "ep")),
    )
    return jax.shard_map(
        on_device,
        mesh=mesh,
        in_specs=placed,
        out_specs=(P(("groups", "ep", "tp"), None), P(("groups", "ep", "tp"), None)),
        check_vma=False,
    )
```

```python
import functools

import jax
import jax.numpy as jnp
from jax import lax
from jax.experimental import pallas as pl
from jax.experimental.pallas import tpu as pltpu
from jax.sharding import PartitionSpec as P

CAP = 16
EPS = 1e-06
ROUTE_SCALE = 2.5
ROPE_BASE = 10000.0
BF16 = jnp.bfloat16
F32 = jnp.float32
VMEM_LIMIT = 40 * 1024 * 1024


def columns_of(ref, index, count, share):
    if share % 128 == 0:
        return ref[:, pl.ds(pl.multiple_of(index * share, 128), share)]
    out = ref[:, 0:share]
    for q in range(1, count):
        out = jnp.where(index == q, ref[:, q * share : (q + 1) * share], out)
    return out


def dispatch_kernel(n_ep, n_tp, routes_hbm, logits_hbm, hidden_hbm, gain_hbm, *refs):
    outs = refs[: n_ep - 4]
    pick_ref, combine_ref, hidden_ref, gain_ref, routes_ref, logits_ref, sems = refs[n_ep - 4 :]
    me = lax.axis_index("ep")
    part = lax.axis_index("tp")
    tokens, width = hidden_ref.shape
    share = width // n_tp
    step = 512 if width % 512 == 0 else width
    starts = range(0, width, step)
    small = [
        pltpu.make_async_copy(routes_hbm, routes_ref, sems.at[0]),
        pltpu.make_async_copy(logits_hbm, logits_ref, sems.at[1]),
        pltpu.make_async_copy(gain_hbm, gain_ref.at[0], sems.at[2]),
    ]
    large = [
        pltpu.make_async_copy(
            hidden_hbm.at[:, c : c + step], hidden_ref.at[:, c : c + step], sems.at[3 + i]
        )
        for i, c in enumerate(starts)
    ]
    for copy in small + large:
        copy.start()
    small[0].wait()
    small[1].wait()
    routes = routes_ref[...]
    affinity = jax.nn.sigmoid(logits_ref[...])
    weight = ROUTE_SCALE * affinity / jnp.sum(affinity, axis=0, keepdims=True)
    weight = weight.astype(BF16).astype(F32)
    expert = lax.broadcasted_iota(jnp.int32, (n_ep, tokens), 0) ^ me
    hit = jnp.zeros((n_ep, tokens), F32)
    gain_of = jnp.zeros((n_ep, tokens), F32)
    for k in range(routes.shape[0]):
        same = routes[k : k + 1, :] == expert
        hit = jnp.where(same, 1.0, hit)
        gain_of = jnp.where(same, weight[k : k + 1, :], gain_of)
    earlier = lax.broadcasted_iota(jnp.int32, (tokens, tokens), 0) < lax.broadcasted_iota(
        jnp.int32, (tokens, tokens), 1
    )
    rank = jnp.dot(hit.astype(BF16), earlier.astype(F32).astype(BF16), preferred_element_type=F32)
    rank = jnp.where(hit > 0, rank, -1.0)
    place = lax.broadcasted_iota(jnp.int32, (CAP, tokens), 0).astype(F32)
    for d in range(n_ep):
        match = rank[d : d + 1, :] == place
        rows = slice(d * CAP, (d + 1) * CAP)
        pick_ref[rows, :] = jnp.where(match, 1.0, 0.0).astype(BF16)
        combine_ref[rows, :] = jnp.where(match, gain_of[d : d + 1, :], 0.0).astype(BF16)
    pick = pick_ref[4 * CAP :, :]
    square = jnp.zeros((pick.shape[0], 1), F32)
    middle = len(large) // 2
    for i, c in enumerate(starts):
        if i == 0 or i == middle:
            for copy in large[:middle] if i < middle else large[i:]:
                copy.wait()
        got = jnp.dot(pick, hidden_ref[:, c : c + step], preferred_element_type=F32)
        square = square + jnp.sum(got * got, axis=1, keepdims=True)
    small[2].wait()
    scale = lax.rsqrt(square / width + EPS)
    got = jnp.dot(pick, columns_of(hidden_ref, part, n_tp, share), preferred_element_type=F32)
    rows = (got * scale * columns_of(gain_ref, part, n_tp, share)).astype(BF16)
    for i, out in enumerate(outs):
        out[...] = rows[i * CAP : (i + 1) * CAP]


def near_kernel(n_tp, pick_ref, hidden_ref, gain_ref, own_ref, core_ref, near_ref):
    share = hidden_ref.shape[1] // n_tp
    got = jnp.dot(pick_ref[: 4 * CAP, :], hidden_ref[...], preferred_element_type=F32)
    scale = lax.rsqrt(jnp.mean(got * got, axis=1, keepdims=True) + EPS)
    whole = (got * scale * gain_ref[...]).astype(BF16)
    own_ref[...] = whole[:CAP]
    for q in range(n_tp):
        columns = slice(q * share, (q + 1) * share)
        core_ref[q * CAP : (q + 1) * CAP, :] = whole[CAP : 2 * CAP, columns]
        near_ref[q * CAP : (q + 1) * CAP, :] = whole[2 * CAP : 3 * CAP, columns]
        near_ref[(n_tp + q) * CAP : (n_tp + q + 1) * CAP, :] = whole[3 * CAP :, columns]


def load_kernel(after_ref, *refs):
    count = (len(refs) - 2) // 2
    mark_ref, sems = refs[-2:]
    copies = [
        pltpu.make_async_copy(refs[i], refs[count + i], sems.at[i]) for i in range(count)
    ]
    for copy in copies:
        copy.start()
    mark_ref[...] = jnp.zeros(mark_ref.shape, F32)
    for copy in copies:
        copy.wait()


def first_kernel(n_tp, own_ref, core_ref, near_ref, cross_ref, mine_ref, *refs):
    gate_ref, up_ref, down_ref, _ = refs[:4]
    outs, (gate_sum_ref, up_sum_ref, head_ref) = refs[4 : n_tp + 4], refs[n_tp + 4 :]
    part = lax.axis_index("tp")
    share = mine_ref.shape[1]
    head_ref[:CAP, :] = own_ref[...]
    for i, ref in enumerate((core_ref, near_ref, cross_ref)):
        for q in range(n_tp):
            rows = slice((i + 1) * CAP, (i + 2) * CAP)
            head_ref[rows, q * share : (q + 1) * share] = ref[q * CAP : (q + 1) * CAP, :]
    depth = pl.ds(pl.multiple_of(part * share, CAP), share)
    gate, upper = (
        jnp.dot(head_ref[...], ref[...], preferred_element_type=F32) for ref in (gate_ref, up_ref)
    )
    for weight_ref, sum_ref in zip((gate_ref, up_ref), (gate_sum_ref, up_sum_ref)):
        sum_ref[...] = jnp.dot(mine_ref[...], weight_ref[depth, :], preferred_element_type=F32)
    inner = (gate / (1.0 + jnp.exp(-gate)) * upper).astype(BF16)
    for d in range(n_tp):
        down = columns_of(down_ref, part ^ d, n_tp, share)
        outs[d][...] = jnp.dot(inner, down, preferred_element_type=F32).astype(BF16)


def expert_kernel(n_tp, *refs):
    rows = refs[: n_tp - 1]
    gate_ref, up_ref, down_ref, gate_sum_ref, up_sum_ref = refs[n_tp - 1 : n_tp + 4]
    outs = refs[n_tp + 4 :]
    part = lax.axis_index("tp")
    share = rows[0].shape[1]
    gate = gate_sum_ref[...]
    upper = up_sum_ref[...]
    for d, ref in zip(partners(n_tp), rows):
        value = ref[...]
        depth = pl.ds(pl.multiple_of((part ^ d) * share, CAP), share)
        gate = gate + jnp.dot(value, gate_ref[depth, :], preferred_element_type=F32)
        upper = upper + jnp.dot(value, up_ref[depth, :], preferred_element_type=F32)
    far = (gate / (1.0 + jnp.exp(-gate)) * upper).astype(BF16)
    count = far.shape[0]
    groups = [
        far[start : start + CAP]
        for at in range(0, count // 2, CAP)
        for start in (at, count // 2 + at)
    ]
    inner = jnp.concatenate(groups, axis=0)
    for d in range(n_tp):
        down = columns_of(down_ref, part ^ d, n_tp, share)
        outs[d][...] = jnp.dot(inner, down, preferred_element_type=F32).astype(BF16)


def sum_kernel(n_tp, *refs):
    parts, outs = refs[:n_tp], refs[n_tp:]
    at = 0
    for out in outs:
        rows = slice(at, at + out.shape[0])
        total = parts[0][rows, :].astype(F32)
        for other in parts[1:]:
            total = total + other[rows, :].astype(F32)
        out[...] = total.astype(BF16)
        at += out.shape[0]


def seats_kernel(
    n_tp,
    seat_cap,
    owners_ref,
    positions_ref,
    combine_ref,
    hidden_ref,
    rows_ref,
    mix_ref,
    at_ref,
):
    part = lax.axis_index("tp")
    tokens, width = hidden_ref.shape
    source_rows = tokens // n_tp
    owners = owners_ref[...] ^ part
    owner = lax.broadcasted_iota(jnp.int32, (n_tp, tokens), 0)
    hot = jnp.where(owners == owner, 1.0, 0.0)
    first = lax.broadcasted_iota(jnp.int32, (tokens, tokens), 0)
    second = lax.broadcasted_iota(jnp.int32, (tokens, tokens), 1)
    earlier = jnp.where((first < second) & (first // source_rows == second // source_rows), 1.0, 0.0)
    before = jnp.dot(hot.astype(BF16), earlier.astype(BF16), preferred_element_type=F32)
    seat = jnp.sum(before * hot, axis=0, keepdims=True).astype(jnp.int32)
    source = lax.broadcasted_iota(jnp.int32, (1, tokens), 1) // source_rows
    code = owners * (n_tp * seat_cap) + source * seat_cap + seat
    seats = n_tp * seat_cap
    held = lax.broadcasted_iota(jnp.int32, (n_tp * seats, tokens), 0) == code
    pick = jnp.where(held, 1.0, 0.0).astype(BF16)
    mix_ref[...] = lax.dot_general(
        pick, combine_ref[...], (((1,), (1,)), ((), ())), preferred_element_type=F32
    ).astype(BF16)
    place = jnp.where(held[:seats], positions_ref[...].astype(F32), 0.0)
    at_ref[...] = jnp.sum(place, axis=1, keepdims=True)
    hidden = columns_of(hidden_ref, part, n_tp, width // n_tp)
    rows_ref[...] = jnp.dot(pick, hidden, preferred_element_type=F32).astype(BF16)


def cache_kernel(n_z, n_tp, cache_width, *refs):
    near, far, core_ref = refs[:4], refs[4 : n_z + 2], refs[n_z + 2]
    mix_ref, rows_ref, gain_ref, weight_ref = refs[n_z + 3 : n_z + 7]
    outs, back_ref = refs[n_z + 7 : n_z + 7 + n_tp], refs[n_z + 7 + n_tp]
    for d in range(4):
        back_ref[d * CAP : (d + 1) * CAP, :] = near[d][...]
    for d in range(n_z - 2):
        at = (2 * d + 4) * CAP
        back_ref[at : at + CAP, :] = far[d][:CAP, :]
        last = (n_z - 3 - d) * CAP
        back_ref[at + CAP : at + 2 * CAP, :] = core_ref[last : last + CAP, :]
    mixed = jnp.dot(mix_ref[...], back_ref[...], preferred_element_type=F32)
    state = rows_ref[...].astype(F32) + mixed
    square = jnp.sum(state * state, axis=1, keepdims=True)
    scaled = (state * gain_ref[...]).astype(BF16)
    value = lax.dot_general(
        scaled, weight_ref[...], (((1,), (1,)), ((), ())), preferred_element_type=F32
    ).astype(BF16)
    high = square.astype(BF16).astype(F32)
    rest = square - high
    middle = rest.astype(BF16).astype(F32)
    low = rest - middle
    seats, wide = outs[0].shape
    lane = lax.broadcasted_iota(jnp.int32, (square.shape[0], wide - cache_width), 1)
    extra = jnp.where(lane == 0, high, jnp.where(lane == 1, middle, jnp.where(lane == 2, low, 0.0)))
    extra = extra.astype(BF16)
    for d in range(n_tp):
        outs[d][:, :cache_width] = value[d * seats : (d + 1) * seats]
        outs[d][:, cache_width:] = extra[d * seats : (d + 1) * seats]


def finish_kernel(n_tp, width, rank_width, *refs):
    parts = refs[:n_tp]
    gain_ref, cos_ref, sin_ref, latent_ref, rotary_ref = refs[n_tp:]
    total = parts[0][...].astype(F32)
    for other in parts[1:]:
        total = total + other[...].astype(F32)
    half = cos_ref.shape[1]
    cache_width = rank_width + 2 * half
    square = jnp.sum(total[:, cache_width : cache_width + 3], axis=1, keepdims=True)
    cache = total[:, :cache_width] * lax.rsqrt(square / width + EPS)
    latent = cache[:, :rank_width]
    scale = lax.rsqrt(jnp.mean(latent * latent, axis=1, keepdims=True) + EPS)
    latent_ref[...] = (latent * scale * gain_ref[...]).astype(BF16)
    first = cache[:, rank_width : rank_width + half]
    second = cache[:, rank_width + half :]
    cosine, sine = cos_ref[...], sin_ref[...]
    rotary_ref[:, :half] = (first * cosine - second * sine).astype(BF16)
    rotary_ref[:, half:] = (second * cosine + first * sine).astype(BF16)


def call(kernel, out_shape, args, scratch=(), flops=0, hbm=()):
    moved = sum(a.size * a.dtype.itemsize for a in args)
    vmem = pl.BlockSpec(memory_space=pltpu.VMEM)
    args = [
        pltpu.with_memory_space_constraint(a, pltpu.HBM) if i in hbm else a
        for i, a in enumerate(args)
    ]
    return pl.pallas_call(
        kernel,
        out_shape=out_shape,
        in_specs=[
            pl.BlockSpec(memory_space=pltpu.HBM) if i in hbm else vmem for i in range(len(args))
        ],
        out_specs=[vmem] * len(out_shape),
        scratch_shapes=list(scratch),
        compiler_params=pltpu.CompilerParams(vmem_limit_bytes=VMEM_LIMIT),
        cost_estimate=pl.CostEstimate(flops=flops, bytes_accessed=moved, transcendentals=0),
    )(*args)


def swap(value, axis, d):
    return lax.ppermute(value, axis, [(i, i ^ d) for i in range(lax.axis_size(axis))])


def partners(n_tp):
    return [*range(n_tp // 2, n_tp), *range(1, n_tp // 2)]


def spread(value, n_tp):
    return [swap(value, "tp", d) for d in partners(n_tp)]


def collect(values):
    return [swap(values[d], "tp", d) for d in partners(len(values))] + [values[0]]


def on_device(
    hidden,
    moe_gain,
    route_logits,
    routes,
    gate_weight,
    up_weight,
    down_weight,
    attn_gain,
    latent_weight,
    latent_gain,
    positions,
    owners,
):
    n_ep = lax.axis_size("ep")
    n_tp = lax.axis_size("tp")
    n_z = n_ep // 2
    tokens, width = hidden.shape
    share = width // n_tp
    ff = gate_weight.shape[2]
    slots = n_ep * CAP
    seat_cap = max(2, tokens // n_tp // 4)
    seats = n_tp * seat_cap
    rank_width = latent_gain.shape[0]
    cache_width = latent_weight.shape[1]
    half = (cache_width - rank_width) // 2
    wide = (cache_width + 3 + 127) // 128 * 128
    struct = jax.ShapeDtypeStruct
    chunks = width // 512 if width % 512 == 0 else 1

    *outgoing, pick, combine, hidden, gain = call(
        functools.partial(dispatch_kernel, n_ep, n_tp),
        [struct((CAP, share), BF16)] * (n_ep - 4)
        + [struct((slots, tokens), BF16)] * 2
        + [struct(hidden.shape, BF16), struct((1, width), F32)],
        (routes.T, route_logits.T, hidden, moe_gain),
        [
            pltpu.VMEM(routes.T.shape, jnp.int32),
            pltpu.VMEM(routes.T.shape, F32),
            pltpu.SemaphoreType.DMA((3 + chunks,)),
        ],
        flops=2 * slots * tokens * width,
        hbm=(0, 1, 2, 3),
    )
    own, to_core, to_near = call(
        functools.partial(near_kernel, n_tp),
        [struct((CAP, width), BF16), struct((n_tp * CAP, share), BF16)]
        + [struct((2 * n_tp * CAP, share), BF16)],
        (pick, hidden, gain),
        flops=8 * CAP * tokens * width,
    )
    order = [*range(4, n_ep, 2), *range(5, n_ep, 2)]
    arrived = [swap(outgoing[d - 4], "ep", d) for d in order]
    near = swap(to_near[: n_tp * CAP], "ep", 2)
    near_crossed = swap(to_near[n_tp * CAP :], "ep", 3)
    from_core = swap(to_core, "ep", 1)
    gate_w, up_w, down_w = gate_weight[0], up_weight[0], down_weight[0]
    *loaded, mark = call(
        load_kernel,
        [struct(w.shape, BF16) for w in (gate_w, up_w, down_w)] + [struct((8, 128), F32)],
        (combine, gate_w, up_w, down_w),
        [pltpu.SemaphoreType.DMA((3,))],
        hbm=(1, 2, 3),
    )
    arrived, from_core = lax.optimization_barrier((arrived, from_core))
    mine = jnp.concatenate(arrived, axis=0)
    shares = spread(mine, n_tp)
    near_rows, far_rows = 4 * CAP, slots - 4 * CAP
    *near_pieces, gate_sum, up_sum = call(
        functools.partial(first_kernel, n_tp),
        [struct((near_rows, share), BF16)] * n_tp + [struct((far_rows, ff), F32)] * 2,
        (own, from_core, near, near_crossed, mine, *loaded, mark),
        [pltpu.VMEM((4 * CAP, width), BF16)],
        flops=2 * slots * width * ff,
    )
    terms = call(
        functools.partial(expert_kernel, n_tp),
        [struct((far_rows, share), BF16)] * n_tp,
        (*shares, *loaded, gate_sum, up_sum),
        flops=2 * slots * width * ff * 3,
    )
    terms = list(terms)
    combine, terms[0] = lax.optimization_barrier((combine, terms[0]))
    rows, mix, at = call(
        functools.partial(seats_kernel, n_tp, seat_cap),
        [
            struct((n_tp * seats, share), BF16),
            struct((n_tp * seats, slots), BF16),
            struct((seats, 1), F32),
        ],
        (owners[None, :], positions[None, :], combine, hidden),
        flops=2 * n_tp * seats * tokens * (share + slots),
    )
    near_pieces, rows, mix = lax.optimization_barrier((near_pieces, rows, mix))
    freqs = ROPE_BASE ** (-jnp.arange(half, dtype=F32) / half)
    angles = at * freqs[None, :]
    cosine, sine = jnp.cos(angles), jnp.sin(angles)

    far_terms = collect(terms)
    near_terms = collect(near_pieces)
    far_done = call(
        functools.partial(sum_kernel, n_tp),
        [struct((2 * CAP, share), BF16)] * (n_z - 2),
        far_terms,
    )
    far_back = [swap(far_done[d - 2], "ep", 2 * d) for d in range(2, n_z)]
    near_done = call(
        functools.partial(sum_kernel, n_tp), [struct((CAP, share), BF16)] * 4, near_terms
    )
    near_back = [near_done[0]] + [swap(near_done[d], "ep", d) for d in (1, 2, 3)]
    crossed = swap(jnp.concatenate([piece[CAP:] for piece in far_back[::-1]], axis=0), "ep", 1)
    partial = call(
        functools.partial(cache_kernel, n_z, n_tp, cache_width),
        [struct((seats, wide), BF16)] * n_tp,
        (*near_back, *far_back, crossed, mix, rows, attn_gain[None, :], latent_weight.T),
        [pltpu.VMEM((slots, share), BF16)],
        flops=2 * n_tp * seats * share * (slots + cache_width),
    )
    return tuple(
        call(
            functools.partial(finish_kernel, n_tp, width, rank_width),
            [struct((seats, rank_width), BF16), struct((seats, 2 * half), BF16)],
            (*collect(partial), latent_gain[None, :], cosine, sine),
        )
    )


def solution(mesh):
    placed = (
        P(("groups", "ep"), None),
        P(),
        P(("groups", "ep"), None),
        P(("groups", "ep"), None),
        P("ep", None, "tp"),
        P("ep", None, "tp"),
        P("ep", "tp", None),
        P("tp"),
        P("tp", None),
        P(),
        P(("groups", "ep")),
        P(("groups", "ep")),
    )
    return jax.shard_map(
        on_device,
        mesh=mesh,
        in_specs=placed,
        out_specs=(P(("groups", "ep", "tp"), None), P(("groups", "ep", "tp"), None)),
        check_vma=False,
    )
```

```python
import functools

import jax
import jax.numpy as jnp
from jax import lax
from jax.experimental import pallas as pl
from jax.experimental.pallas import tpu as pltpu
from jax.sharding import PartitionSpec as P

CAP = 16
EPS = 1e-06
ROUTE_SCALE = 2.5
ROPE_BASE = 10000.0
BF16 = jnp.bfloat16
F32 = jnp.float32
VMEM_LIMIT = 40 * 1024 * 1024


def columns_of(ref, index, count, share):
    if share % 128 == 0:
        return ref[:, pl.ds(pl.multiple_of(index * share, 128), share)]
    out = ref[:, 0:share]
    for q in range(1, count):
        out = jnp.where(index == q, ref[:, q * share : (q + 1) * share], out)
    return out


def dispatch_kernel(n_ep, n_tp, order, routes_hbm, logits_hbm, hidden_hbm, gain_hbm, *refs):
    outs = refs[: len(order)]
    pick_ref, combine_ref, hidden_ref, gain_ref = refs[len(order) : len(order) + 4]
    whole, (routes_ref, logits_ref, sems) = refs[len(order) + 4 : -3], refs[-3:]
    me = lax.axis_index("ep")
    part = lax.axis_index("tp")
    tokens, width = hidden_ref.shape
    share = width // n_tp
    step = 512 if width % 512 == 0 else width
    starts = range(0, width, step)
    small = [
        pltpu.make_async_copy(routes_hbm, routes_ref, sems.at[0]),
        pltpu.make_async_copy(logits_hbm, logits_ref, sems.at[1]),
        pltpu.make_async_copy(gain_hbm, gain_ref.at[0], sems.at[2]),
    ]
    large = [
        pltpu.make_async_copy(
            hidden_hbm.at[:, c : c + step], hidden_ref.at[:, c : c + step], sems.at[3 + i]
        )
        for i, c in enumerate(starts)
    ]
    for copy in small + large:
        copy.start()
    small[0].wait()
    small[1].wait()
    routes = routes_ref[...]
    affinity = jax.nn.sigmoid(logits_ref[...])
    weight = ROUTE_SCALE * affinity / jnp.sum(affinity, axis=0, keepdims=True)
    weight = weight.astype(BF16).astype(F32)
    expert = lax.broadcasted_iota(jnp.int32, (n_ep, tokens), 0) ^ me
    hit = jnp.zeros((n_ep, tokens), F32)
    gain_of = jnp.zeros((n_ep, tokens), F32)
    for k in range(routes.shape[0]):
        same = routes[k : k + 1, :] == expert
        hit = jnp.where(same, 1.0, hit)
        gain_of = jnp.where(same, weight[k : k + 1, :], gain_of)
    earlier = lax.broadcasted_iota(jnp.int32, (tokens, tokens), 0) < lax.broadcasted_iota(
        jnp.int32, (tokens, tokens), 1
    )
    rank = jnp.dot(hit.astype(BF16), earlier.astype(F32).astype(BF16), preferred_element_type=F32)
    rank = jnp.where(hit > 0, rank, -1.0)
    place = lax.broadcasted_iota(jnp.int32, (CAP, tokens), 0).astype(F32)
    for d in range(n_ep):
        match = rank[d : d + 1, :] == place
        rows = slice(d * CAP, (d + 1) * CAP)
        pick_ref[rows, :] = jnp.where(match, 1.0, 0.0).astype(BF16)
        combine_ref[rows, :] = jnp.where(match, gain_of[d : d + 1, :], 0.0).astype(BF16)
    pick = pick_ref[4 * CAP :, :]
    square = jnp.zeros((pick.shape[0], 1), F32)
    middle = len(large) // 2
    for i, c in enumerate(starts):
        if i == 0 or i == middle:
            for copy in large[:middle] if i < middle else large[i:]:
                copy.wait()
        got = jnp.dot(pick, hidden_ref[:, c : c + step], preferred_element_type=F32)
        square = square + jnp.sum(got * got, axis=1, keepdims=True)
    small[2].wait()
    scale = lax.rsqrt(square / width + EPS)
    got = jnp.dot(pick, columns_of(hidden_ref, part, n_tp, share), preferred_element_type=F32)
    rows = (got * scale * columns_of(gain_ref, part, n_tp, share)).astype(BF16)
    for d, out in zip(order, outs):
        out[...] = rows[(d - 4) * CAP : (d - 3) * CAP]
    whole_rows(n_tp, pick_ref, hidden_ref, gain_ref, *whole)


def whole_rows(n_tp, pick_ref, hidden_ref, gain_ref, own_ref, core_ref, *outs):
    share = hidden_ref.shape[1] // n_tp
    pick = jnp.concatenate([pick_ref[: 4 * CAP, :], pick_ref[5 * CAP : 6 * CAP, :]], axis=0)
    got = jnp.dot(pick, hidden_ref[...], preferred_element_type=F32)
    scale = lax.rsqrt(jnp.mean(got * got, axis=1, keepdims=True) + EPS)
    whole = (got * scale * gain_ref[...]).astype(BF16)
    own_ref[...] = whole[:CAP]
    for i, out in enumerate((core_ref, *outs)):
        for q in range(n_tp):
            columns = slice(q * share, (q + 1) * share)
            out[q * CAP : (q + 1) * CAP, :] = whole[(i + 1) * CAP : (i + 2) * CAP, columns]


def load_kernel(after_ref, *refs):
    count = (len(refs) - 2) // 2
    mark_ref, sems = refs[-2:]
    copies = [
        pltpu.make_async_copy(refs[i], refs[count + i], sems.at[i]) for i in range(count)
    ]
    for copy in copies:
        copy.start()
    mark_ref[...] = jnp.zeros(mark_ref.shape, F32)
    for copy in copies:
        copy.wait()


def first_kernel(n_tp, own_ref, core_ref, near_ref, wide_ref, cross_ref, mine_ref, *refs):
    gate_ref, up_ref, down_ref, _ = refs[:4]
    outs, (wide_inner_ref, gate_sum_ref, up_sum_ref, head_ref) = refs[4 : n_tp + 4], refs[n_tp + 4 :]
    part = lax.axis_index("tp")
    share = mine_ref.shape[1]
    head_ref[:CAP, :] = own_ref[...]
    for i, ref in enumerate((core_ref, near_ref, cross_ref, wide_ref)):
        for q in range(n_tp):
            rows = slice((i + 1) * CAP, (i + 2) * CAP)
            head_ref[rows, q * share : (q + 1) * share] = ref[q * CAP : (q + 1) * CAP, :]
    depth = pl.ds(pl.multiple_of(part * share, CAP), share)
    gate, upper = (
        jnp.dot(head_ref[...], ref[...], preferred_element_type=F32) for ref in (gate_ref, up_ref)
    )
    for weight_ref, sum_ref in zip((gate_ref, up_ref), (gate_sum_ref, up_sum_ref)):
        sum_ref[...] = jnp.dot(mine_ref[...], weight_ref[depth, :], preferred_element_type=F32)
    inner = (gate / (1.0 + jnp.exp(-gate)) * upper).astype(BF16)
    wide_inner_ref[...] = inner[4 * CAP :]
    inner = inner[: 4 * CAP]
    for d in range(n_tp):
        down = columns_of(down_ref, part ^ d, n_tp, share)
        outs[d][...] = jnp.dot(inner, down, preferred_element_type=F32).astype(BF16)


def expert_kernel(n_tp, order, *refs):
    rows = refs[: n_tp - 1]
    gate_ref, up_ref, down_ref, wide_ref, gate_sum_ref, up_sum_ref = refs[n_tp - 1 : n_tp + 5]
    outs = refs[n_tp + 5 :]
    part = lax.axis_index("tp")
    share = rows[0].shape[1]
    gate = gate_sum_ref[...]
    upper = up_sum_ref[...]
    for d in range(1, n_tp):
        value = rows[n_tp - 1 - d][...]
        depth = pl.ds(pl.multiple_of((part ^ d) * share, CAP), share)
        gate = gate + jnp.dot(value, gate_ref[depth, :], preferred_element_type=F32)
        upper = upper + jnp.dot(value, up_ref[depth, :], preferred_element_type=F32)
    far = (gate / (1.0 + jnp.exp(-gate)) * upper).astype(BF16)
    groups = {d: far[i * CAP : (i + 1) * CAP] for i, d in enumerate(order)}
    groups[5] = wide_ref[...]
    inner = jnp.concatenate([groups[d] for d in sorted(groups)], axis=0)
    for d in range(n_tp):
        down = columns_of(down_ref, part ^ d, n_tp, share)
        outs[d][...] = jnp.dot(inner, down, preferred_element_type=F32).astype(BF16)


def sum_kernel(n_tp, *refs):
    parts, outs = refs[:n_tp], refs[n_tp:]
    at = 0
    for out in outs:
        rows = slice(at, at + out.shape[0])
        total = parts[0][rows, :].astype(F32)
        for other in parts[1:]:
            total = total + other[rows, :].astype(F32)
        out[...] = total.astype(BF16)
        at += out.shape[0]


def seats_kernel(
    n_tp,
    seat_cap,
    owners_ref,
    positions_ref,
    combine_ref,
    hidden_ref,
    rows_ref,
    mix_ref,
    at_ref,
):
    part = lax.axis_index("tp")
    tokens, width = hidden_ref.shape
    source_rows = tokens // n_tp
    owners = owners_ref[...] ^ part
    owner = lax.broadcasted_iota(jnp.int32, (n_tp, tokens), 0)
    hot = jnp.where(owners == owner, 1.0, 0.0)
    first = lax.broadcasted_iota(jnp.int32, (tokens, tokens), 0)
    second = lax.broadcasted_iota(jnp.int32, (tokens, tokens), 1)
    earlier = jnp.where((first < second) & (first // source_rows == second // source_rows), 1.0, 0.0)
    before = jnp.dot(hot.astype(BF16), earlier.astype(BF16), preferred_element_type=F32)
    seat = jnp.sum(before * hot, axis=0, keepdims=True).astype(jnp.int32)
    source = lax.broadcasted_iota(jnp.int32, (1, tokens), 1) // source_rows
    code = owners * (n_tp * seat_cap) + source * seat_cap + seat
    seats = n_tp * seat_cap
    held = lax.broadcasted_iota(jnp.int32, (n_tp * seats, tokens), 0) == code
    pick = jnp.where(held, 1.0, 0.0).astype(BF16)
    mix_ref[...] = lax.dot_general(
        pick, combine_ref[...], (((1,), (1,)), ((), ())), preferred_element_type=F32
    ).astype(BF16)
    place = jnp.where(held[:seats], positions_ref[...].astype(F32), 0.0)
    at_ref[...] = jnp.sum(place, axis=1, keepdims=True)
    hidden = columns_of(hidden_ref, part, n_tp, width // n_tp)
    rows_ref[...] = jnp.dot(pick, hidden, preferred_element_type=F32).astype(BF16)


def cache_kernel(n_z, n_tp, cache_width, *refs):
    near, far, core_ref = refs[:4], refs[4 : n_z + 2], refs[n_z + 2]
    mix_ref, rows_ref, gain_ref, weight_ref = refs[n_z + 3 : n_z + 7]
    outs, back_ref = refs[n_z + 7 : n_z + 7 + n_tp], refs[n_z + 7 + n_tp]
    for d in range(4):
        back_ref[d * CAP : (d + 1) * CAP, :] = near[d][...]
    for d in range(n_z - 2):
        at = (2 * d + 4) * CAP
        back_ref[at : at + CAP, :] = far[d][:CAP, :]
        last = (n_z - 3 - d) * CAP
        back_ref[at + CAP : at + 2 * CAP, :] = core_ref[last : last + CAP, :]
    mixed = jnp.dot(mix_ref[...], back_ref[...], preferred_element_type=F32)
    state = rows_ref[...].astype(F32) + mixed
    square = jnp.sum(state * state, axis=1, keepdims=True)
    scaled = (state * gain_ref[...]).astype(BF16)
    value = lax.dot_general(
        scaled, weight_ref[...], (((1,), (1,)), ((), ())), preferred_element_type=F32
    ).astype(BF16)
    high = square.astype(BF16).astype(F32)
    rest = square - high
    middle = rest.astype(BF16).astype(F32)
    low = rest - middle
    seats, wide = outs[0].shape
    lane = lax.broadcasted_iota(jnp.int32, (square.shape[0], wide - cache_width), 1)
    extra = jnp.where(lane == 0, high, jnp.where(lane == 1, middle, jnp.where(lane == 2, low, 0.0)))
    extra = extra.astype(BF16)
    for d in range(n_tp):
        outs[d][:, :cache_width] = value[d * seats : (d + 1) * seats]
        outs[d][:, cache_width:] = extra[d * seats : (d + 1) * seats]


def finish_kernel(n_tp, width, rank_width, *refs):
    parts = refs[:n_tp]
    gain_ref, cos_ref, sin_ref, latent_ref, rotary_ref = refs[n_tp:]
    total = parts[0][...].astype(F32)
    for other in parts[1:]:
        total = total + other[...].astype(F32)
    half = cos_ref.shape[1]
    cache_width = rank_width + 2 * half
    square = jnp.sum(total[:, cache_width : cache_width + 3], axis=1, keepdims=True)
    cache = total[:, :cache_width] * lax.rsqrt(square / width + EPS)
    latent = cache[:, :rank_width]
    scale = lax.rsqrt(jnp.mean(latent * latent, axis=1, keepdims=True) + EPS)
    latent_ref[...] = (latent * scale * gain_ref[...]).astype(BF16)
    first = cache[:, rank_width : rank_width + half]
    second = cache[:, rank_width + half :]
    cosine, sine = cos_ref[...], sin_ref[...]
    rotary_ref[:, :half] = (first * cosine - second * sine).astype(BF16)
    rotary_ref[:, half:] = (second * cosine + first * sine).astype(BF16)


def call(kernel, out_shape, args, scratch=(), flops=0, hbm=()):
    moved = sum(a.size * a.dtype.itemsize for a in args)
    vmem = pl.BlockSpec(memory_space=pltpu.VMEM)
    args = [
        pltpu.with_memory_space_constraint(a, pltpu.HBM) if i in hbm else a
        for i, a in enumerate(args)
    ]
    return pl.pallas_call(
        kernel,
        out_shape=out_shape,
        in_specs=[
            pl.BlockSpec(memory_space=pltpu.HBM) if i in hbm else vmem for i in range(len(args))
        ],
        out_specs=[vmem] * len(out_shape),
        scratch_shapes=list(scratch),
        compiler_params=pltpu.CompilerParams(vmem_limit_bytes=VMEM_LIMIT),
        cost_estimate=pl.CostEstimate(flops=flops, bytes_accessed=moved, transcendentals=0),
    )(*args)


def swap(value, axis, d):
    return lax.ppermute(value, axis, [(i, i ^ d) for i in range(lax.axis_size(axis))])


def spread(value, n_tp):
    return [swap(value, "tp", d) for d in reversed(range(1, n_tp))]


def collect(values):
    return [swap(values[d], "tp", d) for d in reversed(range(1, len(values)))] + [values[0]]


def on_device(
    hidden,
    moe_gain,
    route_logits,
    routes,
    gate_weight,
    up_weight,
    down_weight,
    attn_gain,
    latent_weight,
    latent_gain,
    positions,
    owners,
):
    n_ep = lax.axis_size("ep")
    n_tp = lax.axis_size("tp")
    n_z = n_ep // 2
    tokens, width = hidden.shape
    share = width // n_tp
    ff = gate_weight.shape[2]
    slots = n_ep * CAP
    seat_cap = max(2, tokens // n_tp // 4)
    seats = n_tp * seat_cap
    rank_width = latent_gain.shape[0]
    cache_width = latent_weight.shape[1]
    half = (cache_width - rank_width) // 2
    wide = (cache_width + 3 + 127) // 128 * 128
    struct = jax.ShapeDtypeStruct
    chunks = width // 512 if width % 512 == 0 else 1

    order = [*range(4, n_ep, 2), *range(7, n_ep, 2)]
    *outgoing, _, combine, hidden, _, own, to_core, to_near, to_cross, to_wide = call(
        functools.partial(dispatch_kernel, n_ep, n_tp, order),
        [struct((CAP, share), BF16)] * len(order)
        + [struct((slots, tokens), BF16)] * 2
        + [struct(hidden.shape, BF16), struct((1, width), F32), struct((CAP, width), BF16)]
        + [struct((n_tp * CAP, share), BF16)] * 4,
        (routes.T, route_logits.T, hidden, moe_gain),
        [
            pltpu.VMEM(routes.T.shape, jnp.int32),
            pltpu.VMEM(routes.T.shape, F32),
            pltpu.SemaphoreType.DMA((3 + chunks,)),
        ],
        flops=4 * slots * tokens * width,
        hbm=(0, 1, 2, 3),
    )
    arrived = [swap(piece, "ep", d) for d, piece in zip(order, outgoing)]
    wide_rows = swap(to_wide, "ep", 5)
    near = swap(to_near, "ep", 2)
    near_crossed = swap(to_cross, "ep", 3)
    from_core = swap(to_core, "ep", 1)
    gate_w, up_w, down_w = gate_weight[0], up_weight[0], down_weight[0]
    *loaded, mark = call(
        load_kernel,
        [struct(w.shape, BF16) for w in (gate_w, up_w, down_w)] + [struct((8, 128), F32)],
        (combine, gate_w, up_w, down_w),
        [pltpu.SemaphoreType.DMA((3,))],
        hbm=(1, 2, 3),
    )
    arrived, from_core = lax.optimization_barrier((arrived, from_core))
    mine = jnp.concatenate(arrived, axis=0)
    shares = spread(mine, n_tp)
    near_rows, far_rows = 4 * CAP, slots - 4 * CAP
    *near_pieces, wide_inner, gate_sum, up_sum = call(
        functools.partial(first_kernel, n_tp),
        [struct((near_rows, share), BF16)] * n_tp
        + [struct((CAP, ff), BF16)]
        + [struct((len(order) * CAP, ff), F32)] * 2,
        (own, from_core, near, wide_rows, near_crossed, mine, *loaded, mark),
        [pltpu.VMEM((5 * CAP, width), BF16)],
        flops=2 * slots * width * ff,
    )
    terms = call(
        functools.partial(expert_kernel, n_tp, order),
        [struct((far_rows, share), BF16)] * n_tp,
        (*shares, *loaded, wide_inner, gate_sum, up_sum),
        flops=2 * slots * width * ff * 3,
    )
    terms = list(terms)
    combine, terms[0] = lax.optimization_barrier((combine, terms[0]))
    rows, mix, at = call(
        functools.partial(seats_kernel, n_tp, seat_cap),
        [
            struct((n_tp * seats, share), BF16),
            struct((n_tp * seats, slots), BF16),
            struct((seats, 1), F32),
        ],
        (owners[None, :], positions[None, :], combine, hidden),
        flops=2 * n_tp * seats * tokens * (share + slots),
    )
    near_pieces, rows, mix = lax.optimization_barrier((near_pieces, rows, mix))
    freqs = ROPE_BASE ** (-jnp.arange(half, dtype=F32) / half)
    angles = at * freqs[None, :]
    cosine, sine = jnp.cos(angles), jnp.sin(angles)

    far_terms = collect(terms)
    near_terms = collect(near_pieces)
    far_done = call(
        functools.partial(sum_kernel, n_tp),
        [struct((2 * CAP, share), BF16)] * (n_z - 2),
        far_terms,
    )
    far_back = [swap(far_done[d - 2], "ep", 2 * d) for d in range(2, n_z)]
    near_done = call(
        functools.partial(sum_kernel, n_tp), [struct((CAP, share), BF16)] * 4, near_terms
    )
    near_back = [near_done[0]] + [swap(near_done[d], "ep", d) for d in (1, 2, 3)]
    crossed = swap(jnp.concatenate([piece[CAP:] for piece in far_back[::-1]], axis=0), "ep", 1)
    partial = call(
        functools.partial(cache_kernel, n_z, n_tp, cache_width),
        [struct((seats, wide), BF16)] * n_tp,
        (*near_back, *far_back, crossed, mix, rows, attn_gain[None, :], latent_weight.T),
        [pltpu.VMEM((slots, share), BF16)],
        flops=2 * n_tp * seats * share * (slots + cache_width),
    )
    return tuple(
        call(
            functools.partial(finish_kernel, n_tp, width, rank_width),
            [struct((seats, rank_width), BF16), struct((seats, 2 * half), BF16)],
            (*collect(partial), latent_gain[None, :], cosine, sine),
        )
    )


def solution(mesh):
    placed = (
        P(("groups", "ep"), None),
        P(),
        P(("groups", "ep"), None),
        P(("groups", "ep"), None),
        P("ep", None, "tp"),
        P("ep", None, "tp"),
        P("ep", "tp", None),
        P("tp"),
        P("tp", None),
        P(),
        P(("groups", "ep")),
        P(("groups", "ep")),
    )
    return jax.shard_map(
        on_device,
        mesh=mesh,
        in_specs=placed,
        out_specs=(P(("groups", "ep", "tp"), None), P(("groups", "ep", "tp"), None)),
        check_vma=False,
    )
```

```python
import functools

import jax
import jax.numpy as jnp
from jax import lax
from jax.experimental import pallas as pl
from jax.experimental.pallas import tpu as pltpu
from jax.sharding import PartitionSpec as P

CAP = 16
EPS = 1e-06
ROUTE_SCALE = 2.5
ROPE_BASE = 10000.0
BF16 = jnp.bfloat16
F32 = jnp.float32
VMEM_LIMIT = 40 * 1024 * 1024


def columns_of(ref, index, count, share):
    if share % 128 == 0:
        return ref[:, pl.ds(pl.multiple_of(index * share, 128), share)]
    out = ref[:, 0:share]
    for q in range(1, count):
        out = jnp.where(index == q, ref[:, q * share : (q + 1) * share], out)
    return out


def dispatch_kernel(n_ep, n_tp, routes_hbm, logits_hbm, hidden_hbm, gain_hbm, *refs):
    outs = refs[: n_ep - 4]
    pick_ref, combine_ref, hidden_ref, gain_ref, routes_ref, logits_ref, sems = refs[n_ep - 4 :]
    me = lax.axis_index("ep")
    part = lax.axis_index("tp")
    tokens, width = hidden_ref.shape
    share = width // n_tp
    step = 512 if width % 512 == 0 else width
    starts = range(0, width, step)
    small = [
        pltpu.make_async_copy(routes_hbm, routes_ref, sems.at[0]),
        pltpu.make_async_copy(logits_hbm, logits_ref, sems.at[1]),
        pltpu.make_async_copy(gain_hbm, gain_ref.at[0], sems.at[2]),
    ]
    large = [
        pltpu.make_async_copy(
            hidden_hbm.at[:, c : c + step], hidden_ref.at[:, c : c + step], sems.at[3 + i]
        )
        for i, c in enumerate(starts)
    ]
    for copy in small + large:
        copy.start()
    small[0].wait()
    small[1].wait()
    routes = routes_ref[...]
    affinity = jax.nn.sigmoid(logits_ref[...])
    weight = ROUTE_SCALE * affinity / jnp.sum(affinity, axis=0, keepdims=True)
    weight = weight.astype(BF16).astype(F32)
    expert = lax.broadcasted_iota(jnp.int32, (n_ep, tokens), 0) ^ me
    hit = jnp.zeros((n_ep, tokens), F32)
    gain_of = jnp.zeros((n_ep, tokens), F32)
    for k in range(routes.shape[0]):
        same = routes[k : k + 1, :] == expert
        hit = jnp.where(same, 1.0, hit)
        gain_of = jnp.where(same, weight[k : k + 1, :], gain_of)
    earlier = lax.broadcasted_iota(jnp.int32, (tokens, tokens), 0) < lax.broadcasted_iota(
        jnp.int32, (tokens, tokens), 1
    )
    rank = jnp.dot(hit.astype(BF16), earlier.astype(F32).astype(BF16), preferred_element_type=F32)
    rank = jnp.where(hit > 0, rank, -1.0)
    place = lax.broadcasted_iota(jnp.int32, (CAP, tokens), 0).astype(F32)
    for d in range(n_ep):
        match = rank[d : d + 1, :] == place
        rows = slice(d * CAP, (d + 1) * CAP)
        pick_ref[rows, :] = jnp.where(match, 1.0, 0.0).astype(BF16)
        combine_ref[rows, :] = jnp.where(match, gain_of[d : d + 1, :], 0.0).astype(BF16)
    pick = pick_ref[4 * CAP :, :]
    square = jnp.zeros((pick.shape[0], 1), F32)
    middle = len(large) // 2
    for i, c in enumerate(starts):
        if i == 0 or i == middle:
            for copy in large[:middle] if i < middle else large[i:]:
                copy.wait()
        got = jnp.dot(pick, hidden_ref[:, c : c + step], preferred_element_type=F32)
        square = square + jnp.sum(got * got, axis=1, keepdims=True)
    small[2].wait()
    scale = lax.rsqrt(square / width + EPS)
    got = jnp.dot(pick, columns_of(hidden_ref, part, n_tp, share), preferred_element_type=F32)
    rows = (got * scale * columns_of(gain_ref, part, n_tp, share)).astype(BF16)
    for i, out in enumerate(outs):
        out[...] = rows[i * CAP : (i + 1) * CAP]


def near_kernel(n_tp, pick_ref, hidden_ref, gain_ref, own_ref, core_ref, near_ref):
    share = hidden_ref.shape[1] // n_tp
    got = jnp.dot(pick_ref[: 4 * CAP, :], hidden_ref[...], preferred_element_type=F32)
    scale = lax.rsqrt(jnp.mean(got * got, axis=1, keepdims=True) + EPS)
    whole = (got * scale * gain_ref[...]).astype(BF16)
    own_ref[...] = whole[:CAP]
    for q in range(n_tp):
        columns = slice(q * share, (q + 1) * share)
        core_ref[q * CAP : (q + 1) * CAP, :] = whole[CAP : 2 * CAP, columns]
        near_ref[q * CAP : (q + 1) * CAP, :] = whole[2 * CAP : 3 * CAP, columns]
        near_ref[(n_tp + q) * CAP : (n_tp + q + 1) * CAP, :] = whole[3 * CAP :, columns]


def load_kernel(after_ref, *refs):
    count = (len(refs) - 2) // 2
    mark_ref, sems = refs[-2:]
    copies = [
        pltpu.make_async_copy(refs[i], refs[count + i], sems.at[i]) for i in range(count)
    ]
    for copy in copies:
        copy.start()
    mark_ref[...] = jnp.zeros(mark_ref.shape, F32)
    for copy in copies:
        copy.wait()


def first_kernel(n_tp, own_ref, core_ref, near_ref, cross_ref, mine_ref, *refs):
    gate_ref, up_ref, down_ref, _ = refs[:4]
    outs, (gate_sum_ref, up_sum_ref, head_ref) = refs[4 : n_tp + 4], refs[n_tp + 4 :]
    part = lax.axis_index("tp")
    share = mine_ref.shape[1]
    head_ref[:CAP, :] = own_ref[...]
    for i, ref in enumerate((core_ref, near_ref, cross_ref)):
        for q in range(n_tp):
            rows = slice((i + 1) * CAP, (i + 2) * CAP)
            head_ref[rows, q * share : (q + 1) * share] = ref[q * CAP : (q + 1) * CAP, :]
    depth = pl.ds(pl.multiple_of(part * share, CAP), share)
    gate, upper = (
        jnp.dot(head_ref[...], ref[...], preferred_element_type=F32) for ref in (gate_ref, up_ref)
    )
    for weight_ref, sum_ref in zip((gate_ref, up_ref), (gate_sum_ref, up_sum_ref)):
        sum_ref[...] = jnp.dot(mine_ref[...], weight_ref[depth, :], preferred_element_type=F32)
    inner = (gate / (1.0 + jnp.exp(-gate)) * upper).astype(BF16)
    for d in range(n_tp):
        down = columns_of(down_ref, part ^ d, n_tp, share)
        outs[d][...] = jnp.dot(inner, down, preferred_element_type=F32).astype(BF16)


def expert_kernel(n_tp, *refs):
    rows = refs[: n_tp - 1]
    gate_ref, up_ref, down_ref, gate_sum_ref, up_sum_ref = refs[n_tp - 1 : n_tp + 4]
    outs = refs[n_tp + 4 :]
    part = lax.axis_index("tp")
    share = rows[0].shape[1]
    gate = gate_sum_ref[...]
    upper = up_sum_ref[...]
    for d in range(1, n_tp):
        value = rows[n_tp - 1 - d][...]
        depth = pl.ds(pl.multiple_of((part ^ d) * share, CAP), share)
        gate = gate + jnp.dot(value, gate_ref[depth, :], preferred_element_type=F32)
        upper = upper + jnp.dot(value, up_ref[depth, :], preferred_element_type=F32)
    far = (gate / (1.0 + jnp.exp(-gate)) * upper).astype(BF16)
    count = far.shape[0]
    groups = [
        far[start : start + CAP]
        for at in range(0, count // 2, CAP)
        for start in (at, count // 2 + at)
    ]
    inner = jnp.concatenate(groups, axis=0)
    for d in range(n_tp):
        down = columns_of(down_ref, part ^ d, n_tp, share)
        outs[d][...] = jnp.dot(inner, down, preferred_element_type=F32).astype(BF16)


def sum_kernel(n_tp, *refs):
    parts, outs = refs[:n_tp], refs[n_tp:]
    at = 0
    for out in outs:
        rows = slice(at, at + out.shape[0])
        total = parts[0][rows, :].astype(F32)
        for other in parts[1:]:
            total = total + other[rows, :].astype(F32)
        out[...] = total.astype(BF16)
        at += out.shape[0]


def seats_kernel(
    n_tp,
    seat_cap,
    owners_ref,
    positions_ref,
    combine_ref,
    hidden_ref,
    rows_ref,
    mix_ref,
    at_ref,
):
    part = lax.axis_index("tp")
    tokens, width = hidden_ref.shape
    source_rows = tokens // n_tp
    owners = owners_ref[...] ^ part
    owner = lax.broadcasted_iota(jnp.int32, (n_tp, tokens), 0)
    hot = jnp.where(owners == owner, 1.0, 0.0)
    first = lax.broadcasted_iota(jnp.int32, (tokens, tokens), 0)
    second = lax.broadcasted_iota(jnp.int32, (tokens, tokens), 1)
    earlier = jnp.where((first < second) & (first // source_rows == second // source_rows), 1.0, 0.0)
    before = jnp.dot(hot.astype(BF16), earlier.astype(BF16), preferred_element_type=F32)
    seat = jnp.sum(before * hot, axis=0, keepdims=True).astype(jnp.int32)
    source = lax.broadcasted_iota(jnp.int32, (1, tokens), 1) // source_rows
    code = owners * (n_tp * seat_cap) + source * seat_cap + seat
    seats = n_tp * seat_cap
    held = lax.broadcasted_iota(jnp.int32, (n_tp * seats, tokens), 0) == code
    pick = jnp.where(held, 1.0, 0.0).astype(BF16)
    mix_ref[...] = lax.dot_general(
        pick, combine_ref[...], (((1,), (1,)), ((), ())), preferred_element_type=F32
    ).astype(BF16)
    place = jnp.where(held[:seats], positions_ref[...].astype(F32), 0.0)
    at_ref[...] = jnp.sum(place, axis=1, keepdims=True)
    hidden = columns_of(hidden_ref, part, n_tp, width // n_tp)
    rows_ref[...] = jnp.dot(pick, hidden, preferred_element_type=F32).astype(BF16)


def cache_kernel(n_z, n_tp, cache_width, *refs):
    near, far, core_ref = refs[:4], refs[4 : n_z + 2], refs[n_z + 2]
    mix_ref, rows_ref, gain_ref, weight_ref = refs[n_z + 3 : n_z + 7]
    outs, back_ref = refs[n_z + 7 : n_z + 7 + n_tp], refs[n_z + 7 + n_tp]
    for d in range(4):
        back_ref[d * CAP : (d + 1) * CAP, :] = near[d][...]
    for d in range(n_z - 2):
        at = (2 * d + 4) * CAP
        back_ref[at : at + CAP, :] = far[d][:CAP, :]
        last = (n_z - 3 - d) * CAP
        back_ref[at + CAP : at + 2 * CAP, :] = core_ref[last : last + CAP, :]
    mixed = jnp.dot(mix_ref[...], back_ref[...], preferred_element_type=F32)
    state = rows_ref[...].astype(F32) + mixed
    square = jnp.sum(state * state, axis=1, keepdims=True)
    scaled = (state * gain_ref[...]).astype(BF16)
    value = lax.dot_general(
        scaled, weight_ref[...], (((1,), (1,)), ((), ())), preferred_element_type=F32
    ).astype(BF16)
    high = square.astype(BF16).astype(F32)
    rest = square - high
    middle = rest.astype(BF16).astype(F32)
    low = rest - middle
    seats, wide = outs[0].shape
    lane = lax.broadcasted_iota(jnp.int32, (square.shape[0], wide - cache_width), 1)
    extra = jnp.where(lane == 0, high, jnp.where(lane == 1, middle, jnp.where(lane == 2, low, 0.0)))
    extra = extra.astype(BF16)
    for d in range(n_tp):
        outs[d][:, :cache_width] = value[d * seats : (d + 1) * seats]
        outs[d][:, cache_width:] = extra[d * seats : (d + 1) * seats]


def finish_kernel(n_tp, width, rank_width, *refs):
    parts = refs[:n_tp]
    gain_ref, cos_ref, sin_ref, latent_ref, rotary_ref = refs[n_tp:]
    total = parts[0][...].astype(F32)
    for other in parts[1:]:
        total = total + other[...].astype(F32)
    half = cos_ref.shape[1]
    cache_width = rank_width + 2 * half
    square = jnp.sum(total[:, cache_width : cache_width + 3], axis=1, keepdims=True)
    cache = total[:, :cache_width] * lax.rsqrt(square / width + EPS)
    latent = cache[:, :rank_width]
    scale = lax.rsqrt(jnp.mean(latent * latent, axis=1, keepdims=True) + EPS)
    latent_ref[...] = (latent * scale * gain_ref[...]).astype(BF16)
    first = cache[:, rank_width : rank_width + half]
    second = cache[:, rank_width + half :]
    cosine, sine = cos_ref[...], sin_ref[...]
    rotary_ref[:, :half] = (first * cosine - second * sine).astype(BF16)
    rotary_ref[:, half:] = (second * cosine + first * sine).astype(BF16)


def call(kernel, out_shape, args, scratch=(), flops=0, hbm=()):
    moved = sum(a.size * a.dtype.itemsize for a in args)
    vmem = pl.BlockSpec(memory_space=pltpu.VMEM)
    args = [
        pltpu.with_memory_space_constraint(a, pltpu.HBM) if i in hbm else a
        for i, a in enumerate(args)
    ]
    return pl.pallas_call(
        kernel,
        out_shape=out_shape,
        in_specs=[
            pl.BlockSpec(memory_space=pltpu.HBM) if i in hbm else vmem for i in range(len(args))
        ],
        out_specs=[vmem] * len(out_shape),
        scratch_shapes=list(scratch),
        compiler_params=pltpu.CompilerParams(vmem_limit_bytes=VMEM_LIMIT),
        cost_estimate=pl.CostEstimate(flops=flops, bytes_accessed=moved, transcendentals=0),
    )(*args)


def swap(value, axis, d):
    return lax.ppermute(value, axis, [(i, i ^ d) for i in range(lax.axis_size(axis))])


def spread(value, n_tp):
    return [swap(value, "tp", d) for d in reversed(range(1, n_tp))]


def collect(values):
    return [swap(values[d], "tp", d) for d in reversed(range(1, len(values)))] + [values[0]]


def on_device(
    hidden,
    moe_gain,
    route_logits,
    routes,
    gate_weight,
    up_weight,
    down_weight,
    attn_gain,
    latent_weight,
    latent_gain,
    positions,
    owners,
):
    n_ep = lax.axis_size("ep")
    n_tp = lax.axis_size("tp")
    n_z = n_ep // 2
    tokens, width = hidden.shape
    share = width // n_tp
    ff = gate_weight.shape[2]
    slots = n_ep * CAP
    seat_cap = max(2, tokens // n_tp // 4)
    seats = n_tp * seat_cap
    rank_width = latent_gain.shape[0]
    cache_width = latent_weight.shape[1]
    half = (cache_width - rank_width) // 2
    wide = (cache_width + 3 + 127) // 128 * 128
    struct = jax.ShapeDtypeStruct
    chunks = width // 512 if width % 512 == 0 else 1

    *outgoing, pick, combine, hidden, gain = call(
        functools.partial(dispatch_kernel, n_ep, n_tp),
        [struct((CAP, share), BF16)] * (n_ep - 4)
        + [struct((slots, tokens), BF16)] * 2
        + [struct(hidden.shape, BF16), struct((1, width), F32)],
        (routes.T, route_logits.T, hidden, moe_gain),
        [
            pltpu.VMEM(routes.T.shape, jnp.int32),
            pltpu.VMEM(routes.T.shape, F32),
            pltpu.SemaphoreType.DMA((3 + chunks,)),
        ],
        flops=2 * slots * tokens * width,
        hbm=(0, 1, 2, 3),
    )
    own, to_core, to_near = call(
        functools.partial(near_kernel, n_tp),
        [struct((CAP, width), BF16), struct((n_tp * CAP, share), BF16)]
        + [struct((2 * n_tp * CAP, share), BF16)],
        (pick, hidden, gain),
        flops=8 * CAP * tokens * width,
    )
    order = [*range(4, n_ep, 2), *range(5, n_ep, 2)]
    arrived = [swap(outgoing[d - 4], "ep", d) for d in order]
    near = swap(to_near[: n_tp * CAP], "ep", 2)
    near_crossed = swap(to_near[n_tp * CAP :], "ep", 3)
    from_core = swap(to_core, "ep", 1)
    gate_w, up_w, down_w = gate_weight[0], up_weight[0], down_weight[0]
    *loaded, mark = call(
        load_kernel,
        [struct(w.shape, BF16) for w in (gate_w, up_w, down_w)] + [struct((8, 128), F32)],
        (combine, gate_w, up_w, down_w),
        [pltpu.SemaphoreType.DMA((3,))],
        hbm=(1, 2, 3),
    )
    arrived, from_core = lax.optimization_barrier((arrived, from_core))
    mine = jnp.concatenate(arrived, axis=0)
    shares = spread(mine, n_tp)
    near_rows, far_rows = 4 * CAP, slots - 4 * CAP
    *near_pieces, gate_sum, up_sum = call(
        functools.partial(first_kernel, n_tp),
        [struct((near_rows, share), BF16)] * n_tp + [struct((far_rows, ff), F32)] * 2,
        (own, from_core, near, near_crossed, mine, *loaded, mark),
        [pltpu.VMEM((4 * CAP, width), BF16)],
        flops=2 * slots * width * ff,
    )
    combine, gate_sum = lax.optimization_barrier((combine, gate_sum))
    rows, mix, at = call(
        functools.partial(seats_kernel, n_tp, seat_cap),
        [
            struct((n_tp * seats, share), BF16),
            struct((n_tp * seats, slots), BF16),
            struct((seats, 1), F32),
        ],
        (owners[None, :], positions[None, :], combine, hidden),
        flops=2 * n_tp * seats * tokens * (share + slots),
    )
    up_sum, rows, mix = lax.optimization_barrier((up_sum, rows, mix))
    terms = call(
        functools.partial(expert_kernel, n_tp),
        [struct((far_rows, share), BF16)] * n_tp,
        (*shares, *loaded, gate_sum, up_sum),
        flops=2 * slots * width * ff * 3,
    )
    terms = list(terms)
    freqs = ROPE_BASE ** (-jnp.arange(half, dtype=F32) / half)
    angles = at * freqs[None, :]
    cosine, sine = jnp.cos(angles), jnp.sin(angles)

    far_terms = collect(terms)
    near_terms = collect(near_pieces)
    far_done = call(
        functools.partial(sum_kernel, n_tp),
        [struct((2 * CAP, share), BF16)] * (n_z - 2),
        far_terms,
    )
    far_back = [swap(far_done[d - 2], "ep", 2 * d) for d in range(2, n_z)]
    near_done = call(
        functools.partial(sum_kernel, n_tp), [struct((CAP, share), BF16)] * 4, near_terms
    )
    near_back = [near_done[0]] + [swap(near_done[d], "ep", d) for d in (1, 2, 3)]
    crossed = swap(jnp.concatenate([piece[CAP:] for piece in far_back[::-1]], axis=0), "ep", 1)
    partial = call(
        functools.partial(cache_kernel, n_z, n_tp, cache_width),
        [struct((seats, wide), BF16)] * n_tp,
        (*near_back, *far_back, crossed, mix, rows, attn_gain[None, :], latent_weight.T),
        [pltpu.VMEM((slots, share), BF16)],
        flops=2 * n_tp * seats * share * (slots + cache_width),
    )
    last = n_tp - 1
    finish = [swap(partial[d], "tp", d) for d in (last, *range(1, last))] + [partial[0]]
    return tuple(
        call(
            functools.partial(finish_kernel, n_tp, width, rank_width),
            [struct((seats, rank_width), BF16), struct((seats, 2 * half), BF16)],
            (*finish, latent_gain[None, :], cosine, sine),
        )
    )


def solution(mesh):
    placed = (
        P(("groups", "ep"), None),
        P(),
        P(("groups", "ep"), None),
        P(("groups", "ep"), None),
        P("ep", None, "tp"),
        P("ep", None, "tp"),
        P("ep", "tp", None),
        P("tp"),
        P("tp", None),
        P(),
        P(("groups", "ep")),
        P(("groups", "ep")),
    )
    return jax.shard_map(
        on_device,
        mesh=mesh,
        in_specs=placed,
        out_specs=(P(("groups", "ep", "tp"), None), P(("groups", "ep", "tp"), None)),
        check_vma=False,
    )
```

```python
import functools

import jax
import jax.numpy as jnp
from jax import lax
from jax.experimental import pallas as pl
from jax.experimental.pallas import tpu as pltpu
from jax.sharding import PartitionSpec as P

CAP = 16
EPS = 1e-06
ROUTE_SCALE = 2.5
ROPE_BASE = 10000.0
BF16 = jnp.bfloat16
F32 = jnp.float32
VMEM_LIMIT = 40 * 1024 * 1024


def columns_of(ref, index, count, share):
    if share % 128 == 0:
        return ref[:, pl.ds(pl.multiple_of(index * share, 128), share)]
    out = ref[:, 0:share]
    for q in range(1, count):
        out = jnp.where(index == q, ref[:, q * share : (q + 1) * share], out)
    return out


def dispatch_kernel(n_ep, n_tp, routes_hbm, logits_hbm, hidden_hbm, gain_hbm, *refs):
    outs = refs[: n_ep - 4]
    core_ref, pick_ref, combine_ref, hidden_ref, gain_ref = refs[n_ep - 4 : n_ep + 1]
    routes_ref, logits_ref, head_ref, sems = refs[n_ep + 1 :]
    me = lax.axis_index("ep")
    part = lax.axis_index("tp")
    tokens, width = hidden_ref.shape
    share = width // n_tp
    step = 512 if width % 512 == 0 else width
    starts = range(0, width, step)
    small = [
        pltpu.make_async_copy(routes_hbm, routes_ref, sems.at[0]),
        pltpu.make_async_copy(logits_hbm, logits_ref, sems.at[1]),
        pltpu.make_async_copy(gain_hbm, gain_ref.at[0], sems.at[2]),
    ]
    large = [
        pltpu.make_async_copy(
            hidden_hbm.at[:, c : c + step], hidden_ref.at[:, c : c + step], sems.at[3 + i]
        )
        for i, c in enumerate(starts)
    ]
    for copy in small + large:
        copy.start()
    small[0].wait()
    small[1].wait()
    routes = routes_ref[...]
    affinity = jax.nn.sigmoid(logits_ref[...])
    weight = ROUTE_SCALE * affinity / jnp.sum(affinity, axis=0, keepdims=True)
    weight = weight.astype(BF16).astype(F32)
    expert = lax.broadcasted_iota(jnp.int32, (n_ep, tokens), 0) ^ me
    hit = jnp.zeros((n_ep, tokens), F32)
    gain_of = jnp.zeros((n_ep, tokens), F32)
    for k in range(routes.shape[0]):
        same = routes[k : k + 1, :] == expert
        hit = jnp.where(same, 1.0, hit)
        gain_of = jnp.where(same, weight[k : k + 1, :], gain_of)
    earlier = lax.broadcasted_iota(jnp.int32, (tokens, tokens), 0) < lax.broadcasted_iota(
        jnp.int32, (tokens, tokens), 1
    )
    rank = jnp.dot(hit.astype(BF16), earlier.astype(F32).astype(BF16), preferred_element_type=F32)
    rank = jnp.where(hit > 0, rank, -1.0)
    place = lax.broadcasted_iota(jnp.int32, (CAP, tokens), 0).astype(F32)
    for d in range(n_ep):
        match = rank[d : d + 1, :] == place
        rows = slice(d * CAP, (d + 1) * CAP)
        pick_ref[rows, :] = jnp.where(match, 1.0, 0.0).astype(BF16)
        combine_ref[rows, :] = jnp.where(match, gain_of[d : d + 1, :], 0.0).astype(BF16)
    pick = jnp.concatenate([pick_ref[CAP : 2 * CAP, :], pick_ref[4 * CAP :, :]], axis=0)
    square = jnp.zeros((pick.shape[0], 1), F32)
    middle = len(large) // 2
    for i, c in enumerate(starts):
        if i == 0 or i == middle:
            for copy in large[:middle] if i < middle else large[i:]:
                copy.wait()
        got = jnp.dot(pick, hidden_ref[:, c : c + step], preferred_element_type=F32)
        square = square + jnp.sum(got * got, axis=1, keepdims=True)
        head_ref[:, c : c + step] = got[:CAP]
    small[2].wait()
    scale = lax.rsqrt(square / width + EPS)
    head = (head_ref[...] * scale[:CAP] * gain_ref[...]).astype(BF16)
    for q in range(n_tp):
        core_ref[q * CAP : (q + 1) * CAP, :] = head[:, q * share : (q + 1) * share]
    pick, scale = pick[CAP:], scale[CAP:]
    got = jnp.dot(pick, columns_of(hidden_ref, part, n_tp, share), preferred_element_type=F32)
    rows = (got * scale * columns_of(gain_ref, part, n_tp, share)).astype(BF16)
    for i, out in enumerate(outs):
        out[...] = rows[i * CAP : (i + 1) * CAP]


def near_kernel(n_tp, pick_ref, hidden_ref, gain_ref, own_ref, near_ref):
    share = hidden_ref.shape[1] // n_tp
    pick = jnp.concatenate([pick_ref[:CAP, :], pick_ref[2 * CAP : 4 * CAP, :]], axis=0)
    got = jnp.dot(pick, hidden_ref[...], preferred_element_type=F32)
    scale = lax.rsqrt(jnp.mean(got * got, axis=1, keepdims=True) + EPS)
    whole = (got * scale * gain_ref[...]).astype(BF16)
    own_ref[...] = whole[:CAP]
    for q in range(n_tp):
        columns = slice(q * share, (q + 1) * share)
        near_ref[q * CAP : (q + 1) * CAP, :] = whole[CAP : 2 * CAP, columns]
        near_ref[(n_tp + q) * CAP : (n_tp + q + 1) * CAP, :] = whole[2 * CAP :, columns]


def load_kernel(after_ref, *refs):
    count = (len(refs) - 2) // 2
    mark_ref, sems = refs[-2:]
    copies = [
        pltpu.make_async_copy(refs[i], refs[count + i], sems.at[i]) for i in range(count)
    ]
    for copy in copies:
        copy.start()
    mark_ref[...] = jnp.zeros(mark_ref.shape, F32)
    for copy in copies:
        copy.wait()


def first_kernel(n_tp, own_ref, core_ref, near_ref, cross_ref, mine_ref, *refs):
    gate_ref, up_ref, down_ref, _ = refs[:4]
    outs, (gate_sum_ref, up_sum_ref, head_ref) = refs[4 : n_tp + 4], refs[n_tp + 4 :]
    part = lax.axis_index("tp")
    share = mine_ref.shape[1]
    head_ref[:CAP, :] = own_ref[...]
    for i, ref in enumerate((core_ref, near_ref, cross_ref)):
        for q in range(n_tp):
            rows = slice((i + 1) * CAP, (i + 2) * CAP)
            head_ref[rows, q * share : (q + 1) * share] = ref[q * CAP : (q + 1) * CAP, :]
    depth = pl.ds(pl.multiple_of(part * share, CAP), share)
    gate, upper = (
        jnp.dot(head_ref[...], ref[...], preferred_element_type=F32) for ref in (gate_ref, up_ref)
    )
    for weight_ref, sum_ref in zip((gate_ref, up_ref), (gate_sum_ref, up_sum_ref)):
        sum_ref[...] = jnp.dot(mine_ref[...], weight_ref[depth, :], preferred_element_type=F32)
    inner = (gate / (1.0 + jnp.exp(-gate)) * upper).astype(BF16)
    for d in range(n_tp):
        down = columns_of(down_ref, part ^ d, n_tp, share)
        outs[d][...] = jnp.dot(inner, down, preferred_element_type=F32).astype(BF16)


def expert_kernel(n_tp, *refs):
    rows = refs[: n_tp - 1]
    gate_ref, up_ref, down_ref, gate_sum_ref, up_sum_ref = refs[n_tp - 1 : n_tp + 4]
    outs = refs[n_tp + 4 :]
    part = lax.axis_index("tp")
    share = rows[0].shape[1]
    gate = gate_sum_ref[...]
    upper = up_sum_ref[...]
    for d, ref in zip(partners(n_tp), rows):
        value = ref[...]
        depth = pl.ds(pl.multiple_of((part ^ d) * share, CAP), share)
        gate = gate + jnp.dot(value, gate_ref[depth, :], preferred_element_type=F32)
        upper = upper + jnp.dot(value, up_ref[depth, :], preferred_element_type=F32)
    far = (gate / (1.0 + jnp.exp(-gate)) * upper).astype(BF16)
    count = far.shape[0]
    groups = [
        far[start : start + CAP]
        for at in range(0, count // 2, CAP)
        for start in (at, count // 2 + at)
    ]
    inner = jnp.concatenate(groups, axis=0)
    for d in range(n_tp):
        down = columns_of(down_ref, part ^ d, n_tp, share)
        outs[d][...] = jnp.dot(inner, down, preferred_element_type=F32).astype(BF16)


def sum_kernel(n_tp, *refs):
    parts, outs = refs[:n_tp], refs[n_tp:]
    at = 0
    for out in outs:
        rows = slice(at, at + out.shape[0])
        total = parts[0][rows, :].astype(F32)
        for other in parts[1:]:
            total = total + other[rows, :].astype(F32)
        out[...] = total.astype(BF16)
        at += out.shape[0]


def seats_kernel(
    n_tp,
    seat_cap,
    owners_ref,
    positions_ref,
    combine_ref,
    hidden_ref,
    rows_ref,
    mix_ref,
    at_ref,
):
    part = lax.axis_index("tp")
    tokens, width = hidden_ref.shape
    source_rows = tokens // n_tp
    owners = owners_ref[...] ^ part
    owner = lax.broadcasted_iota(jnp.int32, (n_tp, tokens), 0)
    hot = jnp.where(owners == owner, 1.0, 0.0)
    first = lax.broadcasted_iota(jnp.int32, (tokens, tokens), 0)
    second = lax.broadcasted_iota(jnp.int32, (tokens, tokens), 1)
    earlier = jnp.where((first < second) & (first // source_rows == second // source_rows), 1.0, 0.0)
    before = jnp.dot(hot.astype(BF16), earlier.astype(BF16), preferred_element_type=F32)
    seat = jnp.sum(before * hot, axis=0, keepdims=True).astype(jnp.int32)
    source = lax.broadcasted_iota(jnp.int32, (1, tokens), 1) // source_rows
    code = owners * (n_tp * seat_cap) + source * seat_cap + seat
    seats = n_tp * seat_cap
    held = lax.broadcasted_iota(jnp.int32, (n_tp * seats, tokens), 0) == code
    pick = jnp.where(held, 1.0, 0.0).astype(BF16)
    mix_ref[...] = lax.dot_general(
        pick, combine_ref[...], (((1,), (1,)), ((), ())), preferred_element_type=F32
    ).astype(BF16)
    place = jnp.where(held[:seats], positions_ref[...].astype(F32), 0.0)
    at_ref[...] = jnp.sum(place, axis=1, keepdims=True)
    hidden = columns_of(hidden_ref, part, n_tp, width // n_tp)
    rows_ref[...] = jnp.dot(pick, hidden, preferred_element_type=F32).astype(BF16)


def cache_kernel(n_z, n_tp, cache_width, *refs):
    near, far, core_ref = refs[:4], refs[4 : n_z + 2], refs[n_z + 2]
    mix_ref, rows_ref, gain_ref, weight_ref = refs[n_z + 3 : n_z + 7]
    outs, back_ref = refs[n_z + 7 : n_z + 7 + n_tp], refs[n_z + 7 + n_tp]
    for d in range(4):
        back_ref[d * CAP : (d + 1) * CAP, :] = near[d][...]
    for d in range(n_z - 2):
        at = (2 * d + 4) * CAP
        back_ref[at : at + CAP, :] = far[d][:CAP, :]
        back_ref[at + CAP : at + 2 * CAP, :] = core_ref[d * CAP : (d + 1) * CAP, :]
    mixed = jnp.dot(mix_ref[...], back_ref[...], preferred_element_type=F32)
    state = rows_ref[...].astype(F32) + mixed
    square = jnp.sum(state * state, axis=1, keepdims=True)
    scaled = (state * gain_ref[...]).astype(BF16)
    value = lax.dot_general(
        scaled, weight_ref[...], (((1,), (1,)), ((), ())), preferred_element_type=F32
    ).astype(BF16)
    high = square.astype(BF16).astype(F32)
    rest = square - high
    middle = rest.astype(BF16).astype(F32)
    low = rest - middle
    seats, wide = outs[0].shape
    lane = lax.broadcasted_iota(jnp.int32, (square.shape[0], wide - cache_width), 1)
    extra = jnp.where(lane == 0, high, jnp.where(lane == 1, middle, jnp.where(lane == 2, low, 0.0)))
    extra = extra.astype(BF16)
    for d in range(n_tp):
        outs[d][:, :cache_width] = value[d * seats : (d + 1) * seats]
        outs[d][:, cache_width:] = extra[d * seats : (d + 1) * seats]


def finish_kernel(n_tp, width, rank_width, *refs):
    parts = refs[:n_tp]
    gain_ref, cos_ref, sin_ref, latent_ref, rotary_ref = refs[n_tp:]
    total = parts[0][...].astype(F32)
    for other in parts[1:]:
        total = total + other[...].astype(F32)
    half = cos_ref.shape[1]
    cache_width = rank_width + 2 * half
    square = jnp.sum(total[:, cache_width : cache_width + 3], axis=1, keepdims=True)
    cache = total[:, :cache_width] * lax.rsqrt(square / width + EPS)
    latent = cache[:, :rank_width]
    scale = lax.rsqrt(jnp.mean(latent * latent, axis=1, keepdims=True) + EPS)
    latent_ref[...] = (latent * scale * gain_ref[...]).astype(BF16)
    first = cache[:, rank_width : rank_width + half]
    second = cache[:, rank_width + half :]
    cosine, sine = cos_ref[...], sin_ref[...]
    rotary_ref[:, :half] = (first * cosine - second * sine).astype(BF16)
    rotary_ref[:, half:] = (second * cosine + first * sine).astype(BF16)


def call(kernel, out_shape, args, scratch=(), flops=0, hbm=()):
    moved = sum(a.size * a.dtype.itemsize for a in args)
    vmem = pl.BlockSpec(memory_space=pltpu.VMEM)
    args = [
        pltpu.with_memory_space_constraint(a, pltpu.HBM) if i in hbm else a
        for i, a in enumerate(args)
    ]
    return pl.pallas_call(
        kernel,
        out_shape=out_shape,
        in_specs=[
            pl.BlockSpec(memory_space=pltpu.HBM) if i in hbm else vmem for i in range(len(args))
        ],
        out_specs=[vmem] * len(out_shape),
        scratch_shapes=list(scratch),
        compiler_params=pltpu.CompilerParams(vmem_limit_bytes=VMEM_LIMIT),
        cost_estimate=pl.CostEstimate(flops=flops, bytes_accessed=moved, transcendentals=0),
    )(*args)


def swap(value, axis, d):
    return lax.ppermute(value, axis, [(i, i ^ d) for i in range(lax.axis_size(axis))])


def partners(n_tp):
    return [*reversed(range(1, n_tp - 1)), n_tp - 1]


def spread(value, n_tp):
    return [swap(value, "tp", d) for d in partners(n_tp)]


def collect(values):
    return [swap(values[d], "tp", d) for d in reversed(range(1, len(values)))] + [values[0]]


def on_device(
    hidden,
    moe_gain,
    route_logits,
    routes,
    gate_weight,
    up_weight,
    down_weight,
    attn_gain,
    latent_weight,
    latent_gain,
    positions,
    owners,
):
    n_ep = lax.axis_size("ep")
    n_tp = lax.axis_size("tp")
    n_z = n_ep // 2
    tokens, width = hidden.shape
    share = width // n_tp
    ff = gate_weight.shape[2]
    slots = n_ep * CAP
    seat_cap = max(2, tokens // n_tp // 4)
    seats = n_tp * seat_cap
    rank_width = latent_gain.shape[0]
    cache_width = latent_weight.shape[1]
    half = (cache_width - rank_width) // 2
    wide = (cache_width + 3 + 127) // 128 * 128
    struct = jax.ShapeDtypeStruct
    chunks = width // 512 if width % 512 == 0 else 1

    *outgoing, to_core, pick, combine, hidden, gain = call(
        functools.partial(dispatch_kernel, n_ep, n_tp),
        [struct((CAP, share), BF16)] * (n_ep - 4)
        + [struct((n_tp * CAP, share), BF16)]
        + [struct((slots, tokens), BF16)] * 2
        + [struct(hidden.shape, BF16), struct((1, width), F32)],
        (routes.T, route_logits.T, hidden, moe_gain),
        [
            pltpu.VMEM(routes.T.shape, jnp.int32),
            pltpu.VMEM(routes.T.shape, F32),
            pltpu.VMEM((CAP, width), F32),
            pltpu.SemaphoreType.DMA((3 + chunks,)),
        ],
        flops=2 * slots * tokens * width,
        hbm=(0, 1, 2, 3),
    )
    own, to_near = call(
        functools.partial(near_kernel, n_tp),
        [struct((CAP, width), BF16), struct((2 * n_tp * CAP, share), BF16)],
        (pick, hidden, gain),
        flops=6 * CAP * tokens * width,
    )
    order = [*range(4, n_ep, 2), *range(5, n_ep, 2)]
    arrived = [swap(outgoing[d - 4], "ep", d) for d in order]
    near = swap(to_near[: n_tp * CAP], "ep", 2)
    near_crossed = swap(to_near[n_tp * CAP :], "ep", 3)
    from_core = swap(to_core, "ep", 1)
    gate_w, up_w, down_w = gate_weight[0], up_weight[0], down_weight[0]
    *loaded, mark = call(
        load_kernel,
        [struct(w.shape, BF16) for w in (gate_w, up_w, down_w)] + [struct((8, 128), F32)],
        (combine, gate_w, up_w, down_w),
        [pltpu.SemaphoreType.DMA((3,))],
        hbm=(1, 2, 3),
    )
    arrived, from_core = lax.optimization_barrier((arrived, from_core))
    mine = jnp.concatenate(arrived, axis=0)
    shares = spread(mine, n_tp)
    near_rows, far_rows = 4 * CAP, slots - 4 * CAP
    *near_pieces, gate_sum, up_sum = call(
        functools.partial(first_kernel, n_tp),
        [struct((near_rows, share), BF16)] * n_tp + [struct((far_rows, ff), F32)] * 2,
        (own, from_core, near, near_crossed, mine, *loaded, mark),
        [pltpu.VMEM((4 * CAP, width), BF16)],
        flops=2 * slots * width * ff,
    )
    terms = call(
        functools.partial(expert_kernel, n_tp),
        [struct((far_rows, share), BF16)] * n_tp,
        (*shares, *loaded, gate_sum, up_sum),
        flops=2 * slots * width * ff * 3,
    )
    terms = list(terms)
    combine, terms[0] = lax.optimization_barrier((combine, terms[0]))
    rows, mix, at = call(
        functools.partial(seats_kernel, n_tp, seat_cap),
        [
            struct((n_tp * seats, share), BF16),
            struct((n_tp * seats, slots), BF16),
            struct((seats, 1), F32),
        ],
        (owners[None, :], positions[None, :], combine, hidden),
        flops=2 * n_tp * seats * tokens * (share + slots),
    )
    freqs = ROPE_BASE ** (-jnp.arange(half, dtype=F32) / half)
    angles = at * freqs[None, :]
    cosine, sine = jnp.cos(angles), jnp.sin(angles)

    far_terms = collect(terms)
    near_far = swap(near_pieces[n_tp - 1], "tp", n_tp - 1)
    near_far, rows, mix, *near_rest = lax.optimization_barrier(
        (near_far, rows, mix, *near_pieces[1 : n_tp - 1])
    )
    near_terms = [near_far, near_pieces[0]]
    near_terms += [swap(near_rest[d - 1], "tp", d) for d in reversed(range(1, n_tp - 1))]
    far_done = call(
        functools.partial(sum_kernel, n_tp),
        [struct((2 * CAP, share), BF16)] * (n_z - 2),
        far_terms,
    )
    far_back = [swap(far_done[d - 2], "ep", 2 * d) for d in range(2, n_z)]
    near_done = call(
        functools.partial(sum_kernel, n_tp), [struct((CAP, share), BF16)] * 4, near_terms
    )
    near_back = [near_done[0]] + [swap(near_done[d], "ep", d) for d in (1, 2, 3)]
    crossed = swap(jnp.concatenate([piece[CAP:] for piece in far_back], axis=0), "ep", 1)
    partial = call(
        functools.partial(cache_kernel, n_z, n_tp, cache_width),
        [struct((seats, wide), BF16)] * n_tp,
        (*near_back, *far_back, crossed, mix, rows, attn_gain[None, :], latent_weight.T),
        [pltpu.VMEM((slots, share), BF16)],
        flops=2 * n_tp * seats * share * (slots + cache_width),
    )
    return tuple(
        call(
            functools.partial(finish_kernel, n_tp, width, rank_width),
            [struct((seats, rank_width), BF16), struct((seats, 2 * half), BF16)],
            (*collect(partial), latent_gain[None, :], cosine, sine),
        )
    )


def solution(mesh):
    placed = (
        P(("groups", "ep"), None),
        P(),
        P(("groups", "ep"), None),
        P(("groups", "ep"), None),
        P("ep", None, "tp"),
        P("ep", None, "tp"),
        P("ep", "tp", None),
        P("tp"),
        P("tp", None),
        P(),
        P(("groups", "ep")),
        P(("groups", "ep")),
    )
    return jax.shard_map(
        on_device,
        mesh=mesh,
        in_specs=placed,
        out_specs=(P(("groups", "ep", "tp"), None), P(("groups", "ep", "tp"), None)),
        check_vma=False,
    )
```

```python
import functools

import jax
import jax.numpy as jnp
from jax import lax
from jax.experimental import pallas as pl
from jax.experimental.pallas import tpu as pltpu
from jax.sharding import PartitionSpec as P

CAP = 16
EPS = 1e-06
ROUTE_SCALE = 2.5
ROPE_BASE = 10000.0
BF16 = jnp.bfloat16
F32 = jnp.float32
VMEM_LIMIT = 40 * 1024 * 1024


def columns_of(ref, index, count, share):
    if share % 128 == 0:
        return ref[:, pl.ds(pl.multiple_of(index * share, 128), share)]
    out = ref[:, 0:share]
    for q in range(1, count):
        out = jnp.where(index == q, ref[:, q * share : (q + 1) * share], out)
    return out


def dispatch_kernel(n_ep, n_tp, routes_hbm, logits_hbm, hidden_hbm, gain_hbm, *refs):
    outs = refs[: n_ep - 4]
    pick_ref, combine_ref, hidden_ref, gain_ref, routes_ref, logits_ref, sems = refs[n_ep - 4 :]
    me = lax.axis_index("ep")
    part = lax.axis_index("tp")
    tokens, width = hidden_ref.shape
    share = width // n_tp
    step = 512 if width % 512 == 0 else width
    starts = range(0, width, step)
    small = [
        pltpu.make_async_copy(routes_hbm, routes_ref, sems.at[0]),
        pltpu.make_async_copy(logits_hbm, logits_ref, sems.at[1]),
        pltpu.make_async_copy(gain_hbm, gain_ref.at[0], sems.at[2]),
    ]
    large = [
        pltpu.make_async_copy(
            hidden_hbm.at[:, c : c + step], hidden_ref.at[:, c : c + step], sems.at[3 + i]
        )
        for i, c in enumerate(starts)
    ]
    for copy in small + large:
        copy.start()
    small[0].wait()
    small[1].wait()
    routes = routes_ref[...]
    affinity = jax.nn.sigmoid(logits_ref[...])
    weight = ROUTE_SCALE * affinity / jnp.sum(affinity, axis=0, keepdims=True)
    weight = weight.astype(BF16).astype(F32)
    expert = lax.broadcasted_iota(jnp.int32, (n_ep, tokens), 0) ^ me
    hit = jnp.zeros((n_ep, tokens), F32)
    gain_of = jnp.zeros((n_ep, tokens), F32)
    for k in range(routes.shape[0]):
        same = routes[k : k + 1, :] == expert
        hit = jnp.where(same, 1.0, hit)
        gain_of = jnp.where(same, weight[k : k + 1, :], gain_of)
    earlier = lax.broadcasted_iota(jnp.int32, (tokens, tokens), 0) < lax.broadcasted_iota(
        jnp.int32, (tokens, tokens), 1
    )
    rank = jnp.dot(hit.astype(BF16), earlier.astype(F32).astype(BF16), preferred_element_type=F32)
    rank = jnp.where(hit > 0, rank, -1.0)
    place = lax.broadcasted_iota(jnp.int32, (CAP, tokens), 0).astype(F32)
    for d in range(n_ep):
        match = rank[d : d + 1, :] == place
        rows = slice(d * CAP, (d + 1) * CAP)
        pick_ref[rows, :] = jnp.where(match, 1.0, 0.0).astype(BF16)
        combine_ref[rows, :] = jnp.where(match, gain_of[d : d + 1, :], 0.0).astype(BF16)
    pick = pick_ref[4 * CAP :, :]
    square = jnp.zeros((pick.shape[0], 1), F32)
    middle = len(large) // 2
    for i, c in enumerate(starts):
        if i == 0 or i == middle:
            for copy in large[:middle] if i < middle else large[i:]:
                copy.wait()
        got = jnp.dot(pick, hidden_ref[:, c : c + step], preferred_element_type=F32)
        square = square + jnp.sum(got * got, axis=1, keepdims=True)
    small[2].wait()
    scale = lax.rsqrt(square / width + EPS)
    got = jnp.dot(pick, columns_of(hidden_ref, part, n_tp, share), preferred_element_type=F32)
    rows = (got * scale * columns_of(gain_ref, part, n_tp, share)).astype(BF16)
    for i, out in enumerate(outs):
        out[...] = rows[i * CAP : (i + 1) * CAP]


def near_kernel(n_tp, _, pick_ref, hidden_ref, gain_ref, own_ref, core_ref, near_ref):
    share = hidden_ref.shape[1] // n_tp
    got = jnp.dot(pick_ref[: 4 * CAP, :], hidden_ref[...], preferred_element_type=F32)
    scale = lax.rsqrt(jnp.mean(got * got, axis=1, keepdims=True) + EPS)
    whole = (got * scale * gain_ref[...]).astype(BF16)
    own_ref[...] = whole[:CAP]
    for q in range(n_tp):
        columns = slice(q * share, (q + 1) * share)
        core_ref[q * CAP : (q + 1) * CAP, :] = whole[CAP : 2 * CAP, columns]
        near_ref[q * CAP : (q + 1) * CAP, :] = whole[2 * CAP : 3 * CAP, columns]
        near_ref[(n_tp + q) * CAP : (n_tp + q + 1) * CAP, :] = whole[3 * CAP :, columns]


def load_kernel(after_ref, *refs):
    count = (len(refs) - 2) // 2
    mark_ref, sems = refs[-2:]
    copies = [
        pltpu.make_async_copy(refs[i], refs[count + i], sems.at[i]) for i in range(count)
    ]
    for copy in copies:
        copy.start()
    mark_ref[...] = jnp.zeros(mark_ref.shape, F32)
    for copy in copies:
        copy.wait()


def first_kernel(n_tp, own_ref, core_ref, near_ref, cross_ref, mine_ref, *refs):
    gate_ref, up_ref, down_ref, _ = refs[:4]
    outs, (gate_sum_ref, up_sum_ref, head_ref) = refs[4 : n_tp + 4], refs[n_tp + 4 :]
    part = lax.axis_index("tp")
    share = mine_ref.shape[1]
    head_ref[:CAP, :] = own_ref[...]
    for i, ref in enumerate((core_ref, near_ref, cross_ref)):
        for q in range(n_tp):
            rows = slice((i + 1) * CAP, (i + 2) * CAP)
            head_ref[rows, q * share : (q + 1) * share] = ref[q * CAP : (q + 1) * CAP, :]
    depth = pl.ds(pl.multiple_of(part * share, CAP), share)
    gate, upper = (
        jnp.dot(head_ref[...], ref[...], preferred_element_type=F32) for ref in (gate_ref, up_ref)
    )
    for weight_ref, sum_ref in zip((gate_ref, up_ref), (gate_sum_ref, up_sum_ref)):
        sum_ref[...] = jnp.dot(mine_ref[...], weight_ref[depth, :], preferred_element_type=F32)
    inner = (gate / (1.0 + jnp.exp(-gate)) * upper).astype(BF16)
    for d in range(n_tp):
        down = columns_of(down_ref, part ^ d, n_tp, share)
        outs[d][...] = jnp.dot(inner, down, preferred_element_type=F32).astype(BF16)


def expert_kernel(n_tp, *refs):
    rows = refs[: n_tp - 1]
    gate_ref, up_ref, down_ref, gate_sum_ref, up_sum_ref = refs[n_tp - 1 : n_tp + 4]
    outs = refs[n_tp + 4 :]
    part = lax.axis_index("tp")
    share = rows[0].shape[1]
    gate = gate_sum_ref[...]
    upper = up_sum_ref[...]
    for d, ref in zip(partners(n_tp), rows):
        value = ref[...]
        depth = pl.ds(pl.multiple_of((part ^ d) * share, CAP), share)
        gate = gate + jnp.dot(value, gate_ref[depth, :], preferred_element_type=F32)
        upper = upper + jnp.dot(value, up_ref[depth, :], preferred_element_type=F32)
    far = (gate / (1.0 + jnp.exp(-gate)) * upper).astype(BF16)
    count = far.shape[0]
    groups = [
        far[start : start + CAP]
        for at in range(0, count // 2, CAP)
        for start in (at, count // 2 + at)
    ]
    inner = jnp.concatenate(groups, axis=0)
    for d in range(n_tp):
        down = columns_of(down_ref, part ^ d, n_tp, share)
        outs[d][...] = jnp.dot(inner, down, preferred_element_type=F32).astype(BF16)


def sum_kernel(n_tp, *refs):
    parts, outs = refs[:n_tp], refs[n_tp:]
    at = 0
    for out in outs:
        rows = slice(at, at + out.shape[0])
        total = parts[0][rows, :].astype(F32)
        for other in parts[1:]:
            total = total + other[rows, :].astype(F32)
        out[...] = total.astype(BF16)
        at += out.shape[0]


def seats_kernel(
    n_tp,
    seat_cap,
    owners_ref,
    positions_ref,
    combine_ref,
    hidden_ref,
    rows_ref,
    mix_ref,
    at_ref,
):
    part = lax.axis_index("tp")
    tokens, width = hidden_ref.shape
    source_rows = tokens // n_tp
    owners = owners_ref[...] ^ part
    owner = lax.broadcasted_iota(jnp.int32, (n_tp, tokens), 0)
    hot = jnp.where(owners == owner, 1.0, 0.0)
    first = lax.broadcasted_iota(jnp.int32, (tokens, tokens), 0)
    second = lax.broadcasted_iota(jnp.int32, (tokens, tokens), 1)
    earlier = jnp.where((first < second) & (first // source_rows == second // source_rows), 1.0, 0.0)
    before = jnp.dot(hot.astype(BF16), earlier.astype(BF16), preferred_element_type=F32)
    seat = jnp.sum(before * hot, axis=0, keepdims=True).astype(jnp.int32)
    source = lax.broadcasted_iota(jnp.int32, (1, tokens), 1) // source_rows
    code = owners * (n_tp * seat_cap) + source * seat_cap + seat
    seats = n_tp * seat_cap
    held = lax.broadcasted_iota(jnp.int32, (n_tp * seats, tokens), 0) == code
    pick = jnp.where(held, 1.0, 0.0).astype(BF16)
    mix_ref[...] = lax.dot_general(
        pick, combine_ref[...], (((1,), (1,)), ((), ())), preferred_element_type=F32
    ).astype(BF16)
    place = jnp.where(held[:seats], positions_ref[...].astype(F32), 0.0)
    at_ref[...] = jnp.sum(place, axis=1, keepdims=True)
    hidden = columns_of(hidden_ref, part, n_tp, width // n_tp)
    rows_ref[...] = jnp.dot(pick, hidden, preferred_element_type=F32).astype(BF16)


def cache_kernel(n_z, n_tp, cache_width, *refs):
    near, far, core_ref = refs[:4], refs[4 : n_z + 2], refs[n_z + 2]
    mix_ref, rows_ref, gain_ref, weight_ref = refs[n_z + 3 : n_z + 7]
    outs, back_ref = refs[n_z + 7 : n_z + 7 + n_tp], refs[n_z + 7 + n_tp]
    for d in range(4):
        back_ref[d * CAP : (d + 1) * CAP, :] = near[d][...]
    for d in range(n_z - 2):
        at = (2 * d + 4) * CAP
        back_ref[at : at + CAP, :] = far[d][:CAP, :]
        back_ref[at + CAP : at + 2 * CAP, :] = core_ref[d * CAP : (d + 1) * CAP, :]
    mixed = jnp.dot(mix_ref[...], back_ref[...], preferred_element_type=F32)
    state = rows_ref[...].astype(F32) + mixed
    square = jnp.sum(state * state, axis=1, keepdims=True)
    scaled = (state * gain_ref[...]).astype(BF16)
    value = lax.dot_general(
        scaled, weight_ref[...], (((1,), (1,)), ((), ())), preferred_element_type=F32
    ).astype(BF16)
    high = square.astype(BF16).astype(F32)
    rest = square - high
    middle = rest.astype(BF16).astype(F32)
    low = rest - middle
    seats, wide = outs[0].shape
    lane = lax.broadcasted_iota(jnp.int32, (square.shape[0], wide - cache_width), 1)
    extra = jnp.where(lane == 0, high, jnp.where(lane == 1, middle, jnp.where(lane == 2, low, 0.0)))
    extra = extra.astype(BF16)
    for d in range(n_tp):
        outs[d][:, :cache_width] = value[d * seats : (d + 1) * seats]
        outs[d][:, cache_width:] = extra[d * seats : (d + 1) * seats]


def finish_kernel(n_tp, width, rank_width, *refs):
    parts = refs[:n_tp]
    gain_ref, cos_ref, sin_ref, latent_ref, rotary_ref = refs[n_tp:]
    total = parts[0][...].astype(F32)
    for other in parts[1:]:
        total = total + other[...].astype(F32)
    half = cos_ref.shape[1]
    cache_width = rank_width + 2 * half
    square = jnp.sum(total[:, cache_width : cache_width + 3], axis=1, keepdims=True)
    cache = total[:, :cache_width] * lax.rsqrt(square / width + EPS)
    latent = cache[:, :rank_width]
    scale = lax.rsqrt(jnp.mean(latent * latent, axis=1, keepdims=True) + EPS)
    latent_ref[...] = (latent * scale * gain_ref[...]).astype(BF16)
    first = cache[:, rank_width : rank_width + half]
    second = cache[:, rank_width + half :]
    cosine, sine = cos_ref[...], sin_ref[...]
    rotary_ref[:, :half] = (first * cosine - second * sine).astype(BF16)
    rotary_ref[:, half:] = (second * cosine + first * sine).astype(BF16)


def call(kernel, out_shape, args, scratch=(), flops=0, hbm=()):
    moved = sum(a.size * a.dtype.itemsize for a in args)
    vmem = pl.BlockSpec(memory_space=pltpu.VMEM)
    args = [
        pltpu.with_memory_space_constraint(a, pltpu.HBM) if i in hbm else a
        for i, a in enumerate(args)
    ]
    return pl.pallas_call(
        kernel,
        out_shape=out_shape,
        in_specs=[
            pl.BlockSpec(memory_space=pltpu.HBM) if i in hbm else vmem for i in range(len(args))
        ],
        out_specs=[vmem] * len(out_shape),
        scratch_shapes=list(scratch),
        compiler_params=pltpu.CompilerParams(vmem_limit_bytes=VMEM_LIMIT),
        cost_estimate=pl.CostEstimate(flops=flops, bytes_accessed=moved, transcendentals=0),
    )(*args)


def swap(value, axis, d):
    return lax.ppermute(value, axis, [(i, i ^ d) for i in range(lax.axis_size(axis))])


def partners(n_tp):
    return [*reversed(range(1, n_tp - 1)), n_tp - 1]


def spread(value, n_tp):
    return [swap(value, "tp", d) for d in partners(n_tp)]


def collect(values):
    return [swap(values[d], "tp", d) for d in reversed(range(1, len(values)))] + [values[0]]


def on_device(
    hidden,
    moe_gain,
    route_logits,
    routes,
    gate_weight,
    up_weight,
    down_weight,
    attn_gain,
    latent_weight,
    latent_gain,
    positions,
    owners,
):
    n_ep = lax.axis_size("ep")
    n_tp = lax.axis_size("tp")
    n_z = n_ep // 2
    tokens, width = hidden.shape
    share = width // n_tp
    ff = gate_weight.shape[2]
    slots = n_ep * CAP
    seat_cap = max(2, tokens // n_tp // 4)
    seats = n_tp * seat_cap
    rank_width = latent_gain.shape[0]
    cache_width = latent_weight.shape[1]
    half = (cache_width - rank_width) // 2
    wide = (cache_width + 3 + 127) // 128 * 128
    struct = jax.ShapeDtypeStruct
    chunks = width // 512 if width % 512 == 0 else 1

    *outgoing, pick, combine, hidden, gain = call(
        functools.partial(dispatch_kernel, n_ep, n_tp),
        [struct((CAP, share), BF16)] * (n_ep - 4)
        + [struct((slots, tokens), BF16)] * 2
        + [struct(hidden.shape, BF16), struct((1, width), F32)],
        (routes.T, route_logits.T, hidden, moe_gain),
        [
            pltpu.VMEM(routes.T.shape, jnp.int32),
            pltpu.VMEM(routes.T.shape, F32),
            pltpu.SemaphoreType.DMA((3 + chunks,)),
        ],
        flops=2 * slots * tokens * width,
        hbm=(0, 1, 2, 3),
    )
    order = [*range(4, n_ep, 2), *range(5, n_ep, 2)]
    arrived = [swap(outgoing[d - 4], "ep", d) for d in order]
    own, to_core, to_near = call(
        functools.partial(near_kernel, n_tp),
        [struct((CAP, width), BF16), struct((n_tp * CAP, share), BF16)]
        + [struct((2 * n_tp * CAP, share), BF16)],
        (arrived[0], pick, hidden, gain),
        flops=8 * CAP * tokens * width,
    )
    near = swap(to_near[: n_tp * CAP], "ep", 2)
    near_crossed = swap(to_near[n_tp * CAP :], "ep", 3)
    from_core = swap(to_core, "ep", 1)
    gate_w, up_w, down_w = gate_weight[0], up_weight[0], down_weight[0]
    *loaded, mark = call(
        load_kernel,
        [struct(w.shape, BF16) for w in (gate_w, up_w, down_w)] + [struct((8, 128), F32)],
        (combine, gate_w, up_w, down_w),
        [pltpu.SemaphoreType.DMA((3,))],
        hbm=(1, 2, 3),
    )
    arrived, from_core = lax.optimization_barrier((arrived, from_core))
    mine = jnp.concatenate(arrived, axis=0)
    shares = spread(mine, n_tp)
    near_rows, far_rows = 4 * CAP, slots - 4 * CAP
    *near_pieces, gate_sum, up_sum = call(
        functools.partial(first_kernel, n_tp),
        [struct((near_rows, share), BF16)] * n_tp + [struct((far_rows, ff), F32)] * 2,
        (own, from_core, near, near_crossed, mine, *loaded, mark),
        [pltpu.VMEM((4 * CAP, width), BF16)],
        flops=2 * slots * width * ff,
    )
    terms = call(
        functools.partial(expert_kernel, n_tp),
        [struct((far_rows, share), BF16)] * n_tp,
        (*shares, *loaded, gate_sum, up_sum),
        flops=2 * slots * width * ff * 3,
    )
    terms = list(terms)
    combine, terms[0] = lax.optimization_barrier((combine, terms[0]))
    rows, mix, at = call(
        functools.partial(seats_kernel, n_tp, seat_cap),
        [
            struct((n_tp * seats, share), BF16),
            struct((n_tp * seats, slots), BF16),
            struct((seats, 1), F32),
        ],
        (owners[None, :], positions[None, :], combine, hidden),
        flops=2 * n_tp * seats * tokens * (share + slots),
    )
    freqs = ROPE_BASE ** (-jnp.arange(half, dtype=F32) / half)
    angles = at * freqs[None, :]
    cosine, sine = jnp.cos(angles), jnp.sin(angles)

    far_terms = collect(terms)
    near_far = swap(near_pieces[n_tp - 1], "tp", n_tp - 1)
    near_far, rows, mix, *near_rest = lax.optimization_barrier(
        (near_far, rows, mix, *near_pieces[1 : n_tp - 1])
    )
    near_terms = [near_far, near_pieces[0]]
    near_terms += [swap(near_rest[d - 1], "tp", d) for d in reversed(range(1, n_tp - 1))]
    far_done = call(
        functools.partial(sum_kernel, n_tp),
        [struct((2 * CAP, share), BF16)] * (n_z - 2),
        far_terms,
    )
    far_back = [swap(far_done[d - 2], "ep", 2 * d) for d in range(2, n_z)]
    near_done = call(
        functools.partial(sum_kernel, n_tp), [struct((CAP, share), BF16)] * 4, near_terms
    )
    near_back = [near_done[0]] + [swap(near_done[d], "ep", d) for d in (1, 2, 3)]
    crossed = swap(jnp.concatenate([piece[CAP:] for piece in far_back], axis=0), "ep", 1)
    partial = call(
        functools.partial(cache_kernel, n_z, n_tp, cache_width),
        [struct((seats, wide), BF16)] * n_tp,
        (*near_back, *far_back, crossed, mix, rows, attn_gain[None, :], latent_weight.T),
        [pltpu.VMEM((slots, share), BF16)],
        flops=2 * n_tp * seats * share * (slots + cache_width),
    )
    return tuple(
        call(
            functools.partial(finish_kernel, n_tp, width, rank_width),
            [struct((seats, rank_width), BF16), struct((seats, 2 * half), BF16)],
            (*collect(partial), latent_gain[None, :], cosine, sine),
        )
    )


def solution(mesh):
    placed = (
        P(("groups", "ep"), None),
        P(),
        P(("groups", "ep"), None),
        P(("groups", "ep"), None),
        P("ep", None, "tp"),
        P("ep", None, "tp"),
        P("ep", "tp", None),
        P("tp"),
        P("tp", None),
        P(),
        P(("groups", "ep")),
        P(("groups", "ep")),
    )
    return jax.shard_map(
        on_device,
        mesh=mesh,
        in_specs=placed,
        out_specs=(P(("groups", "ep", "tp"), None), P(("groups", "ep", "tp"), None)),
        check_vma=False,
    )
```

```python
import functools

import jax
import jax.numpy as jnp
from jax import lax
from jax.experimental import pallas as pl
from jax.experimental.pallas import tpu as pltpu
from jax.sharding import PartitionSpec as P

CAP = 16
EPS = 1e-06
ROUTE_SCALE = 2.5
ROPE_BASE = 10000.0
BF16 = jnp.bfloat16
F32 = jnp.float32
VMEM_LIMIT = 40 * 1024 * 1024


def columns_of(ref, index, count, share):
    if share % 128 == 0:
        return ref[:, pl.ds(pl.multiple_of(index * share, 128), share)]
    out = ref[:, 0:share]
    for q in range(1, count):
        out = jnp.where(index == q, ref[:, q * share : (q + 1) * share], out)
    return out


def dispatch_kernel(n_ep, n_tp, routes_hbm, logits_hbm, hidden_hbm, gain_hbm, *refs):
    outs = refs[: n_ep - 4]
    pick_ref, combine_ref, hidden_ref, gain_ref, routes_ref, logits_ref, sems = refs[n_ep - 4 :]
    me = lax.axis_index("ep")
    part = lax.axis_index("tp")
    tokens, width = hidden_ref.shape
    share = width // n_tp
    step = 512 if width % 512 == 0 else width
    starts = range(0, width, step)
    small = [
        pltpu.make_async_copy(routes_hbm, routes_ref, sems.at[0]),
        pltpu.make_async_copy(logits_hbm, logits_ref, sems.at[1]),
        pltpu.make_async_copy(gain_hbm, gain_ref.at[0], sems.at[2]),
    ]
    large = [
        pltpu.make_async_copy(
            hidden_hbm.at[:, c : c + step], hidden_ref.at[:, c : c + step], sems.at[3 + i]
        )
        for i, c in enumerate(starts)
    ]
    for copy in small + large:
        copy.start()
    small[0].wait()
    small[1].wait()
    routes = routes_ref[...]
    affinity = jax.nn.sigmoid(logits_ref[...])
    weight = ROUTE_SCALE * affinity / jnp.sum(affinity, axis=0, keepdims=True)
    weight = weight.astype(BF16).astype(F32)
    expert = lax.broadcasted_iota(jnp.int32, (n_ep, tokens), 0) ^ me
    hit = jnp.zeros((n_ep, tokens), F32)
    gain_of = jnp.zeros((n_ep, tokens), F32)
    for k in range(routes.shape[0]):
        same = routes[k : k + 1, :] == expert
        hit = jnp.where(same, 1.0, hit)
        gain_of = jnp.where(same, weight[k : k + 1, :], gain_of)
    earlier = lax.broadcasted_iota(jnp.int32, (tokens, tokens), 0) < lax.broadcasted_iota(
        jnp.int32, (tokens, tokens), 1
    )
    rank = jnp.dot(hit.astype(BF16), earlier.astype(F32).astype(BF16), preferred_element_type=F32)
    rank = jnp.where(hit > 0, rank, -1.0)
    place = lax.broadcasted_iota(jnp.int32, (CAP, tokens), 0).astype(F32)
    for d in range(n_ep):
        match = rank[d : d + 1, :] == place
        rows = slice(d * CAP, (d + 1) * CAP)
        pick_ref[rows, :] = jnp.where(match, 1.0, 0.0).astype(BF16)
        combine_ref[rows, :] = jnp.where(match, gain_of[d : d + 1, :], 0.0).astype(BF16)
    pick = pick_ref[4 * CAP :, :]
    square = jnp.zeros((pick.shape[0], 1), F32)
    middle = len(large) // 2
    for i, c in enumerate(starts):
        if i == 0 or i == middle:
            for copy in large[:middle] if i < middle else large[i:]:
                copy.wait()
        got = jnp.dot(pick, hidden_ref[:, c : c + step], preferred_element_type=F32)
        square = square + jnp.sum(got * got, axis=1, keepdims=True)
    small[2].wait()
    scale = lax.rsqrt(square / width + EPS)
    got = jnp.dot(pick, columns_of(hidden_ref, part, n_tp, share), preferred_element_type=F32)
    rows = (got * scale * columns_of(gain_ref, part, n_tp, share)).astype(BF16)
    for i, out in enumerate(outs):
        out[...] = rows[i * CAP : (i + 1) * CAP]


def near_kernel(n_tp, _, pick_ref, hidden_ref, gain_ref, own_ref, core_ref, near_ref):
    share = hidden_ref.shape[1] // n_tp
    got = jnp.dot(pick_ref[: 4 * CAP, :], hidden_ref[...], preferred_element_type=F32)
    scale = lax.rsqrt(jnp.mean(got * got, axis=1, keepdims=True) + EPS)
    whole = (got * scale * gain_ref[...]).astype(BF16)
    own_ref[...] = whole[:CAP]
    for q in range(n_tp):
        columns = slice(q * share, (q + 1) * share)
        core_ref[q * CAP : (q + 1) * CAP, :] = whole[CAP : 2 * CAP, columns]
        near_ref[q * CAP : (q + 1) * CAP, :] = whole[2 * CAP : 3 * CAP, columns]
        near_ref[(n_tp + q) * CAP : (n_tp + q + 1) * CAP, :] = whole[3 * CAP :, columns]


def load_kernel(after_ref, *refs):
    count = (len(refs) - 2) // 2
    mark_ref, sems = refs[-2:]
    copies = [
        pltpu.make_async_copy(refs[i], refs[count + i], sems.at[i]) for i in range(count)
    ]
    for copy in copies:
        copy.start()
    mark_ref[...] = jnp.zeros(mark_ref.shape, F32)
    for copy in copies:
        copy.wait()


def first_kernel(n_tp, own_ref, core_ref, near_ref, cross_ref, mine_ref, *refs):
    gate_ref, up_ref, down_ref, _ = refs[:4]
    outs, (gate_sum_ref, up_sum_ref, head_ref) = refs[4 : n_tp + 4], refs[n_tp + 4 :]
    part = lax.axis_index("tp")
    share = mine_ref.shape[1]
    head_ref[:CAP, :] = own_ref[...]
    for i, ref in enumerate((core_ref, near_ref, cross_ref)):
        for q in range(n_tp):
            rows = slice((i + 1) * CAP, (i + 2) * CAP)
            head_ref[rows, q * share : (q + 1) * share] = ref[q * CAP : (q + 1) * CAP, :]
    depth = pl.ds(pl.multiple_of(part * share, CAP), share)
    gate, upper = (
        jnp.dot(head_ref[...], ref[...], preferred_element_type=F32) for ref in (gate_ref, up_ref)
    )
    for weight_ref, sum_ref in zip((gate_ref, up_ref), (gate_sum_ref, up_sum_ref)):
        sum_ref[...] = jnp.dot(mine_ref[...], weight_ref[depth, :], preferred_element_type=F32)
    inner = (gate / (1.0 + jnp.exp(-gate)) * upper).astype(BF16)
    for d in range(n_tp):
        down = columns_of(down_ref, part ^ d, n_tp, share)
        outs[d][...] = jnp.dot(inner, down, preferred_element_type=F32).astype(BF16)


def expert_kernel(n_tp, *refs):
    rows = refs[: n_tp - 1]
    gate_ref, up_ref, down_ref, gate_sum_ref, up_sum_ref = refs[n_tp - 1 : n_tp + 4]
    outs = refs[n_tp + 4 :]
    part = lax.axis_index("tp")
    share = rows[0].shape[1]
    gate = gate_sum_ref[...]
    upper = up_sum_ref[...]
    for d, ref in zip(partners(n_tp), rows):
        value = ref[...]
        depth = pl.ds(pl.multiple_of((part ^ d) * share, CAP), share)
        gate = gate + jnp.dot(value, gate_ref[depth, :], preferred_element_type=F32)
        upper = upper + jnp.dot(value, up_ref[depth, :], preferred_element_type=F32)
    far = (gate / (1.0 + jnp.exp(-gate)) * upper).astype(BF16)
    count = far.shape[0]
    groups = [
        far[start : start + CAP]
        for at in range(0, count // 2, CAP)
        for start in (at, count // 2 + at)
    ]
    inner = jnp.concatenate(groups, axis=0)
    for d in range(n_tp):
        down = columns_of(down_ref, part ^ d, n_tp, share)
        outs[d][...] = jnp.dot(inner, down, preferred_element_type=F32).astype(BF16)


def sum_kernel(n_tp, *refs):
    parts, outs = refs[:n_tp], refs[n_tp:]
    at = 0
    for out in outs:
        rows = slice(at, at + out.shape[0])
        total = parts[0][rows, :].astype(F32)
        for other in parts[1:]:
            total = total + other[rows, :].astype(F32)
        out[...] = total.astype(BF16)
        at += out.shape[0]


def seats_kernel(
    n_tp,
    seat_cap,
    owners_ref,
    positions_ref,
    combine_ref,
    hidden_ref,
    rows_ref,
    mix_ref,
    at_ref,
):
    part = lax.axis_index("tp")
    tokens, width = hidden_ref.shape
    source_rows = tokens // n_tp
    owners = owners_ref[...] ^ part
    owner = lax.broadcasted_iota(jnp.int32, (n_tp, tokens), 0)
    hot = jnp.where(owners == owner, 1.0, 0.0)
    first = lax.broadcasted_iota(jnp.int32, (tokens, tokens), 0)
    second = lax.broadcasted_iota(jnp.int32, (tokens, tokens), 1)
    earlier = jnp.where((first < second) & (first // source_rows == second // source_rows), 1.0, 0.0)
    before = jnp.dot(hot.astype(BF16), earlier.astype(BF16), preferred_element_type=F32)
    seat = jnp.sum(before * hot, axis=0, keepdims=True).astype(jnp.int32)
    source = lax.broadcasted_iota(jnp.int32, (1, tokens), 1) // source_rows
    code = owners * (n_tp * seat_cap) + source * seat_cap + seat
    seats = n_tp * seat_cap
    held = lax.broadcasted_iota(jnp.int32, (n_tp * seats, tokens), 0) == code
    pick = jnp.where(held, 1.0, 0.0).astype(BF16)
    mix_ref[...] = lax.dot_general(
        pick, combine_ref[...], (((1,), (1,)), ((), ())), preferred_element_type=F32
    ).astype(BF16)
    place = jnp.where(held[:seats], positions_ref[...].astype(F32), 0.0)
    at_ref[...] = jnp.sum(place, axis=1, keepdims=True)
    hidden = columns_of(hidden_ref, part, n_tp, width // n_tp)
    rows_ref[...] = jnp.dot(pick, hidden, preferred_element_type=F32).astype(BF16)


def state_kernel(mix_ref, rows_ref, *refs):
    pieces, (out_ref, back_ref) = refs[:4], refs[4:]
    for d, piece in enumerate(pieces):
        back_ref[d * CAP : (d + 1) * CAP, :] = piece[...]
    mixed = jnp.dot(mix_ref[:, : 4 * CAP], back_ref[...], preferred_element_type=F32)
    out_ref[...] = rows_ref[...].astype(F32) + mixed


def cache_kernel(n_z, n_tp, cache_width, *refs):
    far, core_ref = refs[: n_z - 2], refs[n_z - 2]
    mix_ref, state_ref, gain_ref, weight_ref = refs[n_z - 1 : n_z + 3]
    outs, back_ref = refs[n_z + 3 : n_z + 3 + n_tp], refs[n_z + 3 + n_tp]
    for d in range(n_z - 2):
        at = 2 * d * CAP
        back_ref[at : at + CAP, :] = far[d][:CAP, :]
        back_ref[at + CAP : at + 2 * CAP, :] = core_ref[d * CAP : (d + 1) * CAP, :]
    mixed = jnp.dot(mix_ref[:, 4 * CAP :], back_ref[...], preferred_element_type=F32)
    state = state_ref[...] + mixed
    square = jnp.sum(state * state, axis=1, keepdims=True)
    scaled = (state * gain_ref[...]).astype(BF16)
    value = lax.dot_general(
        scaled, weight_ref[...], (((1,), (1,)), ((), ())), preferred_element_type=F32
    ).astype(BF16)
    high = square.astype(BF16).astype(F32)
    rest = square - high
    middle = rest.astype(BF16).astype(F32)
    low = rest - middle
    seats, wide = outs[0].shape
    lane = lax.broadcasted_iota(jnp.int32, (square.shape[0], wide - cache_width), 1)
    extra = jnp.where(lane == 0, high, jnp.where(lane == 1, middle, jnp.where(lane == 2, low, 0.0)))
    extra = extra.astype(BF16)
    for d in range(n_tp):
        outs[d][:, :cache_width] = value[d * seats : (d + 1) * seats]
        outs[d][:, cache_width:] = extra[d * seats : (d + 1) * seats]


def finish_kernel(n_tp, width, rank_width, *refs):
    parts = refs[:n_tp]
    gain_ref, cos_ref, sin_ref, latent_ref, rotary_ref = refs[n_tp:]
    total = parts[0][...].astype(F32)
    for other in parts[1:]:
        total = total + other[...].astype(F32)
    half = cos_ref.shape[1]
    cache_width = rank_width + 2 * half
    square = jnp.sum(total[:, cache_width : cache_width + 3], axis=1, keepdims=True)
    cache = total[:, :cache_width] * lax.rsqrt(square / width + EPS)
    latent = cache[:, :rank_width]
    scale = lax.rsqrt(jnp.mean(latent * latent, axis=1, keepdims=True) + EPS)
    latent_ref[...] = (latent * scale * gain_ref[...]).astype(BF16)
    first = cache[:, rank_width : rank_width + half]
    second = cache[:, rank_width + half :]
    cosine, sine = cos_ref[...], sin_ref[...]
    rotary_ref[:, :half] = (first * cosine - second * sine).astype(BF16)
    rotary_ref[:, half:] = (second * cosine + first * sine).astype(BF16)


def call(kernel, out_shape, args, scratch=(), flops=0, hbm=()):
    moved = sum(a.size * a.dtype.itemsize for a in args)
    vmem = pl.BlockSpec(memory_space=pltpu.VMEM)
    args = [
        pltpu.with_memory_space_constraint(a, pltpu.HBM) if i in hbm else a
        for i, a in enumerate(args)
    ]
    return pl.pallas_call(
        kernel,
        out_shape=out_shape,
        in_specs=[
            pl.BlockSpec(memory_space=pltpu.HBM) if i in hbm else vmem for i in range(len(args))
        ],
        out_specs=[vmem] * len(out_shape),
        scratch_shapes=list(scratch),
        compiler_params=pltpu.CompilerParams(vmem_limit_bytes=VMEM_LIMIT),
        cost_estimate=pl.CostEstimate(flops=flops, bytes_accessed=moved, transcendentals=0),
    )(*args)


def swap(value, axis, d):
    return lax.ppermute(value, axis, [(i, i ^ d) for i in range(lax.axis_size(axis))])


def partners(n_tp):
    return [*reversed(range(1, n_tp - 1)), n_tp - 1]


def spread(value, n_tp):
    return [swap(value, "tp", d) for d in partners(n_tp)]


def collect(values):
    return [swap(values[d], "tp", d) for d in reversed(range(1, len(values)))] + [values[0]]


def on_device(
    hidden,
    moe_gain,
    route_logits,
    routes,
    gate_weight,
    up_weight,
    down_weight,
    attn_gain,
    latent_weight,
    latent_gain,
    positions,
    owners,
):
    n_ep = lax.axis_size("ep")
    n_tp = lax.axis_size("tp")
    n_z = n_ep // 2
    tokens, width = hidden.shape
    share = width // n_tp
    ff = gate_weight.shape[2]
    slots = n_ep * CAP
    seat_cap = max(2, tokens // n_tp // 4)
    seats = n_tp * seat_cap
    rank_width = latent_gain.shape[0]
    cache_width = latent_weight.shape[1]
    half = (cache_width - rank_width) // 2
    wide = (cache_width + 3 + 127) // 128 * 128
    struct = jax.ShapeDtypeStruct
    chunks = width // 512 if width % 512 == 0 else 1

    *outgoing, pick, combine, hidden, gain = call(
        functools.partial(dispatch_kernel, n_ep, n_tp),
        [struct((CAP, share), BF16)] * (n_ep - 4)
        + [struct((slots, tokens), BF16)] * 2
        + [struct(hidden.shape, BF16), struct((1, width), F32)],
        (routes.T, route_logits.T, hidden, moe_gain),
        [
            pltpu.VMEM(routes.T.shape, jnp.int32),
            pltpu.VMEM(routes.T.shape, F32),
            pltpu.SemaphoreType.DMA((3 + chunks,)),
        ],
        flops=2 * slots * tokens * width,
        hbm=(0, 1, 2, 3),
    )
    order = [*range(4, n_ep, 2), *range(5, n_ep, 2)]
    arrived = [swap(outgoing[d - 4], "ep", d) for d in order]
    own, to_core, to_near = call(
        functools.partial(near_kernel, n_tp),
        [struct((CAP, width), BF16), struct((n_tp * CAP, share), BF16)]
        + [struct((2 * n_tp * CAP, share), BF16)],
        (arrived[0], pick, hidden, gain),
        flops=8 * CAP * tokens * width,
    )
    near = swap(to_near[: n_tp * CAP], "ep", 2)
    near_crossed = swap(to_near[n_tp * CAP :], "ep", 3)
    from_core = swap(to_core, "ep", 1)
    gate_w, up_w, down_w = gate_weight[0], up_weight[0], down_weight[0]
    *loaded, mark = call(
        load_kernel,
        [struct(w.shape, BF16) for w in (gate_w, up_w, down_w)] + [struct((8, 128), F32)],
        (combine, gate_w, up_w, down_w),
        [pltpu.SemaphoreType.DMA((3,))],
        hbm=(1, 2, 3),
    )
    arrived, from_core = lax.optimization_barrier((arrived, from_core))
    mine = jnp.concatenate(arrived, axis=0)
    shares = spread(mine, n_tp)
    near_rows, far_rows = 4 * CAP, slots - 4 * CAP
    *near_pieces, gate_sum, up_sum = call(
        functools.partial(first_kernel, n_tp),
        [struct((near_rows, share), BF16)] * n_tp + [struct((far_rows, ff), F32)] * 2,
        (own, from_core, near, near_crossed, mine, *loaded, mark),
        [pltpu.VMEM((4 * CAP, width), BF16)],
        flops=2 * slots * width * ff,
    )
    terms = call(
        functools.partial(expert_kernel, n_tp),
        [struct((far_rows, share), BF16)] * n_tp,
        (*shares, *loaded, gate_sum, up_sum),
        flops=2 * slots * width * ff * 3,
    )
    terms = list(terms)
    combine, terms[0] = lax.optimization_barrier((combine, terms[0]))
    rows, mix, at = call(
        functools.partial(seats_kernel, n_tp, seat_cap),
        [
            struct((n_tp * seats, share), BF16),
            struct((n_tp * seats, slots), BF16),
            struct((seats, 1), F32),
        ],
        (owners[None, :], positions[None, :], combine, hidden),
        flops=2 * n_tp * seats * tokens * (share + slots),
    )
    freqs = ROPE_BASE ** (-jnp.arange(half, dtype=F32) / half)
    angles = at * freqs[None, :]
    cosine, sine = jnp.cos(angles), jnp.sin(angles)

    far_terms = collect(terms)
    near_far = swap(near_pieces[n_tp - 1], "tp", n_tp - 1)
    near_far, rows, mix, *near_rest = lax.optimization_barrier(
        (near_far, rows, mix, *near_pieces[1 : n_tp - 1])
    )
    near_terms = [near_far, near_pieces[0]]
    near_terms += [swap(near_rest[d - 1], "tp", d) for d in reversed(range(1, n_tp - 1))]
    far_done = call(
        functools.partial(sum_kernel, n_tp),
        [struct((2 * CAP, share), BF16)] * (n_z - 2),
        far_terms,
    )
    far_back = [swap(far_done[d - 2], "ep", 2 * d) for d in range(2, n_z)]
    near_done = call(
        functools.partial(sum_kernel, n_tp), [struct((CAP, share), BF16)] * 4, near_terms
    )
    near_back = [near_done[0]] + [swap(near_done[d], "ep", d) for d in (1, 2, 3)]
    crossed = swap(jnp.concatenate([piece[CAP:] for piece in far_back], axis=0), "ep", 1)
    (state,) = call(
        state_kernel,
        [struct((n_tp * seats, share), F32)],
        (mix, rows, *near_back),
        [pltpu.VMEM((4 * CAP, share), BF16)],
        flops=8 * n_tp * seats * share * CAP,
    )
    partial = call(
        functools.partial(cache_kernel, n_z, n_tp, cache_width),
        [struct((seats, wide), BF16)] * n_tp,
        (*far_back, crossed, mix, state, attn_gain[None, :], latent_weight.T),
        [pltpu.VMEM((slots - 4 * CAP, share), BF16)],
        flops=2 * n_tp * seats * share * (slots + cache_width),
    )
    return tuple(
        call(
            functools.partial(finish_kernel, n_tp, width, rank_width),
            [struct((seats, rank_width), BF16), struct((seats, 2 * half), BF16)],
            (*collect(partial), latent_gain[None, :], cosine, sine),
        )
    )


def solution(mesh):
    placed = (
        P(("groups", "ep"), None),
        P(),
        P(("groups", "ep"), None),
        P(("groups", "ep"), None),
        P("ep", None, "tp"),
        P("ep", None, "tp"),
        P("ep", "tp", None),
        P("tp"),
        P("tp", None),
        P(),
        P(("groups", "ep")),
        P(("groups", "ep")),
    )
    return jax.shard_map(
        on_device,
        mesh=mesh,
        in_specs=placed,
        out_specs=(P(("groups", "ep", "tp"), None), P(("groups", "ep", "tp"), None)),
        check_vma=False,
    )
```

```python
import functools

import jax
import jax.numpy as jnp
from jax import lax
from jax.experimental import pallas as pl
from jax.experimental.pallas import tpu as pltpu
from jax.sharding import PartitionSpec as P

CAP = 16
EPS = 1e-06
ROUTE_SCALE = 2.5
ROPE_BASE = 10000.0
BF16 = jnp.bfloat16
F32 = jnp.float32
VMEM_LIMIT = 40 * 1024 * 1024


def columns_of(ref, index, count, share):
    if share % 128 == 0:
        return ref[:, pl.ds(pl.multiple_of(index * share, 128), share)]
    out = ref[:, 0:share]
    for q in range(1, count):
        out = jnp.where(index == q, ref[:, q * share : (q + 1) * share], out)
    return out


def dispatch_kernel(n_ep, n_tp, routes_hbm, logits_hbm, hidden_hbm, gain_hbm, *refs):
    outs = refs[: n_ep - 4]
    pick_ref, combine_ref, hidden_ref, gain_ref, routes_ref, logits_ref, sems = refs[n_ep - 4 :]
    me = lax.axis_index("ep")
    part = lax.axis_index("tp")
    tokens, width = hidden_ref.shape
    share = width // n_tp
    step = 512 if width % 512 == 0 else width
    starts = range(0, width, step)
    small = [
        pltpu.make_async_copy(routes_hbm, routes_ref, sems.at[0]),
        pltpu.make_async_copy(logits_hbm, logits_ref, sems.at[1]),
        pltpu.make_async_copy(gain_hbm, gain_ref.at[0], sems.at[2]),
    ]
    large = [
        pltpu.make_async_copy(
            hidden_hbm.at[:, c : c + step], hidden_ref.at[:, c : c + step], sems.at[3 + i]
        )
        for i, c in enumerate(starts)
    ]
    for copy in small + large:
        copy.start()
    small[0].wait()
    small[1].wait()
    routes = routes_ref[...]
    affinity = jax.nn.sigmoid(logits_ref[...])
    weight = ROUTE_SCALE * affinity / jnp.sum(affinity, axis=0, keepdims=True)
    weight = weight.astype(BF16).astype(F32)
    expert = lax.broadcasted_iota(jnp.int32, (n_ep, tokens), 0) ^ me
    hit = jnp.zeros((n_ep, tokens), F32)
    gain_of = jnp.zeros((n_ep, tokens), F32)
    for k in range(routes.shape[0]):
        same = routes[k : k + 1, :] == expert
        hit = jnp.where(same, 1.0, hit)
        gain_of = jnp.where(same, weight[k : k + 1, :], gain_of)
    earlier = lax.broadcasted_iota(jnp.int32, (tokens, tokens), 0) < lax.broadcasted_iota(
        jnp.int32, (tokens, tokens), 1
    )
    rank = jnp.dot(hit.astype(BF16), earlier.astype(F32).astype(BF16), preferred_element_type=F32)
    rank = jnp.where(hit > 0, rank, -1.0)
    place = lax.broadcasted_iota(jnp.int32, (CAP, tokens), 0).astype(F32)
    for d in range(n_ep):
        match = rank[d : d + 1, :] == place
        rows = slice(d * CAP, (d + 1) * CAP)
        pick_ref[rows, :] = jnp.where(match, 1.0, 0.0).astype(BF16)
        combine_ref[rows, :] = jnp.where(match, gain_of[d : d + 1, :], 0.0).astype(BF16)
    pick = pick_ref[4 * CAP :, :]
    square = jnp.zeros((pick.shape[0], 1), F32)
    middle = len(large) // 2
    for i, c in enumerate(starts):
        if i == 0 or i == middle:
            for copy in large[:middle] if i < middle else large[i:]:
                copy.wait()
        got = jnp.dot(pick, hidden_ref[:, c : c + step], preferred_element_type=F32)
        square = square + jnp.sum(got * got, axis=1, keepdims=True)
    small[2].wait()
    scale = lax.rsqrt(square / width + EPS)
    got = jnp.dot(pick, columns_of(hidden_ref, part, n_tp, share), preferred_element_type=F32)
    rows = (got * scale * columns_of(gain_ref, part, n_tp, share)).astype(BF16)
    for i, out in enumerate(outs):
        out[...] = rows[i * CAP : (i + 1) * CAP]


def near_kernel(n_tp, pick_ref, hidden_ref, gain_ref, own_ref, core_ref, near_ref):
    share = hidden_ref.shape[1] // n_tp
    got = jnp.dot(pick_ref[: 4 * CAP, :], hidden_ref[...], preferred_element_type=F32)
    scale = lax.rsqrt(jnp.mean(got * got, axis=1, keepdims=True) + EPS)
    whole = (got * scale * gain_ref[...]).astype(BF16)
    own_ref[...] = whole[:CAP]
    for q in range(n_tp):
        columns = slice(q * share, (q + 1) * share)
        core_ref[q * CAP : (q + 1) * CAP, :] = whole[CAP : 2 * CAP, columns]
        near_ref[q * CAP : (q + 1) * CAP, :] = whole[2 * CAP : 3 * CAP, columns]
        near_ref[(n_tp + q) * CAP : (n_tp + q + 1) * CAP, :] = whole[3 * CAP :, columns]


def load_kernel(after_ref, *refs):
    count = (len(refs) - 2) // 2
    mark_ref, sems = refs[-2:]
    copies = [
        pltpu.make_async_copy(refs[i], refs[count + i], sems.at[i]) for i in range(count)
    ]
    for copy in copies:
        copy.start()
    mark_ref[...] = jnp.zeros(mark_ref.shape, F32)
    for copy in copies:
        copy.wait()


def first_kernel(n_tp, own_ref, core_ref, near_ref, cross_ref, mine_ref, *refs):
    gate_ref, up_ref, down_ref, _ = refs[:4]
    outs, (gate_sum_ref, up_sum_ref, head_ref) = refs[4 : n_tp + 4], refs[n_tp + 4 :]
    part = lax.axis_index("tp")
    share = mine_ref.shape[1]
    head_ref[:CAP, :] = own_ref[...]
    for i, ref in enumerate((core_ref, near_ref, cross_ref)):
        for q in range(n_tp):
            rows = slice((i + 1) * CAP, (i + 2) * CAP)
            head_ref[rows, q * share : (q + 1) * share] = ref[q * CAP : (q + 1) * CAP, :]
    depth = pl.ds(pl.multiple_of(part * share, CAP), share)
    gate, upper = (
        jnp.dot(head_ref[...], ref[...], preferred_element_type=F32) for ref in (gate_ref, up_ref)
    )
    for weight_ref, sum_ref in zip((gate_ref, up_ref), (gate_sum_ref, up_sum_ref)):
        sum_ref[...] = jnp.dot(mine_ref[...], weight_ref[depth, :], preferred_element_type=F32)
    inner = (gate / (1.0 + jnp.exp(-gate)) * upper).astype(BF16)
    for d in range(n_tp):
        down = columns_of(down_ref, part ^ d, n_tp, share)
        outs[d][...] = jnp.dot(inner, down, preferred_element_type=F32).astype(BF16)


def expert_kernel(n_tp, *refs):
    rows = refs[: n_tp - 1]
    gate_ref, up_ref, down_ref, gate_sum_ref, up_sum_ref = refs[n_tp - 1 : n_tp + 4]
    outs = refs[n_tp + 4 :]
    part = lax.axis_index("tp")
    share = rows[0].shape[1]
    gate = gate_sum_ref[...]
    upper = up_sum_ref[...]
    for d in range(1, n_tp):
        value = rows[n_tp - 1 - d][...]
        depth = pl.ds(pl.multiple_of((part ^ d) * share, CAP), share)
        gate = gate + jnp.dot(value, gate_ref[depth, :], preferred_element_type=F32)
        upper = upper + jnp.dot(value, up_ref[depth, :], preferred_element_type=F32)
    far = (gate / (1.0 + jnp.exp(-gate)) * upper).astype(BF16)
    count = far.shape[0]
    groups = [
        far[start : start + CAP]
        for at in range(0, count // 2, CAP)
        for start in (at, count // 2 + at)
    ]
    inner = jnp.concatenate(groups, axis=0)
    for d in range(n_tp):
        down = columns_of(down_ref, part ^ d, n_tp, share)
        outs[d][...] = jnp.dot(inner, down, preferred_element_type=F32).astype(BF16)


def sum_kernel(n_tp, *refs):
    parts, outs = refs[:n_tp], refs[n_tp:]
    at = 0
    for out in outs:
        rows = slice(at, at + out.shape[0])
        total = parts[0][rows, :].astype(F32)
        for other in parts[1:]:
            total = total + other[rows, :].astype(F32)
        out[...] = total.astype(BF16)
        at += out.shape[0]


def seats_kernel(
    n_tp,
    seat_cap,
    owners_ref,
    positions_ref,
    combine_ref,
    hidden_ref,
    rows_ref,
    mix_ref,
    at_ref,
):
    part = lax.axis_index("tp")
    tokens, width = hidden_ref.shape
    source_rows = tokens // n_tp
    owners = owners_ref[...] ^ part
    owner = lax.broadcasted_iota(jnp.int32, (n_tp, tokens), 0)
    hot = jnp.where(owners == owner, 1.0, 0.0)
    first = lax.broadcasted_iota(jnp.int32, (tokens, tokens), 0)
    second = lax.broadcasted_iota(jnp.int32, (tokens, tokens), 1)
    earlier = jnp.where((first < second) & (first // source_rows == second // source_rows), 1.0, 0.0)
    before = jnp.dot(hot.astype(BF16), earlier.astype(BF16), preferred_element_type=F32)
    seat = jnp.sum(before * hot, axis=0, keepdims=True).astype(jnp.int32)
    source = lax.broadcasted_iota(jnp.int32, (1, tokens), 1) // source_rows
    code = owners * (n_tp * seat_cap) + source * seat_cap + seat
    seats = n_tp * seat_cap
    held = lax.broadcasted_iota(jnp.int32, (n_tp * seats, tokens), 0) == code
    pick = jnp.where(held, 1.0, 0.0).astype(BF16)
    mix_ref[...] = lax.dot_general(
        pick, combine_ref[...], (((1,), (1,)), ((), ())), preferred_element_type=F32
    ).astype(BF16)
    place = jnp.where(held[:seats], positions_ref[...].astype(F32), 0.0)
    at_ref[...] = jnp.sum(place, axis=1, keepdims=True)
    hidden = columns_of(hidden_ref, part, n_tp, width // n_tp)
    rows_ref[...] = jnp.dot(pick, hidden, preferred_element_type=F32).astype(BF16)


def cache_kernel(n_z, n_tp, cache_width, *refs):
    near, far, core_ref = refs[:4], refs[4 : n_z + 2], refs[n_z + 2]
    mix_ref, rows_ref, gain_ref, weight_ref = refs[n_z + 3 : n_z + 7]
    outs, back_ref = refs[n_z + 7 : n_z + 7 + n_tp], refs[n_z + 7 + n_tp]
    for d in range(4):
        back_ref[d * CAP : (d + 1) * CAP, :] = near[d][...]
    for d in range(n_z - 2):
        at = (2 * d + 4) * CAP
        back_ref[at : at + CAP, :] = far[d][:CAP, :]
        last = (n_z - 3 - d) * CAP
        back_ref[at + CAP : at + 2 * CAP, :] = core_ref[last : last + CAP, :]
    mixed = jnp.dot(mix_ref[...], back_ref[...], preferred_element_type=F32)
    state = rows_ref[...].astype(F32) + mixed
    square = jnp.sum(state * state, axis=1, keepdims=True)
    scaled = (state * gain_ref[...]).astype(BF16)
    value = lax.dot_general(
        scaled, weight_ref[...], (((1,), (1,)), ((), ())), preferred_element_type=F32
    ).astype(BF16)
    high = square.astype(BF16).astype(F32)
    rest = square - high
    middle = rest.astype(BF16).astype(F32)
    low = rest - middle
    seats, wide = outs[0].shape
    lane = lax.broadcasted_iota(jnp.int32, (square.shape[0], wide - cache_width), 1)
    extra = jnp.where(lane == 0, high, jnp.where(lane == 1, middle, jnp.where(lane == 2, low, 0.0)))
    extra = extra.astype(BF16)
    for d in range(n_tp):
        outs[d][:, :cache_width] = value[d * seats : (d + 1) * seats]
        outs[d][:, cache_width:] = extra[d * seats : (d + 1) * seats]


def finish_kernel(n_tp, width, rank_width, *refs):
    parts = refs[:n_tp]
    gain_ref, cos_ref, sin_ref, latent_ref, rotary_ref = refs[n_tp:]
    total = parts[0][...].astype(F32)
    for other in parts[1:]:
        total = total + other[...].astype(F32)
    half = cos_ref.shape[1]
    cache_width = rank_width + 2 * half
    square = jnp.sum(total[:, cache_width : cache_width + 3], axis=1, keepdims=True)
    cache = total[:, :cache_width] * lax.rsqrt(square / width + EPS)
    latent = cache[:, :rank_width]
    scale = lax.rsqrt(jnp.mean(latent * latent, axis=1, keepdims=True) + EPS)
    latent_ref[...] = (latent * scale * gain_ref[...]).astype(BF16)
    first = cache[:, rank_width : rank_width + half]
    second = cache[:, rank_width + half :]
    cosine, sine = cos_ref[...], sin_ref[...]
    rotary_ref[:, :half] = (first * cosine - second * sine).astype(BF16)
    rotary_ref[:, half:] = (second * cosine + first * sine).astype(BF16)


def call(kernel, out_shape, args, scratch=(), flops=0, hbm=()):
    moved = sum(a.size * a.dtype.itemsize for a in args)
    vmem = pl.BlockSpec(memory_space=pltpu.VMEM)
    args = [
        pltpu.with_memory_space_constraint(a, pltpu.HBM) if i in hbm else a
        for i, a in enumerate(args)
    ]
    return pl.pallas_call(
        kernel,
        out_shape=out_shape,
        in_specs=[
            pl.BlockSpec(memory_space=pltpu.HBM) if i in hbm else vmem for i in range(len(args))
        ],
        out_specs=[vmem] * len(out_shape),
        scratch_shapes=list(scratch),
        compiler_params=pltpu.CompilerParams(vmem_limit_bytes=VMEM_LIMIT),
        cost_estimate=pl.CostEstimate(flops=flops, bytes_accessed=moved, transcendentals=0),
    )(*args)


def swap(value, axis, d):
    return lax.ppermute(value, axis, [(i, i ^ d) for i in range(lax.axis_size(axis))])


def spread(value, n_tp):
    return [swap(value, "tp", d) for d in reversed(range(1, n_tp))]


def collect(values):
    return [swap(values[d], "tp", d) for d in reversed(range(1, len(values)))] + [values[0]]


def on_device(
    hidden,
    moe_gain,
    route_logits,
    routes,
    gate_weight,
    up_weight,
    down_weight,
    attn_gain,
    latent_weight,
    latent_gain,
    positions,
    owners,
):
    n_ep = lax.axis_size("ep")
    n_tp = lax.axis_size("tp")
    n_z = n_ep // 2
    tokens, width = hidden.shape
    share = width // n_tp
    ff = gate_weight.shape[2]
    slots = n_ep * CAP
    seat_cap = max(2, tokens // n_tp // 4)
    seats = n_tp * seat_cap
    rank_width = latent_gain.shape[0]
    cache_width = latent_weight.shape[1]
    half = (cache_width - rank_width) // 2
    wide = (cache_width + 3 + 127) // 128 * 128
    struct = jax.ShapeDtypeStruct
    chunks = width // 512 if width % 512 == 0 else 1

    *outgoing, pick, combine, hidden, gain = call(
        functools.partial(dispatch_kernel, n_ep, n_tp),
        [struct((CAP, share), BF16)] * (n_ep - 4)
        + [struct((slots, tokens), BF16)] * 2
        + [struct(hidden.shape, BF16), struct((1, width), F32)],
        (routes.T, route_logits.T, hidden, moe_gain),
        [
            pltpu.VMEM(routes.T.shape, jnp.int32),
            pltpu.VMEM(routes.T.shape, F32),
            pltpu.SemaphoreType.DMA((3 + chunks,)),
        ],
        flops=2 * slots * tokens * width,
        hbm=(0, 1, 2, 3),
    )
    own, to_core, to_near = call(
        functools.partial(near_kernel, n_tp),
        [struct((CAP, width), BF16), struct((n_tp * CAP, share), BF16)]
        + [struct((2 * n_tp * CAP, share), BF16)],
        (pick, hidden, gain),
        flops=8 * CAP * tokens * width,
    )
    order = [*range(4, n_ep, 2), *range(5, n_ep, 2)]
    arrived = [swap(outgoing[d - 4], "ep", d) for d in order]
    near = swap(to_near[: n_tp * CAP], "ep", 2)
    near_crossed = swap(to_near[n_tp * CAP :], "ep", 3)
    from_core = swap(to_core, "ep", 1)
    gate_w, up_w, down_w = gate_weight[0], up_weight[0], down_weight[0]
    *loaded, mark = call(
        load_kernel,
        [struct(w.shape, BF16) for w in (gate_w, up_w, down_w)] + [struct((8, 128), F32)],
        (combine, gate_w, up_w, down_w),
        [pltpu.SemaphoreType.DMA((3,))],
        hbm=(1, 2, 3),
    )
    arrived, from_core = lax.optimization_barrier((arrived, from_core))
    mine = jnp.concatenate(arrived, axis=0)
    shares = spread(mine, n_tp)
    near_rows, far_rows = 4 * CAP, slots - 4 * CAP
    *near_pieces, gate_sum, up_sum = call(
        functools.partial(first_kernel, n_tp),
        [struct((near_rows, share), BF16)] * n_tp + [struct((far_rows, ff), F32)] * 2,
        (own, from_core, near, near_crossed, mine, *loaded, mark),
        [pltpu.VMEM((4 * CAP, width), BF16)],
        flops=2 * slots * width * ff,
    )
    combine, gate_sum = lax.optimization_barrier((combine, gate_sum))
    rows, mix, at = call(
        functools.partial(seats_kernel, n_tp, seat_cap),
        [
            struct((n_tp * seats, share), BF16),
            struct((n_tp * seats, slots), BF16),
            struct((seats, 1), F32),
        ],
        (owners[None, :], positions[None, :], combine, hidden),
        flops=2 * n_tp * seats * tokens * (share + slots),
    )
    up_sum, rows, mix = lax.optimization_barrier((up_sum, rows, mix))
    terms = call(
        functools.partial(expert_kernel, n_tp),
        [struct((far_rows, share), BF16)] * n_tp,
        (*shares, *loaded, gate_sum, up_sum),
        flops=2 * slots * width * ff * 3,
    )
    terms = list(terms)
    freqs = ROPE_BASE ** (-jnp.arange(half, dtype=F32) / half)
    angles = at * freqs[None, :]
    cosine, sine = jnp.cos(angles), jnp.sin(angles)

    far_terms = collect(terms)
    near_terms = collect(near_pieces)
    far_done = call(
        functools.partial(sum_kernel, n_tp),
        [struct((2 * CAP, share), BF16)] * (n_z - 2),
        far_terms,
    )
    far_back = [swap(far_done[d - 2], "ep", 2 * d) for d in range(2, n_z)]
    near_done = call(
        functools.partial(sum_kernel, n_tp), [struct((CAP, share), BF16)] * 4, near_terms
    )
    near_back = [near_done[0]] + [swap(near_done[d], "ep", d) for d in (1, 2, 3)]
    crossed = swap(jnp.concatenate([piece[CAP:] for piece in far_back[::-1]], axis=0), "ep", 1)
    partial = call(
        functools.partial(cache_kernel, n_z, n_tp, cache_width),
        [struct((seats, wide), BF16)] * n_tp,
        (*near_back, *far_back, crossed, mix, rows, attn_gain[None, :], latent_weight.T),
        [pltpu.VMEM((slots, share), BF16)],
        flops=2 * n_tp * seats * share * (slots + cache_width),
    )
    return tuple(
        call(
            functools.partial(finish_kernel, n_tp, width, rank_width),
            [struct((seats, rank_width), BF16), struct((seats, 2 * half), BF16)],
            (*collect(partial), latent_gain[None, :], cosine, sine),
        )
    )


def solution(mesh):
    placed = (
        P(("groups", "ep"), None),
        P(),
        P(("groups", "ep"), None),
        P(("groups", "ep"), None),
        P("ep", None, "tp"),
        P("ep", None, "tp"),
        P("ep", "tp", None),
        P("tp"),
        P("tp", None),
        P(),
        P(("groups", "ep")),
        P(("groups", "ep")),
    )
    return jax.shard_map(
        on_device,
        mesh=mesh,
        in_specs=placed,
        out_specs=(P(("groups", "ep", "tp"), None), P(("groups", "ep", "tp"), None)),
        check_vma=False,
    )
```
